32 devices in a mesh: wide: 8 (over z, y), narrow: 4 (over x, core).
Axes of the slice: x: 2, y: 2, z: 4, core: 2. Of those that a mesh axis runs over, the one named last changes fastest.
Arguments:
- images: float32 [3, 64, 1024], P(None, ('wide', 'narrow')), may hold values from -0.5 to 0.49
- noise_seeds: int32 [64], P(('wide', 'narrow')), may hold values from 0 to 1073741823
- valid_shape: int32 [64, 2], P(('wide', 'narrow')), may hold values from 11 to 32, as said below
- conv_in: float32 [378, 512], P(None, 'narrow')
- mixer: float32 [3, 512, 512], P(None, None, 'narrow')
- conv_out: float32 [512, 756], P('narrow')
- hidden_bias: float32 [3, 2, 512], P(None, None, 'narrow')
- flow_params: float32 [3852], replicated
- conv_in_first: float32 [378, 512], P(None, 'narrow')
- mixer_first: float32 [3, 512, 512], P(None, None, 'narrow')
- conv_out_first: float32 [512, 756], P('narrow')
- bias_first: float32 [3, 2, 512], P(None, None, 'narrow')
- flow_first: float32 [3852], replicated, may hold values from -0.1 to 0.1
- conv_in_second: float32 [378, 512], P(None, 'narrow'), may hold values from 3.8146972e-08 to 1.5258789e-07
- mixer_second: float32 [3, 512, 512], P(None, None, 'narrow'), may hold values from 3.8146972e-08 to 1.5258789e-07
- conv_out_second: float32 [512, 756], P('narrow'), may hold values from 3.8146972e-08 to 1.5258789e-07
- bias_second: float32 [3, 2, 512], P(None, None, 'narrow'), may hold values from 1.5258789e-07 to 6.1035155e-07
- flow_second: float32 [3852], replicated, may hold values from 0.0004 to 0.0016
Outputs:
- conv_in_new: float32 [378, 512], P(None, 'narrow')
- mixer_new: float32 [3, 512, 512], P(None, None, 'narrow')
- conv_out_new: float32 [512, 756], P('narrow')
- bias_new: float32 [3, 2, 512], P(None, None, 'narrow')
- flow_new: float32 [3852], replicated
- conv_in_moment: float32 [378, 512], P(None, 'narrow')
- mixer_moment: float32 [3, 512, 512], P(None, None, 'narrow')
- conv_out_moment: float32 [512, 756], P('narrow')
- bias_moment: float32 [3, 2, 512], P(None, None, 'narrow')
- flow_moment: float32 [3852], replicated
- conv_in_square: float32 [378, 512], P(None, 'narrow')
- mixer_square: float32 [3, 512, 512], P(None, None, 'narrow')
- conv_out_square: float32 [512, 756], P('narrow')
- bias_square: float32 [3, 2, 512], P(None, None, 'narrow')
- flow_square: float32 [3852], replicated
- conv_in_half: bfloat16 [378, 512], P(None, 'narrow')
- mixer_half: bfloat16 [3, 512, 512], P(None, None, 'narrow')
- conv_out_half: bfloat16 [512, 756], P('narrow')
- weight_norms: float32 [15], replicated
- update_norms: float32 [15], replicated
- loss_sum: float32 [], replicated
- valid_dims: float32 [], replicated
The draws below stay inside these ranges and needn't reach their ends.
Inputs may be any that keep to these rules, and one draw needn't show every extreme that they name: A pixel of image b is valid where its row is under valid_shape[b,0] and its column under valid_shape[b,1].
All inputs are finite; a program needn't handle non-finite values.
Results may differ from the reference program's by a relative error of at most 0.0013.
The reference program's roundings to bfloat16 on the way (of `active_one` and `active_two`) count: a program that leaves them out, or rounds other values in their place, can miss the bound.
Values may be sent and summed in bfloat16 or wider, within the bound.
No kernel may reach another device: no remote copies, remote signals or barrier semaphores. Data moves between devices by JAX's collectives and lax.ppermute only.
A program may use at most 128 MiB of HBM per device.

```python
import math
import jax
import jax.numpy as jnp
from jax import lax

HIDDEN_SIZE = 512
C1 = 12
IMG_SIDE = 32
STEP = 5
IMG_DEV = 8
IMAGES = 64
IMG_LOC = 2
ROWS_IN = 378
COLS_OUT = 756
FLOW = 3852


def rising(length):
    return 0.5 + jnp.arange(length, dtype=jnp.float32) / (length - 1)


def grad_size():
    return 0.05 * (IMAGES * IMG_SIDE * IMG_SIDE) ** (-0.5)


def normal_of(key, shape):
    return jnp.clip(jax.random.normal(key, shape, jnp.float32), -5.0, 5.0)


def draw_valid_shape(key, part):
    device_count = IMAGES // IMG_LOC
    image_index = jnp.arange(IMAGES, dtype=jnp.int32)
    device_index = image_index // IMG_LOC
    low_side = IMG_SIDE * 7 // 16
    baseline = low_side + (IMG_SIDE - low_side) * device_index // max(device_count - 1, 1)
    jitter = jax.random.randint(jax.random.fold_in(key, 11), (IMAGES, 2), 0, 4)
    shaped = baseline[:, None] - jitter
    chosen = (device_count - 1) * IMG_LOC + jax.random.randint(jax.random.fold_in(key, 12), (), 0, IMG_LOC)
    shaped = jnp.where((image_index == chosen)[:, None], IMG_SIDE, shaped)
    shaped = jnp.where((image_index == 0)[:, None], low_side - 3, shaped)
    return shaped.astype(jnp.int32)


def conv_in_scale():
    row_index = jnp.arange(ROWS_IN)
    first_end = 9 * C1 // 2
    fan_in = jnp.where(row_index < first_end, 9 * C1 // 2, jnp.where(row_index < 3 * first_end, 9 * C1, 18 * C1))
    return fan_in.astype(jnp.float32) ** (-0.5)


def draw_conv_in(key, part):
    values = normal_of(jax.random.fold_in(key, 21), (ROWS_IN, HIDDEN_SIZE))
    return values * conv_in_scale()[:, None] * rising(HIDDEN_SIZE)[None, :]


def draw_mixer(key, part):
    values = normal_of(jax.random.fold_in(key, 22), (3, HIDDEN_SIZE, HIDDEN_SIZE))
    return values * HIDDEN_SIZE ** (-0.5) * rising(HIDDEN_SIZE)[None, None, :]


def draw_conv_out(key, part):
    values = normal_of(jax.random.fold_in(key, 23), (HIDDEN_SIZE, COLS_OUT))
    return values * (9 * HIDDEN_SIZE) ** (-0.5) * rising(HIDDEN_SIZE)[:, None]


def draw_hidden_bias(key, part):
    values = normal_of(jax.random.fold_in(key, 24), (3, 2, HIDDEN_SIZE))
    return 0.5 * values * rising(HIDDEN_SIZE)[None, None, :]


def draw_conv_in_first(key, part):
    values = normal_of(jax.random.fold_in(key, 31), (ROWS_IN, HIDDEN_SIZE))
    return grad_size() * values * rising(HIDDEN_SIZE)[None, :]


def draw_mixer_first(key, part):
    values = normal_of(jax.random.fold_in(key, 32), (3, HIDDEN_SIZE, HIDDEN_SIZE))
    return grad_size() * values * rising(HIDDEN_SIZE)[None, None, :]


def draw_conv_out_first(key, part):
    values = normal_of(jax.random.fold_in(key, 33), (HIDDEN_SIZE, COLS_OUT))
    return grad_size() * values * rising(HIDDEN_SIZE)[:, None]


def draw_bias_first(key, part):
    values = normal_of(jax.random.fold_in(key, 34), (3, 2, HIDDEN_SIZE))
    return 2.0 * grad_size() * values * rising(HIDDEN_SIZE)[None, None, :]


def draw_flow_params(key, part):
    pieces = []
    for level_index in range(3):
        channels = C1 * 2 ** level_index
        half = channels // 2
        level_key = jax.random.fold_in(jax.random.fold_in(key, 41), level_index)
        subkeys = jax.random.split(level_key, 7)
        pieces.append(0.2 * normal_of(subkeys[0], (channels,)))
        pieces.append(0.2 * normal_of(subkeys[1], (channels,)))
        spread = jnp.where(jnp.eye(channels) > 0.5, 0.15, 0.3 * channels ** (-0.5))
        pieces.append((normal_of(subkeys[2], (channels, channels)) * spread).reshape(-1))
        pieces.append(0.3 * normal_of(subkeys[3], (channels,)))
        pieces.append(jax.random.uniform(subkeys[4], (channels,), jnp.float32, -0.3, 0.1))
        if level_index == 2:
            pieces.append(0.3 * normal_of(subkeys[5], (2 * channels,)))
        else:
            pieces.append(normal_of(subkeys[5], (half * channels,)) * (0.3 * half ** (-0.5)))
            pieces.append(0.2 * normal_of(subkeys[6], (channels,)))
    return jnp.concatenate(pieces)


def plant(drawn, own_key, least, high):
    longest = drawn.shape.index(max(drawn.shape))
    spots = []
    for shift in (0, 1):
        where = [jax.random.randint(jax.random.fold_in(own_key, axis), (), 0, length) for axis, length in enumerate(drawn.shape)]
        where[longest] = (where[longest] + shift) % drawn.shape[longest]
        spots.append(tuple(where))
    return drawn.at[spots[0]].set(least).at[spots[1]].set(high)


def block_scale(stream_key, shape, cuts, low, largest):
    def one(dim, parts):
        steps = jax.random.uniform(jax.random.fold_in(jax.random.fold_in(stream_key, 6), dim), (parts,), jnp.float32, low / len(cuts), largest / len(cuts))
        return jnp.repeat(jnp.exp(steps), shape[dim] // parts).reshape((-1,) + (1,) * (len(shape) - dim - 1))

    factor_of = one(*cuts[0])
    for cut in cuts[1:]:
        factor_of = factor_of * one(*cut)
    return factor_of


def noise(key, shape, width, most, held_as=jnp.bfloat16):
    return jnp.clip(width * jax.random.normal(key, shape, jnp.float32), -most, most).astype(held_as)


def setup_inputs(seed: int = 0) -> dict:
    key_list = jax.random.split(jax.random.key(seed), 19)
    images = jnp.clip(-0.5 + 0.99 * jax.random.uniform(key_list[0], (3, IMAGES, IMG_SIDE * IMG_SIDE), jnp.float32) ** block_scale(key_list[0], (3, IMAGES, IMG_SIDE * IMG_SIDE), ((1, 32),), -0.2, 0.2), -0.5, 0.49)
    noise_seeds = plant(jax.random.randint(key_list[1], (IMAGES,), 0, 1073741824), jax.random.fold_in(key_list[1], 1), 0, 1073741823).astype(jnp.int32)
    valid_shape = draw_valid_shape(jax.random.fold_in(key_list[18], 71), 0)
    conv_in = draw_conv_in(jax.random.fold_in(key_list[18], 71), 0)
    mixer = draw_mixer(jax.random.fold_in(key_list[18], 71), 0)
    conv_out = draw_conv_out(jax.random.fold_in(key_list[18], 71), 0)
    hidden_bias = draw_hidden_bias(jax.random.fold_in(key_list[18], 71), 0)
    flow_params = draw_flow_params(jax.random.fold_in(key_list[18], 71), 0)
    conv_in_first = draw_conv_in_first(jax.random.fold_in(key_list[18], 71), 0)
    mixer_first = draw_mixer_first(jax.random.fold_in(key_list[18], 71), 0)
    conv_out_first = draw_conv_out_first(jax.random.fold_in(key_list[18], 71), 0)
    bias_first = draw_bias_first(jax.random.fold_in(key_list[18], 71), 0)
    flow_first = noise(key_list[12], (FLOW,), 0.02, 0.1, jnp.float32)
    conv_in_second = jnp.clip(jnp.exp(math.log(1.5258788721439487e-07) - 1.3862944 * jax.random.uniform(key_list[13], (ROWS_IN, HIDDEN_SIZE), jnp.float32) ** block_scale(key_list[13], (ROWS_IN, HIDDEN_SIZE), ((1, 4),), -0.2, 0.2)), 3.814697180359872e-08, 1.5258788721439487e-07)
    mixer_second = jnp.clip(jnp.exp(math.log(1.5258788721439487e-07) - 1.3862944 * jax.random.uniform(key_list[14], (3, HIDDEN_SIZE, HIDDEN_SIZE), jnp.float32) ** block_scale(key_list[14], (3, HIDDEN_SIZE, HIDDEN_SIZE), ((2, 4),), -0.2, 0.2)), 3.814697180359872e-08, 1.5258788721439487e-07)
    conv_out_second = jnp.clip(jnp.exp(math.log(1.5258788721439487e-07) - 1.3862944 * jax.random.uniform(key_list[15], (HIDDEN_SIZE, COLS_OUT), jnp.float32) ** block_scale(key_list[15], (HIDDEN_SIZE, COLS_OUT), ((0, 4),), -0.2, 0.2)), 3.814697180359872e-08, 1.5258788721439487e-07)
    bias_second = jnp.clip(jnp.exp(math.log(6.103515488575795e-07) - 1.3862944 * jax.random.uniform(key_list[16], (3, 2, HIDDEN_SIZE), jnp.float32) ** block_scale(key_list[16], (3, 2, HIDDEN_SIZE), ((2, 4),), -0.2, 0.2)), 1.5258788721439487e-07, 6.103515488575795e-07)
    flow_second = jnp.clip(jnp.exp(jax.random.uniform(key_list[17], (FLOW,), jnp.float32, math.log(0.0004), math.log(0.0016))), 0.0004, 0.0016)
    return {"images": images, "noise_seeds": noise_seeds, "valid_shape": valid_shape, "conv_in": conv_in, "mixer": mixer, "conv_out": conv_out, "hidden_bias": hidden_bias, "flow_params": flow_params, "conv_in_first": conv_in_first, "mixer_first": mixer_first, "conv_out_first": conv_out_first, "bias_first": bias_first, "flow_first": flow_first, "conv_in_second": conv_in_second, "mixer_second": mixer_second, "conv_out_second": conv_out_second, "bias_second": bias_second, "flow_second": flow_second}


HIGHEST_PRECISION = lax.Precision.HIGHEST
LOG_TWO_PI = 1.8378770664093453
LOG_TWO = 0.6931471805599453
FIRST_BETA = 0.5
SECOND_BETA = 0.5
EPSILON = 1e-06
WEIGHT_DECAY = 0.01
LEARN_RATE = 0.25
TAP_OFFSETS = [(-1, -1), (-1, 0), (-1, 1), (0, -1), (0, 0), (0, 1), (1, -1), (1, 0), (1, 1)]

@jax.custom_vjp
def low(v):
    return lax.optimization_barrier(v.astype(jnp.bfloat16)).astype(jnp.float32)

@jax.custom_vjp
def low_back(v):
    return v

def low_keep(v):
    return (low(v), None)

def low_pass(kept, grad):
    return (grad,)

def back_keep(v):
    return (v, None)

def back_low(kept, grad):
    return (low(grad),)
low.defvjp(low_keep, low_pass)
low_back.defvjp(back_keep, back_low)

def noise_field(seed_values, grid_side):
    pixel_count = grid_side * grid_side
    position = jnp.arange(3 * pixel_count, dtype=jnp.int32).reshape(3, 1, pixel_count)
    hashed = seed_values.astype(jnp.int32).reshape(1, -1, 1) + position * jnp.int32(-1640531527)
    hashed = hashed ^ lax.shift_right_logical(hashed, jnp.full_like(hashed, 15))
    hashed = hashed * jnp.int32(739267321)
    hashed = hashed ^ lax.shift_right_logical(hashed, jnp.full_like(hashed, 13))
    return ((hashed & jnp.int32(16777215)).astype(jnp.float32) + 0.5) * 2.0 ** (-24)

def pixel_weights(valid_shape, image_side, level_index):
    block_side = 2 ** level_index
    grid_side = image_side // block_side
    starts = jnp.arange(grid_side, dtype=jnp.int32) * block_side
    row_share = jnp.clip(valid_shape[:, 0:1] - starts[None, :], 0, block_side).astype(jnp.float32) / block_side
    col_share = jnp.clip(valid_shape[:, 1:2] - starts[None, :], 0, block_side).astype(jnp.float32) / block_side
    return (row_share[:, :, None] * col_share[:, None, :]).reshape(1, -1)

def squeeze_grid(values, image_count, grid_side):
    channels = values.shape[0]
    half_side = grid_side // 2
    values = values.reshape(channels, image_count, half_side, 2, half_side, 2).transpose(0, 3, 5, 1, 2, 4)
    return values.reshape(channels * 4, image_count * half_side * half_side)

def tap_sum(values, image_count, grid_side, direction):
    channels = values.shape[0] // 9
    padded = jnp.pad(values.reshape(9, channels, image_count, grid_side, grid_side), ((0, 0), (0, 0), (0, 0), (1, 1), (1, 1)))
    result = jnp.zeros((channels, image_count, grid_side, grid_side), values.dtype)
    for tap_index, (row_step, col_step) in enumerate(TAP_OFFSETS):
        row_start = 1 + direction * row_step
        col_start = 1 + direction * col_step
        result = result + padded[tap_index, :, :, row_start:row_start + grid_side, col_start:col_start + grid_side]
    return result.reshape(channels, -1)

def tap_stack(values, image_count, grid_side, direction):
    channels = values.shape[0]
    padded = jnp.pad(values.reshape(channels, image_count, grid_side, grid_side), ((0, 0), (0, 0), (1, 1), (1, 1)))
    shifted = []
    for row_step, col_step in TAP_OFFSETS:
        row_start = 1 + direction * row_step
        col_start = 1 + direction * col_step
        shifted.append(padded[:, :, row_start:row_start + grid_side, col_start:col_start + grid_side])
    return jnp.stack(shifted, 0).reshape(9 * channels, image_count * grid_side * grid_side)

def row_bounds(base):
    return [0, 9 * base // 2, 27 * base // 2, 63 * base // 2]

def col_bounds(base):
    return [0, 9 * base, 27 * base, 63 * base]

def flow_bounds(base):
    lengths = [5 * base + 3 * base * base // 2, 10 * base + 6 * base * base, 24 * base + 16 * base * base]
    return [0, lengths[0], lengths[0] + lengths[1], lengths[0] + lengths[1] + lengths[2]]

def unpack_level(segment, channels, is_last):
    half = channels // 2
    names = ['bias', 'logs', 'block', 'outbias', 'outscale']
    lengths = [channels, channels, channels * channels, channels, channels]
    if is_last:
        names = names + ['priorbias']
        lengths = lengths + [2 * channels]
    else:
        names = names + ['priormatrix', 'priorbias']
        lengths = lengths + [half * channels, channels]
    pieces = {}
    offset = 0
    for name, length in zip(names, lengths):
        pieces[name] = segment[offset:offset + length]
        offset = offset + length
    pieces['block'] = pieces['block'].reshape(channels, channels)
    if not is_last:
        pieces['priormatrix'] = pieces['priormatrix'].reshape(half, channels)
    return pieces

def mixing_matrix(block):
    channels = block.shape[0]
    lower = jnp.tril(block, -1) + jnp.eye(channels, dtype=block.dtype)
    signs = (1 - 2 * (jnp.arange(channels) % 2)).astype(block.dtype)
    upper = jnp.triu(block, 1) + jnp.diag(signs * jnp.exp(jnp.diagonal(block)))
    return jnp.dot(lower, upper, precision=HIGHEST_PRECISION)[::-1]

def gaussian_log(latent, mean, log_scale):
    return -0.5 * (LOG_TWO_PI + 2.0 * log_scale + (latent - mean) ** 2 * jnp.exp(-2.0 * log_scale))

def level_pre(flow_state, segment, share_total, channels, is_last):
    pieces = unpack_level(segment, channels, is_last)
    normed = (flow_state + pieces['bias'][:, None]) * jnp.exp(pieces['logs'])[:, None]
    mixed = jnp.dot(mixing_matrix(pieces['block']), normed, precision=HIGHEST_PRECISION)
    pre_term = -share_total * (jnp.sum(pieces['logs']) + jnp.sum(jnp.diagonal(pieces['block'])))
    return (mixed[:channels // 2], mixed[channels // 2:], pre_term)

def level_post(first_half, second_half, net_raw, segment, shares, channels, is_last, image_count, grid_side):
    pieces = unpack_level(segment, channels, is_last)
    half = channels // 2
    output = (net_raw + pieces['outbias'][:, None]) * jnp.exp(3.0 * pieces['outscale'])[:, None]
    logit = output[half:] + 2.0
    latent = (second_half + output[:half]) * jax.nn.sigmoid(logit)
    log_det = jnp.sum(shares * jax.nn.log_sigmoid(logit))
    if is_last:
        joined = jnp.concatenate([first_half, latent], 0)
        prior_bias = pieces['priorbias']
        log_prior = jnp.sum(shares * gaussian_log(joined, prior_bias[:channels, None], prior_bias[channels:, None]))
        after = first_half
    else:
        stats = jnp.dot(pieces['priormatrix'].T, first_half, precision=HIGHEST_PRECISION) + pieces['priorbias'][:, None]
        log_prior = jnp.sum(shares * gaussian_log(latent, stats[:half], stats[half:]))
        after = squeeze_grid(first_half, image_count, grid_side)
    return (after, latent, -(log_det + log_prior))

def coupling_net(first_half, rows_in, mix_matrix, rows_out, biases, image_count, grid_side):
    stacked = tap_stack(low(first_half), image_count, grid_side, 1)
    hidden_one = low_back(jnp.dot(low(rows_in).T, stacked, precision=HIGHEST_PRECISION) + biases[0][:, None])
    active_one = low(jax.nn.silu(hidden_one))
    hidden_two = low_back(jnp.dot(low(mix_matrix).T, active_one, precision=HIGHEST_PRECISION) + biases[1][:, None])
    active_two = low(jax.nn.silu(hidden_two))
    spread = jnp.dot(low(rows_out).T, active_two, precision=HIGHEST_PRECISION)
    return low_back(tap_sum(spread, image_count, grid_side, 1))

def group_loss(weights, pixels, valid_shape):
    conv_in, mixer, conv_out, hidden_bias, flow_params = weights
    image_count = valid_shape.shape[0]
    flow_state = squeeze_grid(pixels, image_count, IMG_SIDE)
    row_edges, col_edges, seg_edges = (row_bounds(C1), col_bounds(C1), flow_bounds(C1))
    loss_total = jnp.zeros((), jnp.float32)
    for level_index in range(3):
        channels = C1 * 2 ** level_index
        grid_side = IMG_SIDE // 2 ** (level_index + 1)
        is_last = level_index == 2
        shares = pixel_weights(valid_shape, IMG_SIDE, level_index + 1)
        segment = flow_params[seg_edges[level_index]:seg_edges[level_index + 1]]
        first_half, second_half, pre_term = level_pre(flow_state, segment, jnp.sum(shares), channels, is_last)
        net_raw = coupling_net(first_half, conv_in[row_edges[level_index]:row_edges[level_index + 1]], mixer[level_index], conv_out[:, col_edges[level_index]:col_edges[level_index + 1]], hidden_bias[level_index], image_count, grid_side)
        flow_state, latent, post_term = level_post(first_half, second_half, net_raw, segment, shares, channels, is_last, image_count, grid_side)
        loss_total = loss_total + pre_term + post_term
    return loss_total

def lamb_moments(weight, gradient, first_old, second_old):
    first_new = FIRST_BETA * first_old + (1.0 - FIRST_BETA) * gradient
    second_new = SECOND_BETA * second_old + (1.0 - SECOND_BETA) * gradient * gradient
    update = first_new / (1.0 - FIRST_BETA ** STEP) / (jnp.sqrt(second_new / (1.0 - SECOND_BETA ** STEP)) + EPSILON) + WEIGHT_DECAY * weight
    return (first_new, second_new, update)

def group_squares(arrays, base):
    row_edges, col_edges, seg_edges = (row_bounds(base), col_bounds(base), flow_bounds(base))
    sums = [jnp.sum(arrays[0][row_edges[index]:row_edges[index + 1]] ** 2) for index in range(3)]
    sums = sums + [jnp.sum(arrays[1][index] ** 2) for index in range(3)]
    sums = sums + [jnp.sum(arrays[2][:, col_edges[index]:col_edges[index + 1]] ** 2) for index in range(3)]
    sums = sums + [jnp.sum(arrays[3][index] ** 2) for index in range(3)]
    sums = sums + [jnp.sum(arrays[4][seg_edges[index]:seg_edges[index + 1]] ** 2) for index in range(3)]
    return jnp.stack(sums)

def apply_ratio(weights, updates, ratio, base):
    row_edges, col_edges, seg_edges = (row_bounds(base), col_bounds(base), flow_bounds(base))
    new_in = jnp.concatenate([weights[0][row_edges[index]:row_edges[index + 1]] - LEARN_RATE * ratio[index] * updates[0][row_edges[index]:row_edges[index + 1]] for index in range(3)], 0)
    new_mix = weights[1] - LEARN_RATE * ratio[3:6][:, None, None] * updates[1]
    new_out = jnp.concatenate([weights[2][:, col_edges[index]:col_edges[index + 1]] - LEARN_RATE * ratio[6 + index] * updates[2][:, col_edges[index]:col_edges[index + 1]] for index in range(3)], 1)
    new_bias = weights[3] - LEARN_RATE * ratio[9:12][:, None, None] * updates[3]
    new_flow = jnp.concatenate([weights[4][seg_edges[index]:seg_edges[index + 1]] - LEARN_RATE * ratio[12 + index] * updates[4][seg_edges[index]:seg_edges[index + 1]] for index in range(3)])
    return (new_in, new_mix, new_out, new_bias, new_flow)

def reference(images, noise_seeds, valid_shape, conv_in, mixer, conv_out, hidden_bias, flow_params, conv_in_first, mixer_first, conv_out_first, bias_first, flow_first, conv_in_second, mixer_second, conv_out_second, bias_second, flow_second):
    valid_dims = 3.0 * jnp.sum((valid_shape[:, 0] * valid_shape[:, 1]).astype(jnp.float32))
    group_count = images.shape[1] // IMG_DEV
    pixels = images + noise_field(noise_seeds, IMG_SIDE) / 256.0
    blocks = pixels.reshape(3, group_count, IMG_DEV * IMG_SIDE * IMG_SIDE).transpose(1, 0, 2)
    valid_blocks = valid_shape.reshape(group_count, IMG_DEV, 2)
    weights = (conv_in, mixer, conv_out, hidden_bias, flow_params)
    saved_loss = jax.checkpoint(group_loss)

    def whole_loss(params_now):

        def scan_step(carry_sum, block_data):
            return (carry_sum + saved_loss(params_now, block_data[0], block_data[1]), None)
        result, unused = lax.scan(scan_step, jnp.zeros((), jnp.float32), (blocks, valid_blocks))
        return result
    loss_total, pull_back = jax.vjp(whole_loss, weights)
    gradients = pull_back(1.0 / (valid_dims * LOG_TWO))[0]
    firsts_old = (conv_in_first, mixer_first, conv_out_first, bias_first, flow_first)
    seconds_old = (conv_in_second, mixer_second, conv_out_second, bias_second, flow_second)
    moved = [lamb_moments(weight, gradient, first_old, second_old) for weight, gradient, first_old, second_old in zip(weights, gradients, firsts_old, seconds_old)]
    updates = tuple((entry[2] for entry in moved))
    weight_norms = jnp.sqrt(group_squares(weights, C1))
    update_norms = jnp.sqrt(group_squares(updates, C1))
    fresh = apply_ratio(weights, updates, weight_norms / update_norms, C1)
    loss_sum = loss_total / LOG_TWO + 8.0 * valid_dims
    return (fresh[0], fresh[1], fresh[2], fresh[3], fresh[4], moved[0][0], moved[1][0], moved[2][0], moved[3][0], moved[4][0], moved[0][1], moved[1][1], moved[2][1], moved[3][1], moved[4][1], fresh[0].astype(jnp.bfloat16), fresh[1].astype(jnp.bfloat16), fresh[2].astype(jnp.bfloat16), weight_norms, update_norms, loss_sum, valid_dims)
```

```python
import functools
import jax
import jax.numpy as jnp
from jax import lax
from jax.experimental import pallas as pl
from jax.experimental.pallas import tpu as pltpu
from jax.sharding import PartitionSpec as P

C1 = 12
IMG_SIDE = 32
STEP = 5
HIGHEST_PRECISION = lax.Precision.HIGHEST
LOG_TWO_PI = 1.8378770664093453
LOG_TWO = 0.6931471805599453
FIRST_BETA = 0.5
SECOND_BETA = 0.5
EPSILON = 1e-06
WEIGHT_DECAY = 0.01
LEARN_RATE = 0.25
TAPS = [(-1, -1), (-1, 0), (-1, 1), (0, -1), (0, 0), (0, 1), (1, -1), (1, 0), (1, 1)]
F32 = jnp.float32
BF16 = jnp.bfloat16
HID = 512
LANE = 128
LEVELS = 3
FLOW_ROWS = 32
LOSS_ROW = 31
VMEM_BYTES = 50 * 1024 * 1024


def round_up(value, unit):
    return (value + unit - 1) // unit * unit


def chan(level):
    return C1 * 2**level


def side(level):
    return IMG_SIDE // 2 ** (level + 1)


def real_positions(level, images):
    return images * side(level) ** 2


def positions(level, images):
    return round_up(real_positions(level, images), LANE)


def in_rows(level):
    return 9 * chan(level) // 2


def first_rows(level):
    return round_up(in_rows(level) + 6, 16)


def second_bias_row(level):
    return first_rows(level) - 4


def last_rows(level):
    return round_up(9 * chan(level), 16)


def pack_rows(level):
    return first_rows(level) + HID + last_rows(level)


def flow_lengths():
    return [5 * C1 + 3 * C1 * C1 // 2, 10 * C1 + 6 * C1 * C1, 24 * C1 + 16 * C1 * C1]


def flow_size():
    return sum(flow_lengths())


def flow_offsets(level):
    start = sum(flow_lengths()[:level])
    channels = chan(level)
    offsets = {"bias": start, "logs": start + channels, "block": start + 2 * channels}
    start = start + 2 * channels + channels * channels
    offsets["outbias"] = start
    offsets["outscale"] = start + channels
    start = start + 2 * channels
    if level < LEVELS - 1:
        offsets["priormatrix"] = start
        start = start + channels // 2 * channels
    offsets["priorbias"] = start
    return offsets


def column_names(level):
    channels = chan(level)
    offsets = flow_offsets(level)
    names = [
        ("bias", offsets["bias"]),
        ("logs", offsets["logs"]),
        ("outbias", offsets["outbias"]),
        ("outscale", offsets["outscale"]),
        ("priorbias", offsets["priorbias"]),
    ]
    if level == LEVELS - 1:
        names = names + [("priorscale", offsets["priorbias"] + channels)]
    return names


def exact_dot(first, second):
    return jnp.dot(first, second, precision=HIGHEST_PRECISION, preferred_element_type=F32)


def exact_rows(first, second):
    return lax.dot_general(
        first,
        second,
        (((0,), (0,)), ((), ())),
        precision=HIGHEST_PRECISION,
        preferred_element_type=F32,
    )


def exact_columns(first, second):
    return lax.dot_general(
        first,
        second,
        (((1,), (1,)), ((), ())),
        precision=HIGHEST_PRECISION,
        preferred_element_type=F32,
    )


def plain_dot(first, second):
    return jnp.dot(first, second, preferred_element_type=F32)


def contract_rows(first, second):
    return lax.dot_general(first, second, (((0,), (0,)), ((), ())), preferred_element_type=F32)


def contract_columns(first, second):
    return lax.dot_general(first, second, (((1,), (1,)), ((), ())), preferred_element_type=F32)


def iota(shape, axis):
    return lax.broadcasted_iota(jnp.int32, shape, axis)


def rounded(values):
    return values.astype(BF16).astype(F32)


def split_three(values):
    high = rounded(values)
    rest = values - high
    middle = rounded(rest)
    return [high, middle, rest - middle]


def move_lanes(values, chooser, transposed=False):
    rows = values.shape[0]
    padded = round_up(rows, 8)
    if padded > rows:
        values = jnp.concatenate([values, jnp.zeros((padded - rows, values.shape[1]), F32)], 0)
    pieces = jnp.concatenate(split_three(values), 0).astype(BF16)
    moved = contract_columns(pieces, chooser) if transposed else plain_dot(pieces, chooser)
    moved = moved[:padded] + moved[padded : 2 * padded] + moved[2 * padded :]
    return moved[:rows]


def squeeze_chooser(grid, images):
    count = images * grid * grid
    source = iota((count, count), 0)
    target = iota((count, count), 1)
    shift = grid.bit_length() - 1
    image = lax.shift_right_logical(source, 2 * shift)
    row = lax.shift_right_logical(source, shift) & (grid - 1)
    column = source & (grid - 1)
    half = grid // 2
    place = (
        ((row & 1) * 2 + (column & 1)) * (images * half * half)
        + image * (half * half)
        + lax.shift_right_logical(row, 1) * half
        + lax.shift_right_logical(column, 1)
    )
    return (place == target).astype(F32).astype(BF16)


def order_chooser(channels, stride):
    row = iota((4 * channels, 4 * stride), 0)
    column = iota((4 * channels, 4 * stride), 1)
    return ((row & 3) * stride + lax.shift_right_logical(row, 2) == column).astype(F32)


def squeeze(values, chooser, lanes_out):
    channels, count = values.shape
    moved = move_lanes(values, chooser)
    quarter = count // 4
    stacked = jnp.concatenate([moved[:, k * quarter : (k + 1) * quarter] for k in range(4)], 0)
    ordered = exact_dot(order_chooser(channels, channels), stacked)
    if lanes_out > quarter:
        ordered = jnp.concatenate([ordered, jnp.zeros((4 * channels, lanes_out - quarter), F32)], 1)
    return ordered


def unsqueeze(values, chooser, count):
    channels = values.shape[0] // 4
    quarter = count // 4
    stacked = exact_rows(order_chooser(channels, channels), values)
    laid = jnp.concatenate(
        [stacked[k * channels : (k + 1) * channels, :quarter] for k in range(4)], 1
    )
    return move_lanes(laid, chooser, transposed=True)


def slope_roll(values, step):
    step = step % LANE
    while step:
        part = 16 if step >= 16 else 1 << (step.bit_length() - 1)
        values = pltpu.roll(values, 0, 1, stride=part, stride_axis=0)
        step = step - part
    return values


def flow_block(flat, offset, rows, width):
    padded = round_up(rows, 8)
    start = offset + width * iota((padded, FLOW_ROWS), 0)
    line = lax.shift_right_logical(start, 7)
    column = iota((padded, FLOW_ROWS), 1)
    base = -offset % LANE
    if base:
        flat = pltpu.roll(flat, base, 1)
    here = exact_dot((line == column).astype(F32), flat)
    after = exact_dot((line + 1 == column).astype(F32), flat)
    here = slope_roll(here, -width)
    after = slope_roll(after, -width)
    lane = iota((padded, LANE), 1)
    begin = (offset + width * iota((padded, LANE), 0)) & (LANE - 1)
    chosen = jnp.where(lane + begin < LANE, here, after)
    return chosen[:rows, :width]


def flow_block_back(values, offset, rows, width):
    padded = round_up(rows, 8)
    base = offset % LANE
    over = max(base + width - LANE, 0)
    parts = [values[:, width - over :]] if over else []
    if base > over:
        parts.append(jnp.zeros((rows, base - over), F32))
    parts.append(values[:, : width - over])
    if base + width < LANE:
        parts.append(jnp.zeros((rows, LANE - base - width), F32))
    block = jnp.concatenate(parts, 1)
    if padded > rows:
        block = jnp.concatenate([block, jnp.zeros((padded - rows, LANE), F32)], 0)
    block = slope_roll(block, width)
    lane = iota((padded, LANE), 1)
    begin = (offset + width * iota((padded, LANE), 0)) & (LANE - 1)
    here = jnp.where(lane >= begin, block, 0.0)
    after = jnp.where(lane >= begin, 0.0, block)
    line = lax.shift_right_logical(offset + width * iota((FLOW_ROWS, padded), 1), 7)
    row = iota((FLOW_ROWS, padded), 0)
    return exact_dot((line == row).astype(F32), here) + exact_dot(
        (line + 1 == row).astype(F32), after
    )


def flow_column(turned, offset, length):
    line, begin = offset // LANE, offset % LANE
    if begin + length <= LANE:
        return turned[begin : begin + length, line : line + 1]
    return jnp.concatenate(
        [turned[begin:, line : line + 1], turned[: begin + length - LANE, line + 1 : line + 2]], 0
    )


def flow_column_back(values, offset):
    length = values.shape[0]
    line, begin = offset // LANE, offset % LANE
    lane = iota((LANE, LANE), 1)
    head = min(length, LANE - begin)
    parts = []
    if begin:
        parts.append(jnp.zeros((begin, 1), F32))
    parts.append(values[:head])
    if begin + head < LANE:
        parts.append(jnp.zeros((LANE - begin - head, 1), F32))
    column = jnp.concatenate(parts, 0) if len(parts) > 1 else parts[0]
    term = jnp.where(lane == line, column, 0.0)
    if head < length:
        column = jnp.concatenate([values[head:], jnp.zeros((LANE - length + head, 1), F32)], 0)
        term = term + jnp.where(lane == line + 1, column, 0.0)
    return term


def to_flat_rows(values):
    size = values.shape[0]
    row = values.reshape(1, size)
    row = jnp.concatenate([row, jnp.zeros((1, FLOW_ROWS * LANE - size), F32)], 1)
    return row.reshape(FLOW_ROWS, LANE)


def from_flat_rows(values, size):
    return values.reshape(1, FLOW_ROWS * LANE)[:, :size].reshape(size)


def triangles(block):
    channels = block.shape[0]
    row = iota((channels, channels), 0)
    column = iota((channels, channels), 1)
    signs = (1 - 2 * (row & 1)).astype(F32)
    diagonal = signs * jnp.exp(jnp.where(row == column, block, 0.0))
    lower = jnp.where(row > column, block, jnp.where(row == column, 1.0, 0.0))
    upper = jnp.where(row < column, block, jnp.where(row == column, diagonal, 0.0))
    reverse = (row + column == channels - 1).astype(F32)
    return lower, upper, reverse, diagonal


def tap_masks(level, images):
    grid = side(level)
    count = positions(level, images)
    lane = iota((8, count), 1)
    shift = grid.bit_length() - 1
    row = lax.shift_right_logical(lane, shift) & (grid - 1)
    column = lane & (grid - 1)
    inside = lane < real_positions(level, images)
    masks = {}
    for row_step in (-1, 0, 1):
        for column_step in (-1, 0, 1):
            good = (
                (row + row_step >= 0)
                & (row + row_step < grid)
                & (column + column_step >= 0)
                & (column + column_step < grid)
                & inside
            )
            masks[(row_step, column_step)] = jnp.where(good, 1.0, 0.0)[0:1]
    return masks


def tap_read(values, masks, level, row_step, column_step):
    count = values.shape[1]
    offset = (row_step * side(level) + column_step) % count
    if offset:
        values = pltpu.roll(values, count - offset, 1)
    if (row_step, column_step) != (0, 0):
        values = values * masks[(row_step, column_step)]
    return values


def tap_stack(values, masks, level, direction):
    return [
        tap_read(values, masks, level, direction * row_step, direction * column_step)
        for row_step, column_step in TAPS
    ]


def tap_sum(values, masks, level, direction, channels):
    total = None
    for tap, (row_step, column_step) in enumerate(TAPS):
        term = tap_read(
            values[tap * channels : (tap + 1) * channels],
            masks,
            level,
            direction * row_step,
            direction * column_step,
        )
        total = term if total is None else total + term
    return total


def pack_kernel(conv_in_ref, mixer_ref, conv_out_ref, bias_ref, *out_refs):
    in_start = 0
    out_start = 0
    turned = jnp.concatenate(
        [
            conv_out_ref[...],
            jnp.zeros((LANE, round_up(conv_out_ref.shape[1], LANE) - conv_out_ref.shape[1]), F32),
        ],
        1,
    ).T
    for level in range(LEVELS):
        out_ref = out_refs[level]
        rows, columns = in_rows(level), 9 * chan(level)
        top = first_rows(level)
        ones = split_three(bias_ref[level, 0:1, :])
        twos = split_three(bias_ref[level, 1:2, :])
        gap = second_bias_row(level) - rows - 3
        pieces = [conv_in_ref[in_start : in_start + rows, :]] + ones
        if gap:
            pieces.append(jnp.zeros((gap, LANE), F32))
        pieces = pieces + twos + [jnp.zeros((1, LANE), F32)]
        out_ref[0:top, :] = jnp.concatenate(pieces, 0).astype(BF16)
        out_ref[top : top + HID, :] = mixer_ref[level].astype(BF16)
        tail = turned[out_start : out_start + columns]
        if last_rows(level) > columns:
            tail = jnp.concatenate([tail, jnp.zeros((last_rows(level) - columns, LANE), F32)], 0)
        out_ref[top + HID :, :] = tail.astype(BF16)
        in_start = in_start + rows
        out_start = out_start + columns


def flow_pre_kernel(seed_ref, valid_ref, image_ref, flow_ref, *out_refs):
    images = image_ref.shape[1]
    flat = to_flat_rows(flow_ref[...])
    turned = jnp.concatenate([flat, jnp.zeros((LANE - FLOW_ROWS, LANE), F32)], 0).T
    blocks = IMG_SIDE * IMG_SIDE // 256
    pieces = []
    for image in range(images):
        position = iota((8, IMG_SIDE * IMG_SIDE), 0) * (IMG_SIDE * IMG_SIDE) + iota(
            (8, IMG_SIDE * IMG_SIDE), 1
        )
        hashed = seed_ref[image] + position * jnp.int32(-1640531527)
        hashed = hashed ^ lax.shift_right_logical(hashed, jnp.full_like(hashed, 15))
        hashed = hashed * jnp.int32(739267321)
        hashed = hashed ^ lax.shift_right_logical(hashed, jnp.full_like(hashed, 13))
        field = ((hashed & jnp.int32(16777215)).astype(F32) + 0.5) * 2.0 ** (-24)
        pixel = jnp.concatenate(
            [image_ref[:, image, :], jnp.zeros((5, IMG_SIDE * IMG_SIDE), F32)], 0
        )
        pixel = pixel + field / 256.0
        for block in range(blocks):
            pieces.append(pixel[:, block * 256 : (block + 1) * 256])
    stacked = jnp.concatenate(pieces, 0)
    source = iota((256, 256), 0)
    target = iota((256, 256), 1)
    row = lax.shift_right_logical(source, 5)
    column = source & 31
    place = (
        ((row & 1) * 2 + (column & 1)) * 64
        + lax.shift_right_logical(row, 1) * 16
        + lax.shift_right_logical(column, 1)
    )
    moved = move_lanes(stacked, (place == target).astype(F32).astype(BF16))
    quarters = []
    for k in range(4):
        quarters.append(
            jnp.concatenate(
                [
                    moved[piece * 8 : (piece + 1) * 8, k * 64 : (k + 1) * 64]
                    for piece in range(images * blocks)
                ],
                1,
            )
        )
    state = exact_dot(order_chooser(3, 8), jnp.concatenate(quarters, 0))
    at = 0
    for level in range(LEVELS):
        channels = chan(level)
        grid = side(level)
        count = positions(level, images)
        offsets = flow_offsets(level)
        block = flow_block(flat, offsets["block"], channels, channels)
        names = column_names(level)
        columns = [flow_column(turned, offset, channels) for _, offset in names]
        lane = iota((channels, LANE), 1)
        held = jnp.zeros((channels, LANE), F32)
        for index, column in enumerate(columns):
            held = jnp.where(lane == index, column, held)
        normed = (state + columns[0]) * jnp.exp(columns[1])
        lower, upper, reverse, _ = triangles(block)
        mixing = exact_dot(exact_dot(reverse, lower), upper)
        mixed = exact_dot(mixing, normed)
        lane = iota((8, count), 1)
        shift = grid.bit_length() - 1
        image = lax.shift_right_logical(lane, 2 * shift)
        row = lax.shift_right_logical(lane, shift) & (grid - 1)
        column = lane & (grid - 1)
        high = jnp.zeros((8, count), jnp.int32)
        wide = jnp.zeros((8, count), jnp.int32)
        for index in range(images):
            high = jnp.where(image == index, valid_ref[index, 0], high)
            wide = jnp.where(image == index, valid_ref[index, 1], wide)
        unit = 2 ** (level + 1)
        row_share = jnp.clip(high - row * unit, 0, unit).astype(F32) / unit
        column_share = jnp.clip(wide - column * unit, 0, unit).astype(F32) / unit
        share = jnp.where(image < images, row_share * column_share, 0.0)
        normed_ref, mixed_ref, share_ref, held_ref, block_ref = out_refs[at : at + 5]
        at = at + 5
        normed_ref[...] = normed
        mixed_ref[...] = mixed
        share_ref[...] = share
        held_ref[...] = held
        block_ref[...] = jnp.concatenate(
            [block, jnp.zeros((channels, LANE - channels), F32)], 1
        )
        if level < LEVELS - 1:
            prior = flow_block(flat, offsets["priormatrix"], channels // 2, channels)
            out_refs[at][...] = jnp.concatenate(
                [prior, jnp.zeros((channels // 2, LANE - channels), F32)], 1
            )
            at = at + 1
            state = squeeze(
                mixed[: channels // 2], squeeze_chooser(grid, images), positions(level + 1, images)
            )


def silu_parts(values):
    sigmoid = 1.0 / (1.0 + jnp.exp(-values))
    active = values * sigmoid
    slope = sigmoid + active * (1.0 - sigmoid)
    return active, slope


def net_kernel(level, images, narrow, *refs):
    is_last = level == LEVELS - 1
    index_ref = refs[0]
    weight_refs = refs[1 : 1 + narrow]
    mixed_ref, share_ref, held_ref = refs[1 + narrow : 4 + narrow]
    at = 4 + narrow
    prior_ref = None
    if not is_last:
        prior_ref = refs[at]
        at = at + 1
    keep_ref, send_ref, grad_ref, small_ref = refs[at : at + 4]
    at = at + 4
    prior_grad_ref = None
    if not is_last:
        prior_grad_ref = refs[at]
        at = at + 1
    order_ref, slope_one_ref, slope_two_ref, one_ref, two_ref = refs[at:]
    me = index_ref[0]
    channels = chan(level)
    half = channels // 2
    count = positions(level, images)
    top, rows = first_rows(level), in_rows(level)
    tail, used = last_rows(level), 9 * channels
    masks = tap_masks(level, images)
    width = HID // narrow

    def weights(start, length):
        return jnp.concatenate([ref[start : start + length, :] for ref in weight_refs], 1)

    for r_in in range(narrow):
        start = pl.multiple_of(top + (me ^ r_in) * width, 16)
        for r_out in range(narrow):
            order_ref[r_in * width : (r_in + 1) * width, r_out * LANE : (r_out + 1) * LANE] = (
                weight_refs[r_out][pl.ds(start, width), :]
            )
    weight_in = weights(0, top)
    weight_mix = order_ref[...]
    weight_out = weights(top + HID, tail)
    first = mixed_ref[0:half, :]
    second = mixed_ref[half:channels, :]
    share = share_ref[0:1, :]
    pieces = tap_stack(rounded(first), masks, level, 1)
    pieces.append(jnp.ones((3, count), F32))
    pieces.append(jnp.zeros((top - rows - 3, count), F32))
    stacked = jnp.concatenate(pieces, 0).astype(BF16)
    pick = jnp.where(
        (iota((16, count), 0) >= 12) & (iota((16, count), 0) < 15), 1.0, 0.0
    ).astype(BF16)
    hidden_one = contract_rows(weight_in, stacked)
    active, slope = silu_parts(hidden_one)
    slope_one_ref[...] = slope
    one_ref[...] = active.astype(BF16)
    hidden_two = contract_rows(weight_mix, one_ref[...]) + contract_rows(weights(top - 16, 16), pick)
    active, slope = silu_parts(hidden_two)
    slope_two_ref[...] = slope
    two_ref[...] = active.astype(BF16)
    spread = plain_dot(weight_out, two_ref[...])
    net_raw = tap_sum(spread, masks, level, 1, channels)
    held = held_ref[...]
    out_bias, out_scale = held[:, 2:3], held[:, 3:4]
    growth = jnp.exp(3.0 * out_scale)
    output = (net_raw + out_bias) * growth
    logit = output[half:] + 2.0
    sigmoid = 1.0 / (1.0 + jnp.exp(-logit))
    latent = (second + output[:half]) * sigmoid
    log_sigmoid = jnp.minimum(logit, 0.0) - jnp.log1p(jnp.exp(-jnp.abs(logit)))
    if is_last:
        joined = jnp.concatenate([first, latent], 0)
        mean, scale = held[:, 4:5], held[:, 5:6]
        mean = jnp.broadcast_to(mean, joined.shape)
        scale = jnp.broadcast_to(scale, joined.shape)
    else:
        joined = latent
        prior = prior_ref[...][:, :channels]
        stats = exact_rows(prior, first) + held[:, 4:5]
        mean, scale = stats[:half], stats[half:]
    gap = joined - mean
    shrink = jnp.exp(-2.0 * scale)
    square = gap * gap * shrink
    log_prior = -0.5 * (LOG_TWO_PI + 2.0 * scale + square)
    total = jnp.sum(jnp.sum(share * log_sigmoid, 0, keepdims=True), 1, keepdims=True) + jnp.sum(
        jnp.sum(share * log_prior, 0, keepdims=True), 1, keepdims=True
    )
    logs_total = jnp.sum(held[:, 1:2], 0, keepdims=True)
    share_total = jnp.sum(share, 1, keepdims=True)
    grad_joined = share * (gap * shrink)
    grad_scale = share * (1.0 - square)
    grad_latent = grad_joined[half:] if is_last else grad_joined
    grad_logit = (grad_latent * latent - share) * (1.0 - sigmoid)
    grad_second = grad_latent * sigmoid
    grad_output = jnp.concatenate([grad_second, grad_logit], 0)
    grad_net = grad_output * growth
    lane = iota((channels, LANE), 1)
    small = jnp.zeros((channels, LANE), F32)

    def put(small, index, values):
        return jnp.where(lane == index, jnp.sum(values, 1, keepdims=True), small)

    small = put(small, 2, grad_net)
    small = put(small, 3, 3.0 * grad_output * output)
    if is_last:
        small = put(small, 4, -grad_joined)
        small = put(small, 5, grad_scale)
        grad_first = grad_joined[:half]
    else:
        grad_stats = jnp.concatenate([-grad_joined, grad_scale], 0)
        small = put(small, 4, grad_stats)
        grad_first = exact_dot(prior, grad_stats)
        prior_grad = exact_columns(first, grad_stats)
        prior_grad_ref[...] = jnp.concatenate(
            [prior_grad, jnp.zeros((half, LANE - channels), F32)], 1
        )
    small = jnp.where(lane == 6, -total, small)
    small = jnp.where(lane == 7, share_total, small)
    small_ref[...] = small
    pieces = tap_stack(rounded(grad_net), masks, level, -1)
    if tail > used:
        pieces.append(jnp.zeros((tail - used, count), F32))
    grad_spread = jnp.concatenate(pieces, 0).astype(BF16)

    def store(start, values):
        for r in range(narrow):
            ref = send_ref if r & 1 else keep_ref
            ref[r // 2, start : start + values.shape[0], :] = values[:, r * LANE : (r + 1) * LANE]

    store(top + HID, contract_columns(grad_spread, two_ref[...]))
    grad_two = (contract_rows(weight_out, grad_spread) * slope_two_ref[...]).astype(BF16)
    grad_mix = contract_columns(one_ref[...], grad_two)
    for r_in in range(narrow):
        start = pl.multiple_of(top + (me ^ r_in) * width, 16)
        for r_out in range(narrow):
            ref = send_ref if r_out & 1 else keep_ref
            ref[r_out // 2, pl.ds(start, width), :] = grad_mix[
                r_in * width : (r_in + 1) * width, r_out * LANE : (r_out + 1) * LANE
            ]
    grad_one = (plain_dot(weight_mix, grad_two) * slope_one_ref[...]).astype(BF16)
    grad_in = contract_columns(stacked, grad_one)
    store(0, grad_in[: top - 16])
    store(top - 16, grad_in[top - 16 :] + contract_columns(pick, grad_two))
    grad_stack = plain_dot(weight_in, grad_one)
    grad_first = grad_first + tap_sum(grad_stack, masks, level, -1, half)
    grad_ref[...] = jnp.concatenate([grad_first, grad_second], 0)


def flow_post_kernel(images, *refs):
    count_ref = refs[0]
    out_ref = refs[-1]
    at = 1
    per_level = []
    for level in range(LEVELS):
        number = 5 if level == LEVELS - 1 else 6
        per_level.append(refs[at : at + number])
        at = at + number
    turned = jnp.zeros((LANE, LANE), F32)
    flat = jnp.zeros((FLOW_ROWS, LANE), F32)
    loss = jnp.zeros((1, 1), F32)
    carried = None
    for level in (2, 1, 0):
        channels = chan(level)
        half = channels // 2
        grad_ref, normed_ref, held_ref, block_ref, small_ref = per_level[level][:5]
        offsets = flow_offsets(level)
        grad = grad_ref[...]
        if carried is not None:
            grad = grad + jnp.concatenate([carried, jnp.zeros_like(carried)], 0)
        normed = normed_ref[...]
        held = held_ref[...]
        small = small_ref[...]
        block = block_ref[...][:, :channels]
        lower, upper, reverse, diagonal = triangles(block)
        mixing_left = exact_dot(reverse, lower)
        grad_normed = exact_rows(exact_dot(mixing_left, upper), grad)
        grad_mixing = exact_dot(reverse, exact_columns(grad, normed))
        grad_lower = exact_columns(grad_mixing, upper)
        grad_upper = exact_rows(lower, grad_mixing)
        share_total = small[0:1, 7:8]
        row = iota((channels, channels), 0)
        column = iota((channels, channels), 1)
        grad_block = jnp.where(
            row > column,
            grad_lower,
            jnp.where(row < column, grad_upper, grad_upper * diagonal - share_total),
        )
        growth = jnp.exp(held[:, 1:2])
        grad_state = grad_normed * growth
        grad_bias = jnp.sum(grad_state, 1, keepdims=True)
        grad_logs = jnp.sum(grad_normed * normed, 1, keepdims=True) - share_total
        flat = flat + flow_block_back(grad_block, offsets["block"], channels, channels)
        for index, (name, offset) in enumerate(column_names(level)):
            if name == "bias":
                values = grad_bias
            elif name == "logs":
                values = grad_logs
            else:
                values = small[:, index : index + 1]
            turned = turned + flow_column_back(values, offset)
        if level < LEVELS - 1:
            flat = flat + flow_block_back(
                per_level[level][5][...][:, :channels], offsets["priormatrix"], half, channels
            )
        logs_total = jnp.sum(held[:, 1:2], 0, keepdims=True)
        trace = jnp.sum(
            jnp.sum(jnp.where(row == column, block, 0.0), 0, keepdims=True), 1, keepdims=True
        )
        loss = loss + small[0:1, 6:7] - share_total * (logs_total + trace)
        if level > 0:
            grid = side(level - 1)
            carried = unsqueeze(
                grad_state, squeeze_chooser(grid, images), images * grid * grid
            )
    flat = flat + turned.T[:FLOW_ROWS]
    pixels = jnp.zeros((), F32)
    for index in range(images):
        pixels = pixels + (count_ref[index, 0] * count_ref[index, 1]).astype(F32)
    row = iota((FLOW_ROWS, LANE), 0)
    lane = iota((FLOW_ROWS, LANE), 1)
    flat = jnp.where((row == LOSS_ROW) & (lane == 0), loss, flat)
    flat = jnp.where((row == LOSS_ROW) & (lane == 1), pixels, flat)
    out_ref[...] = flat


def moments(weight, gradient, first_old, second_old):
    first_new = FIRST_BETA * first_old + (1.0 - FIRST_BETA) * gradient
    second_new = SECOND_BETA * second_old + (1.0 - SECOND_BETA) * gradient * gradient
    update = (
        first_new
        / (1.0 - FIRST_BETA**STEP)
        / (jnp.sqrt(second_new / (1.0 - SECOND_BETA**STEP)) + EPSILON)
        + WEIGHT_DECAY * weight
    )
    return first_new, second_new, update


def total_of(values):
    return jnp.sum(jnp.sum(values, 0, keepdims=True), 1, keepdims=True)


def squares_rows(sums):
    row = iota((16, LANE), 0)
    held = jnp.zeros((16, LANE), F32)
    for index, value in enumerate(sums):
        held = jnp.where(row == index, value, held)
    return held


def group_totals(values_in, values_mix, values_out, values_bias):
    row = iota(values_in.shape, 0)
    lane = iota(values_out.shape, 1)
    sums = []
    start = 0
    for level in range(LEVELS):
        inside = (row >= start) & (row < start + in_rows(level))
        sums.append(total_of(jnp.where(inside, values_in, 0.0)))
        start = start + in_rows(level)
    for level in range(LEVELS):
        sums.append(total_of(values_mix[level]))
    start = 0
    for level in range(LEVELS):
        inside = (lane >= start) & (lane < start + 9 * chan(level))
        sums.append(total_of(jnp.where(inside, values_out, 0.0)))
        start = start + 9 * chan(level)
    for level in range(LEVELS):
        sums.append(total_of(values_bias[2 * level : 2 * level + 2]))
    return sums


def flow_masks():
    place = iota((FLOW_ROWS, LANE), 0) * LANE + iota((FLOW_ROWS, LANE), 1)
    masks = []
    start = 0
    for length in flow_lengths():
        masks.append((place >= start) & (place < start + length))
        start = start + length
    return masks


def moment_kernel(
    grad_refs_and_rest_count,
    *refs,
):
    grads = refs[:3]
    flow_grad_ref = refs[3]
    weight_in, weight_mix, weight_out, weight_bias = refs[4:8]
    first_in, first_mix, first_out, first_bias = refs[8:12]
    second_in, second_mix, second_out, second_bias = refs[12:16]
    outs = refs[16:]
    total = flow_grad_ref[LOSS_ROW : LOSS_ROW + 1, :]
    valid_dims = 3.0 * total[:, 1:2]
    scale = 1.0 / (valid_dims * LOG_TWO)
    grad_in = jnp.concatenate([grads[level][0 : in_rows(level), :] for level in range(LEVELS)], 0)
    columns = weight_out.shape[1]
    tails = [
        grads[level][first_rows(level) + HID : first_rows(level) + HID + 9 * chan(level), :]
        for level in range(LEVELS)
    ]
    tails.append(jnp.zeros((round_up(columns, LANE) - columns, LANE), F32))
    grad_out = jnp.concatenate(tails, 0).T[:, :columns]
    bias_rows = []
    for level in range(LEVELS):
        bias_rows.append(grads[level][in_rows(level) : in_rows(level) + 1, :])
        bias_rows.append(grads[level][second_bias_row(level) : second_bias_row(level) + 1, :])
    grad_bias = jnp.concatenate(bias_rows, 0)
    bias = weight_bias[...].reshape(2 * LEVELS, LANE)
    new_in = moments(weight_in[...], grad_in * scale, first_in[...], second_in[...])
    new_out = moments(weight_out[...], grad_out * scale, first_out[...], second_out[...])
    new_bias = moments(
        bias,
        grad_bias * scale,
        first_bias[...].reshape(2 * LEVELS, LANE),
        second_bias[...].reshape(2 * LEVELS, LANE),
    )
    mix_squares = []
    mix_updates = []
    for level in range(LEVELS):
        top = first_rows(level)
        new_mix = moments(
            weight_mix[level],
            grads[level][top : top + HID, :] * scale,
            first_mix[level],
            second_mix[level],
        )
        outs[1][level] = new_mix[0]
        outs[5][level] = new_mix[1]
        outs[9][level] = new_mix[2]
        mix_squares.append(weight_mix[level] * weight_mix[level])
        mix_updates.append(new_mix[2] * new_mix[2])
    for index, values in ((0, new_in), (2, new_out), (3, new_bias)):
        for kind in range(3):
            value = values[kind]
            if index == 3:
                value = value.reshape(LEVELS, 2, LANE)
            outs[4 * kind + index][...] = value
    weight_sums = group_totals(
        weight_in[...] * weight_in[...], mix_squares, weight_out[...] * weight_out[...], bias * bias
    )
    update_sums = group_totals(
        new_in[2] * new_in[2], mix_updates, new_out[2] * new_out[2], new_bias[2] * new_bias[2]
    )
    lane = iota((16, LANE), 1)
    outs[12][...] = jnp.where(lane == 0, squares_rows(weight_sums), squares_rows(update_sums))


def apply_kernel(*refs):
    sums_ref, flow_grad_ref = refs[0:2]
    weight_in, weight_mix, weight_out, weight_bias = refs[2:6]
    update_in, update_mix, update_out, update_bias = refs[6:10]
    flow_ref, flow_first_ref, flow_second_ref = refs[10:13]
    (
        new_in,
        new_mix,
        new_out,
        new_bias,
        new_flow,
        half_in,
        half_mix,
        half_out,
        flow_moment,
        flow_square,
        norm_ref,
    ) = refs[13:]
    total = flow_grad_ref[LOSS_ROW : LOSS_ROW + 1, :]
    valid_dims = 3.0 * total[:, 1:2]
    scale = 1.0 / (valid_dims * LOG_TWO)
    flow = to_flat_rows(flow_ref[...])
    size = flow_ref.shape[0]
    place = iota((FLOW_ROWS, LANE), 0) * LANE + iota((FLOW_ROWS, LANE), 1)
    flow_grad = jnp.where(place < size, flow_grad_ref[...] * scale, 0.0)
    first_new, second_new, update = moments(
        flow, flow_grad, to_flat_rows(flow_first_ref[...]), to_flat_rows(flow_second_ref[...])
    )
    sums = sums_ref[...]
    weight_norms = [jnp.sqrt(sums[index : index + 1, 0:1]) for index in range(12)]
    update_norms = [jnp.sqrt(sums[index : index + 1, 1:2]) for index in range(12)]
    masks = flow_masks()
    for mask in masks:
        weight_norms.append(jnp.sqrt(total_of(jnp.where(mask, flow * flow, 0.0))))
        update_norms.append(jnp.sqrt(total_of(jnp.where(mask, update * update, 0.0))))
    rates = [
        LEARN_RATE * (weight_norm / update_norm)
        for weight_norm, update_norm in zip(weight_norms, update_norms)
    ]
    rate = jnp.zeros((FLOW_ROWS, LANE), F32)
    for mask, value in zip(masks, rates[12:]):
        rate = jnp.where(mask, value, rate)
    new_flow[...] = from_flat_rows(flow - rate * update, size)
    flow_moment[...] = from_flat_rows(first_new, size)
    flow_square[...] = from_flat_rows(second_new, size)
    row = iota(weight_in.shape, 0)
    edge_one, edge_two = in_rows(0), in_rows(0) + in_rows(1)
    rate = jnp.where(row < edge_one, rates[0], jnp.where(row < edge_two, rates[1], rates[2]))
    fresh = weight_in[...] - rate * update_in[...]
    new_in[...] = fresh
    half_in[...] = fresh.astype(BF16)
    for level in range(LEVELS):
        fresh = weight_mix[level] - rates[3 + level] * update_mix[level]
        new_mix[level] = fresh
        half_mix[level] = fresh.astype(BF16)
    lane = iota(weight_out.shape, 1)
    edge_one, edge_two = 9 * chan(0), 9 * chan(0) + 9 * chan(1)
    rate = jnp.where(lane < edge_one, rates[6], jnp.where(lane < edge_two, rates[7], rates[8]))
    fresh = weight_out[...] - rate * update_out[...]
    new_out[...] = fresh
    half_out[...] = fresh.astype(BF16)
    for level in range(LEVELS):
        new_bias[level] = weight_bias[level] - rates[9 + level] * update_bias[level]
    lane = iota((8, LANE), 1)
    row = iota((8, LANE), 0)
    held = jnp.zeros((8, LANE), F32)
    for index in range(15):
        held = jnp.where((row == 0) & (lane == index), weight_norms[index], held)
        held = jnp.where((row == 1) & (lane == index), update_norms[index], held)
    loss_sum = total[:, 0:1] / LOG_TWO + 8.0 * valid_dims
    held = jnp.where((row == 2) & (lane == 0), loss_sum, held)
    held = jnp.where((row == 2) & (lane == 1), valid_dims, held)
    norm_ref[...] = held


def spec_vmem():
    return pl.BlockSpec(memory_space=pltpu.VMEM)


def spec_smem():
    return pl.BlockSpec(memory_space=pltpu.SMEM)


def call(kernel, outs, scalars, arrays, scratch=(), name=None):
    return pl.pallas_call(
        kernel,
        out_shape=tuple(jax.ShapeDtypeStruct(shape, dtype) for shape, dtype in outs),
        in_specs=[spec_smem()] * len(scalars) + [spec_vmem()] * len(arrays),
        out_specs=tuple(spec_vmem() for _ in outs),
        scratch_shapes=list(scratch),
        compiler_params=pltpu.CompilerParams(vmem_limit_bytes=VMEM_BYTES),
        name=name,
    )(*scalars, *arrays)


def run_pack(conv_in, mixer, conv_out, hidden_bias):
    outs = [((pack_rows(level), LANE), BF16) for level in range(LEVELS)]
    return call(pack_kernel, outs, (), (conv_in, mixer, conv_out, hidden_bias), name="pack")


def run_flow_pre(noise_seeds, valid_shape, images, flow_params):
    count = images.shape[1]
    outs = []
    for level in range(LEVELS):
        channels = chan(level)
        places = positions(level, count)
        outs = outs + [
            ((channels, places), F32),
            ((channels, places), F32),
            ((8, places), F32),
            ((channels, LANE), F32),
            ((channels, LANE), F32),
        ]
        if level < LEVELS - 1:
            outs.append(((channels // 2, LANE), F32))
    flat = call(
        flow_pre_kernel, outs, (noise_seeds, valid_shape), (images, flow_params), name="flow_pre"
    )
    grouped = []
    at = 0
    for level in range(LEVELS):
        number = 6 if level < LEVELS - 1 else 5
        grouped.append(flat[at : at + number])
        at = at + number
    return grouped


def run_net(level, images, index, weights, pre):
    narrow = len(weights)
    channels = chan(level)
    count = positions(level, images)
    outs = [
        ((narrow // 2, pack_rows(level), LANE), F32),
        ((narrow // 2, pack_rows(level), LANE), F32),
        ((channels, count), F32),
        ((channels, LANE), F32),
    ]
    arrays = list(weights) + [pre[1], pre[2], pre[3]]
    if level < LEVELS - 1:
        arrays.append(pre[5])
        outs.append(((channels // 2, LANE), F32))
    scratch = [
        pltpu.VMEM((HID, HID), BF16),
        pltpu.VMEM((HID, count), F32),
        pltpu.VMEM((HID, count), F32),
        pltpu.VMEM((HID, count), BF16),
        pltpu.VMEM((HID, count), BF16),
    ]
    return call(
        functools.partial(net_kernel, level, images, narrow),
        outs,
        (index,),
        arrays,
        scratch,
        name="net_%d" % (level + 1),
    )


def run_flow_post(images, valid_shape, pre, results):
    arrays = []
    for level in range(LEVELS):
        arrays = arrays + [
            results[level][2],
            pre[level][0],
            pre[level][3],
            pre[level][4],
            results[level][3],
        ]
        if level < LEVELS - 1:
            arrays.append(results[level][4])
    return call(
        functools.partial(flow_post_kernel, images),
        [((FLOW_ROWS, LANE), F32)],
        (valid_shape,),
        arrays,
        name="flow_post",
    )[0]


def swap(values, axis, step):
    size = lax.axis_size(axis)
    return lax.ppermute(values, axis, [(index, index ^ step) for index in range(size)])


def gather_narrow(shard):
    held = [shard]
    step = 1
    while step < lax.axis_size("narrow"):
        held = held + [swap(value, "narrow", step) for value in held]
        step = 2 * step
    return held


def sum_everywhere(values):
    for axis in ("narrow", "wide"):
        step = 1
        while step < lax.axis_size(axis):
            values = values + swap(values, axis, step)
            step = 2 * step
    return values


def halve(values, axis, step):
    index = lax.axis_index(axis)
    rows = values.shape[0] // 2
    upper = (index & step) != 0
    low, high = values[:rows], values[rows:]
    sent = jnp.where(upper, low, high)
    kept = jnp.where(upper, high, low)
    return kept + swap(sent, axis, step)


def unhalve(values, axis, step):
    upper = (lax.axis_index(axis) & step) != 0
    other = swap(values, axis, step)
    return jnp.concatenate([jnp.where(upper, other, values), jnp.where(upper, values, other)], 0)


def sum_wide(values):
    rows = values.shape[0]
    size = lax.axis_size("wide")
    steps = []
    step = 1
    while step < size:
        steps.append(step)
        step = 2 * step
    split = [step for step in steps if step < 8]
    unit = 8 * 2 ** len(split)
    padded = round_up(rows, unit)
    if padded > rows:
        values = jnp.pad(values, ((0, padded - rows), (0, 0)))
    for step in split:
        values = halve(values, "wide", step)
    for step in steps[len(split) :]:
        values = values + swap(values, "wide", step)
    for step in split[::-1]:
        values = unhalve(values, "wide", step)
    return values


def reduce_level(keep, send):
    paired = keep + swap(send, "narrow", 1)
    shard = paired[0] + swap(paired[1], "narrow", 2)
    return sum_wide(shard)


def body(
    images,
    noise_seeds,
    valid_shape,
    conv_in,
    mixer,
    conv_out,
    hidden_bias,
    flow_params,
    conv_in_first,
    mixer_first,
    conv_out_first,
    bias_first,
    flow_first,
    conv_in_second,
    mixer_second,
    conv_out_second,
    bias_second,
    flow_second,
):
    count = images.shape[1]
    index = lax.axis_index("narrow").astype(jnp.int32).reshape(1)
    packed = run_pack(conv_in, mixer, conv_out, hidden_bias)
    gathered = [None] * LEVELS
    for level in (2, 1, 0):
        gathered[level] = gather_narrow(packed[level])
    pre = run_flow_pre(noise_seeds, valid_shape, images, flow_params)
    results = [None] * LEVELS
    grads = [None] * LEVELS
    for level in (2, 1, 0):
        results[level] = run_net(level, count, index, gathered[level], pre[level])
        grads[level] = reduce_level(results[level][0], results[level][1])
    flow_grad = sum_everywhere(run_flow_post(count, valid_shape, pre, results))
    weights = (conv_in, mixer, conv_out, hidden_bias)
    shapes = [(weight.shape, F32) for weight in weights]
    moved = call(
        functools.partial(moment_kernel, 0),
        shapes * 3 + [((16, LANE), F32)],
        (),
        tuple(grads)
        + (flow_grad,)
        + weights
        + (conv_in_first, mixer_first, conv_out_first, bias_first)
        + (conv_in_second, mixer_second, conv_out_second, bias_second),
        name="moments",
    )
    sums = moved[12]
    step = 1
    while step < lax.axis_size("narrow"):
        sums = sums + swap(sums, "narrow", step)
        step = 2 * step
    flow_shape = (flow_params.shape, F32)
    fresh = call(
        apply_kernel,
        shapes
        + [flow_shape]
        + [(weight.shape, BF16) for weight in weights[:3]]
        + [flow_shape, flow_shape, ((8, LANE), F32)],
        (),
        (sums, flow_grad)
        + weights
        + tuple(moved[8:12])
        + (flow_params, flow_first, flow_second),
        name="apply",
    )
    norms = fresh[10]
    return (
        fresh[0],
        fresh[1],
        fresh[2],
        fresh[3],
        fresh[4],
        moved[0],
        moved[1],
        moved[2],
        moved[3],
        fresh[8],
        moved[4],
        moved[5],
        moved[6],
        moved[7],
        fresh[9],
        fresh[5],
        fresh[6],
        fresh[7],
        norms[0, :15],
        norms[1, :15],
        norms[2, 0],
        norms[2, 1],
    )


def solution(mesh):
    placed = (
        P(None, ("wide", "narrow"), None),
        P(("wide", "narrow")),
        P(("wide", "narrow"), None),
        P(None, "narrow"),
        P(None, None, "narrow"),
        P("narrow", None),
        P(None, None, "narrow"),
        P(),
    )
    state = (P(None, "narrow"), P(None, None, "narrow"), P("narrow", None), P(None, None, "narrow"), P())
    return jax.shard_map(
        body,
        mesh=mesh,
        in_specs=placed + state + state,
        out_specs=state * 3 + state[:3] + (P(),) * 4,
        check_vma=False,
    )
```

```python
import functools
import jax
import jax.numpy as jnp
from jax import lax
from jax.experimental import pallas as pl
from jax.experimental.pallas import tpu as pltpu
from jax.sharding import PartitionSpec as P

C1 = 12
IMG_SIDE = 32
STEP = 5
HIGHEST_PRECISION = lax.Precision.HIGHEST
LOG_TWO_PI = 1.8378770664093453
LOG_TWO = 0.6931471805599453
FIRST_BETA = 0.5
SECOND_BETA = 0.5
EPSILON = 1e-06
WEIGHT_DECAY = 0.01
LEARN_RATE = 0.25
TAPS = [(-1, -1), (-1, 0), (-1, 1), (0, -1), (0, 0), (0, 1), (1, -1), (1, 0), (1, 1)]
F32 = jnp.float32
BF16 = jnp.bfloat16
HID = 512
LANE = 128
LEVELS = 3
FLOW_ROWS = 32
STATS_ROWS = 8
VMEM_BYTES = 20 * 1024 * 1024


def round_up(value, unit):
    return (value + unit - 1) // unit * unit


def chan(level):
    return C1 * 2**level


def side(level):
    return IMG_SIDE // 2 ** (level + 1)


def real_positions(level, images):
    return images * side(level) ** 2


def positions(level, images):
    return round_up(real_positions(level, images), LANE)


def in_rows(level):
    return 9 * chan(level) // 2


def first_rows(level):
    return round_up(in_rows(level) + 6, 16)


def second_bias_row(level):
    return first_rows(level) - 4


def last_rows(level):
    return round_up(9 * chan(level), 16)


def pack_rows(level):
    return first_rows(level) + HID + last_rows(level)


def pack_start(level):
    return sum(pack_rows(other) for other in range(LEVELS - 1, level, -1))


def flow_block_rows(narrow):
    return round_up(FLOW_ROWS // narrow, 8) + STATS_ROWS


def grad_rows(level, narrow):
    rows = pack_rows(level) + (flow_block_rows(narrow) if level == 0 else 0)
    return round_up(rows, 64)


def stage_rows(level):
    padded = round_up(chan(level), 8)
    half = round_up(chan(level) // 2, 8)
    sizes = [
        ("normed", padded),
        ("mixed", padded),
        ("share", 8),
        ("held", padded),
        ("block", padded),
        ("prior", half),
        ("grad", padded),
        ("small", padded),
        ("prior_grad", half),
    ]
    starts = {}
    at = 0
    for name, size in sizes[:6]:
        starts[name] = at
        at = at + size
    starts["rows"] = at
    at = 0
    for name, size in sizes[6:]:
        starts[name] = at
        at = at + size
    starts["result_rows"] = at
    return starts


def flow_lengths():
    return [5 * C1 + 3 * C1 * C1 // 2, 10 * C1 + 6 * C1 * C1, 24 * C1 + 16 * C1 * C1]


def flow_size():
    return sum(flow_lengths())


def flow_offsets(level):
    start = sum(flow_lengths()[:level])
    channels = chan(level)
    offsets = {"bias": start, "logs": start + channels, "block": start + 2 * channels}
    start = start + 2 * channels + channels * channels
    offsets["outbias"] = start
    offsets["outscale"] = start + channels
    start = start + 2 * channels
    if level < LEVELS - 1:
        offsets["priormatrix"] = start
        start = start + channels // 2 * channels
    offsets["priorbias"] = start
    return offsets


def column_names(level):
    channels = chan(level)
    offsets = flow_offsets(level)
    names = [
        ("bias", offsets["bias"]),
        ("logs", offsets["logs"]),
        ("outbias", offsets["outbias"]),
        ("outscale", offsets["outscale"]),
        ("priorbias", offsets["priorbias"]),
    ]
    if level == LEVELS - 1:
        names = names + [("priorscale", offsets["priorbias"] + channels)]
    return names


def exact_dot(first, second):
    return jnp.dot(first, second, precision=HIGHEST_PRECISION, preferred_element_type=F32)


def exact_rows(first, second):
    return lax.dot_general(
        first,
        second,
        (((0,), (0,)), ((), ())),
        precision=HIGHEST_PRECISION,
        preferred_element_type=F32,
    )


def exact_columns(first, second):
    return lax.dot_general(
        first,
        second,
        (((1,), (1,)), ((), ())),
        precision=HIGHEST_PRECISION,
        preferred_element_type=F32,
    )


def plain_dot(first, second):
    return jnp.dot(first, second, preferred_element_type=F32)


def contract_rows(first, second):
    return lax.dot_general(first, second, (((0,), (0,)), ((), ())), preferred_element_type=F32)


def contract_columns(first, second):
    return lax.dot_general(first, second, (((1,), (1,)), ((), ())), preferred_element_type=F32)


def iota(shape, axis):
    return lax.broadcasted_iota(jnp.int32, shape, axis)


def rounded(values):
    return values.astype(BF16).astype(F32)


def split_three(values):
    high = rounded(values)
    rest = values - high
    middle = rounded(rest)
    return [high, middle, rest - middle]


def move_lanes(values, chooser, transposed=False):
    rows = values.shape[0]
    padded = round_up(rows, 8)
    if padded > rows:
        values = jnp.concatenate([values, jnp.zeros((padded - rows, values.shape[1]), F32)], 0)
    pieces = jnp.concatenate(split_three(values), 0).astype(BF16)
    moved = contract_columns(pieces, chooser) if transposed else plain_dot(pieces, chooser)
    moved = moved[:padded] + moved[padded : 2 * padded] + moved[2 * padded :]
    return moved[:rows]


def squeeze_chooser(grid, images):
    count = images * grid * grid
    source = iota((count, count), 0)
    target = iota((count, count), 1)
    shift = grid.bit_length() - 1
    image = lax.shift_right_logical(source, 2 * shift)
    row = lax.shift_right_logical(source, shift) & (grid - 1)
    column = source & (grid - 1)
    half = grid // 2
    place = (
        ((row & 1) * 2 + (column & 1)) * (images * half * half)
        + image * (half * half)
        + lax.shift_right_logical(row, 1) * half
        + lax.shift_right_logical(column, 1)
    )
    return (place == target).astype(F32).astype(BF16)


def order_chooser(channels, stride):
    row = iota((4 * channels, 4 * stride), 0)
    column = iota((4 * channels, 4 * stride), 1)
    return ((row & 3) * stride + lax.shift_right_logical(row, 2) == column).astype(F32)


def squeeze(values, chooser, lanes_out):
    channels, count = values.shape
    moved = move_lanes(values, chooser)
    quarter = count // 4
    stacked = jnp.concatenate([moved[:, k * quarter : (k + 1) * quarter] for k in range(4)], 0)
    ordered = exact_dot(order_chooser(channels, channels), stacked)
    if lanes_out > quarter:
        ordered = jnp.concatenate([ordered, jnp.zeros((4 * channels, lanes_out - quarter), F32)], 1)
    return ordered


def unsqueeze(values, chooser, count):
    channels = values.shape[0] // 4
    quarter = count // 4
    stacked = exact_rows(order_chooser(channels, channels), values)
    laid = jnp.concatenate(
        [stacked[k * channels : (k + 1) * channels, :quarter] for k in range(4)], 1
    )
    return move_lanes(laid, chooser, transposed=True)


def slope_roll(values, step):
    step = step % LANE
    while step:
        part = 16 if step >= 16 else 1 << (step.bit_length() - 1)
        values = pltpu.roll(values, 0, 1, stride=part, stride_axis=0)
        step = step - part
    return values


def flow_block(flat, offset, rows, width):
    padded = round_up(rows, 8)
    start = offset + width * iota((padded, FLOW_ROWS), 0)
    line = lax.shift_right_logical(start, 7)
    column = iota((padded, FLOW_ROWS), 1)
    base = -offset % LANE
    if base:
        flat = pltpu.roll(flat, base, 1)
    here = exact_dot((line == column).astype(F32), flat)
    after = exact_dot((line + 1 == column).astype(F32), flat)
    here = slope_roll(here, -width)
    after = slope_roll(after, -width)
    lane = iota((padded, LANE), 1)
    begin = (offset + width * iota((padded, LANE), 0)) & (LANE - 1)
    chosen = jnp.where(lane + begin < LANE, here, after)
    return chosen[:rows, :width]


def flow_block_back(values, offset, rows, width):
    padded = round_up(rows, 8)
    base = offset % LANE
    over = max(base + width - LANE, 0)
    parts = [values[:, width - over :]] if over else []
    if base > over:
        parts.append(jnp.zeros((rows, base - over), F32))
    parts.append(values[:, : width - over])
    if base + width < LANE:
        parts.append(jnp.zeros((rows, LANE - base - width), F32))
    block = jnp.concatenate(parts, 1)
    if padded > rows:
        block = jnp.concatenate([block, jnp.zeros((padded - rows, LANE), F32)], 0)
    block = slope_roll(block, width)
    lane = iota((padded, LANE), 1)
    begin = (offset + width * iota((padded, LANE), 0)) & (LANE - 1)
    here = jnp.where(lane >= begin, block, 0.0)
    after = jnp.where(lane >= begin, 0.0, block)
    line = lax.shift_right_logical(offset + width * iota((FLOW_ROWS, padded), 1), 7)
    row = iota((FLOW_ROWS, padded), 0)
    return exact_dot((line == row).astype(F32), here) + exact_dot(
        (line + 1 == row).astype(F32), after
    )


def flow_column(turned, offset, length):
    line, begin = offset // LANE, offset % LANE
    if begin + length <= LANE:
        return turned[begin : begin + length, line : line + 1]
    return jnp.concatenate(
        [turned[begin:, line : line + 1], turned[: begin + length - LANE, line + 1 : line + 2]], 0
    )


def flow_column_back(values, offset):
    length = values.shape[0]
    line, begin = offset // LANE, offset % LANE
    lane = iota((LANE, LANE), 1)
    head = min(length, LANE - begin)
    parts = []
    if begin:
        parts.append(jnp.zeros((begin, 1), F32))
    parts.append(values[:head])
    if begin + head < LANE:
        parts.append(jnp.zeros((LANE - begin - head, 1), F32))
    column = jnp.concatenate(parts, 0) if len(parts) > 1 else parts[0]
    term = jnp.where(lane == line, column, 0.0)
    if head < length:
        column = jnp.concatenate([values[head:], jnp.zeros((LANE - length + head, 1), F32)], 0)
        term = term + jnp.where(lane == line + 1, column, 0.0)
    return term


def to_flat_rows(values):
    size = values.shape[0]
    row = values.reshape(1, size)
    row = jnp.concatenate([row, jnp.zeros((1, FLOW_ROWS * LANE - size), F32)], 1)
    return row.reshape(FLOW_ROWS, LANE)


def from_flat_rows(values, size):
    return values.reshape(1, FLOW_ROWS * LANE)[:, :size].reshape(size)


def triangles(block):
    channels = block.shape[0]
    row = iota((channels, channels), 0)
    column = iota((channels, channels), 1)
    signs = (1 - 2 * (row & 1)).astype(F32)
    diagonal = signs * jnp.exp(jnp.where(row == column, block, 0.0))
    lower = jnp.where(row > column, block, jnp.where(row == column, 1.0, 0.0))
    upper = jnp.where(row < column, block, jnp.where(row == column, diagonal, 0.0))
    reverse = (row + column == channels - 1).astype(F32)
    return lower, upper, reverse, diagonal


def tap_masks(level, images):
    grid = side(level)
    count = positions(level, images)
    lane = iota((8, count), 1)
    shift = grid.bit_length() - 1
    row = lax.shift_right_logical(lane, shift) & (grid - 1)
    column = lane & (grid - 1)
    inside = lane < real_positions(level, images)
    masks = {}
    for row_step in (-1, 0, 1):
        for column_step in (-1, 0, 1):
            good = (
                (row + row_step >= 0)
                & (row + row_step < grid)
                & (column + column_step >= 0)
                & (column + column_step < grid)
                & inside
            )
            masks[(row_step, column_step)] = jnp.where(good, 1.0, 0.0)[0:1]
    return masks


def tap_read(values, masks, level, row_step, column_step):
    count = values.shape[1]
    offset = (row_step * side(level) + column_step) % count
    if offset:
        values = pltpu.roll(values, count - offset, 1)
    if (row_step, column_step) != (0, 0):
        values = values * masks[(row_step, column_step)]
    return values


def tap_stack(values, masks, level, direction):
    return [
        tap_read(values, masks, level, direction * row_step, direction * column_step)
        for row_step, column_step in TAPS
    ]


def tap_sum(values, masks, level, direction, channels):
    total = None
    for tap, (row_step, column_step) in enumerate(TAPS):
        term = tap_read(
            values[tap * channels : (tap + 1) * channels],
            masks,
            level,
            direction * row_step,
            direction * column_step,
        )
        total = term if total is None else total + term
    return total


def pack_kernel(conv_in_ref, mixer_ref, conv_out_ref, bias_ref, *out_refs):
    in_start = 0
    out_start = 0
    for level in range(LEVELS):
        out_ref = out_refs[level]
        rows, columns = in_rows(level), 9 * chan(level)
        top = first_rows(level)
        ones = split_three(bias_ref[level, 0:1, :])
        twos = split_three(bias_ref[level, 1:2, :])
        gap = second_bias_row(level) - rows - 3
        pieces = [conv_in_ref[in_start : in_start + rows, :]] + ones
        if gap:
            pieces.append(jnp.zeros((gap, LANE), F32))
        pieces = pieces + twos + [jnp.zeros((1, LANE), F32)]
        out_ref[0:top, :] = jnp.concatenate(pieces, 0).astype(BF16)
        out_ref[top : top + HID, :] = mixer_ref[level].astype(BF16)
        tail = conv_out_ref[out_start : out_start + columns, :]
        if last_rows(level) > columns:
            tail = jnp.concatenate([tail, jnp.zeros((last_rows(level) - columns, LANE), F32)], 0)
        out_ref[top + HID :, :] = tail.astype(BF16)
        out_refs[LEVELS][pack_start(level) : pack_start(level) + pack_rows(level), :] = out_ref[...]
        in_start = in_start + rows
        out_start = out_start + columns


def flow_pre_kernel(seed_ref, valid_ref, image_ref, flow_ref, *out_refs):
    images = image_ref.shape[1]
    flat = to_flat_rows(flow_ref[...])
    turned = jnp.concatenate([flat, jnp.zeros((LANE - FLOW_ROWS, LANE), F32)], 0).T
    blocks = IMG_SIDE * IMG_SIDE // 256
    pieces = []
    for image in range(images):
        position = iota((8, IMG_SIDE * IMG_SIDE), 0) * (IMG_SIDE * IMG_SIDE) + iota(
            (8, IMG_SIDE * IMG_SIDE), 1
        )
        hashed = seed_ref[image] + position * jnp.int32(-1640531527)
        hashed = hashed ^ lax.shift_right_logical(hashed, jnp.full_like(hashed, 15))
        hashed = hashed * jnp.int32(739267321)
        hashed = hashed ^ lax.shift_right_logical(hashed, jnp.full_like(hashed, 13))
        field = ((hashed & jnp.int32(16777215)).astype(F32) + 0.5) * 2.0 ** (-24)
        pixel = jnp.concatenate(
            [image_ref[:, image, :], jnp.zeros((5, IMG_SIDE * IMG_SIDE), F32)], 0
        )
        pixel = pixel + field / 256.0
        for block in range(blocks):
            pieces.append(pixel[:, block * 256 : (block + 1) * 256])
    stacked = jnp.concatenate(pieces, 0)
    source = iota((256, 256), 0)
    target = iota((256, 256), 1)
    row = lax.shift_right_logical(source, 5)
    column = source & 31
    place = (
        ((row & 1) * 2 + (column & 1)) * 64
        + lax.shift_right_logical(row, 1) * 16
        + lax.shift_right_logical(column, 1)
    )
    moved = move_lanes(stacked, (place == target).astype(F32).astype(BF16))
    quarters = []
    for k in range(4):
        quarters.append(
            jnp.concatenate(
                [
                    moved[piece * 8 : (piece + 1) * 8, k * 64 : (k + 1) * 64]
                    for piece in range(images * blocks)
                ],
                1,
            )
        )
    state = exact_dot(order_chooser(3, 8), jnp.concatenate(quarters, 0))
    for level in range(LEVELS):
        channels = chan(level)
        grid = side(level)
        count = positions(level, images)
        offsets = flow_offsets(level)
        block = flow_block(flat, offsets["block"], channels, channels)
        names = column_names(level)
        columns = [flow_column(turned, offset, channels) for _, offset in names]
        lane = iota((channels, LANE), 1)
        held = jnp.zeros((channels, LANE), F32)
        for index, column in enumerate(columns):
            held = jnp.where(lane == index, column, held)
        normed = (state + columns[0]) * jnp.exp(columns[1])
        lower, upper, reverse, _ = triangles(block)
        mixing = exact_dot(exact_dot(reverse, lower), upper)
        mixed = exact_dot(mixing, normed)
        lane = iota((8, count), 1)
        shift = grid.bit_length() - 1
        image = lax.shift_right_logical(lane, 2 * shift)
        row = lax.shift_right_logical(lane, shift) & (grid - 1)
        column = lane & (grid - 1)
        high = jnp.zeros((8, count), jnp.int32)
        wide = jnp.zeros((8, count), jnp.int32)
        for index in range(images):
            high = jnp.where(image == index, valid_ref[index, 0], high)
            wide = jnp.where(image == index, valid_ref[index, 1], wide)
        unit = 2 ** (level + 1)
        row_share = jnp.clip(high - row * unit, 0, unit).astype(F32) / unit
        column_share = jnp.clip(wide - column * unit, 0, unit).astype(F32) / unit
        share = jnp.where(image < images, row_share * column_share, 0.0)
        out_ref = out_refs[level]
        starts = stage_rows(level)
        out_ref[starts["normed"] : starts["normed"] + channels, :] = normed
        out_ref[starts["mixed"] : starts["mixed"] + channels, :] = mixed
        out_ref[starts["share"] : starts["share"] + 8, :] = share
        out_ref[starts["held"] : starts["held"] + channels, 0:LANE] = held
        out_ref[starts["block"] : starts["block"] + channels, 0:channels] = block
        if level < LEVELS - 1:
            out_ref[starts["prior"] : starts["prior"] + channels // 2, 0:channels] = flow_block(
                flat, offsets["priormatrix"], channels // 2, channels
            )
            state = squeeze(
                mixed[: channels // 2], squeeze_chooser(grid, images), positions(level + 1, images)
            )


def silu_parts(values):
    sigmoid = 1.0 / (1.0 + jnp.exp(-values))
    active = values * sigmoid
    slope = sigmoid + active * (1.0 - sigmoid)
    return active, slope


def net_kernel(level, images, narrow, *refs):
    is_last = level == LEVELS - 1
    index_ref = refs[0]
    weight_refs = refs[1 : 1 + narrow]
    bases = [pack_start(level) if ref.shape[0] > pack_rows(level) else 0 for ref in weight_refs]
    stage_ref, keep_ref, send_ref, result_ref = refs[1 + narrow : 5 + narrow]
    order_ref, slope_one_ref, slope_two_ref, one_ref, two_ref = refs[5 + narrow :]
    starts = stage_rows(level)
    me = index_ref[0, 0]
    channels = chan(level)
    half = channels // 2
    count = positions(level, images)
    top, rows = first_rows(level), in_rows(level)
    tail, used = last_rows(level), 9 * channels
    masks = tap_masks(level, images)
    width = HID // narrow

    def weights(start, length):
        return jnp.concatenate(
            [ref[base + start : base + start + length, :] for ref, base in zip(weight_refs, bases)], 1
        )

    for r_in in range(narrow):
        for r_out in range(narrow):
            start = pl.multiple_of(bases[r_out] + top + (me ^ r_in) * width, 16)
            order_ref[r_in * width : (r_in + 1) * width, r_out * LANE : (r_out + 1) * LANE] = (
                weight_refs[r_out][pl.ds(start, width), :]
            )
    weight_in = weights(0, top)
    weight_mix = order_ref[...]
    weight_out = weights(top + HID, tail)
    mixed = starts["mixed"]
    first = stage_ref[mixed : mixed + half, :]
    second = stage_ref[mixed + half : mixed + channels, :]
    share = stage_ref[starts["share"] : starts["share"] + 1, :]
    pieces = tap_stack(rounded(first), masks, level, 1)
    pieces.append(jnp.ones((3, count), F32))
    pieces.append(jnp.zeros((top - rows - 3, count), F32))
    stacked = jnp.concatenate(pieces, 0).astype(BF16)
    pick = jnp.where(
        (iota((16, count), 0) >= 12) & (iota((16, count), 0) < 15), 1.0, 0.0
    ).astype(BF16)
    hidden_one = contract_rows(weight_in, stacked)
    active, slope = silu_parts(hidden_one)
    slope_one_ref[...] = slope
    one_ref[...] = active.astype(BF16)
    hidden_two = contract_rows(weight_mix, one_ref[...]) + contract_rows(weights(top - 16, 16), pick)
    active, slope = silu_parts(hidden_two)
    slope_two_ref[...] = slope
    two_ref[...] = active.astype(BF16)
    spread = plain_dot(weight_out, two_ref[...])
    net_raw = tap_sum(spread, masks, level, 1, channels)
    held = stage_ref[starts["held"] : starts["held"] + channels, 0:LANE]
    out_bias, out_scale = held[:, 2:3], held[:, 3:4]
    growth = jnp.exp(3.0 * out_scale)
    output = (net_raw + out_bias) * growth
    logit = output[half:] + 2.0
    sigmoid = 1.0 / (1.0 + jnp.exp(-logit))
    latent = (second + output[:half]) * sigmoid
    log_sigmoid = jnp.minimum(logit, 0.0) - jnp.log1p(jnp.exp(-jnp.abs(logit)))
    if is_last:
        joined = jnp.concatenate([first, latent], 0)
        mean, scale = held[:, 4:5], held[:, 5:6]
        mean = jnp.broadcast_to(mean, joined.shape)
        scale = jnp.broadcast_to(scale, joined.shape)
    else:
        joined = latent
        prior = stage_ref[starts["prior"] : starts["prior"] + half, 0:channels]
        stats = exact_rows(prior, first) + held[:, 4:5]
        mean, scale = stats[:half], stats[half:]
    gap = joined - mean
    shrink = jnp.exp(-2.0 * scale)
    square = gap * gap * shrink
    log_prior = -0.5 * (LOG_TWO_PI + 2.0 * scale + square)
    total = jnp.sum(jnp.sum(share * log_sigmoid, 0, keepdims=True), 1, keepdims=True) + jnp.sum(
        jnp.sum(share * log_prior, 0, keepdims=True), 1, keepdims=True
    )
    share_total = jnp.sum(share, 1, keepdims=True)
    grad_joined = share * (gap * shrink)
    grad_scale = share * (1.0 - square)
    grad_latent = grad_joined[half:] if is_last else grad_joined
    grad_logit = (grad_latent * latent - share) * (1.0 - sigmoid)
    grad_second = grad_latent * sigmoid
    grad_output = jnp.concatenate([grad_second, grad_logit], 0)
    grad_net = grad_output * growth
    lane = iota((channels, LANE), 1)
    small = jnp.zeros((channels, LANE), F32)

    def put(small, index, values):
        return jnp.where(lane == index, jnp.sum(values, 1, keepdims=True), small)

    small = put(small, 2, grad_net)
    small = put(small, 3, 3.0 * grad_output * output)
    if is_last:
        small = put(small, 4, -grad_joined)
        small = put(small, 5, grad_scale)
        grad_first = grad_joined[:half]
    else:
        grad_stats = jnp.concatenate([-grad_joined, grad_scale], 0)
        small = put(small, 4, grad_stats)
        grad_first = exact_dot(prior, grad_stats)
        prior_grad = exact_columns(first, grad_stats)
        start = starts["prior_grad"]
        result_ref[start : start + half, 0:channels] = prior_grad
    small = jnp.where(lane == 6, -total, small)
    small = jnp.where(lane == 7, share_total, small)
    result_ref[starts["small"] : starts["small"] + channels, 0:LANE] = small
    pieces = tap_stack(rounded(grad_net), masks, level, -1)
    if tail > used:
        pieces.append(jnp.zeros((tail - used, count), F32))
    grad_spread = jnp.concatenate(pieces, 0).astype(BF16)

    def store(start, values):
        for r in range(narrow):
            ref = send_ref if r & 1 else keep_ref
            ref[r // 2, start : start + values.shape[0], :] = values[:, r * LANE : (r + 1) * LANE]

    store(top + HID, contract_columns(grad_spread, two_ref[...]))
    grad_two = (contract_rows(weight_out, grad_spread) * slope_two_ref[...]).astype(BF16)
    grad_mix = contract_columns(one_ref[...], grad_two)
    for r_in in range(narrow):
        start = pl.multiple_of(top + (me ^ r_in) * width, 16)
        for r_out in range(narrow):
            ref = send_ref if r_out & 1 else keep_ref
            ref[r_out // 2, pl.ds(start, width), :] = grad_mix[
                r_in * width : (r_in + 1) * width, r_out * LANE : (r_out + 1) * LANE
            ]
    grad_one = (plain_dot(weight_mix, grad_two) * slope_one_ref[...]).astype(BF16)
    grad_in = contract_columns(stacked, grad_one)
    store(0, grad_in[: top - 16])
    store(top - 16, grad_in[top - 16 :] + contract_columns(pick, grad_two))
    rest = keep_ref.shape[1] - pack_rows(level)
    if rest and level > 0:
        for ref in (keep_ref, send_ref):
            ref[:, pack_rows(level) :, :] = jnp.zeros((narrow // 2, rest, LANE), F32)
    grad_stack = plain_dot(weight_in, grad_one)
    grad_first = grad_first + tap_sum(grad_stack, masks, level, -1, half)
    result_ref[0:half, :] = grad_first
    result_ref[half:channels, :] = grad_second


def flow_level(level, images, stage_ref, result_ref, carried, flat):
    channels = chan(level)
    half = channels // 2
    starts = stage_rows(level)

    def part(ref, name, rows, lanes):
        return ref[starts[name] : starts[name] + rows, 0:lanes]

    count = positions(level, images)
    offsets = flow_offsets(level)
    grad = part(result_ref, "grad", channels, count)
    if carried is not None:
        grad = grad + jnp.concatenate([carried, jnp.zeros_like(carried)], 0)
    normed = part(stage_ref, "normed", channels, count)
    held = part(stage_ref, "held", channels, LANE)
    small = part(result_ref, "small", channels, LANE)
    block = part(stage_ref, "block", channels, channels)
    lower, upper, reverse, diagonal = triangles(block)
    mixing_left = exact_dot(reverse, lower)
    grad_normed = exact_rows(exact_dot(mixing_left, upper), grad)
    grad_mixing = exact_dot(reverse, exact_columns(grad, normed))
    grad_lower = exact_columns(grad_mixing, upper)
    grad_upper = exact_rows(lower, grad_mixing)
    share_total = small[0:1, 7:8]
    row = iota((channels, channels), 0)
    column = iota((channels, channels), 1)
    grad_block = jnp.where(
        row > column,
        grad_lower,
        jnp.where(row < column, grad_upper, grad_upper * diagonal - share_total),
    )
    growth = jnp.exp(held[:, 1:2])
    grad_state = grad_normed * growth
    grad_bias = jnp.sum(grad_state, 1, keepdims=True)
    grad_logs = jnp.sum(grad_normed * normed, 1, keepdims=True) - share_total
    term = flow_block_back(grad_block, offsets["block"], channels, channels)
    turned = jnp.zeros((LANE, LANE), F32)
    for index, (name, offset) in enumerate(column_names(level)):
        if name == "bias":
            values = grad_bias
        elif name == "logs":
            values = grad_logs
        else:
            values = small[:, index : index + 1]
        turned = turned + flow_column_back(values, offset)
    if level < LEVELS - 1:
        term = term + flow_block_back(
            part(result_ref, "prior_grad", half, channels), offsets["priormatrix"], half, channels
        )
    logs_total = jnp.sum(held[:, 1:2], 0, keepdims=True)
    trace = jnp.sum(
        jnp.sum(jnp.where(row == column, block, 0.0), 0, keepdims=True), 1, keepdims=True
    )
    loss = small[0:1, 6:7] - share_total * (logs_total + trace)
    term = term + turned.T[:FLOW_ROWS]
    row = iota((FLOW_ROWS, LANE), 0)
    lane = iota((FLOW_ROWS, LANE), 1)
    term = term + jnp.where((row == FLOW_ROWS - 1) & (lane == 0), loss, 0.0)
    flat = term if flat is None else flat + term
    carried = None
    if level > 0:
        grid = side(level - 1)
        carried = unsqueeze(grad_state, squeeze_chooser(grid, images), images * grid * grid)
    return carried, flat


def flow_kernel(level, images, *refs):
    stage_ref, result_ref = refs[:2]
    carried, flat = None, None
    if level < LEVELS - 1:
        carried, flat = refs[2][...], refs[3][...]
    carried, flat = flow_level(level, images, stage_ref, result_ref, carried, flat)
    refs[-2][...] = carried
    refs[-1][...] = flat


def last_kernel(images, narrow, *refs):
    count_ref, index_ref = refs[:2]
    mine = refs[2 : 2 + narrow]
    stage_ref, carried_ref, partial_ref, keep_ref, send_ref = refs[2 + narrow : 7 + narrow]
    result_ref, flat_ref = refs[7 + narrow : 9 + narrow]
    scratch = refs[9 + narrow :]
    net_kernel(
        0, images, narrow, index_ref, *mine, stage_ref, keep_ref, send_ref, result_ref, *scratch
    )
    _, flat = flow_level(0, images, stage_ref, result_ref, carried_ref[...], partial_ref[...])
    loss = flat[FLOW_ROWS - 1 : FLOW_ROWS, 0:1]
    pixels = jnp.zeros((), F32)
    for index in range(images):
        pixels = pixels + (count_ref[index, 0] * count_ref[index, 1]).astype(F32)
    lane = iota((STATS_ROWS, LANE), 1)
    stats = jnp.where(lane == 0, loss, jnp.where(lane == 1, pixels, 0.0))
    flat_ref[...] = flat
    share = FLOW_ROWS // narrow
    start = pack_rows(0)
    me = index_ref[0, 0]
    for r in range(narrow):
        ref = send_ref if r & 1 else keep_ref
        ref[r // 2, start : start + share, :] = flat_ref[
            pl.ds(pl.multiple_of((me ^ r) * share, share), share), :
        ]
        ref[r // 2, start + share : start + share + STATS_ROWS, :] = stats
        rest = ref.shape[1] - start - share - STATS_ROWS
        if rest:
            ref[r // 2, start + share + STATS_ROWS :, :] = jnp.zeros((rest, LANE), F32)


def copy_kernel(from_ref, to_ref):
    to_ref[...] = from_ref[...]


def merge_kernel(exact_in, stage, exact_out, *refs):
    index_ref, kept_ref, other_ref = refs[:3]
    rows = kept_ref.shape[1]

    def total(shards, place, length):
        return kept_ref[shards, place, :] + other_ref[shards, place, :].astype(F32)

    if stage == "shard":
        keep_ref, send_ref = refs[3:5]
        count = keep_ref.shape[0]
        everything = pl.ds(0, rows)
        keep_ref[...] = total(pl.ds(0, count), everything, rows)
        sent = total(pl.ds(count, count), everything, rows)
        send_ref[:, 0:rows, :] = sent.astype(send_ref.dtype)
        if exact_out:
            start = pack_rows(0)
            for shard in range(count):
                pieces = split_three(sent[shard, start : start + exact_out])
                send_ref[shard, rows:, :] = jnp.concatenate(pieces, 0).astype(BF16)
        return
    if stage is None:
        refs[3][...] = total(pl.ds(0, kept_ref.shape[0]), pl.ds(0, rows), rows)
        return
    keep_ref, send_ref = refs[3:5]
    half = rows // 2
    shards = pl.ds(0, kept_ref.shape[0])
    upper = jnp.where((index_ref[1, 0] & stage) != 0, 1, 0)
    for ref, place in ((keep_ref, upper), (send_ref, 1 - upper)):
        ref[...] = total(shards, pl.ds(pl.multiple_of(place * half, 16), half), half).astype(
            ref.dtype
        )
    if exact_in:
        start = pack_rows(0)
        for shard in range(kept_ref.shape[0]):
            pieces = other_ref[shard, rows:, :].astype(F32)
            whole = pieces[:exact_in] + pieces[exact_in : 2 * exact_in] + pieces[2 * exact_in :]
            whole = kept_ref[shard, start : start + exact_in, :] + whole

            @pl.when(upper == 1)
            def _():
                keep_ref[shard, start - half : start - half + exact_in, :] = whole

            @pl.when(upper == 0)
            def _():
                send_ref[shard, start - half : start - half + exact_in, :] = whole


def join_kernel(bit, index_ref, mine_ref, other_ref, out_ref):
    half = mine_ref.shape[1]
    upper = jnp.where((index_ref[1, 0] & bit) != 0, 1, 0)
    out_ref[:, pl.ds(pl.multiple_of(upper * half, 8), half), :] = mine_ref[...]
    out_ref[:, pl.ds(pl.multiple_of((1 - upper) * half, 8), half), :] = other_ref[...]


def moments(weight, gradient, first_old, second_old):
    first_new = FIRST_BETA * first_old + (1.0 - FIRST_BETA) * gradient
    second_new = SECOND_BETA * second_old + (1.0 - SECOND_BETA) * gradient * gradient
    update = (
        first_new
        / (1.0 - FIRST_BETA**STEP)
        / (jnp.sqrt(second_new / (1.0 - SECOND_BETA**STEP)) + EPSILON)
        + WEIGHT_DECAY * weight
    )
    return first_new, second_new, update


def total_of(values):
    return jnp.sum(jnp.sum(values, 0, keepdims=True), 1, keepdims=True)


def squares_rows(sums):
    row = iota((16, LANE), 0)
    held = jnp.zeros((16, LANE), F32)
    for index, value in enumerate(sums):
        held = jnp.where(row == index, value, held)
    return held


def group_totals(values_in, values_mix, values_out, values_bias):
    row = iota(values_in.shape, 0)
    line = iota(values_out.shape, 0)
    sums = []
    start = 0
    for level in range(LEVELS):
        inside = (row >= start) & (row < start + in_rows(level))
        sums.append(total_of(jnp.where(inside, values_in, 0.0)))
        start = start + in_rows(level)
    for level in range(LEVELS):
        sums.append(total_of(values_mix[level]))
    start = 0
    for level in range(LEVELS):
        inside = (line >= start) & (line < start + 9 * chan(level))
        sums.append(total_of(jnp.where(inside, values_out, 0.0)))
        start = start + 9 * chan(level)
    for level in range(LEVELS):
        sums.append(total_of(values_bias[2 * level : 2 * level + 2]))
    return sums


def flow_masks():
    place = iota((FLOW_ROWS, LANE), 0) * LANE + iota((FLOW_ROWS, LANE), 1)
    masks = []
    start = 0
    for length in flow_lengths():
        masks.append((place >= start) & (place < start + length))
        start = start + length
    return masks


def moment_kernel(share, *refs):
    grads = [ref.at[0] for ref in refs[:3]]
    weight_in, weight_mix, weight_out, weight_bias = refs[3:7]
    first_in, first_mix, first_out, first_bias = refs[7:11]
    second_in, second_mix, second_out, second_bias = refs[11:15]
    outs = refs[15:]
    stats_row = pack_rows(0) + share
    total = grads[0][stats_row : stats_row + 1, :]
    valid_dims = 3.0 * total[:, 1:2]
    scale = 1.0 / (valid_dims * LOG_TWO)
    grad_in = jnp.concatenate([grads[level][0 : in_rows(level), :] for level in range(LEVELS)], 0)
    tails = [
        grads[level][first_rows(level) + HID : first_rows(level) + HID + 9 * chan(level), :]
        for level in range(LEVELS)
    ]
    grad_out = jnp.concatenate(tails, 0)
    bias_rows = []
    for level in range(LEVELS):
        bias_rows.append(grads[level][in_rows(level) : in_rows(level) + 1, :])
        bias_rows.append(grads[level][second_bias_row(level) : second_bias_row(level) + 1, :])
    grad_bias = jnp.concatenate(bias_rows, 0)
    bias = weight_bias[...].reshape(2 * LEVELS, LANE)
    new_in = moments(weight_in[...], grad_in * scale, first_in[...], second_in[...])
    new_out = moments(weight_out[...], grad_out * scale, first_out[...], second_out[...])
    new_bias = moments(
        bias,
        grad_bias * scale,
        first_bias[...].reshape(2 * LEVELS, LANE),
        second_bias[...].reshape(2 * LEVELS, LANE),
    )
    mix_squares = []
    mix_updates = []
    for level in range(LEVELS):
        top = first_rows(level)
        new_mix = moments(
            weight_mix[level],
            grads[level][top : top + HID, :] * scale,
            first_mix[level],
            second_mix[level],
        )
        outs[1][level] = new_mix[0]
        outs[5][level] = new_mix[1]
        outs[9][level] = new_mix[2]
        mix_squares.append(weight_mix[level] * weight_mix[level])
        mix_updates.append(new_mix[2] * new_mix[2])
    for index, values in ((0, new_in), (2, new_out), (3, new_bias)):
        for kind in range(3):
            value = values[kind]
            if index == 3:
                value = value.reshape(LEVELS, 2, LANE)
            outs[4 * kind + index][...] = value
    weight_sums = group_totals(
        weight_in[...] * weight_in[...], mix_squares, weight_out[...] * weight_out[...], bias * bias
    )
    update_sums = group_totals(
        new_in[2] * new_in[2], mix_updates, new_out[2] * new_out[2], new_bias[2] * new_bias[2]
    )
    lane = iota((16, LANE), 1)
    outs[12][0:16, :] = jnp.where(lane == 0, squares_rows(weight_sums), squares_rows(update_sums))
    outs[12][16 : 16 + share, :] = grads[0][pack_rows(0) : pack_rows(0) + share, :]
    outs[12][16 + share :, :] = grads[0][stats_row : stats_row + STATS_ROWS, :]


def apply_kernel(narrow, *refs):
    index_ref = refs[0]
    block_refs = refs[1 : 1 + narrow]
    at = 1 + narrow
    weight_in, weight_mix, weight_out, weight_bias = refs[at : at + 4]
    update_in, update_mix, update_out, update_bias = refs[at + 4 : at + 8]
    flow_ref, flow_first_ref, flow_second_ref = refs[at + 8 : at + 11]
    at = at + 11
    (
        new_in,
        new_mix,
        new_out,
        new_bias,
        new_flow,
        half_in,
        half_mix,
        half_out,
        flow_moment,
        flow_square,
        weight_norm_ref,
        update_norm_ref,
        loss_ref,
        valid_ref,
        order_ref,
    ) = refs[at:]
    for part in range(narrow):
        order_ref[index_ref[0, 0] ^ part] = block_refs[part][...]
    share = FLOW_ROWS // narrow
    sums = order_ref[0, 0:16, :]
    for part in range(1, narrow):
        sums = sums + order_ref[part, 0:16, :]
    flow_grad = jnp.concatenate([order_ref[part, 16 : 16 + share, :] for part in range(narrow)], 0)
    total = block_refs[0][16 + share : 17 + share, :]
    valid_dims = 3.0 * total[:, 1:2]
    scale = 1.0 / (valid_dims * LOG_TWO)
    flow = to_flat_rows(flow_ref[...])
    size = flow_ref.shape[0]
    place = iota((FLOW_ROWS, LANE), 0) * LANE + iota((FLOW_ROWS, LANE), 1)
    flow_grad = jnp.where(place < size, flow_grad * scale, 0.0)
    first_new, second_new, update = moments(
        flow, flow_grad, to_flat_rows(flow_first_ref[...]), to_flat_rows(flow_second_ref[...])
    )
    weight_norms = [jnp.sqrt(sums[index : index + 1, 0:1]) for index in range(12)]
    update_norms = [jnp.sqrt(sums[index : index + 1, 1:2]) for index in range(12)]
    masks = flow_masks()
    for mask in masks:
        weight_norms.append(jnp.sqrt(total_of(jnp.where(mask, flow * flow, 0.0))))
        update_norms.append(jnp.sqrt(total_of(jnp.where(mask, update * update, 0.0))))
    rates = [
        LEARN_RATE * (weight_norm / update_norm)
        for weight_norm, update_norm in zip(weight_norms, update_norms)
    ]
    rate = jnp.zeros((FLOW_ROWS, LANE), F32)
    for mask, value in zip(masks, rates[12:]):
        rate = jnp.where(mask, value, rate)
    new_flow[...] = from_flat_rows(flow - rate * update, size)
    flow_moment[...] = from_flat_rows(first_new, size)
    flow_square[...] = from_flat_rows(second_new, size)
    row = iota(weight_in.shape, 0)
    edge_one, edge_two = in_rows(0), in_rows(0) + in_rows(1)
    rate = jnp.where(row < edge_one, rates[0], jnp.where(row < edge_two, rates[1], rates[2]))
    fresh = weight_in[...] - rate * update_in[...]
    new_in[...] = fresh
    half_in[...] = fresh.astype(BF16)
    for level in range(LEVELS):
        fresh = weight_mix[level] - rates[3 + level] * update_mix[level]
        new_mix[level] = fresh
        half_mix[level] = fresh.astype(BF16)
    row = iota(weight_out.shape, 0)
    edge_one, edge_two = 9 * chan(0), 9 * chan(0) + 9 * chan(1)
    rate = jnp.where(row < edge_one, rates[6], jnp.where(row < edge_two, rates[7], rates[8]))
    fresh = weight_out[...] - rate * update_out[...]
    new_out[...] = fresh
    half_out[...] = fresh.astype(BF16)
    for level in range(LEVELS):
        new_bias[level] = weight_bias[level] - rates[9 + level] * update_bias[level]
    lane = iota((1, LANE), 1)
    for ref, norms in ((weight_norm_ref, weight_norms), (update_norm_ref, update_norms)):
        held = jnp.zeros((1, LANE), F32)
        for index in range(15):
            held = jnp.where(lane == index, norms[index], held)
        ref[...] = held[:, :15].reshape(15)
    loss_ref[...] = total[:, 0:1] / LOG_TWO + 8.0 * valid_dims
    valid_ref[...] = valid_dims


def spec_vmem():
    return pl.BlockSpec(memory_space=pltpu.VMEM)


def spec_smem():
    return pl.BlockSpec(memory_space=pltpu.SMEM)


def call(kernel, outs, scalars, arrays, scratch=(), name=None, after=(), vmem=20):
    number = len(scalars) + len(arrays)

    def run(*refs):
        kernel(*refs[:number], *refs[number + len(after) :])

    return pl.pallas_call(
        run,
        out_shape=tuple(jax.ShapeDtypeStruct(shape, dtype) for shape, dtype in outs),
        in_specs=[spec_smem()] * len(scalars)
        + [spec_vmem()] * len(arrays)
        + [pl.BlockSpec(memory_space=pl.ANY)] * len(after),
        out_specs=tuple(spec_vmem() for _ in outs),
        scratch_shapes=list(scratch),
        compiler_params=pltpu.CompilerParams(vmem_limit_bytes=vmem * 1024 * 1024),
        cost_estimate=pl.CostEstimate(
            flops=1000, bytes_accessed=1000, transcendentals=0
        ),
        name=name,
    )(*scalars, *arrays, *after)


def run_pack(conv_in, mixer, conv_out, hidden_bias):
    outs = [((pack_rows(level), LANE), BF16) for level in range(LEVELS)]
    outs.append(((sum(pack_rows(level) for level in range(LEVELS)), LANE), BF16))
    return call(pack_kernel, outs, (), (conv_in, mixer, conv_out, hidden_bias), name="pack", vmem=56)


def run_flow_pre(noise_seeds, valid_shape, images, flow_params, after):
    count = images.shape[1]
    outs = [((stage_rows(level)["rows"], positions(level, count)), F32) for level in range(LEVELS)]
    return call(
        flow_pre_kernel,
        outs,
        (noise_seeds, valid_shape),
        (images, flow_params),
        name="flow_pre",
        after=after,
    )


def run_net(level, images, index, weights, stage, after):
    narrow = len(weights)
    count = positions(level, images)
    outs = [
        ((narrow // 2, grad_rows(level, narrow), LANE), F32),
        ((narrow // 2, grad_rows(level, narrow), LANE), F32),
        ((stage_rows(level)["result_rows"], count), F32),
    ]
    return call(
        functools.partial(net_kernel, level, images, narrow),
        outs,
        (),
        [index] + list(weights) + [stage],
        net_scratch(count),
        name="net_%d" % (level + 1),
        after=after,
    )


def run_flow(level, images, stage, result, carried, after):
    grid = side(level - 1)
    outs = [((chan(level - 1) // 2, images * grid * grid), F32), ((FLOW_ROWS, LANE), F32)]
    return call(
        functools.partial(flow_kernel, level, images),
        outs,
        (),
        [stage, result] + list(carried),
        name="flow_%d" % (level + 1),
        after=after,
    )


def net_scratch(count):
    return [
        pltpu.VMEM((HID, HID), BF16),
        pltpu.VMEM((HID, count), F32),
        pltpu.VMEM((HID, count), F32),
        pltpu.VMEM((HID, count), BF16),
        pltpu.VMEM((HID, count), BF16),
    ]


def run_last(images, index, valid_shape, weights, stage, carried, after):
    narrow = len(weights)
    count = positions(0, images)
    outs = [((narrow // 2, grad_rows(0, narrow), LANE), F32)] * 2
    scratch = [
        pltpu.VMEM((stage_rows(0)["result_rows"], count), F32),
        pltpu.VMEM((FLOW_ROWS, LANE), F32),
    ]
    return call(
        functools.partial(last_kernel, images, narrow),
        outs,
        (valid_shape,),
        [index] + list(weights) + [stage] + list(carried),
        scratch + net_scratch(count),
        name="net_1_and_flow",
        after=after,
    )


def swap(values, axis, step):
    size = lax.axis_size(axis)
    return lax.ppermute(values, axis, [(index, index ^ step) for index in range(size)])


def wide_steps():
    steps = []
    step = 1
    while step < lax.axis_size("wide"):
        steps.append(step)
        step = 2 * step
    return steps


class Summation:
    def __init__(self, level, index, stages, exact):
        self.level, self.index, self.exact = level, index, exact
        self.stages = stages
        self.at = -1
        self.joins = [stage for stage in stages if stage != "shard"][::-1]

    def start(self, keep, send):
        self.kept = keep
        self.other = swap(send, "narrow", 1)

    def merge(self, after):
        exact_in = self.exact if self.at == 0 else 0
        self.at = self.at + 1
        shards, rows, _ = self.kept.shape
        if self.at == len(self.stages):
            (total,) = call(
                functools.partial(merge_kernel, 0, None, 0),
                [((shards, rows, LANE), F32)],
                (),
                (self.index, self.kept, self.other),
                name="total_%d" % (self.level + 1),
                after=after,
            )
            for step in wide_steps():
                if step not in self.stages:
                    total = total + swap(total, "wide", step)
            self.kept = total
            self.other = swap(total, "wide", self.joins[0])
            return total
        stage = self.stages[self.at]
        exact_out = self.exact if self.at == 0 else 0
        if stage == "shard":
            keep, send = (shards // 2, rows, LANE), (shards // 2, rows + 3 * exact_out, LANE)
        else:
            keep = send = (shards, rows // 2, LANE)
        self.kept, sent = call(
            functools.partial(merge_kernel, exact_in, stage, exact_out),
            [(keep, F32), (send, BF16 if self.at == 0 else F32)],
            (),
            (self.index, self.kept, self.other),
            name="merge_%d_%d" % (self.level + 1, self.at),
            after=after,
        )
        if stage == "shard":
            self.other = swap(sent, "narrow", 2)
        else:
            self.other = swap(sent, "wide", stage)
        return self.kept

    def join(self, after):
        step = self.joins.pop(0)
        shards, rows, _ = self.kept.shape
        (self.kept,) = call(
            functools.partial(join_kernel, step),
            [((shards, 2 * rows, LANE), F32)],
            (),
            (self.index, self.kept, self.other),
            name="join_%d" % (self.level + 1),
            after=after,
        )
        if self.joins:
            self.other = swap(self.kept, "wide", self.joins[0])
        return self.kept


def body(
    images,
    noise_seeds,
    valid_shape,
    conv_in,
    mixer,
    conv_out,
    hidden_bias,
    flow_params,
    conv_in_first,
    mixer_first,
    conv_out_first,
    bias_first,
    flow_first,
    conv_in_second,
    mixer_second,
    conv_out_second,
    bias_second,
    flow_second,
):
    count = images.shape[1]
    conv_out, conv_out_first, conv_out_second = conv_out.T, conv_out_first.T, conv_out_second.T
    row = lax.broadcasted_iota(jnp.int32, (8, LANE), 0)
    index = jnp.where(row == 0, lax.axis_index("narrow"), lax.axis_index("wide")).astype(jnp.int32)
    narrow = lax.axis_size("narrow")
    packed = run_pack(conv_in, mixer, conv_out, hidden_bias)
    paired = swap(packed[LEVELS], "narrow", 1)
    crossed = [None] * LEVELS
    for level in (2, 1, 0):
        crossed[level] = swap(packed[level], "narrow", 2)
    stage = run_flow_pre(noise_seeds, valid_shape, images, flow_params, (packed[0],))

    def gather(level, after):
        (copied,) = call(
            copy_kernel,
            [(crossed[level].shape, BF16)],
            (),
            (crossed[level],),
            name="copy_%d" % (level + 1),
            after=after,
        )
        return (packed[level], paired, crossed[level], swap(copied, "narrow", 1)), copied

    bits = [step for step in wide_steps() if step < 8]
    third = Summation(2, index, bits[:1] + ["shard"] + bits[1:], 0)
    second = Summation(1, index, ["shard"] + bits, 0)
    first = Summation(0, index, ["shard"] + bits, flow_block_rows(narrow))
    gathered, token = gather(2, (stage[0],))
    keep, send, result = run_net(2, count, index, gathered, stage[2], (token,))
    third.start(keep, send)
    gathered, token = gather(1, (keep,))
    carried = run_flow(2, count, stage[2], result, (), (token,))
    keep, send, result = run_net(1, count, index, gathered, stage[1], (carried[1],))
    second.start(keep, send)
    gathered, token = gather(0, (keep,))
    token = third.merge((token,))
    carried = run_flow(1, count, stage[1], result, carried, (token,))
    token = second.merge((carried[1],))
    keep, send = run_last(count, index, valid_shape, gathered, stage[0], carried, (token,))
    first.start(keep, send)
    token = first.merge((keep,))
    for _ in range(len(bits) + 1):
        for summation in (second, third, first):
            token = summation.merge((token,))
    for _ in range(len(bits)):
        for summation in (second, third, first):
            token = summation.join((token,))
    grads = (first.kept, second.kept, third.kept)
    weights = (conv_in, mixer, conv_out, hidden_bias)
    shapes = [(weight.shape, F32) for weight in weights]
    share = FLOW_ROWS // narrow
    moved = call(
        functools.partial(moment_kernel, share),
        shapes * 3 + [((16 + share + STATS_ROWS, LANE), F32)],
        (),
        grads
        + weights
        + (conv_in_first, mixer_first, conv_out_first, bias_first)
        + (conv_in_second, mixer_second, conv_out_second, bias_second),
        name="moments",
    )
    blocks = [moved[12]] + [swap(moved[12], "narrow", part) for part in range(1, narrow)]
    flow_shape = (flow_params.shape, F32)
    fresh = call(
        functools.partial(apply_kernel, narrow),
        shapes
        + [flow_shape]
        + [(weight.shape, BF16) for weight in weights[:3]]
        + [flow_shape, flow_shape, ((15,), F32), ((15,), F32), ((1, 1), F32), ((1, 1), F32)],

        (),
        (index,)
        + tuple(blocks)
        + weights
        + tuple(moved[8:12])
        + (flow_params, flow_first, flow_second),
        scratch=[pltpu.VMEM((narrow,) + moved[12].shape, F32)],
        name="apply",
    )
    return (
        fresh[0],
        fresh[1],
        fresh[2].T,
        fresh[3],
        fresh[4],
        moved[0],
        moved[1],
        moved[2].T,
        moved[3],
        fresh[8],
        moved[4],
        moved[5],
        moved[6].T,
        moved[7],
        fresh[9],
        fresh[5],
        fresh[6],
        fresh[7].T,
        fresh[10],
        fresh[11],
        fresh[12].reshape(()),
        fresh[13].reshape(()),
    )


def solution(mesh):
    placed = (
        P(None, ("wide", "narrow"), None),
        P(("wide", "narrow")),
        P(("wide", "narrow"), None),
        P(None, "narrow"),
        P(None, None, "narrow"),
        P("narrow", None),
        P(None, None, "narrow"),
        P(),
    )
    state = (P(None, "narrow"), P(None, None, "narrow"), P("narrow", None), P(None, None, "narrow"), P())
    return jax.shard_map(
        body,
        mesh=mesh,
        in_specs=placed + state + state,
        out_specs=state * 3 + state[:3] + (P(),) * 4,
        check_vma=False,
    )
```

```python
import functools
import jax
import jax.numpy as jnp
from jax import lax
from jax.experimental import pallas as pl
from jax.experimental.pallas import tpu as pltpu
from jax.sharding import PartitionSpec as P

C1 = 12
IMG_SIDE = 32
STEP = 5
HIGHEST_PRECISION = lax.Precision.HIGHEST
LOG_TWO_PI = 1.8378770664093453
LOG_TWO = 0.6931471805599453
FIRST_BETA = 0.5
SECOND_BETA = 0.5
EPSILON = 1e-06
WEIGHT_DECAY = 0.01
LEARN_RATE = 0.25
TAPS = [(-1, -1), (-1, 0), (-1, 1), (0, -1), (0, 0), (0, 1), (1, -1), (1, 0), (1, 1)]
F32 = jnp.float32
BF16 = jnp.bfloat16
HID = 512
LANE = 128
LEVELS = 3
FLOW_ROWS = 32
STATS_ROWS = 8
CODE_BLOCK = 16
CODE_RANGE = 84.0
VMEM_BYTES = 20 * 1024 * 1024


def round_up(value, unit):
    return (value + unit - 1) // unit * unit


def chan(level):
    return C1 * 2**level


def side(level):
    return IMG_SIDE // 2 ** (level + 1)


def real_positions(level, images):
    return images * side(level) ** 2


def positions(level, images):
    return round_up(real_positions(level, images), LANE)


def in_rows(level):
    return 9 * chan(level) // 2


def bias_in_tail(level):
    return round_up(9 * chan(level), 16) - 9 * chan(level) >= 4 and in_rows(level) % 16 > 10


def first_rows(level):
    return round_up(in_rows(level) + (3 if bias_in_tail(level) else 6), 16)


def second_bias_row(level):
    return (pack_rows(level) if bias_in_tail(level) else first_rows(level)) - 4


def last_rows(level):
    return round_up(9 * chan(level), 16)


def pack_rows(level):
    return first_rows(level) + HID + last_rows(level)


def pack_start(level):
    return sum(pack_rows(other) for other in range(LEVELS - 1, level, -1))


def flow_block_rows(narrow):
    return round_up(FLOW_ROWS // narrow, 8) + STATS_ROWS


CHUNKS = ((0, 1), (2,))


def chunk_start(level):
    for chunk, levels in enumerate(CHUNKS):
        if level in levels:
            return chunk, sum(pack_rows(other) for other in levels if other < level)
    return None


def flow_start():
    return sum(pack_rows(level) for level in CHUNKS[-1])


def chunk_rows(chunk, narrow):
    rows = sum(pack_rows(level) for level in CHUNKS[chunk])
    if chunk == len(CHUNKS) - 1:
        rows = rows + flow_block_rows(narrow)
    return round_up(rows, 8 * CODE_BLOCK)


def stage_rows(level):
    padded = round_up(chan(level), 8)
    half = round_up(chan(level) // 2, 8)
    sizes = [
        ("normed", padded),
        ("mixed", padded),
        ("share", 8),
        ("held", padded),
        ("block", padded),
        ("prior", half),
        ("mixing", padded),
        ("turn", padded),
        ("grad", padded),
        ("small", padded),
        ("prior_grad", half),
    ]
    starts = {}
    at = 0
    for name, size in sizes[:8]:
        starts[name] = at
        at = at + size
    starts["rows"] = at
    at = 0
    for name, size in sizes[8:]:
        starts[name] = at
        at = at + size
    starts["result_rows"] = at
    return starts


def flow_lengths():
    return [5 * C1 + 3 * C1 * C1 // 2, 10 * C1 + 6 * C1 * C1, 24 * C1 + 16 * C1 * C1]


def flow_size():
    return sum(flow_lengths())


def flow_offsets(level):
    start = sum(flow_lengths()[:level])
    channels = chan(level)
    offsets = {"bias": start, "logs": start + channels, "block": start + 2 * channels}
    start = start + 2 * channels + channels * channels
    offsets["outbias"] = start
    offsets["outscale"] = start + channels
    start = start + 2 * channels
    if level < LEVELS - 1:
        offsets["priormatrix"] = start
        start = start + channels // 2 * channels
    offsets["priorbias"] = start
    return offsets


def column_names(level):
    channels = chan(level)
    offsets = flow_offsets(level)
    names = [
        ("bias", offsets["bias"]),
        ("logs", offsets["logs"]),
        ("outbias", offsets["outbias"]),
        ("outscale", offsets["outscale"]),
        ("priorbias", offsets["priorbias"]),
    ]
    if level == LEVELS - 1:
        names = names + [("priorscale", offsets["priorbias"] + channels)]
    return names


def exact_dot(first, second):
    return jnp.dot(first, second, precision=HIGHEST_PRECISION, preferred_element_type=F32)


def exact_rows(first, second):
    return lax.dot_general(
        first,
        second,
        (((0,), (0,)), ((), ())),
        precision=HIGHEST_PRECISION,
        preferred_element_type=F32,
    )


def exact_columns(first, second):
    return lax.dot_general(
        first,
        second,
        (((1,), (1,)), ((), ())),
        precision=HIGHEST_PRECISION,
        preferred_element_type=F32,
    )


def plain_dot(first, second):
    return jnp.dot(first, second, preferred_element_type=F32)


def contract_rows(first, second):
    return lax.dot_general(first, second, (((0,), (0,)), ((), ())), preferred_element_type=F32)


def contract_columns(first, second):
    return lax.dot_general(first, second, (((1,), (1,)), ((), ())), preferred_element_type=F32)


def iota(shape, axis):
    return lax.broadcasted_iota(jnp.int32, shape, axis)


def rounded(values):
    return values.astype(BF16).astype(F32)


def split_three(values):
    high = rounded(values)
    rest = values - high
    middle = rounded(rest)
    return [high, middle, rest - middle]


def move_lanes(values, chooser, transposed=False):
    rows = values.shape[0]
    padded = round_up(rows, 8)
    if padded > rows:
        values = jnp.concatenate([values, jnp.zeros((padded - rows, values.shape[1]), F32)], 0)
    pieces = jnp.concatenate(split_three(values), 0).astype(BF16)
    moved = contract_columns(pieces, chooser) if transposed else plain_dot(pieces, chooser)
    moved = moved[:padded] + moved[padded : 2 * padded] + moved[2 * padded :]
    return moved[:rows]


def squeeze_chooser(grid, images):
    count = images * grid * grid
    source = iota((count, count), 0)
    target = iota((count, count), 1)
    shift = grid.bit_length() - 1
    image = lax.shift_right_logical(source, 2 * shift)
    row = lax.shift_right_logical(source, shift) & (grid - 1)
    column = source & (grid - 1)
    half = grid // 2
    place = (
        ((row & 1) * 2 + (column & 1)) * (images * half * half)
        + image * (half * half)
        + lax.shift_right_logical(row, 1) * half
        + lax.shift_right_logical(column, 1)
    )
    return (place == target).astype(F32).astype(BF16)


def order_chooser(channels, stride):
    row = iota((4 * channels, 4 * stride), 0)
    column = iota((4 * channels, 4 * stride), 1)
    return ((row & 3) * stride + lax.shift_right_logical(row, 2) == column).astype(F32)


def squeeze(values, chooser, lanes_out):
    channels, count = values.shape
    moved = move_lanes(values, chooser)
    quarter = count // 4
    stacked = jnp.concatenate([moved[:, k * quarter : (k + 1) * quarter] for k in range(4)], 0)
    ordered = exact_dot(order_chooser(channels, channels), stacked)
    if lanes_out > quarter:
        ordered = jnp.concatenate([ordered, jnp.zeros((4 * channels, lanes_out - quarter), F32)], 1)
    return ordered


def unsqueeze(stacked, chooser, count):
    channels = stacked.shape[0] // 4
    quarter = count // 4
    laid = jnp.concatenate(
        [stacked[k * channels : (k + 1) * channels, :quarter] for k in range(4)], 1
    )
    return move_lanes(laid, chooser, transposed=True)


def slope_roll(values, step):
    step = step % LANE
    while step:
        part = 16 if step >= 16 else 1 << (step.bit_length() - 1)
        values = pltpu.roll(values, 0, 1, stride=part, stride_axis=0)
        step = step - part
    return values


def flow_block(flat, offset, rows, width):
    padded = round_up(rows, 8)
    start = offset + width * iota((padded, FLOW_ROWS), 0)
    line = lax.shift_right_logical(start, 7)
    column = iota((padded, FLOW_ROWS), 1)
    base = -offset % LANE
    if base:
        flat = pltpu.roll(flat, base, 1)
    here = exact_dot((line == column).astype(F32), flat)
    after = exact_dot((line + 1 == column).astype(F32), flat)
    here = slope_roll(here, -width)
    after = slope_roll(after, -width)
    lane = iota((padded, LANE), 1)
    begin = (offset + width * iota((padded, LANE), 0)) & (LANE - 1)
    chosen = jnp.where(lane + begin < LANE, here, after)
    return chosen[:rows, :width]


def flow_block_back(values, offset, rows, width):
    padded = round_up(rows, 8)
    base = offset % LANE
    over = max(base + width - LANE, 0)
    parts = [values[:, width - over :]] if over else []
    if base > over:
        parts.append(jnp.zeros((rows, base - over), F32))
    parts.append(values[:, : width - over])
    if base + width < LANE:
        parts.append(jnp.zeros((rows, LANE - base - width), F32))
    block = jnp.concatenate(parts, 1)
    if padded > rows:
        block = jnp.concatenate([block, jnp.zeros((padded - rows, LANE), F32)], 0)
    block = slope_roll(block, width)
    lane = iota((padded, LANE), 1)
    begin = (offset + width * iota((padded, LANE), 0)) & (LANE - 1)
    here = jnp.where(lane >= begin, block, 0.0)
    after = jnp.where(lane >= begin, 0.0, block)
    line = lax.shift_right_logical(offset + width * iota((FLOW_ROWS, padded), 1), 7)
    row = iota((FLOW_ROWS, padded), 0)
    return exact_dot((line == row).astype(F32), here) + exact_dot(
        (line + 1 == row).astype(F32), after
    )


def flow_column(turned, offset, length):
    line, begin = offset // LANE, offset % LANE
    if begin + length <= LANE:
        return turned[begin : begin + length, line : line + 1]
    return jnp.concatenate(
        [turned[begin:, line : line + 1], turned[: begin + length - LANE, line + 1 : line + 2]], 0
    )


def flow_column_back(values, offset):
    length = values.shape[0]
    line, begin = offset // LANE, offset % LANE
    lane = iota((LANE, LANE), 1)
    head = min(length, LANE - begin)
    parts = []
    if begin:
        parts.append(jnp.zeros((begin, 1), F32))
    parts.append(values[:head])
    if begin + head < LANE:
        parts.append(jnp.zeros((LANE - begin - head, 1), F32))
    column = jnp.concatenate(parts, 0) if len(parts) > 1 else parts[0]
    term = jnp.where(lane == line, column, 0.0)
    if head < length:
        column = jnp.concatenate([values[head:], jnp.zeros((LANE - length + head, 1), F32)], 0)
        term = term + jnp.where(lane == line + 1, column, 0.0)
    return term


def to_flat_rows(values):
    size = values.shape[0]
    row = values.reshape(1, size)
    row = jnp.concatenate([row, jnp.zeros((1, FLOW_ROWS * LANE - size), F32)], 1)
    return row.reshape(FLOW_ROWS, LANE)


def from_flat_rows(values, size):
    return values.reshape(1, FLOW_ROWS * LANE)[:, :size].reshape(size)


def triangles(block):
    channels = block.shape[0]
    row = iota((channels, channels), 0)
    column = iota((channels, channels), 1)
    signs = (1 - 2 * (row & 1)).astype(F32)
    diagonal = signs * jnp.exp(jnp.where(row == column, block, 0.0))
    lower = jnp.where(row > column, block, jnp.where(row == column, 1.0, 0.0))
    upper = jnp.where(row < column, block, jnp.where(row == column, diagonal, 0.0))
    reverse = (row + column == channels - 1).astype(F32)
    return lower, upper, reverse, diagonal


def tap_masks(level, images):
    grid = side(level)
    count = positions(level, images)
    lane = iota((8, count), 1)
    shift = grid.bit_length() - 1
    row = lax.shift_right_logical(lane, shift) & (grid - 1)
    column = lane & (grid - 1)
    inside = lane < real_positions(level, images)
    masks = {}
    for row_step in (-1, 0, 1):
        for column_step in (-1, 0, 1):
            good = (
                (row + row_step >= 0)
                & (row + row_step < grid)
                & (column + column_step >= 0)
                & (column + column_step < grid)
                & inside
            )
            masks[(row_step, column_step)] = jnp.where(good, 1.0, 0.0)[0:1]
    return masks


def tap_read(values, masks, level, row_step, column_step):
    count = values.shape[1]
    offset = (row_step * side(level) + column_step) % count
    if offset:
        values = pltpu.roll(values, count - offset, 1)
    if (row_step, column_step) != (0, 0):
        values = values * masks[(row_step, column_step)]
    return values


def tap_stack(values, masks, level, direction):
    return [
        tap_read(values, masks, level, direction * row_step, direction * column_step)
        for row_step, column_step in TAPS
    ]


def tap_sum(values, masks, level, direction, channels):
    total = None
    for tap, (row_step, column_step) in enumerate(TAPS):
        term = tap_read(
            values[tap * channels : (tap + 1) * channels],
            masks,
            level,
            direction * row_step,
            direction * column_step,
        )
        total = term if total is None else total + term
    return total


def pack_kernel(conv_in_ref, mixer_ref, conv_out_ref, bias_ref, whole_ref):
    in_start = 0
    out_start = 0
    for level in range(LEVELS):
        out_ref = whole_ref.at[pack_start(level) : pack_start(level) + pack_rows(level)]
        rows, columns = in_rows(level), 9 * chan(level)
        top = first_rows(level)
        ones = split_three(bias_ref[level, 0:1, :])
        twos = split_three(bias_ref[level, 1:2, :]) + [jnp.zeros((1, LANE), F32)]
        head = [conv_in_ref[in_start : in_start + rows, :]] + ones
        tail = [conv_out_ref[out_start : out_start + columns, :]]
        for part, size, chosen in (
            (head, top, not bias_in_tail(level)),
            (tail, last_rows(level), bias_in_tail(level)),
        ):
            used = sum(piece.shape[0] for piece in part) + (4 if chosen else 0)
            if size > used:
                part.append(jnp.zeros((size - used, LANE), F32))
            if chosen:
                part.extend(twos)
        out_ref[0:top, :] = jnp.concatenate(head, 0).astype(BF16)
        out_ref[top : top + HID, :] = mixer_ref[level].astype(BF16)
        out_ref[top + HID :, :] = jnp.concatenate(tail, 0).astype(BF16)
        in_start = in_start + rows
        out_start = out_start + columns


def flow_pre_kernel(seed_ref, valid_ref, image_ref, flow_ref, *out_refs):
    images = image_ref.shape[1]
    flat = to_flat_rows(flow_ref[...])
    turned = jnp.concatenate([flat, jnp.zeros((LANE - FLOW_ROWS, LANE), F32)], 0).T
    blocks = IMG_SIDE * IMG_SIDE // 256
    pieces = []
    for image in range(images):
        position = iota((8, IMG_SIDE * IMG_SIDE), 0) * (IMG_SIDE * IMG_SIDE) + iota(
            (8, IMG_SIDE * IMG_SIDE), 1
        )
        hashed = seed_ref[image] + position * jnp.int32(-1640531527)
        hashed = hashed ^ lax.shift_right_logical(hashed, jnp.full_like(hashed, 15))
        hashed = hashed * jnp.int32(739267321)
        hashed = hashed ^ lax.shift_right_logical(hashed, jnp.full_like(hashed, 13))
        field = ((hashed & jnp.int32(16777215)).astype(F32) + 0.5) * 2.0 ** (-24)
        pixel = jnp.concatenate(
            [image_ref[:, image, :], jnp.zeros((5, IMG_SIDE * IMG_SIDE), F32)], 0
        )
        pixel = pixel + field / 256.0
        for block in range(blocks):
            pieces.append(pixel[:, block * 256 : (block + 1) * 256])
    stacked = jnp.concatenate(pieces, 0)
    source = iota((256, 256), 0)
    target = iota((256, 256), 1)
    row = lax.shift_right_logical(source, 5)
    column = source & 31
    place = (
        ((row & 1) * 2 + (column & 1)) * 64
        + lax.shift_right_logical(row, 1) * 16
        + lax.shift_right_logical(column, 1)
    )
    moved = move_lanes(stacked, (place == target).astype(F32).astype(BF16))
    quarters = []
    for k in range(4):
        quarters.append(
            jnp.concatenate(
                [
                    moved[piece * 8 : (piece + 1) * 8, k * 64 : (k + 1) * 64]
                    for piece in range(images * blocks)
                ],
                1,
            )
        )
    state = exact_dot(order_chooser(3, 8), jnp.concatenate(quarters, 0))
    for level in range(LEVELS):
        channels = chan(level)
        grid = side(level)
        count = positions(level, images)
        offsets = flow_offsets(level)
        block = flow_block(flat, offsets["block"], channels, channels)
        names = column_names(level)
        columns = [flow_column(turned, offset, channels) for _, offset in names]
        lane = iota((channels, LANE), 1)
        held = jnp.zeros((channels, LANE), F32)
        for index, column in enumerate(columns):
            held = jnp.where(lane == index, column, held)
        growth = jnp.exp(columns[1])
        normed = (state + columns[0]) * growth
        lower, upper, reverse, _ = triangles(block)
        mixing = exact_dot(exact_dot(reverse, lower), upper)
        mixed = exact_dot(mixing, normed)
        lane = iota((8, count), 1)
        shift = grid.bit_length() - 1
        image = lax.shift_right_logical(lane, 2 * shift)
        row = lax.shift_right_logical(lane, shift) & (grid - 1)
        column = lane & (grid - 1)
        high = jnp.zeros((8, count), jnp.int32)
        wide = jnp.zeros((8, count), jnp.int32)
        for index in range(images):
            high = jnp.where(image == index, valid_ref[index, 0], high)
            wide = jnp.where(image == index, valid_ref[index, 1], wide)
        unit = 2 ** (level + 1)
        row_share = jnp.clip(high - row * unit, 0, unit).astype(F32) / unit
        column_share = jnp.clip(wide - column * unit, 0, unit).astype(F32) / unit
        share = jnp.where(image < images, row_share * column_share, 0.0)
        out_ref = out_refs[level]
        starts = stage_rows(level)
        out_ref[starts["normed"] : starts["normed"] + channels, :] = normed
        out_ref[starts["mixed"] : starts["mixed"] + channels, :] = mixed
        out_ref[starts["share"] : starts["share"] + 8, :] = share
        out_ref[starts["held"] : starts["held"] + channels, 0:LANE] = held
        out_ref[starts["block"] : starts["block"] + channels, 0:channels] = block
        out_ref[starts["mixing"] : starts["mixing"] + channels, 0:channels] = mixing
        if level > 0:
            order = order_chooser(channels // 4, channels // 4)
            out_ref[starts["turn"] : starts["turn"] + channels, 0:channels] = exact_dot(
                mixing, growth * order
            )
        if level < LEVELS - 1:
            out_ref[starts["prior"] : starts["prior"] + channels // 2, 0:channels] = flow_block(
                flat, offsets["priormatrix"], channels // 2, channels
            )
            state = squeeze(
                mixed[: channels // 2], squeeze_chooser(grid, images), positions(level + 1, images)
            )


def silu_parts(values):
    sigmoid = 1.0 / (1.0 + jnp.exp(-values))
    active = values * sigmoid
    slope = sigmoid + active * (1.0 - sigmoid)
    return active, slope


def net_kernel(level, images, narrow, *refs):
    is_last = level == LEVELS - 1
    index_ref = refs[0]
    weight_refs = refs[1 : 1 + narrow]
    base = pack_start(level)
    out_base = chunk_start(level)[1]
    stage_ref, keep_ref, send_ref, result_ref = refs[1 + narrow : 5 + narrow]
    order_ref, slope_one_ref, slope_two_ref, one_ref, two_ref = refs[5 + narrow :]
    starts = stage_rows(level)
    me = index_ref[0, 0]
    channels = chan(level)
    half = channels // 2
    count = positions(level, images)
    top, rows = first_rows(level), in_rows(level)
    tail, used = last_rows(level), 9 * channels
    bias_block = second_bias_row(level) - 12
    masks = tap_masks(level, images)
    width = HID // narrow

    def weights(start, length):
        return jnp.concatenate(
            [ref[base + start : base + start + length, :] for ref in weight_refs], 1
        )

    for r_in in range(narrow):
        for r_out in range(narrow):
            start = pl.multiple_of(base + top + (me ^ r_in) * width, 16)
            order_ref[r_in * width : (r_in + 1) * width, r_out * LANE : (r_out + 1) * LANE] = (
                weight_refs[r_out][pl.ds(start, width), :]
            )
    weight_in = weights(0, top)
    weight_mix = order_ref[...]
    weight_out = weights(top + HID, tail)
    mixed = starts["mixed"]
    first = stage_ref[mixed : mixed + half, :]
    second = stage_ref[mixed + half : mixed + channels, :]
    share = stage_ref[starts["share"] : starts["share"] + 1, :]
    pieces = tap_stack(rounded(first), masks, level, 1)
    pieces.append(jnp.ones((3, count), F32))
    pieces.append(jnp.zeros((top - rows - 3, count), F32))
    stacked = jnp.concatenate(pieces, 0).astype(BF16)
    pick = jnp.where(
        (iota((16, count), 0) >= 12) & (iota((16, count), 0) < 15), 1.0, 0.0
    ).astype(BF16)
    hidden_one = contract_rows(weight_in, stacked)
    active, slope = silu_parts(hidden_one)
    slope_one_ref[...] = slope
    one_ref[...] = active.astype(BF16)
    hidden_two = contract_rows(weight_mix, one_ref[...]) + contract_rows(
        weights(bias_block, 16), pick
    )
    active, slope = silu_parts(hidden_two)
    slope_two_ref[...] = slope
    two_ref[...] = active.astype(BF16)
    spread = plain_dot(weight_out, two_ref[...])
    net_raw = tap_sum(spread, masks, level, 1, channels)
    held = stage_ref[starts["held"] : starts["held"] + channels, 0:LANE]
    out_bias, out_scale = held[:, 2:3], held[:, 3:4]
    growth = jnp.exp(3.0 * out_scale)
    output = (net_raw + out_bias) * growth
    logit = output[half:] + 2.0
    sigmoid = 1.0 / (1.0 + jnp.exp(-logit))
    latent = (second + output[:half]) * sigmoid
    log_sigmoid = jnp.minimum(logit, 0.0) - jnp.log1p(jnp.exp(-jnp.abs(logit)))
    if is_last:
        joined = jnp.concatenate([first, latent], 0)
        mean, scale = held[:, 4:5], held[:, 5:6]
        mean = jnp.broadcast_to(mean, joined.shape)
        scale = jnp.broadcast_to(scale, joined.shape)
    else:
        joined = latent
        prior = stage_ref[starts["prior"] : starts["prior"] + half, 0:channels]
        stats = exact_rows(prior, first) + held[:, 4:5]
        mean, scale = stats[:half], stats[half:]
    gap = joined - mean
    shrink = jnp.exp(-2.0 * scale)
    square = gap * gap * shrink
    log_prior = -0.5 * (LOG_TWO_PI + 2.0 * scale + square)
    total = jnp.sum(jnp.sum(share * log_sigmoid, 0, keepdims=True), 1, keepdims=True) + jnp.sum(
        jnp.sum(share * log_prior, 0, keepdims=True), 1, keepdims=True
    )
    share_total = jnp.sum(share, 1, keepdims=True)
    grad_joined = share * (gap * shrink)
    grad_scale = share * (1.0 - square)
    grad_latent = grad_joined[half:] if is_last else grad_joined
    grad_logit = (grad_latent * latent - share) * (1.0 - sigmoid)
    grad_second = grad_latent * sigmoid
    grad_output = jnp.concatenate([grad_second, grad_logit], 0)
    grad_net = grad_output * growth
    lane = iota((channels, LANE), 1)
    small = jnp.zeros((channels, LANE), F32)

    def put(small, index, values):
        return jnp.where(lane == index, jnp.sum(values, 1, keepdims=True), small)

    small = put(small, 2, grad_net)
    small = put(small, 3, 3.0 * grad_output * output)
    if is_last:
        small = put(small, 4, -grad_joined)
        small = put(small, 5, grad_scale)
        grad_first = grad_joined[:half]
    else:
        grad_stats = jnp.concatenate([-grad_joined, grad_scale], 0)
        small = put(small, 4, grad_stats)
        grad_first = exact_dot(prior, grad_stats)
        prior_grad = exact_columns(first, grad_stats)
        start = starts["prior_grad"]
        result_ref[start : start + half, 0:channels] = prior_grad
    small = jnp.where(lane == 6, -total, small)
    small = jnp.where(lane == 7, share_total, small)
    result_ref[starts["small"] : starts["small"] + channels, 0:LANE] = small
    pieces = tap_stack(rounded(grad_net), masks, level, -1)
    if tail > used:
        pieces.append(jnp.zeros((tail - used, count), F32))
    grad_spread = jnp.concatenate(pieces, 0).astype(BF16)

    def store(start, values):
        for r in range(narrow):
            ref = send_ref if r & 1 else keep_ref
            rows = slice(out_base + start, out_base + start + values.shape[0])
            ref[r // 2, rows, :] = values[:, r * LANE : (r + 1) * LANE]

    grad_out = contract_columns(grad_spread, two_ref[...])
    grad_two = (contract_rows(weight_out, grad_spread) * slope_two_ref[...]).astype(BF16)
    grad_mix = contract_columns(one_ref[...], grad_two)
    for r_in in range(narrow):
        start = pl.multiple_of(out_base + top + (me ^ r_in) * width, 16)
        for r_out in range(narrow):
            ref = send_ref if r_out & 1 else keep_ref
            ref[r_out // 2, pl.ds(start, width), :] = grad_mix[
                r_in * width : (r_in + 1) * width, r_out * LANE : (r_out + 1) * LANE
            ]
    grad_one = (plain_dot(weight_mix, grad_two) * slope_one_ref[...]).astype(BF16)
    grad_in = contract_columns(stacked, grad_one)
    grad_bias = contract_columns(pick, grad_two)
    if bias_in_tail(level):
        grad_out = jnp.concatenate([grad_out[: tail - 16], grad_out[tail - 16 :] + grad_bias], 0)
    else:
        grad_in = jnp.concatenate([grad_in[: top - 16], grad_in[top - 16 :] + grad_bias], 0)
    store(0, grad_in)
    store(top + HID, grad_out)
    grad_stack = plain_dot(weight_in, grad_one)
    grad_first = grad_first + tap_sum(grad_stack, masks, level, -1, half)
    result_ref[0:half, :] = grad_first
    result_ref[half:channels, :] = grad_second


def stage_part(level, ref, name, rows, lanes):
    start = stage_rows(level)[name]
    return ref[start : start + rows, 0:lanes]


def flow_chain(images, stages, results):
    grads = [None] * LEVELS
    carried = None
    for level in (2, 1, 0):
        channels = chan(level)
        count = positions(level, images)
        grad = stage_part(level, results[level], "grad", channels, count)
        if carried is not None:
            grad = grad + jnp.concatenate([carried, jnp.zeros_like(carried)], 0)
        grads[level] = grad
        if level > 0:
            turn = stage_part(level, stages[level], "turn", channels, channels)
            grid = side(level - 1)
            carried = unsqueeze(
                exact_rows(turn, grad), squeeze_chooser(grid, images), images * grid * grid
            )
    return grads


def flow_level(level, images, stage_ref, result_ref, grad):
    channels = chan(level)
    half = channels // 2
    count = positions(level, images)
    offsets = flow_offsets(level)
    normed = stage_part(level, stage_ref, "normed", channels, count)
    held = stage_part(level, stage_ref, "held", channels, LANE)
    block = stage_part(level, stage_ref, "block", channels, channels)
    mixing = stage_part(level, stage_ref, "mixing", channels, channels)
    small = stage_part(level, result_ref, "small", channels, LANE)
    lower, upper, reverse, diagonal = triangles(block)
    grad_normed = exact_rows(mixing, grad)
    grad_mixing = exact_dot(reverse, exact_columns(grad, normed))
    grad_lower = exact_columns(grad_mixing, upper)
    grad_upper = exact_rows(lower, grad_mixing)
    share_total = small[0:1, 7:8]
    row = iota((channels, channels), 0)
    column = iota((channels, channels), 1)
    grad_block = jnp.where(
        row > column,
        grad_lower,
        jnp.where(row < column, grad_upper, grad_upper * diagonal - share_total),
    )
    growth = jnp.exp(held[:, 1:2])
    grad_bias = jnp.sum(grad_normed, 1, keepdims=True) * growth
    grad_logs = jnp.sum(grad_normed * normed, 1, keepdims=True) - share_total
    flat = flow_block_back(grad_block, offsets["block"], channels, channels)
    turned = jnp.zeros((LANE, LANE), F32)
    for index, (name, offset) in enumerate(column_names(level)):
        if name == "bias":
            values = grad_bias
        elif name == "logs":
            values = grad_logs
        else:
            values = small[:, index : index + 1]
        turned = turned + flow_column_back(values, offset)
    if level < LEVELS - 1:
        flat = flat + flow_block_back(
            stage_part(level, result_ref, "prior_grad", half, channels),
            offsets["priormatrix"],
            half,
            channels,
        )
    logs_total = jnp.sum(held[:, 1:2], 0, keepdims=True)
    trace = jnp.sum(
        jnp.sum(jnp.where(row == column, block, 0.0), 0, keepdims=True), 1, keepdims=True
    )
    return flat, turned, small[0:1, 6:7] - share_total * (logs_total + trace)


def flow_back(images, narrow, me, count_ref, stages, results, flat_ref, keep_ref, send_ref):
    grads = flow_chain(images, stages, results)
    parts = [
        flow_level(level, images, stages[level], results[level], grads[level])
        for level in range(LEVELS)
    ]
    flat = sum(part[0] for part in parts) + sum(part[1] for part in parts).T[:FLOW_ROWS]
    loss = sum(part[2] for part in parts)
    pixels = jnp.zeros((), F32)
    for index in range(images):
        pixels = pixels + (count_ref[index, 0] * count_ref[index, 1]).astype(F32)
    lane = iota((STATS_ROWS, LANE), 1)
    stats = jnp.where(lane == 0, loss, jnp.where(lane == 1, pixels, 0.0))
    flat_ref[...] = flat
    share = FLOW_ROWS // narrow
    start = flow_start()
    for r in range(narrow):
        ref = send_ref if r & 1 else keep_ref
        ref[r // 2, start : start + share, :] = flat_ref[
            pl.ds(pl.multiple_of((me ^ r) * share, share), share), :
        ]
        ref[r // 2, start + share : start + share + STATS_ROWS, :] = stats
    zero_rows((keep_ref, send_ref), start + share + STATS_ROWS)


def zero_rows(refs, start):
    for ref in refs:
        rest = ref.shape[1] - start
        if rest:
            ref[:, start:, :] = jnp.zeros((ref.shape[0], rest, LANE), F32)


def nets_kernel(levels, images, narrow, *refs):
    index_ref = refs[0]
    mine = refs[1 : 1 + narrow]
    at = 1 + narrow
    stages = refs[at : at + len(levels)]
    at = at + len(levels)
    keep_ref, send_ref = refs[at : at + 2]
    results = refs[at + 2 : at + 2 + len(levels)]
    at = at + 2 + len(levels)
    for place, level in enumerate(levels):
        net_kernel(
            level,
            images,
            narrow,
            index_ref,
            *mine,
            stages[place],
            keep_ref,
            send_ref,
            results[place],
            *refs[at + 5 * place : at + 5 * place + 5],
        )
    zero_rows((keep_ref, send_ref), sum(pack_rows(level) for level in levels))


def last_kernel(images, narrow, *refs):
    level = LEVELS - 1
    count_ref, index_ref = refs[:2]
    mine = refs[2 : 2 + narrow]
    at = 2 + narrow
    stages = refs[at : at + LEVELS]
    at = at + LEVELS
    results = refs[at : at + LEVELS - 1]
    at = at + LEVELS - 1
    keep_ref, send_ref, result_ref, flat_ref = refs[at : at + 4]
    net_kernel(
        level,
        images,
        narrow,
        index_ref,
        *mine,
        stages[level],
        keep_ref,
        send_ref,
        result_ref,
        *refs[at + 4 :],
    )
    flow_back(
        images,
        narrow,
        index_ref[0, 0],
        count_ref,
        stages,
        list(results) + [result_ref],
        flat_ref,
        keep_ref,
        send_ref,
    )


def copy_kernel(*refs):
    half = len(refs) // 2
    for from_ref, to_ref in zip(refs[:half], refs[half:]):
        to_ref[...] = from_ref[...]


def piece_rows(rows, exact):
    return rows + round_up(rows // CODE_BLOCK, 16) + 3 * exact


def write_piece(ref, values, exact_values=None):
    rows = values.shape[0]
    blocks = values.reshape(rows // CODE_BLOCK, CODE_BLOCK, LANE)
    scale = rounded(jnp.max(jnp.abs(blocks), axis=1) * 1.01)
    factor = jnp.where(scale > 0.0, CODE_RANGE / scale, 0.0)
    code = jnp.exp(blocks * factor[:, None, :])
    ref[0:rows, :] = code.reshape(rows, LANE).astype(BF16)
    size = round_up(rows // CODE_BLOCK, 16)
    if size > rows // CODE_BLOCK:
        scale = jnp.concatenate([scale, jnp.zeros((size - rows // CODE_BLOCK, LANE), F32)], 0)
    ref[rows : rows + size, :] = scale.astype(BF16)
    if exact_values is not None:
        ref[rows + size :, :] = jnp.concatenate(split_three(exact_values), 0).astype(BF16)


def read_piece(ref, rows):
    blocks = jnp.log(ref[0:rows, :].astype(F32)).reshape(rows // CODE_BLOCK, CODE_BLOCK, LANE)
    scale = ref[rows : rows + round_up(rows // CODE_BLOCK, 16), :].astype(F32)
    factor = scale[: rows // CODE_BLOCK] * (1.0 / CODE_RANGE)
    return (blocks * factor[:, None, :]).reshape(rows, LANE)


def read_exact(ref, rows, exact):
    start = rows + round_up(rows // CODE_BLOCK, 16)
    pieces = ref[start : start + 3 * exact, :].astype(F32)
    return pieces[:exact] + pieces[exact : 2 * exact] + pieces[2 * exact :]


def wide_bit(index_ref, bit):
    return jnp.where((index_ref[1, 0] & bit) != 0, 1, 0)


def exact_place(rows):
    return flow_start() // rows, flow_start() % rows


def square_kernel(exact, index_ref, keep_ref, other_ref, mine_ref, *sent_refs):
    half = keep_ref.shape[1] // 2
    upper = wide_bit(index_ref, 1)

    def total(shard, flipped):
        place = 1 - upper if flipped else upper
        picked = pl.ds(pl.multiple_of(place * half, 16), half)
        return keep_ref[shard, picked, :] + other_ref[shard, picked, :]

    mine_ref[...] = total(0, 0)
    for ref, (shard, flipped) in zip(sent_refs, ((1, 0), (0, 1), (1, 1))):
        exact_values = None
        if exact:
            picked = slice(flow_start(), flow_start() + exact)
            exact_values = keep_ref[shard, picked, :] + other_ref[shard, picked, :]
        write_piece(ref, total(shard, flipped), exact_values)


def column_kernel(exact, index_ref, mine_ref, *refs):
    others, (keep_ref, sent_ref, total_ref) = refs[:3], refs[3:]
    rows = mine_ref.shape[0]
    half = rows // 2
    total = mine_ref[...]
    for other in others:
        total = total + read_piece(other, rows)
    total_ref[...] = total
    exact_values = None
    if exact:
        part, start = exact_place(rows)
        exact_values = mine_ref[start : start + exact, :]
        for other in others:
            exact_values = exact_values + read_exact(other, rows, exact)

        @pl.when(wide_bit(index_ref, 1) == part)
        def _():
            total_ref[start : start + exact, :] = exact_values

    place = wide_bit(index_ref, 2)
    keep_ref[...] = total_ref[pl.ds(pl.multiple_of(place * half, 16), half), :]
    values = total_ref[pl.ds(pl.multiple_of((1 - place) * half, 16), half), :]
    write_piece(sent_ref, values, exact_values)


def code_kernel(exact, index_ref, mine_ref, other_ref, out_ref):
    rows = mine_ref.shape[0]
    exact_values = None
    if exact:
        _, start = exact_place(rows)
        exact_values = mine_ref[start : start + exact, :] + read_exact(other_ref, rows, exact)
    write_piece(out_ref, mine_ref[...] + read_piece(other_ref, rows), exact_values)


def recode_kernel(exact, rows, index_ref, mine_ref, other_ref, out_ref):
    exact_values = None
    if exact:
        exact_values = read_exact(mine_ref, rows, exact) + read_exact(other_ref, rows, exact)
    write_piece(out_ref, read_piece(mine_ref, rows) + read_piece(other_ref, rows), exact_values)


def decode_kernel(exact, index_ref, *refs):
    parts, out_ref = refs[:4], refs[4]
    rows = out_ref.shape[0] // 4
    place = 2 * wide_bit(index_ref, 1) + wide_bit(index_ref, 2)
    for flip, ref in enumerate(parts):
        start = pl.multiple_of((place ^ flip) * rows, 16)
        out_ref[pl.ds(start, rows), :] = read_piece(ref, rows)
    if exact:
        part, start = exact_place(rows)
        for flip, ref in enumerate(parts):

            @pl.when((place ^ flip) == part)
            def _():
                out_ref[flow_start() : flow_start() + exact, :] = read_exact(ref, rows, exact)


def moments(weight, gradient, first_old, second_old):
    first_new = FIRST_BETA * first_old + (1.0 - FIRST_BETA) * gradient
    second_new = SECOND_BETA * second_old + (1.0 - SECOND_BETA) * gradient * gradient
    update = (
        first_new
        / (1.0 - FIRST_BETA**STEP)
        / (jnp.sqrt(second_new / (1.0 - SECOND_BETA**STEP)) + EPSILON)
        + WEIGHT_DECAY * weight
    )
    return first_new, second_new, update


def total_of(values):
    return jnp.sum(jnp.sum(values, 0, keepdims=True), 1, keepdims=True)


def squares_rows(sums):
    row = iota((16, LANE), 0)
    held = jnp.zeros((16, LANE), F32)
    for index, value in enumerate(sums):
        held = jnp.where(row == index, value, held)
    return held


def group_totals(values_in, values_mix, values_out, values_bias):
    row = iota(values_in.shape, 0)
    line = iota(values_out.shape, 0)
    sums = []
    start = 0
    for level in range(LEVELS):
        inside = (row >= start) & (row < start + in_rows(level))
        sums.append(total_of(jnp.where(inside, values_in, 0.0)))
        start = start + in_rows(level)
    for level in range(LEVELS):
        sums.append(total_of(values_mix[level]))
    start = 0
    for level in range(LEVELS):
        inside = (line >= start) & (line < start + 9 * chan(level))
        sums.append(total_of(jnp.where(inside, values_out, 0.0)))
        start = start + 9 * chan(level)
    for level in range(LEVELS):
        sums.append(total_of(values_bias[2 * level : 2 * level + 2]))
    return sums


def flow_masks():
    place = iota((FLOW_ROWS, LANE), 0) * LANE + iota((FLOW_ROWS, LANE), 1)
    masks = []
    start = 0
    for length in flow_lengths():
        masks.append((place >= start) & (place < start + length))
        start = start + length
    return masks


def moment_kernel(share, *refs):
    chunks = refs[:2]
    grads = []
    for level in range(LEVELS):
        chunk, start = chunk_start(level)
        grads.append(chunks[chunk].at[start : start + pack_rows(level)])
    weight_in, weight_mix, weight_out, weight_bias = refs[2:6]
    first_in, first_mix, first_out, first_bias = refs[6:10]
    second_in, second_mix, second_out, second_bias = refs[10:14]
    outs = refs[14:]
    flow_ref = chunks[-1].at[flow_start() : flow_start() + share + STATS_ROWS]
    total = flow_ref[share : share + 1, :]
    valid_dims = 3.0 * total[:, 1:2]
    scale = 1.0 / (valid_dims * LOG_TWO)
    grad_in = jnp.concatenate([grads[level][0 : in_rows(level), :] for level in range(LEVELS)], 0)
    tails = [
        grads[level][first_rows(level) + HID : first_rows(level) + HID + 9 * chan(level), :]
        for level in range(LEVELS)
    ]
    grad_out = jnp.concatenate(tails, 0)
    bias_rows = []
    for level in range(LEVELS):
        bias_rows.append(grads[level][in_rows(level) : in_rows(level) + 1, :])
        bias_rows.append(grads[level][second_bias_row(level) : second_bias_row(level) + 1, :])
    grad_bias = jnp.concatenate(bias_rows, 0)
    bias = weight_bias[...].reshape(2 * LEVELS, LANE)
    new_in = moments(weight_in[...], grad_in * scale, first_in[...], second_in[...])
    new_out = moments(weight_out[...], grad_out * scale, first_out[...], second_out[...])
    new_bias = moments(
        bias,
        grad_bias * scale,
        first_bias[...].reshape(2 * LEVELS, LANE),
        second_bias[...].reshape(2 * LEVELS, LANE),
    )
    mix_squares = []
    mix_updates = []
    for level in range(LEVELS):
        top = first_rows(level)
        new_mix = moments(
            weight_mix[level],
            grads[level][top : top + HID, :] * scale,
            first_mix[level],
            second_mix[level],
        )
        outs[1][level] = new_mix[0]
        outs[5][level] = new_mix[1]
        outs[9][level] = new_mix[2]
        mix_squares.append(weight_mix[level] * weight_mix[level])
        mix_updates.append(new_mix[2] * new_mix[2])
    for index, values in ((0, new_in), (2, new_out), (3, new_bias)):
        for kind in range(3):
            value = values[kind]
            if index == 3:
                value = value.reshape(LEVELS, 2, LANE)
            outs[4 * kind + index][...] = value
    weight_sums = group_totals(
        weight_in[...] * weight_in[...], mix_squares, weight_out[...] * weight_out[...], bias * bias
    )
    update_sums = group_totals(
        new_in[2] * new_in[2], mix_updates, new_out[2] * new_out[2], new_bias[2] * new_bias[2]
    )
    lane = iota((16, LANE), 1)
    outs[12][0:16, :] = jnp.where(lane == 0, squares_rows(weight_sums), squares_rows(update_sums))
    outs[12][16:, :] = flow_ref[...]


def apply_kernel(narrow, *refs):
    index_ref = refs[0]
    block_refs = refs[1 : 1 + narrow]
    at = 1 + narrow
    weight_in, weight_mix, weight_out, weight_bias = refs[at : at + 4]
    update_in, update_mix, update_out, update_bias = refs[at + 4 : at + 8]
    flow_ref, flow_first_ref, flow_second_ref = refs[at + 8 : at + 11]
    at = at + 11
    (
        new_in,
        new_mix,
        new_out,
        new_bias,
        new_flow,
        half_in,
        half_mix,
        half_out,
        flow_moment,
        flow_square,
        weight_norm_ref,
        update_norm_ref,
        loss_ref,
        valid_ref,
        order_ref,
    ) = refs[at:]
    for part in range(narrow):
        order_ref[index_ref[0, 0] ^ part] = block_refs[part][...]
    share = FLOW_ROWS // narrow
    sums = order_ref[0, 0:16, :]
    for part in range(1, narrow):
        sums = sums + order_ref[part, 0:16, :]
    flow_grad = jnp.concatenate([order_ref[part, 16 : 16 + share, :] for part in range(narrow)], 0)
    total = block_refs[0][16 + share : 17 + share, :]
    valid_dims = 3.0 * total[:, 1:2]
    scale = 1.0 / (valid_dims * LOG_TWO)
    flow = to_flat_rows(flow_ref[...])
    size = flow_ref.shape[0]
    place = iota((FLOW_ROWS, LANE), 0) * LANE + iota((FLOW_ROWS, LANE), 1)
    flow_grad = jnp.where(place < size, flow_grad * scale, 0.0)
    first_new, second_new, update = moments(
        flow, flow_grad, to_flat_rows(flow_first_ref[...]), to_flat_rows(flow_second_ref[...])
    )
    weight_norms = [jnp.sqrt(sums[index : index + 1, 0:1]) for index in range(12)]
    update_norms = [jnp.sqrt(sums[index : index + 1, 1:2]) for index in range(12)]
    masks = flow_masks()
    for mask in masks:
        weight_norms.append(jnp.sqrt(total_of(jnp.where(mask, flow * flow, 0.0))))
        update_norms.append(jnp.sqrt(total_of(jnp.where(mask, update * update, 0.0))))
    rates = [
        LEARN_RATE * (weight_norm / update_norm)
        for weight_norm, update_norm in zip(weight_norms, update_norms)
    ]
    rate = jnp.zeros((FLOW_ROWS, LANE), F32)
    for mask, value in zip(masks, rates[12:]):
        rate = jnp.where(mask, value, rate)
    new_flow[...] = from_flat_rows(flow - rate * update, size)
    flow_moment[...] = from_flat_rows(first_new, size)
    flow_square[...] = from_flat_rows(second_new, size)
    row = iota(weight_in.shape, 0)
    edge_one, edge_two = in_rows(0), in_rows(0) + in_rows(1)
    rate = jnp.where(row < edge_one, rates[0], jnp.where(row < edge_two, rates[1], rates[2]))
    fresh = weight_in[...] - rate * update_in[...]
    new_in[...] = fresh
    half_in[...] = fresh.astype(BF16)
    for level in range(LEVELS):
        fresh = weight_mix[level] - rates[3 + level] * update_mix[level]
        new_mix[level] = fresh
        half_mix[level] = fresh.astype(BF16)
    row = iota(weight_out.shape, 0)
    edge_one, edge_two = 9 * chan(0), 9 * chan(0) + 9 * chan(1)
    rate = jnp.where(row < edge_one, rates[6], jnp.where(row < edge_two, rates[7], rates[8]))
    fresh = weight_out[...] - rate * update_out[...]
    new_out[...] = fresh
    half_out[...] = fresh.astype(BF16)
    for level in range(LEVELS):
        new_bias[level] = weight_bias[level] - rates[9 + level] * update_bias[level]
    lane = iota((1, LANE), 1)
    for ref, norms in ((weight_norm_ref, weight_norms), (update_norm_ref, update_norms)):
        held = jnp.zeros((1, LANE), F32)
        for index in range(15):
            held = jnp.where(lane == index, norms[index], held)
        ref[...] = held[:, :15].reshape(15)
    loss_ref[...] = total[:, 0:1] / LOG_TWO + 8.0 * valid_dims
    valid_ref[...] = valid_dims


def spec_vmem():
    return pl.BlockSpec(memory_space=pltpu.VMEM)


def spec_smem():
    return pl.BlockSpec(memory_space=pltpu.SMEM)


def call(kernel, outs, scalars, arrays, scratch=(), name=None, after=(), vmem=20):
    number = len(scalars) + len(arrays)

    def run(*refs):
        kernel(*refs[:number], *refs[number + len(after) :])

    return pl.pallas_call(
        run,
        out_shape=tuple(jax.ShapeDtypeStruct(shape, dtype) for shape, dtype in outs),
        in_specs=[spec_smem()] * len(scalars)
        + [spec_vmem()] * len(arrays)
        + [pl.BlockSpec(memory_space=pl.ANY)] * len(after),
        out_specs=tuple(spec_vmem() for _ in outs),
        scratch_shapes=list(scratch),
        compiler_params=pltpu.CompilerParams(vmem_limit_bytes=vmem * 1024 * 1024),
        cost_estimate=pl.CostEstimate(
            flops=1000, bytes_accessed=1000, transcendentals=0
        ),
        name=name,
    )(*scalars, *arrays, *after)


def run_pack(conv_in, mixer, conv_out, hidden_bias):
    outs = [((sum(pack_rows(level) for level in range(LEVELS)), LANE), BF16)]
    return call(pack_kernel, outs, (), (conv_in, mixer, conv_out, hidden_bias), name="pack", vmem=56)


def run_flow_pre(noise_seeds, valid_shape, images, flow_params, after):
    count = images.shape[1]
    outs = [((stage_rows(level)["rows"], positions(level, count)), F32) for level in range(LEVELS)]
    return call(
        flow_pre_kernel,
        outs,
        (noise_seeds, valid_shape),
        (images, flow_params),
        name="flow_pre",
        after=after,
    )


def run_nets(levels, images, index, weights, stages, after):
    narrow = len(weights)
    rows = chunk_rows(chunk_start(levels[0])[0], narrow)
    outs = [((narrow // 2, rows, LANE), F32)] * 2
    scratch = []
    for level in levels:
        count = positions(level, images)
        outs = outs + [((stage_rows(level)["result_rows"], count), F32)]
        scratch = scratch + net_scratch(count)
    return call(
        functools.partial(nets_kernel, levels, images, narrow),
        outs,
        (),
        [index] + list(weights) + [stages[level] for level in levels],
        scratch,
        name="nets_" + "_".join(str(level + 1) for level in levels),
        after=after,
    )


def net_scratch(count):
    return [
        pltpu.VMEM((HID, HID), BF16),
        pltpu.VMEM((HID, count), F32),
        pltpu.VMEM((HID, count), F32),
        pltpu.VMEM((HID, count), BF16),
        pltpu.VMEM((HID, count), BF16),
    ]


def run_last(images, index, valid_shape, weights, stages, results, after):
    narrow = len(weights)
    level = LEVELS - 1
    count = positions(level, images)
    return call(
        functools.partial(last_kernel, images, narrow),
        [((narrow // 2, chunk_rows(len(CHUNKS) - 1, narrow), LANE), F32)] * 2,
        (valid_shape,),
        [index] + list(weights) + list(stages) + list(results),
        [
            pltpu.VMEM((stage_rows(level)["result_rows"], count), F32),
            pltpu.VMEM((FLOW_ROWS, LANE), F32),
        ]
        + net_scratch(count),
        name="net_3_and_flow",
        after=after,
    )


def swap(values, wide, narrow):
    width = lax.axis_size("narrow")
    mask = wide * width + narrow
    count = lax.axis_size("wide") * width
    return lax.ppermute(values, ("wide", "narrow"), [(place, place ^ mask) for place in range(count)])


class Summation:
    def __init__(self, chunk, index, exact):
        self.name, self.index, self.exact = "abc"[chunk], index, exact

    def start(self, keep, send):
        self.kept, self.others = keep, [swap(send, 0, 1)]

    def run(self, kernel, outs, arrays, after, name, scratch=()):
        return call(
            kernel,
            outs,
            (),
            (self.index, *arrays),
            scratch,
            name=name + "_" + self.name,
            after=after,
        )

    def square(self, after):
        rows = self.kept.shape[1] // 2
        self.kept, *sent = self.run(
            functools.partial(square_kernel, self.exact),
            [((rows, LANE), F32)] + [((piece_rows(rows, self.exact), LANE), BF16)] * 3,
            (self.kept, *self.others),
            after,
            "square",
        )
        self.others = [swap(sent[0], 0, 2), swap(sent[1], 1, 0), swap(sent[2], 1, 2)]
        return self.kept

    def column(self, after):
        rows = self.kept.shape[0]
        self.rows = rows // 2
        self.piece = ((piece_rows(self.rows, self.exact), LANE), BF16)
        self.kept, sent = self.run(
            functools.partial(column_kernel, self.exact),
            [((self.rows, LANE), F32), self.piece],
            (self.kept, *self.others),
            after,
            "column",
            [pltpu.VMEM((rows, LANE), F32)],
        )
        self.others = [swap(sent, 2, 0)]
        return self.kept

    def code(self, after):
        (self.kept,) = self.run(
            functools.partial(code_kernel, self.exact),
            [self.piece],
            (self.kept, *self.others),
            after,
            "code",
        )
        self.others = [swap(self.kept, 4, 0)]
        return self.kept

    def spread(self, after):
        step = 4
        while step < lax.axis_size("wide"):
            (self.kept,) = self.run(
                functools.partial(recode_kernel, self.exact, self.rows),
                [self.piece],
                (self.kept, *self.others),
                after,
                "recode_%d" % step,
            )
            step = 2 * step
            if step < lax.axis_size("wide"):
                self.others = [swap(self.kept, step, 0)]
        self.others = [swap(self.kept, 2, 0), swap(self.kept, 1, 0), swap(self.kept, 3, 0)]
        return self.kept

    def decode(self, rows, after):
        (self.kept,) = self.run(
            functools.partial(decode_kernel, self.exact),
            [((rows, LANE), F32)],
            (self.kept, *self.others),
            after,
            "decode",
        )
        return self.kept


def body(
    images,
    noise_seeds,
    valid_shape,
    conv_in,
    mixer,
    conv_out,
    hidden_bias,
    flow_params,
    conv_in_first,
    mixer_first,
    conv_out_first,
    bias_first,
    flow_first,
    conv_in_second,
    mixer_second,
    conv_out_second,
    bias_second,
    flow_second,
):
    count = images.shape[1]
    conv_out, conv_out_first, conv_out_second = conv_out.T, conv_out_first.T, conv_out_second.T
    row = lax.broadcasted_iota(jnp.int32, (8, LANE), 0)
    index = jnp.where(row == 0, lax.axis_index("narrow"), lax.axis_index("wide")).astype(jnp.int32)
    narrow = lax.axis_size("narrow")
    (packed,) = run_pack(conv_in, mixer, conv_out, hidden_bias)
    paired = swap(packed, 0, 1)
    crossed = swap(packed, 0, 2)
    stages = run_flow_pre(noise_seeds, valid_shape, images, flow_params, ())
    arrays = (crossed, *stages)
    copied, *stages = call(
        copy_kernel, [(array.shape, array.dtype) for array in arrays], (), arrays, name="copy"
    )
    gathered = (packed, paired, crossed, swap(copied, 0, 1))
    one = Summation(0, index, 0)
    two = Summation(1, index, flow_block_rows(narrow))
    keep, send, *results = run_nets(CHUNKS[0], count, index, gathered, stages, (copied,))
    one.start(keep, send)
    keep, send = run_last(count, index, valid_shape, gathered, stages, results, (keep,))
    two.start(keep, send)
    sizes = one.kept.shape[1], two.kept.shape[1]
    token = one.square((keep,))
    token = two.square((token,))
    token = one.column((token,))
    token = two.column((token,))
    token = one.code((token,))
    token = two.code((token,))
    token = one.spread((token,))
    token = two.spread((token,))
    token = one.decode(sizes[0], (token,))
    token = two.decode(sizes[1], (token,))
    grads = (one.kept, two.kept)
    weights = (conv_in, mixer, conv_out, hidden_bias)
    shapes = [(weight.shape, F32) for weight in weights]
    share = FLOW_ROWS // narrow
    moved = call(
        functools.partial(moment_kernel, share),
        shapes * 3 + [((16 + share + STATS_ROWS, LANE), F32)],
        (),
        grads
        + weights
        + (conv_in_first, mixer_first, conv_out_first, bias_first)
        + (conv_in_second, mixer_second, conv_out_second, bias_second),
        name="moments",
    )
    blocks = [moved[12]] + [swap(moved[12], 0, part) for part in range(1, narrow)]
    flow_shape = (flow_params.shape, F32)
    fresh = call(
        functools.partial(apply_kernel, narrow),
        shapes
        + [flow_shape]
        + [(weight.shape, BF16) for weight in weights[:3]]
        + [flow_shape, flow_shape, ((15,), F32), ((15,), F32), ((1, 1), F32), ((1, 1), F32)],

        (),
        (index,)
        + tuple(blocks)
        + weights
        + tuple(moved[8:12])
        + (flow_params, flow_first, flow_second),
        scratch=[pltpu.VMEM((narrow,) + moved[12].shape, F32)],
        name="apply",
    )
    return (
        fresh[0],
        fresh[1],
        fresh[2].T,
        fresh[3],
        fresh[4],
        moved[0],
        moved[1],
        moved[2].T,
        moved[3],
        fresh[8],
        moved[4],
        moved[5],
        moved[6].T,
        moved[7],
        fresh[9],
        fresh[5],
        fresh[6],
        fresh[7].T,
        fresh[10],
        fresh[11],
        fresh[12].reshape(()),
        fresh[13].reshape(()),
    )


def solution(mesh):
    placed = (
        P(None, ("wide", "narrow"), None),
        P(("wide", "narrow")),
        P(("wide", "narrow"), None),
        P(None, "narrow"),
        P(None, None, "narrow"),
        P("narrow", None),
        P(None, None, "narrow"),
        P(),
    )
    state = (P(None, "narrow"), P(None, None, "narrow"), P("narrow", None), P(None, None, "narrow"), P())
    return jax.shard_map(
        body,
        mesh=mesh,
        in_specs=placed + state + state,
        out_specs=state * 3 + state[:3] + (P(),) * 4,
        check_vma=False,
    )
```

```python
import functools
import jax
import jax.numpy as jnp
from jax import lax
from jax.experimental import pallas as pl
from jax.experimental.pallas import tpu as pltpu
from jax.sharding import PartitionSpec as P

C1 = 12
IMG_SIDE = 32
STEP = 5
HIGHEST_PRECISION = lax.Precision.HIGHEST
LOG_TWO_PI = 1.8378770664093453
LOG_TWO = 0.6931471805599453
FIRST_BETA = 0.5
SECOND_BETA = 0.5
EPSILON = 1e-06
WEIGHT_DECAY = 0.01
LEARN_RATE = 0.25
TAPS = [(-1, -1), (-1, 0), (-1, 1), (0, -1), (0, 0), (0, 1), (1, -1), (1, 0), (1, 1)]
F32 = jnp.float32
BF16 = jnp.bfloat16
HID = 512
LANE = 128
LEVELS = 3
FLOW_ROWS = 32
STATS_ROWS = 8
CODE_BLOCK = 16
CODE_RANGE = 84.0
VMEM_BYTES = 20 * 1024 * 1024


def round_up(value, unit):
    return (value + unit - 1) // unit * unit


def chan(level):
    return C1 * 2**level


def side(level):
    return IMG_SIDE // 2 ** (level + 1)


def real_positions(level, images):
    return images * side(level) ** 2


def positions(level, images):
    return round_up(real_positions(level, images), LANE)


def in_rows(level):
    return 9 * chan(level) // 2


def bias_in_tail(level):
    return round_up(9 * chan(level), 16) - 9 * chan(level) >= 4 and in_rows(level) % 16 > 10


def first_rows(level):
    return round_up(in_rows(level) + (3 if bias_in_tail(level) else 6), 16)


def second_bias_row(level):
    return (pack_rows(level) if bias_in_tail(level) else first_rows(level)) - 4


def last_rows(level):
    return round_up(9 * chan(level), 16)


def pack_rows(level):
    return first_rows(level) + HID + last_rows(level)


def pack_start(level):
    return sum(pack_rows(other) for other in range(LEVELS - 1, level, -1))


CHUNKS = ((0, 1), (2,))


def chunk_of(level):
    for chunk, levels in enumerate(CHUNKS):
        if level in levels:
            return chunk, sum(pack_rows(other) for other in levels[: levels.index(level)])
    return None


def quarter_rows(chunk):
    return round_up(sum(pack_rows(level) for level in CHUNKS[chunk]), 4 * CODE_BLOCK) // 4


def flow_part(chunk):
    return FLOW_ROWS if chunk == len(CHUNKS) - 1 else 0


def stage_rows(level):
    padded = round_up(chan(level), 8)
    half = round_up(chan(level) // 2, 8)
    sizes = [
        ("normed", padded),
        ("mixed", padded),
        ("share", 8),
        ("held", padded),
        ("block", padded),
        ("prior", half),
        ("mixing", padded),
        ("turn", padded),
        ("grad", padded),
        ("small", padded),
        ("prior_grad", half),
    ]
    starts = {}
    at = 0
    for name, size in sizes[:8]:
        starts[name] = at
        at = at + size
    starts["rows"] = at
    at = 0
    for name, size in sizes[8:]:
        starts[name] = at
        at = at + size
    starts["result_rows"] = at
    return starts


def flow_lengths():
    return [5 * C1 + 3 * C1 * C1 // 2, 10 * C1 + 6 * C1 * C1, 24 * C1 + 16 * C1 * C1]


def flow_size():
    return sum(flow_lengths())


def flow_offsets(level):
    start = sum(flow_lengths()[:level])
    channels = chan(level)
    offsets = {"bias": start, "logs": start + channels, "block": start + 2 * channels}
    start = start + 2 * channels + channels * channels
    offsets["outbias"] = start
    offsets["outscale"] = start + channels
    start = start + 2 * channels
    if level < LEVELS - 1:
        offsets["priormatrix"] = start
        start = start + channels // 2 * channels
    offsets["priorbias"] = start
    return offsets


def column_names(level):
    channels = chan(level)
    offsets = flow_offsets(level)
    names = [
        ("bias", offsets["bias"]),
        ("logs", offsets["logs"]),
        ("outbias", offsets["outbias"]),
        ("outscale", offsets["outscale"]),
        ("priorbias", offsets["priorbias"]),
    ]
    if level == LEVELS - 1:
        names = names + [("priorscale", offsets["priorbias"] + channels)]
    return names


def exact_dot(first, second):
    return jnp.dot(first, second, precision=HIGHEST_PRECISION, preferred_element_type=F32)


def exact_rows(first, second):
    return lax.dot_general(
        first,
        second,
        (((0,), (0,)), ((), ())),
        precision=HIGHEST_PRECISION,
        preferred_element_type=F32,
    )


def exact_columns(first, second):
    return lax.dot_general(
        first,
        second,
        (((1,), (1,)), ((), ())),
        precision=HIGHEST_PRECISION,
        preferred_element_type=F32,
    )


def plain_dot(first, second):
    return jnp.dot(first, second, preferred_element_type=F32)


def contract_rows(first, second):
    return lax.dot_general(first, second, (((0,), (0,)), ((), ())), preferred_element_type=F32)


def contract_columns(first, second):
    return lax.dot_general(first, second, (((1,), (1,)), ((), ())), preferred_element_type=F32)


def iota(shape, axis):
    return lax.broadcasted_iota(jnp.int32, shape, axis)


def rounded(values):
    return values.astype(BF16).astype(F32)


def split_three(values):
    high = rounded(values)
    rest = values - high
    middle = rounded(rest)
    return [high, middle, rest - middle]


def move_lanes(values, chooser, transposed=False):
    rows = values.shape[0]
    padded = round_up(rows, 8)
    if padded > rows:
        values = jnp.concatenate([values, jnp.zeros((padded - rows, values.shape[1]), F32)], 0)
    pieces = jnp.concatenate(split_three(values), 0).astype(BF16)
    moved = contract_columns(pieces, chooser) if transposed else plain_dot(pieces, chooser)
    moved = moved[:padded] + moved[padded : 2 * padded] + moved[2 * padded :]
    return moved[:rows]


def squeeze_chooser(grid, images):
    count = images * grid * grid
    source = iota((count, count), 0)
    target = iota((count, count), 1)
    shift = grid.bit_length() - 1
    image = lax.shift_right_logical(source, 2 * shift)
    row = lax.shift_right_logical(source, shift) & (grid - 1)
    column = source & (grid - 1)
    half = grid // 2
    place = (
        ((row & 1) * 2 + (column & 1)) * (images * half * half)
        + image * (half * half)
        + lax.shift_right_logical(row, 1) * half
        + lax.shift_right_logical(column, 1)
    )
    return (place == target).astype(F32).astype(BF16)


def order_chooser(channels, stride):
    row = iota((4 * channels, 4 * stride), 0)
    column = iota((4 * channels, 4 * stride), 1)
    return ((row & 3) * stride + lax.shift_right_logical(row, 2) == column).astype(F32)


def squeeze(values, chooser, lanes_out):
    channels, count = values.shape
    moved = move_lanes(values, chooser)
    quarter = count // 4
    stacked = jnp.concatenate([moved[:, k * quarter : (k + 1) * quarter] for k in range(4)], 0)
    ordered = exact_dot(order_chooser(channels, channels), stacked)
    if lanes_out > quarter:
        ordered = jnp.concatenate([ordered, jnp.zeros((4 * channels, lanes_out - quarter), F32)], 1)
    return ordered


def unsqueeze(stacked, chooser, count):
    channels = stacked.shape[0] // 4
    quarter = count // 4
    laid = jnp.concatenate(
        [stacked[k * channels : (k + 1) * channels, :quarter] for k in range(4)], 1
    )
    return move_lanes(laid, chooser, transposed=True)


def slope_roll(values, step):
    step = step % LANE
    while step:
        part = 16 if step >= 16 else 1 << (step.bit_length() - 1)
        values = pltpu.roll(values, 0, 1, stride=part, stride_axis=0)
        step = step - part
    return values


def flow_block(flat, offset, rows, width):
    padded = round_up(rows, 8)
    start = offset + width * iota((padded, FLOW_ROWS), 0)
    line = lax.shift_right_logical(start, 7)
    column = iota((padded, FLOW_ROWS), 1)
    base = -offset % LANE
    if base:
        flat = pltpu.roll(flat, base, 1)
    here = exact_dot((line == column).astype(F32), flat)
    after = exact_dot((line + 1 == column).astype(F32), flat)
    here = slope_roll(here, -width)
    after = slope_roll(after, -width)
    lane = iota((padded, LANE), 1)
    begin = (offset + width * iota((padded, LANE), 0)) & (LANE - 1)
    chosen = jnp.where(lane + begin < LANE, here, after)
    return chosen[:rows, :width]


def flow_block_back(values, offset, rows, width):
    padded = round_up(rows, 8)
    base = offset % LANE
    over = max(base + width - LANE, 0)
    parts = [values[:, width - over :]] if over else []
    if base > over:
        parts.append(jnp.zeros((rows, base - over), F32))
    parts.append(values[:, : width - over])
    if base + width < LANE:
        parts.append(jnp.zeros((rows, LANE - base - width), F32))
    block = jnp.concatenate(parts, 1)
    if padded > rows:
        block = jnp.concatenate([block, jnp.zeros((padded - rows, LANE), F32)], 0)
    block = slope_roll(block, width)
    lane = iota((padded, LANE), 1)
    begin = (offset + width * iota((padded, LANE), 0)) & (LANE - 1)
    here = jnp.where(lane >= begin, block, 0.0)
    after = jnp.where(lane >= begin, 0.0, block)
    line = lax.shift_right_logical(offset + width * iota((FLOW_ROWS, padded), 1), 7)
    row = iota((FLOW_ROWS, padded), 0)
    return exact_dot((line == row).astype(F32), here) + exact_dot(
        (line + 1 == row).astype(F32), after
    )


def flow_column(turned, offset, length):
    line, begin = offset // LANE, offset % LANE
    if begin + length <= LANE:
        return turned[begin : begin + length, line : line + 1]
    return jnp.concatenate(
        [turned[begin:, line : line + 1], turned[: begin + length - LANE, line + 1 : line + 2]], 0
    )


def flow_column_back(values, offset):
    length = values.shape[0]
    line, begin = offset // LANE, offset % LANE
    lane = iota((LANE, LANE), 1)
    head = min(length, LANE - begin)
    parts = []
    if begin:
        parts.append(jnp.zeros((begin, 1), F32))
    parts.append(values[:head])
    if begin + head < LANE:
        parts.append(jnp.zeros((LANE - begin - head, 1), F32))
    column = jnp.concatenate(parts, 0) if len(parts) > 1 else parts[0]
    term = jnp.where(lane == line, column, 0.0)
    if head < length:
        column = jnp.concatenate([values[head:], jnp.zeros((LANE - length + head, 1), F32)], 0)
        term = term + jnp.where(lane == line + 1, column, 0.0)
    return term


def to_flat_rows(values):
    size = values.shape[0]
    row = values.reshape(1, size)
    row = jnp.concatenate([row, jnp.zeros((1, FLOW_ROWS * LANE - size), F32)], 1)
    return row.reshape(FLOW_ROWS, LANE)


def from_flat_rows(values, size):
    return values.reshape(1, FLOW_ROWS * LANE)[:, :size].reshape(size)


def triangles(block):
    channels = block.shape[0]
    row = iota((channels, channels), 0)
    column = iota((channels, channels), 1)
    signs = (1 - 2 * (row & 1)).astype(F32)
    diagonal = signs * jnp.exp(jnp.where(row == column, block, 0.0))
    lower = jnp.where(row > column, block, jnp.where(row == column, 1.0, 0.0))
    upper = jnp.where(row < column, block, jnp.where(row == column, diagonal, 0.0))
    reverse = (row + column == channels - 1).astype(F32)
    return lower, upper, reverse, diagonal


def tap_masks(level, images):
    grid = side(level)
    count = positions(level, images)
    lane = iota((8, count), 1)
    shift = grid.bit_length() - 1
    row = lax.shift_right_logical(lane, shift) & (grid - 1)
    column = lane & (grid - 1)
    inside = lane < real_positions(level, images)
    masks = {}
    for row_step in (-1, 0, 1):
        for column_step in (-1, 0, 1):
            good = (
                (row + row_step >= 0)
                & (row + row_step < grid)
                & (column + column_step >= 0)
                & (column + column_step < grid)
                & inside
            )
            masks[(row_step, column_step)] = jnp.where(good, 1.0, 0.0)[0:1]
    return masks


def tap_read(values, masks, level, row_step, column_step):
    count = values.shape[1]
    offset = (row_step * side(level) + column_step) % count
    if offset:
        values = pltpu.roll(values, count - offset, 1)
    if (row_step, column_step) != (0, 0):
        values = values * masks[(row_step, column_step)]
    return values


def tap_stack(values, masks, level, direction):
    return [
        tap_read(values, masks, level, direction * row_step, direction * column_step)
        for row_step, column_step in TAPS
    ]


def tap_sum(values, masks, level, direction, channels):
    total = None
    for tap, (row_step, column_step) in enumerate(TAPS):
        term = tap_read(
            values[tap * channels : (tap + 1) * channels],
            masks,
            level,
            direction * row_step,
            direction * column_step,
        )
        total = term if total is None else total + term
    return total


def pack_kernel(valid_ref, conv_in_ref, mixer_ref, conv_out_ref, bias_ref, whole_ref):
    in_start = 0
    out_start = 0
    for level in range(LEVELS):
        out_ref = whole_ref.at[pack_start(level) : pack_start(level) + pack_rows(level)]
        rows, columns = in_rows(level), 9 * chan(level)
        top = first_rows(level)
        ones = split_three(bias_ref[level, 0:1, :])
        twos = split_three(bias_ref[level, 1:2, :]) + [jnp.zeros((1, LANE), F32)]
        head = [conv_in_ref[in_start : in_start + rows, :]] + ones
        tail = [conv_out_ref[out_start : out_start + columns, :]]
        for part, size, chosen in (
            (head, top, not bias_in_tail(level)),
            (tail, last_rows(level), bias_in_tail(level)),
        ):
            used = sum(piece.shape[0] for piece in part) + (4 if chosen else 0)
            if size > used:
                part.append(jnp.zeros((size - used, LANE), F32))
            if chosen:
                part.extend(twos)
        out_ref[0:top, :] = jnp.concatenate(head, 0).astype(BF16)
        out_ref[top : top + HID, :] = mixer_ref[level].astype(BF16)
        out_ref[top + HID :, :] = jnp.concatenate(tail, 0).astype(BF16)
        in_start = in_start + rows
        out_start = out_start + columns
    pixels = jnp.int32(0)
    for image in range(valid_ref.shape[0]):
        pixels = pixels + valid_ref[image, 0] * valid_ref[image, 1]
    lane = iota((16, LANE), 1)
    digits = jnp.where(lane == 0, pixels & 127, 0)
    for place in (1, 2):
        digits = jnp.where(lane == place, lax.shift_right_logical(pixels, 7 * place) & 127, digits)
    whole_ref[pack_start(-1) :, :] = digits.astype(F32).astype(BF16)


def flow_pre_kernel(seed_ref, valid_ref, image_ref, flow_ref, *out_refs):
    images = image_ref.shape[1]
    flat = to_flat_rows(flow_ref[...])
    turned = jnp.concatenate([flat, jnp.zeros((LANE - FLOW_ROWS, LANE), F32)], 0).T
    blocks = IMG_SIDE * IMG_SIDE // 256
    pieces = []
    for image in range(images):
        position = iota((8, IMG_SIDE * IMG_SIDE), 0) * (IMG_SIDE * IMG_SIDE) + iota(
            (8, IMG_SIDE * IMG_SIDE), 1
        )
        hashed = seed_ref[image] + position * jnp.int32(-1640531527)
        hashed = hashed ^ lax.shift_right_logical(hashed, jnp.full_like(hashed, 15))
        hashed = hashed * jnp.int32(739267321)
        hashed = hashed ^ lax.shift_right_logical(hashed, jnp.full_like(hashed, 13))
        field = ((hashed & jnp.int32(16777215)).astype(F32) + 0.5) * 2.0 ** (-24)
        pixel = jnp.concatenate(
            [image_ref[:, image, :], jnp.zeros((5, IMG_SIDE * IMG_SIDE), F32)], 0
        )
        pixel = pixel + field / 256.0
        for block in range(blocks):
            pieces.append(pixel[:, block * 256 : (block + 1) * 256])
    stacked = jnp.concatenate(pieces, 0)
    source = iota((256, 256), 0)
    target = iota((256, 256), 1)
    row = lax.shift_right_logical(source, 5)
    column = source & 31
    place = (
        ((row & 1) * 2 + (column & 1)) * 64
        + lax.shift_right_logical(row, 1) * 16
        + lax.shift_right_logical(column, 1)
    )
    moved = move_lanes(stacked, (place == target).astype(F32).astype(BF16))
    quarters = []
    for k in range(4):
        quarters.append(
            jnp.concatenate(
                [
                    moved[piece * 8 : (piece + 1) * 8, k * 64 : (k + 1) * 64]
                    for piece in range(images * blocks)
                ],
                1,
            )
        )
    state = exact_dot(order_chooser(3, 8), jnp.concatenate(quarters, 0))
    for level in range(LEVELS):
        channels = chan(level)
        grid = side(level)
        count = positions(level, images)
        offsets = flow_offsets(level)
        block = flow_block(flat, offsets["block"], channels, channels)
        names = column_names(level)
        columns = [flow_column(turned, offset, channels) for _, offset in names]
        lane = iota((channels, LANE), 1)
        held = jnp.zeros((channels, LANE), F32)
        for index, column in enumerate(columns):
            held = jnp.where(lane == index, column, held)
        growth = jnp.exp(columns[1])
        normed = (state + columns[0]) * growth
        lower, upper, reverse, _ = triangles(block)
        mixing = exact_dot(exact_dot(reverse, lower), upper)
        mixed = exact_dot(mixing, normed)
        lane = iota((8, count), 1)
        shift = grid.bit_length() - 1
        image = lax.shift_right_logical(lane, 2 * shift)
        row = lax.shift_right_logical(lane, shift) & (grid - 1)
        column = lane & (grid - 1)
        high = jnp.zeros((8, count), jnp.int32)
        wide = jnp.zeros((8, count), jnp.int32)
        for index in range(images):
            high = jnp.where(image == index, valid_ref[index, 0], high)
            wide = jnp.where(image == index, valid_ref[index, 1], wide)
        unit = 2 ** (level + 1)
        row_share = jnp.clip(high - row * unit, 0, unit).astype(F32) / unit
        column_share = jnp.clip(wide - column * unit, 0, unit).astype(F32) / unit
        share = jnp.where(image < images, row_share * column_share, 0.0)
        out_ref = out_refs[level]
        starts = stage_rows(level)
        out_ref[starts["normed"] : starts["normed"] + channels, :] = normed
        out_ref[starts["mixed"] : starts["mixed"] + channels, :] = mixed
        out_ref[starts["share"] : starts["share"] + 8, :] = share
        out_ref[starts["held"] : starts["held"] + channels, 0:LANE] = held
        out_ref[starts["block"] : starts["block"] + channels, 0:channels] = block
        out_ref[starts["mixing"] : starts["mixing"] + channels, 0:channels] = mixing
        if level > 0:
            order = order_chooser(channels // 4, channels // 4)
            out_ref[starts["turn"] : starts["turn"] + channels, 0:channels] = exact_dot(
                mixing, growth * order
            )
        if level < LEVELS - 1:
            out_ref[starts["prior"] : starts["prior"] + channels // 2, 0:channels] = flow_block(
                flat, offsets["priormatrix"], channels // 2, channels
            )
            state = squeeze(
                mixed[: channels // 2], squeeze_chooser(grid, images), positions(level + 1, images)
            )


def silu_parts(values):
    sigmoid = 1.0 / (1.0 + jnp.exp(-values))
    active = values * sigmoid
    slope = sigmoid + active * (1.0 - sigmoid)
    return active, slope


def net_kernel(level, images, narrow, *refs):
    is_last = level == LEVELS - 1
    index_ref = refs[0]
    weight_refs = refs[1 : 1 + narrow]
    base = pack_start(level)
    out_base = chunk_of(level)[1]
    stage_ref, keep_ref, send_ref, result_ref = refs[1 + narrow : 5 + narrow]
    order_ref, slope_one_ref, slope_two_ref, one_ref, two_ref = refs[5 + narrow :]
    starts = stage_rows(level)
    me = index_ref[0, 0]
    channels = chan(level)
    half = channels // 2
    count = positions(level, images)
    top, rows = first_rows(level), in_rows(level)
    tail, used = last_rows(level), 9 * channels
    bias_block = second_bias_row(level) - 12
    masks = tap_masks(level, images)
    width = HID // narrow

    def weights(start, length):
        return jnp.concatenate(
            [ref[base + start : base + start + length, :] for ref in weight_refs], 1
        )

    for r_in in range(narrow):
        for r_out in range(narrow):
            start = pl.multiple_of(base + top + (me ^ r_in) * width, 16)
            order_ref[r_in * width : (r_in + 1) * width, r_out * LANE : (r_out + 1) * LANE] = (
                weight_refs[r_out][pl.ds(start, width), :]
            )
    weight_in = weights(0, top)
    weight_mix = order_ref[...]
    weight_out = weights(top + HID, tail)
    mixed = starts["mixed"]
    first = stage_ref[mixed : mixed + half, :]
    second = stage_ref[mixed + half : mixed + channels, :]
    share = stage_ref[starts["share"] : starts["share"] + 1, :]
    pieces = tap_stack(rounded(first), masks, level, 1)
    pieces.append(jnp.ones((3, count), F32))
    pieces.append(jnp.zeros((top - rows - 3, count), F32))
    stacked = jnp.concatenate(pieces, 0).astype(BF16)
    pick = jnp.where(
        (iota((16, count), 0) >= 12) & (iota((16, count), 0) < 15), 1.0, 0.0
    ).astype(BF16)
    hidden_one = contract_rows(weight_in, stacked)
    active, slope = silu_parts(hidden_one)
    slope_one_ref[...] = slope
    one_ref[...] = active.astype(BF16)
    hidden_two = contract_rows(weight_mix, one_ref[...]) + contract_rows(
        weights(bias_block, 16), pick
    )
    active, slope = silu_parts(hidden_two)
    slope_two_ref[...] = slope
    two_ref[...] = active.astype(BF16)
    spread = plain_dot(weight_out, two_ref[...])
    net_raw = tap_sum(spread, masks, level, 1, channels)
    held = stage_ref[starts["held"] : starts["held"] + channels, 0:LANE]
    out_bias, out_scale = held[:, 2:3], held[:, 3:4]
    growth = jnp.exp(3.0 * out_scale)
    output = (net_raw + out_bias) * growth
    logit = output[half:] + 2.0
    sigmoid = 1.0 / (1.0 + jnp.exp(-logit))
    latent = (second + output[:half]) * sigmoid
    log_sigmoid = jnp.minimum(logit, 0.0) - jnp.log1p(jnp.exp(-jnp.abs(logit)))
    if is_last:
        joined = jnp.concatenate([first, latent], 0)
        mean, scale = held[:, 4:5], held[:, 5:6]
        mean = jnp.broadcast_to(mean, joined.shape)
        scale = jnp.broadcast_to(scale, joined.shape)
    else:
        joined = latent
        prior = stage_ref[starts["prior"] : starts["prior"] + half, 0:channels]
        stats = exact_rows(prior, first) + held[:, 4:5]
        mean, scale = stats[:half], stats[half:]
    gap = joined - mean
    shrink = jnp.exp(-2.0 * scale)
    square = gap * gap * shrink
    log_prior = -0.5 * (LOG_TWO_PI + 2.0 * scale + square)
    total = jnp.sum(jnp.sum(share * log_sigmoid, 0, keepdims=True), 1, keepdims=True) + jnp.sum(
        jnp.sum(share * log_prior, 0, keepdims=True), 1, keepdims=True
    )
    share_total = jnp.sum(share, 1, keepdims=True)
    grad_joined = share * (gap * shrink)
    grad_scale = share * (1.0 - square)
    grad_latent = grad_joined[half:] if is_last else grad_joined
    grad_logit = (grad_latent * latent - share) * (1.0 - sigmoid)
    grad_second = grad_latent * sigmoid
    grad_output = jnp.concatenate([grad_second, grad_logit], 0)
    grad_net = grad_output * growth
    lane = iota((channels, LANE), 1)
    small = jnp.zeros((channels, LANE), F32)

    def put(small, index, values):
        return jnp.where(lane == index, jnp.sum(values, 1, keepdims=True), small)

    small = put(small, 2, grad_net)
    small = put(small, 3, 3.0 * grad_output * output)
    if is_last:
        small = put(small, 4, -grad_joined)
        small = put(small, 5, grad_scale)
        grad_first = grad_joined[:half]
    else:
        grad_stats = jnp.concatenate([-grad_joined, grad_scale], 0)
        small = put(small, 4, grad_stats)
        grad_first = exact_dot(prior, grad_stats)
        prior_grad = exact_columns(first, grad_stats)
        start = starts["prior_grad"]
        result_ref[start : start + half, 0:channels] = prior_grad
    small = jnp.where(lane == 6, -total, small)
    small = jnp.where(lane == 7, share_total, small)
    result_ref[starts["small"] : starts["small"] + channels, 0:LANE] = small
    pieces = tap_stack(rounded(grad_net), masks, level, -1)
    if tail > used:
        pieces.append(jnp.zeros((tail - used, count), F32))
    grad_spread = jnp.concatenate(pieces, 0).astype(BF16)

    def store(start, values):
        for r in range(narrow):
            ref = send_ref if r & 1 else keep_ref
            rows = slice(out_base + start, out_base + start + values.shape[0])
            ref[r // 2, rows, :] = values[:, r * LANE : (r + 1) * LANE]

    grad_out = contract_columns(grad_spread, two_ref[...])
    grad_two = (contract_rows(weight_out, grad_spread) * slope_two_ref[...]).astype(BF16)
    grad_mix = contract_columns(one_ref[...], grad_two)
    for r_in in range(narrow):
        start = pl.multiple_of(out_base + top + (me ^ r_in) * width, 16)
        for r_out in range(narrow):
            ref = send_ref if r_out & 1 else keep_ref
            ref[r_out // 2, pl.ds(start, width), :] = grad_mix[
                r_in * width : (r_in + 1) * width, r_out * LANE : (r_out + 1) * LANE
            ]
    grad_one = (plain_dot(weight_mix, grad_two) * slope_one_ref[...]).astype(BF16)
    grad_in = contract_columns(stacked, grad_one)
    grad_bias = contract_columns(pick, grad_two)
    if bias_in_tail(level):
        grad_out = jnp.concatenate([grad_out[: tail - 16], grad_out[tail - 16 :] + grad_bias], 0)
    else:
        grad_in = jnp.concatenate([grad_in[: top - 16], grad_in[top - 16 :] + grad_bias], 0)
    store(0, grad_in)
    store(top + HID, grad_out)
    grad_stack = plain_dot(weight_in, grad_one)
    grad_first = grad_first + tap_sum(grad_stack, masks, level, -1, half)
    result_ref[0:half, :] = grad_first
    result_ref[half:channels, :] = grad_second


def stage_part(level, ref, name, rows, lanes):
    start = stage_rows(level)[name]
    return ref[start : start + rows, 0:lanes]


def flow_chain(images, stages, results):
    grads = [None] * LEVELS
    carried = None
    for level in (2, 1, 0):
        channels = chan(level)
        count = positions(level, images)
        grad = stage_part(level, results[level], "grad", channels, count)
        if carried is not None:
            grad = grad + jnp.concatenate([carried, jnp.zeros_like(carried)], 0)
        grads[level] = grad
        if level > 0:
            turn = stage_part(level, stages[level], "turn", channels, channels)
            grid = side(level - 1)
            carried = unsqueeze(
                exact_rows(turn, grad), squeeze_chooser(grid, images), images * grid * grid
            )
    return grads


def flow_level(level, images, stage_ref, result_ref, grad):
    channels = chan(level)
    half = channels // 2
    count = positions(level, images)
    offsets = flow_offsets(level)
    normed = stage_part(level, stage_ref, "normed", channels, count)
    held = stage_part(level, stage_ref, "held", channels, LANE)
    block = stage_part(level, stage_ref, "block", channels, channels)
    mixing = stage_part(level, stage_ref, "mixing", channels, channels)
    small = stage_part(level, result_ref, "small", channels, LANE)
    lower, upper, reverse, diagonal = triangles(block)
    grad_normed = exact_rows(mixing, grad)
    grad_mixing = exact_dot(reverse, exact_columns(grad, normed))
    grad_lower = exact_columns(grad_mixing, upper)
    grad_upper = exact_rows(lower, grad_mixing)
    share_total = small[0:1, 7:8]
    row = iota((channels, channels), 0)
    column = iota((channels, channels), 1)
    grad_block = jnp.where(
        row > column,
        grad_lower,
        jnp.where(row < column, grad_upper, grad_upper * diagonal - share_total),
    )
    growth = jnp.exp(held[:, 1:2])
    grad_bias = jnp.sum(grad_normed, 1, keepdims=True) * growth
    grad_logs = jnp.sum(grad_normed * normed, 1, keepdims=True) - share_total
    flat = flow_block_back(grad_block, offsets["block"], channels, channels)
    turned = jnp.zeros((LANE, LANE), F32)
    for index, (name, offset) in enumerate(column_names(level)):
        if name == "bias":
            values = grad_bias
        elif name == "logs":
            values = grad_logs
        else:
            values = small[:, index : index + 1]
        turned = turned + flow_column_back(values, offset)
    if level < LEVELS - 1:
        flat = flat + flow_block_back(
            stage_part(level, result_ref, "prior_grad", half, channels),
            offsets["priormatrix"],
            half,
            channels,
        )
    logs_total = jnp.sum(held[:, 1:2], 0, keepdims=True)
    trace = jnp.sum(
        jnp.sum(jnp.where(row == column, block, 0.0), 0, keepdims=True), 1, keepdims=True
    )
    return flat, turned, small[0:1, 6:7] - share_total * (logs_total + trace)


def flow_back(images, stages, results, weights, out_ref):
    grads = flow_chain(images, stages, results)
    parts = [
        flow_level(level, images, stages[level], results[level], grads[level])
        for level in range(LEVELS)
    ]
    flat = sum(part[0] for part in parts) + sum(part[1] for part in parts).T[:FLOW_ROWS]
    loss = sum(part[2] for part in parts)
    pixels = jnp.zeros((1, 1), F32)
    start = pack_start(-1)
    for ref in weights:
        digits = ref[start : start + 16, :].astype(F32)
        for place in range(3):
            pixels = pixels + 128.0**place * digits[0:1, place : place + 1]
    lane = iota((STATS_ROWS, LANE), 1)
    out_ref[0:FLOW_ROWS, :] = flat
    out_ref[FLOW_ROWS:, :] = jnp.where(lane == 0, loss, jnp.where(lane == 1, pixels, 0.0))


def zero_rows(refs, start):
    for ref in refs:
        rest = ref.shape[1] - start
        if rest:
            ref[:, start:, :] = jnp.zeros((ref.shape[0], rest, LANE), F32)


def nets_kernel(chunk, images, narrow, *refs):
    levels = CHUNKS[chunk]
    number = len(levels)
    index_ref = refs[0]
    mine = refs[1 : 1 + narrow]
    at = 1 + narrow
    stages = refs[at : at + number]
    at = at + number
    keep_ref, send_ref = refs[at : at + 2]
    results = refs[at + 2 : at + 2 + number]
    at = at + 2 + number
    for place, level in enumerate(levels):
        net_kernel(
            level,
            images,
            narrow,
            index_ref,
            *mine,
            stages[place],
            keep_ref,
            send_ref,
            results[place],
            *refs[at + 5 * place : at + 5 * place + 5],
        )
    zero_rows((keep_ref, send_ref), sum(pack_rows(level) for level in levels))


def flow_kernel(images, narrow, *refs):
    stages, results = refs[:LEVELS], refs[LEVELS : 2 * LEVELS]
    weights, out_ref = refs[2 * LEVELS : -1], refs[-1]
    flow_back(images, stages, results, weights, out_ref)


def copy_kernel(*refs):
    half = len(refs) // 2
    for from_ref, to_ref in zip(refs[:half], refs[half:]):
        to_ref[...] = from_ref[...]


def piece_rows(rows):
    return rows + round_up(rows // CODE_BLOCK, 16)


def write_piece(ref, start, values, extra=None):
    rows = values.shape[0]
    blocks = values.reshape(rows // CODE_BLOCK, CODE_BLOCK, LANE)
    scale = rounded(jnp.max(jnp.abs(blocks), axis=1) * 1.01)
    factor = jnp.where(scale > 0.0, CODE_RANGE / scale, 0.0)
    code = jnp.exp(blocks * factor[:, None, :])
    ref[start : start + rows, :] = code.reshape(rows, LANE).astype(BF16)
    tail = [scale] + ([] if extra is None else split_three(extra))
    used = sum(part.shape[0] for part in tail)
    size = round_up(rows // CODE_BLOCK, 16)
    if size > used:
        tail.append(jnp.zeros((size - used, LANE), F32))
    ref[start + rows : start + rows + size, :] = jnp.concatenate(tail, 0).astype(BF16)


def read_piece(ref, start, rows):
    blocks = jnp.log(ref[start : start + rows, :].astype(F32))
    blocks = blocks.reshape(rows // CODE_BLOCK, CODE_BLOCK, LANE)
    scale = ref[start + rows : start + piece_rows(rows), :].astype(F32)
    factor = scale[: rows // CODE_BLOCK] * (1.0 / CODE_RANGE)
    return (blocks * factor[:, None, :]).reshape(rows, LANE)


def read_stats(ref, start, rows):
    first = start + rows + rows // CODE_BLOCK
    tail = ref[first : first + 3, :].astype(F32)
    return tail[0:1] + tail[1:2] + tail[2:3]


def wide_bit(index_ref, bit):
    return jnp.where((index_ref[1, 0] & bit) != 0, 1, 0)


def square_kernel(chunk, index_ref, keep_ref, other_ref, *refs):
    flow = None
    if flow_part(chunk):
        flow_ref, mine_ref, own_flow_ref, *sent_refs = refs
        flow = flow_ref[0:FLOW_ROWS, :]
        stats = flow_ref[FLOW_ROWS : FLOW_ROWS + 1, :]
        write_piece(own_flow_ref, 0, flow, stats)
    else:
        mine_ref, *sent_refs = refs
    half = 2 * quarter_rows(chunk)
    upper = wide_bit(index_ref, 1)

    def total(shard, flipped):
        place = 1 - upper if flipped else upper
        picked = pl.ds(pl.multiple_of(place * half, CODE_BLOCK), half)
        return keep_ref[shard, picked, :] + other_ref[shard, picked, :]

    mine_ref[...] = total(0, 0)
    for ref, (shard, flipped) in zip(sent_refs, ((1, 0), (0, 1), (1, 1))):
        values = total(shard, flipped)
        if flow is None:
            write_piece(ref, 0, values)
        else:
            write_piece(ref, 0, jnp.concatenate([values, flow], 0), stats)


def column_kernel(chunk, index_ref, mine_ref, *refs):
    rows = 2 * quarter_rows(chunk)
    more = flow_part(chunk)
    if more:
        own_flow_ref, *others, keep_ref, own_next_ref, sent_ref, total_ref = refs
    else:
        *others, keep_ref, sent_ref, total_ref = refs
    total = mine_ref[...]
    for flip, other in enumerate(others, 1):
        values = read_piece(other, 0, rows + more)
        total = total + values[:rows]
        if more and flip == 2:
            flow = read_piece(own_flow_ref, 0, FLOW_ROWS) + values[rows:]
            stats = read_stats(own_flow_ref, 0, FLOW_ROWS) + read_stats(other, 0, rows + more)
    total_ref[...] = total
    half = rows // 2
    place = wide_bit(index_ref, 2)
    keep_ref[...] = total_ref[pl.ds(pl.multiple_of(place * half, CODE_BLOCK), half), :]
    values = total_ref[pl.ds(pl.multiple_of((1 - place) * half, CODE_BLOCK), half), :]
    if more:
        write_piece(own_next_ref, 0, flow, stats)
        write_piece(sent_ref, 0, jnp.concatenate([values, flow], 0), stats)
    else:
        write_piece(sent_ref, 0, values)


def code_kernel(chunk, index_ref, mine_ref, *refs):
    rows = quarter_rows(chunk)
    more = flow_part(chunk)
    if more:
        own_flow_ref, other_ref, out_ref = refs
    else:
        other_ref, out_ref = refs
    values = read_piece(other_ref, 0, rows + more)
    total = mine_ref[...] + values[:rows]
    if more:
        flow = read_piece(own_flow_ref, 0, FLOW_ROWS) + values[rows:]
        stats = read_stats(own_flow_ref, 0, FLOW_ROWS) + read_stats(other_ref, 0, rows + more)
        write_piece(out_ref, 0, jnp.concatenate([total, flow], 0), stats)
    else:
        write_piece(out_ref, 0, total)


def recode_kernel(chunk, index_ref, mine_ref, other_ref, out_ref):
    rows = quarter_rows(chunk) + flow_part(chunk)
    stats = None
    if flow_part(chunk):
        stats = read_stats(mine_ref, 0, rows) + read_stats(other_ref, 0, rows)
    write_piece(out_ref, 0, read_piece(mine_ref, 0, rows) + read_piece(other_ref, 0, rows), stats)


def decode_kernel(chunk, index_ref, *refs):
    parts, outs = refs[:4], refs[4:]
    place = 2 * wide_bit(index_ref, 1) + wide_bit(index_ref, 2)
    rows, more = quarter_rows(chunk), flow_part(chunk)
    for flip, ref in enumerate(parts):
        values = read_piece(ref, 0, rows + more)
        start = pl.multiple_of((place ^ flip) * rows, CODE_BLOCK)
        outs[0][pl.ds(start, rows), :] = values[:rows]
        if more and flip == 0:
            outs[1][0:FLOW_ROWS, :] = values[rows:]
            outs[1][FLOW_ROWS:, :] = jnp.broadcast_to(
                read_stats(ref, 0, rows + more), (STATS_ROWS, LANE)
            )


def moments(weight, gradient, first_old, second_old):
    first_new = FIRST_BETA * first_old + (1.0 - FIRST_BETA) * gradient
    second_new = SECOND_BETA * second_old + (1.0 - SECOND_BETA) * gradient * gradient
    update = (
        first_new
        / (1.0 - FIRST_BETA**STEP)
        / (jnp.sqrt(second_new / (1.0 - SECOND_BETA**STEP)) + EPSILON)
        + WEIGHT_DECAY * weight
    )
    return first_new, second_new, update


def total_of(values):
    return jnp.sum(jnp.sum(values, 0, keepdims=True), 1, keepdims=True)


def squares_rows(sums):
    row = iota((16, LANE), 0)
    held = jnp.zeros((16, LANE), F32)
    for index, value in enumerate(sums):
        held = jnp.where(row == index, value, held)
    return held


def group_totals(values_in, values_mix, values_out, values_bias):
    row = iota(values_in.shape, 0)
    line = iota(values_out.shape, 0)
    sums = []
    start = 0
    for level in range(LEVELS):
        inside = (row >= start) & (row < start + in_rows(level))
        sums.append(total_of(jnp.where(inside, values_in, 0.0)))
        start = start + in_rows(level)
    for level in range(LEVELS):
        sums.append(total_of(values_mix[level]))
    start = 0
    for level in range(LEVELS):
        inside = (line >= start) & (line < start + 9 * chan(level))
        sums.append(total_of(jnp.where(inside, values_out, 0.0)))
        start = start + 9 * chan(level)
    for level in range(LEVELS):
        sums.append(total_of(values_bias[2 * level : 2 * level + 2]))
    return sums


def flow_masks():
    place = iota((FLOW_ROWS, LANE), 0) * LANE + iota((FLOW_ROWS, LANE), 1)
    masks = []
    start = 0
    for length in flow_lengths():
        masks.append((place >= start) & (place < start + length))
        start = start + length
    return masks


def split_grads(refs, scale):
    ins, mixes, outs, biases = [], [], [], []
    for level in range(LEVELS):
        chunk, start = chunk_of(level)
        ref = refs[chunk]

        def rows(first, count):
            return ref[start + first : start + first + count, :] * scale

        top = first_rows(level)
        ins.append(rows(0, in_rows(level)))
        mixes.append(rows(top, HID))
        outs.append(rows(top + HID, 9 * chan(level)))
        biases.append(rows(in_rows(level), 1))
        biases.append(rows(second_bias_row(level), 1))
    return jnp.concatenate(ins, 0), mixes, jnp.concatenate(outs, 0), jnp.concatenate(biases, 0)


def norm_kernel(*refs):
    parts, flow_ref = refs[:2], refs[2]
    weight_in, weight_mix, weight_out, weight_bias = refs[3:7]
    first_in, first_mix, first_out, first_bias = refs[7:11]
    second_in, second_mix, second_out, second_bias = refs[11:15]
    grad_in_ref, grad_mix_ref, grad_out_ref, grad_bias_ref = refs[15:19]
    update_in, update_mix, update_out, update_bias, block_ref = refs[19:]
    stats = flow_ref[FLOW_ROWS : FLOW_ROWS + 1, :]
    scale = 1.0 / (3.0 * stats[:, 1:2] * LOG_TWO)
    grad_in, grad_mix, grad_out, grad_bias = split_grads(parts, scale)
    grad_in_ref[...] = grad_in
    grad_out_ref[...] = grad_out
    grad_bias_ref[...] = grad_bias
    bias = weight_bias[...].reshape(2 * LEVELS, LANE)
    new_in = moments(weight_in[...], grad_in, first_in[...], second_in[...])[2]
    new_out = moments(weight_out[...], grad_out, first_out[...], second_out[...])[2]
    new_bias = moments(
        bias,
        grad_bias,
        first_bias[...].reshape(2 * LEVELS, LANE),
        second_bias[...].reshape(2 * LEVELS, LANE),
    )[2]
    update_in[...] = new_in
    update_out[...] = new_out
    update_bias[...] = new_bias.reshape(LEVELS, 2, LANE)
    mix_squares = []
    mix_updates = []
    for level in range(LEVELS):
        grad_mix_ref[level] = grad_mix[level]
        new_mix = moments(weight_mix[level], grad_mix[level], first_mix[level], second_mix[level])[2]
        update_mix[level] = new_mix
        mix_squares.append(weight_mix[level] * weight_mix[level])
        mix_updates.append(new_mix * new_mix)
    weight_sums = group_totals(
        weight_in[...] * weight_in[...], mix_squares, weight_out[...] * weight_out[...], bias * bias
    )
    update_sums = group_totals(new_in * new_in, mix_updates, new_out * new_out, new_bias * new_bias)
    lane = iota((16, LANE), 1)
    block_ref[0:16, :] = jnp.where(lane == 0, squares_rows(weight_sums), squares_rows(update_sums))
    block_ref[16:, :] = flow_ref[...]


def moment_kernel(*refs):
    grads, firsts, seconds = refs[0:4], refs[4:8], refs[8:12]
    new_firsts, new_seconds = refs[12:16], refs[16:20]
    for grad, first, second, new_first, new_second in zip(
        grads, firsts, seconds, new_firsts, new_seconds
    ):
        gradient = grad[...].reshape(first.shape)
        new_first[...] = FIRST_BETA * first[...] + (1.0 - FIRST_BETA) * gradient
        new_second[...] = SECOND_BETA * second[...] + (1.0 - SECOND_BETA) * gradient * gradient


def apply_kernel(narrow, *refs):
    index_ref = refs[0]
    block_refs = refs[1 : 1 + narrow]
    at = 1 + narrow
    weight_in, weight_mix, weight_out, weight_bias = refs[at : at + 4]
    update_in, update_mix, update_out, update_bias = refs[at + 4 : at + 8]
    flow_ref, flow_first_ref, flow_second_ref = refs[at + 8 : at + 11]
    at = at + 11
    (
        new_in,
        new_mix,
        new_out,
        new_bias,
        new_flow,
        half_in,
        half_mix,
        half_out,
        flow_moment,
        flow_square,
        weight_norm_ref,
        update_norm_ref,
        loss_ref,
        valid_ref,
        order_ref,
    ) = refs[at:]
    for part in range(narrow):
        order_ref[index_ref[0, 0] ^ part] = block_refs[part][...]
    whole = order_ref[0]
    for part in range(1, narrow):
        whole = whole + order_ref[part]
    sums = whole[0:16]
    flow_grad = whole[16 : 16 + FLOW_ROWS]
    loss = whole[16 + FLOW_ROWS : 17 + FLOW_ROWS, 0:1]
    valid_dims = 3.0 * block_refs[0][16 + FLOW_ROWS : 17 + FLOW_ROWS, 1:2]
    scale = 1.0 / (valid_dims * LOG_TWO)
    flow = to_flat_rows(flow_ref[...])
    size = flow_ref.shape[0]
    place = iota((FLOW_ROWS, LANE), 0) * LANE + iota((FLOW_ROWS, LANE), 1)
    flow_grad = jnp.where(place < size, flow_grad * scale, 0.0)
    first_new, second_new, update = moments(
        flow, flow_grad, to_flat_rows(flow_first_ref[...]), to_flat_rows(flow_second_ref[...])
    )
    weight_norms = [jnp.sqrt(sums[index : index + 1, 0:1]) for index in range(12)]
    update_norms = [jnp.sqrt(sums[index : index + 1, 1:2]) for index in range(12)]
    masks = flow_masks()
    for mask in masks:
        weight_norms.append(jnp.sqrt(total_of(jnp.where(mask, flow * flow, 0.0))))
        update_norms.append(jnp.sqrt(total_of(jnp.where(mask, update * update, 0.0))))
    rates = [
        LEARN_RATE * (weight_norm / update_norm)
        for weight_norm, update_norm in zip(weight_norms, update_norms)
    ]
    rate = jnp.zeros((FLOW_ROWS, LANE), F32)
    for mask, value in zip(masks, rates[12:]):
        rate = jnp.where(mask, value, rate)
    new_flow[...] = from_flat_rows(flow - rate * update, size)
    flow_moment[...] = from_flat_rows(first_new, size)
    flow_square[...] = from_flat_rows(second_new, size)
    row = iota(weight_in.shape, 0)
    edge_one, edge_two = in_rows(0), in_rows(0) + in_rows(1)
    rate = jnp.where(row < edge_one, rates[0], jnp.where(row < edge_two, rates[1], rates[2]))
    fresh = weight_in[...] - rate * update_in[...]
    new_in[...] = fresh
    half_in[...] = fresh.astype(BF16)
    for level in range(LEVELS):
        fresh = weight_mix[level] - rates[3 + level] * update_mix[level]
        new_mix[level] = fresh
        half_mix[level] = fresh.astype(BF16)
    row = iota(weight_out.shape, 0)
    edge_one, edge_two = 9 * chan(0), 9 * chan(0) + 9 * chan(1)
    rate = jnp.where(row < edge_one, rates[6], jnp.where(row < edge_two, rates[7], rates[8]))
    fresh = weight_out[...] - rate * update_out[...]
    new_out[...] = fresh
    half_out[...] = fresh.astype(BF16)
    for level in range(LEVELS):
        new_bias[level] = weight_bias[level] - rates[9 + level] * update_bias[level]
    lane = iota((1, LANE), 1)
    for ref, norms in ((weight_norm_ref, weight_norms), (update_norm_ref, update_norms)):
        held = jnp.zeros((1, LANE), F32)
        for index in range(15):
            held = jnp.where(lane == index, norms[index], held)
        ref[...] = held[:, :15].reshape(15)
    loss_ref[...] = loss / LOG_TWO + 8.0 * valid_dims
    valid_ref[...] = valid_dims


def spec_vmem():
    return pl.BlockSpec(memory_space=pltpu.VMEM)


def spec_smem():
    return pl.BlockSpec(memory_space=pltpu.SMEM)


def call(kernel, outs, scalars, arrays, scratch=(), name=None, after=(), vmem=20):
    number = len(scalars) + len(arrays)

    def run(*refs):
        kernel(*refs[:number], *refs[number + len(after) :])

    return pl.pallas_call(
        run,
        out_shape=tuple(jax.ShapeDtypeStruct(shape, dtype) for shape, dtype in outs),
        in_specs=[spec_smem()] * len(scalars)
        + [spec_vmem()] * len(arrays)
        + [pl.BlockSpec(memory_space=pl.ANY)] * len(after),
        out_specs=tuple(spec_vmem() for _ in outs),
        scratch_shapes=list(scratch),
        compiler_params=pltpu.CompilerParams(vmem_limit_bytes=vmem * 1024 * 1024),
        cost_estimate=pl.CostEstimate(
            flops=1000, bytes_accessed=1000, transcendentals=0
        ),
        name=name,
    )(*scalars, *arrays, *after)


def run_pack(valid_shape, conv_in, mixer, conv_out, hidden_bias):
    outs = [((pack_start(-1) + 16, LANE), BF16)]
    return call(pack_kernel, outs, (valid_shape,), (conv_in, mixer, conv_out, hidden_bias), name="pack", vmem=56)


def run_flow_pre(noise_seeds, valid_shape, images, flow_params, after):
    count = images.shape[1]
    outs = [((stage_rows(level)["rows"], positions(level, count)), F32) for level in range(LEVELS)]
    return call(
        flow_pre_kernel,
        outs,
        (noise_seeds, valid_shape),
        (images, flow_params),
        name="flow_pre",
        after=after,
    )


def run_nets(chunk, images, index, weights, stages, after):
    narrow = len(weights)
    outs = [((narrow // 2, 4 * quarter_rows(chunk), LANE), F32)] * 2
    scratch = []
    for level in CHUNKS[chunk]:
        count = positions(level, images)
        outs = outs + [((stage_rows(level)["result_rows"], count), F32)]
        scratch = scratch + net_scratch(count)
    return call(
        functools.partial(nets_kernel, chunk, images, narrow),
        outs,
        (),
        [index] + list(weights) + [stages[level] for level in CHUNKS[chunk]],
        scratch,
        name="nets_" + "ab"[chunk],
        after=after,
    )


def net_scratch(count):
    return [
        pltpu.VMEM((HID, HID), BF16),
        pltpu.VMEM((HID, count), F32),
        pltpu.VMEM((HID, count), F32),
        pltpu.VMEM((HID, count), BF16),
        pltpu.VMEM((HID, count), BF16),
    ]


def run_flow(images, weights, stages, results, after):
    (out,) = call(
        functools.partial(flow_kernel, images, len(weights)),
        [((FLOW_ROWS + STATS_ROWS, LANE), F32)],
        (),
        list(stages) + list(results) + list(weights),
        name="flow_back",
        after=after,
    )
    return out


def swap(values, wide, narrow):
    width = lax.axis_size("narrow")
    mask = wide * width + narrow
    count = lax.axis_size("wide") * width
    return lax.ppermute(values, ("wide", "narrow"), [(place, place ^ mask) for place in range(count)])


class Summation:
    def __init__(self, chunk, index, send):
        self.chunk, self.index = chunk, index
        self.others = [swap(send, 0, 1)]
        rows, more = quarter_rows(chunk), flow_part(chunk)
        self.own_piece = [((piece_rows(FLOW_ROWS), LANE), BF16)] if more else []
        self.own = ()
        self.square_piece = ((piece_rows(2 * rows + more), LANE), BF16)
        self.piece = ((piece_rows(rows + more), LANE), BF16)

    def run(self, kernel, outs, name, after, scratch=(), extra=()):
        return call(
            functools.partial(kernel, self.chunk),
            outs,
            (),
            (self.index, self.kept, *extra, *self.others),
            scratch,
            name=name + "_" + "ab"[self.chunk],
            after=after,
        )

    def square(self, keep, flow, after):
        rows = 2 * quarter_rows(self.chunk)
        self.kept, *rest = call(
            functools.partial(square_kernel, self.chunk),
            [((rows, LANE), F32)] + self.own_piece + [self.square_piece] * 3,
            (),
            (self.index, keep, *self.others, *flow),
            name="square_" + "ab"[self.chunk],
            after=after,
        )
        self.own, sent = tuple(rest[:-3]), rest[-3:]
        self.others = [swap(sent[0], 0, 2), swap(sent[1], 1, 0), swap(sent[2], 1, 2)]
        return self.kept

    def column(self, after):
        rows = quarter_rows(self.chunk)
        self.kept, *rest = self.run(
            column_kernel,
            [((rows, LANE), F32)] + self.own_piece + [self.piece],
            "column",
            after,
            [pltpu.VMEM((2 * rows, LANE), F32)],
            self.own,
        )
        self.own = tuple(rest[:-1])
        self.others = [swap(rest[-1], 2, 0)]
        return self.kept

    def code(self, after):
        (self.kept,) = self.run(code_kernel, [self.piece], "code", after, (), self.own)
        self.others = [swap(self.kept, 4, 0)]
        return self.kept

    def spread(self, after):
        step = 4
        while step < lax.axis_size("wide"):
            (self.kept,) = self.run(recode_kernel, [self.piece], "recode_%d" % step, after)
            step = 2 * step
            if step < lax.axis_size("wide"):
                self.others = [swap(self.kept, step, 0)]
        self.others = [swap(self.kept, 2, 0), swap(self.kept, 1, 0), swap(self.kept, 3, 0)]
        return self.kept

    def decode(self, after):
        shape = [((4 * quarter_rows(self.chunk), LANE), F32)]
        if flow_part(self.chunk):
            shape.append(((FLOW_ROWS + STATS_ROWS, LANE), F32))
        return self.run(decode_kernel, shape, "decode", after)


def body(
    images,
    noise_seeds,
    valid_shape,
    conv_in,
    mixer,
    conv_out,
    hidden_bias,
    flow_params,
    conv_in_first,
    mixer_first,
    conv_out_first,
    bias_first,
    flow_first,
    conv_in_second,
    mixer_second,
    conv_out_second,
    bias_second,
    flow_second,
):
    count = images.shape[1]
    conv_out, conv_out_first, conv_out_second = conv_out.T, conv_out_first.T, conv_out_second.T
    row = lax.broadcasted_iota(jnp.int32, (8, LANE), 0)
    index = jnp.where(row == 0, lax.axis_index("narrow"), lax.axis_index("wide")).astype(jnp.int32)
    narrow = lax.axis_size("narrow")
    (packed,) = run_pack(valid_shape, conv_in, mixer, conv_out, hidden_bias)
    paired = swap(packed, 0, 1)
    crossed = swap(packed, 0, 2)
    stages = run_flow_pre(noise_seeds, valid_shape, images, flow_params, ())
    arrays = (crossed, *stages)
    copied, *stages = call(
        copy_kernel, [(array.shape, array.dtype) for array in arrays], (), arrays, name="copy"
    )
    gathered = (packed, paired, crossed, swap(copied, 0, 1))
    keep_one, send, *results = run_nets(0, count, index, gathered, stages, ())
    one = Summation(0, index, send)
    keep_two, send, *more = run_nets(1, count, index, gathered, stages, (keep_one,))
    results = results + more
    two = Summation(1, index, send)
    token = one.square(keep_one, (), (keep_two,))
    flow = run_flow(count, gathered, stages, results, (token,))
    token = two.square(keep_two, (flow,), ())
    token = one.column((token,))
    token = two.column((token,))
    token = one.code((token,))
    token = two.code((token,))
    token = one.spread((token,))
    token = two.spread((token,))
    parts = one.decode((token,))
    parts = list(parts) + list(two.decode((parts[0],)))
    weights = (conv_in, mixer, conv_out, hidden_bias)
    firsts = (conv_in_first, mixer_first, conv_out_first, bias_first)
    seconds = (conv_in_second, mixer_second, conv_out_second, bias_second)
    shapes = [(weight.shape, F32) for weight in weights]
    grad_shapes = shapes[:3] + [((2 * LEVELS, LANE), F32)]
    *grads, update_in, update_mix, update_out, update_bias, block = call(
        norm_kernel,
        grad_shapes + shapes + [((16 + FLOW_ROWS + STATS_ROWS, LANE), F32)],
        (),
        tuple(parts) + weights + firsts + seconds,
        name="norms",
    )
    blocks = [block] + [swap(block, 0, part) for part in range(1, narrow)]
    moved = call(
        moment_kernel,
        shapes * 2,
        (),
        tuple(grads) + firsts + seconds,
        name="moments",
    )
    flow_shape = (flow_params.shape, F32)
    fresh = call(
        functools.partial(apply_kernel, narrow),
        shapes
        + [flow_shape]
        + [(weight.shape, BF16) for weight in weights[:3]]
        + [flow_shape, flow_shape, ((15,), F32), ((15,), F32), ((1, 1), F32), ((1, 1), F32)],

        (),
        (index,)
        + tuple(blocks)
        + weights
        + (update_in, update_mix, update_out, update_bias)
        + (flow_params, flow_first, flow_second),
        scratch=[pltpu.VMEM((narrow,) + block.shape, F32)],
        after=(moved[3],),
        name="apply",
    )
    return (
        fresh[0],
        fresh[1],
        fresh[2].T,
        fresh[3],
        fresh[4],
        moved[0],
        moved[1],
        moved[2].T,
        moved[3],
        fresh[8],
        moved[4],
        moved[5],
        moved[6].T,
        moved[7],
        fresh[9],
        fresh[5],
        fresh[6],
        fresh[7].T,
        fresh[10],
        fresh[11],
        fresh[12].reshape(()),
        fresh[13].reshape(()),
    )


def solution(mesh):
    placed = (
        P(None, ("wide", "narrow"), None),
        P(("wide", "narrow")),
        P(("wide", "narrow"), None),
        P(None, "narrow"),
        P(None, None, "narrow"),
        P("narrow", None),
        P(None, None, "narrow"),
        P(),
    )
    state = (P(None, "narrow"), P(None, None, "narrow"), P("narrow", None), P(None, None, "narrow"), P())
    return jax.shard_map(
        body,
        mesh=mesh,
        in_specs=placed + state + state,
        out_specs=state * 3 + state[:3] + (P(),) * 4,
        check_vma=False,
    )
```

```python
import functools
import jax
import jax.numpy as jnp
from jax import lax
from jax.experimental import pallas as pl
from jax.experimental.pallas import tpu as pltpu
from jax.sharding import PartitionSpec as P

C1 = 12
IMG_SIDE = 32
STEP = 5
HIGHEST_PRECISION = lax.Precision.HIGHEST
LOG_TWO_PI = 1.8378770664093453
LOG_TWO = 0.6931471805599453
FIRST_BETA = 0.5
SECOND_BETA = 0.5
EPSILON = 1e-06
WEIGHT_DECAY = 0.01
LEARN_RATE = 0.25
TAPS = [(-1, -1), (-1, 0), (-1, 1), (0, -1), (0, 0), (0, 1), (1, -1), (1, 0), (1, 1)]
F32 = jnp.float32
BF16 = jnp.bfloat16
HID = 512
LANE = 128
LEVELS = 3
FLOW_ROWS = 32
STATS_ROWS = 8
CODE_BLOCK = 16
CODE_RANGE = 84.0
VMEM_BYTES = 20 * 1024 * 1024


def round_up(value, unit):
    return (value + unit - 1) // unit * unit


def chan(level):
    return C1 * 2**level


def side(level):
    return IMG_SIDE // 2 ** (level + 1)


def real_positions(level, images):
    return images * side(level) ** 2


def positions(level, images):
    return round_up(real_positions(level, images), LANE)


def in_rows(level):
    return 9 * chan(level) // 2


def bias_in_tail(level):
    return round_up(9 * chan(level), 16) - 9 * chan(level) >= 4 and in_rows(level) % 16 > 10


def first_rows(level):
    return round_up(in_rows(level) + (3 if bias_in_tail(level) else 6), 16)


def second_bias_row(level):
    return (pack_rows(level) if bias_in_tail(level) else first_rows(level)) - 4


def last_rows(level):
    return round_up(9 * chan(level), 16)


def pack_rows(level):
    return first_rows(level) + HID + last_rows(level)


def pack_start(level):
    return sum(pack_rows(other) for other in range(LEVELS - 1, level, -1))


CHUNKS = ((2,), (0, 1))


def gather_start(level):
    return pack_start(level) - (0 if level in CHUNKS[0] else pack_start(CHUNKS[0][0] - 1))


def chunk_of(level):
    for chunk, levels in enumerate(CHUNKS):
        if level in levels:
            return chunk, sum(pack_rows(other) for other in levels[: levels.index(level)])
    return None


def quarter_rows(chunk):
    return round_up(sum(pack_rows(level) for level in CHUNKS[chunk]), 4 * CODE_BLOCK) // 4


def flow_part(chunk):
    return FLOW_ROWS if chunk == len(CHUNKS) - 1 else 0


def stage_rows(level):
    padded = round_up(chan(level), 8)
    half = round_up(chan(level) // 2, 8)
    sizes = [
        ("normed", padded),
        ("mixed", padded),
        ("share", 8),
        ("held", padded),
        ("block", padded),
        ("prior", half),
        ("mixing", padded),
        ("turn", padded),
        ("grad", padded),
        ("small", padded),
        ("prior_grad", half),
    ]
    starts = {}
    at = 0
    for name, size in sizes[:8]:
        starts[name] = at
        at = at + size
    starts["rows"] = at
    at = 0
    for name, size in sizes[8:]:
        starts[name] = at
        at = at + size
    starts["result_rows"] = at
    return starts


def flow_lengths():
    return [5 * C1 + 3 * C1 * C1 // 2, 10 * C1 + 6 * C1 * C1, 24 * C1 + 16 * C1 * C1]


def flow_size():
    return sum(flow_lengths())


def flow_offsets(level):
    start = sum(flow_lengths()[:level])
    channels = chan(level)
    offsets = {"bias": start, "logs": start + channels, "block": start + 2 * channels}
    start = start + 2 * channels + channels * channels
    offsets["outbias"] = start
    offsets["outscale"] = start + channels
    start = start + 2 * channels
    if level < LEVELS - 1:
        offsets["priormatrix"] = start
        start = start + channels // 2 * channels
    offsets["priorbias"] = start
    return offsets


def column_names(level):
    channels = chan(level)
    offsets = flow_offsets(level)
    names = [
        ("bias", offsets["bias"]),
        ("logs", offsets["logs"]),
        ("outbias", offsets["outbias"]),
        ("outscale", offsets["outscale"]),
        ("priorbias", offsets["priorbias"]),
    ]
    if level == LEVELS - 1:
        names = names + [("priorscale", offsets["priorbias"] + channels)]
    return names


def exact_dot(first, second):
    return jnp.dot(first, second, precision=HIGHEST_PRECISION, preferred_element_type=F32)


def exact_rows(first, second):
    return lax.dot_general(
        first,
        second,
        (((0,), (0,)), ((), ())),
        precision=HIGHEST_PRECISION,
        preferred_element_type=F32,
    )


def exact_columns(first, second):
    return lax.dot_general(
        first,
        second,
        (((1,), (1,)), ((), ())),
        precision=HIGHEST_PRECISION,
        preferred_element_type=F32,
    )


def plain_dot(first, second):
    return jnp.dot(first, second, preferred_element_type=F32)


def contract_rows(first, second):
    return lax.dot_general(first, second, (((0,), (0,)), ((), ())), preferred_element_type=F32)


def contract_columns(first, second):
    return lax.dot_general(first, second, (((1,), (1,)), ((), ())), preferred_element_type=F32)


def iota(shape, axis):
    return lax.broadcasted_iota(jnp.int32, shape, axis)


def rounded(values):
    return values.astype(BF16).astype(F32)


def split_three(values):
    high = rounded(values)
    rest = values - high
    middle = rounded(rest)
    return [high, middle, rest - middle]


def move_lanes(values, chooser, transposed=False):
    rows = values.shape[0]
    padded = round_up(rows, 8)
    if padded > rows:
        values = jnp.concatenate([values, jnp.zeros((padded - rows, values.shape[1]), F32)], 0)
    pieces = jnp.concatenate(split_three(values), 0).astype(BF16)
    moved = contract_columns(pieces, chooser) if transposed else plain_dot(pieces, chooser)
    moved = moved[:padded] + moved[padded : 2 * padded] + moved[2 * padded :]
    return moved[:rows]


def squeeze_chooser(grid, images):
    count = images * grid * grid
    source = iota((count, count), 0)
    target = iota((count, count), 1)
    shift = grid.bit_length() - 1
    image = lax.shift_right_logical(source, 2 * shift)
    row = lax.shift_right_logical(source, shift) & (grid - 1)
    column = source & (grid - 1)
    half = grid // 2
    place = (
        ((row & 1) * 2 + (column & 1)) * (images * half * half)
        + image * (half * half)
        + lax.shift_right_logical(row, 1) * half
        + lax.shift_right_logical(column, 1)
    )
    return (place == target).astype(F32).astype(BF16)


def order_chooser(channels, stride):
    row = iota((4 * channels, 4 * stride), 0)
    column = iota((4 * channels, 4 * stride), 1)
    return ((row & 3) * stride + lax.shift_right_logical(row, 2) == column).astype(F32)


def squeeze(values, chooser, lanes_out):
    channels, count = values.shape
    moved = move_lanes(values, chooser)
    quarter = count // 4
    stacked = jnp.concatenate([moved[:, k * quarter : (k + 1) * quarter] for k in range(4)], 0)
    ordered = exact_dot(order_chooser(channels, channels), stacked)
    if lanes_out > quarter:
        ordered = jnp.concatenate([ordered, jnp.zeros((4 * channels, lanes_out - quarter), F32)], 1)
    return ordered


def unsqueeze(stacked, chooser, count):
    channels = stacked.shape[0] // 4
    quarter = count // 4
    laid = jnp.concatenate(
        [stacked[k * channels : (k + 1) * channels, :quarter] for k in range(4)], 1
    )
    return move_lanes(laid, chooser, transposed=True)


def slope_roll(values, step):
    step = step % LANE
    while step:
        part = 16 if step >= 16 else 1 << (step.bit_length() - 1)
        values = pltpu.roll(values, 0, 1, stride=part, stride_axis=0)
        step = step - part
    return values


def flow_block(flat, offset, rows, width):
    padded = round_up(rows, 8)
    start = offset + width * iota((padded, FLOW_ROWS), 0)
    line = lax.shift_right_logical(start, 7)
    column = iota((padded, FLOW_ROWS), 1)
    base = -offset % LANE
    if base:
        flat = pltpu.roll(flat, base, 1)
    here = exact_dot((line == column).astype(F32), flat)
    after = exact_dot((line + 1 == column).astype(F32), flat)
    here = slope_roll(here, -width)
    after = slope_roll(after, -width)
    lane = iota((padded, LANE), 1)
    begin = (offset + width * iota((padded, LANE), 0)) & (LANE - 1)
    chosen = jnp.where(lane + begin < LANE, here, after)
    return chosen[:rows, :width]


def flow_block_back(values, offset, rows, width):
    padded = round_up(rows, 8)
    base = offset % LANE
    over = max(base + width - LANE, 0)
    parts = [values[:, width - over :]] if over else []
    if base > over:
        parts.append(jnp.zeros((rows, base - over), F32))
    parts.append(values[:, : width - over])
    if base + width < LANE:
        parts.append(jnp.zeros((rows, LANE - base - width), F32))
    block = jnp.concatenate(parts, 1)
    if padded > rows:
        block = jnp.concatenate([block, jnp.zeros((padded - rows, LANE), F32)], 0)
    block = slope_roll(block, width)
    lane = iota((padded, LANE), 1)
    begin = (offset + width * iota((padded, LANE), 0)) & (LANE - 1)
    here = jnp.where(lane >= begin, block, 0.0)
    after = jnp.where(lane >= begin, 0.0, block)
    line = lax.shift_right_logical(offset + width * iota((FLOW_ROWS, padded), 1), 7)
    row = iota((FLOW_ROWS, padded), 0)
    return exact_dot((line == row).astype(F32), here) + exact_dot(
        (line + 1 == row).astype(F32), after
    )


def flow_column(turned, offset, length):
    line, begin = offset // LANE, offset % LANE
    if begin + length <= LANE:
        return turned[begin : begin + length, line : line + 1]
    return jnp.concatenate(
        [turned[begin:, line : line + 1], turned[: begin + length - LANE, line + 1 : line + 2]], 0
    )


def flow_column_back(values, offset):
    length = values.shape[0]
    line, begin = offset // LANE, offset % LANE
    lane = iota((LANE, LANE), 1)
    head = min(length, LANE - begin)
    parts = []
    if begin:
        parts.append(jnp.zeros((begin, 1), F32))
    parts.append(values[:head])
    if begin + head < LANE:
        parts.append(jnp.zeros((LANE - begin - head, 1), F32))
    column = jnp.concatenate(parts, 0) if len(parts) > 1 else parts[0]
    term = jnp.where(lane == line, column, 0.0)
    if head < length:
        column = jnp.concatenate([values[head:], jnp.zeros((LANE - length + head, 1), F32)], 0)
        term = term + jnp.where(lane == line + 1, column, 0.0)
    return term


def to_flat_rows(values):
    size = values.shape[0]
    row = values.reshape(1, size)
    row = jnp.concatenate([row, jnp.zeros((1, FLOW_ROWS * LANE - size), F32)], 1)
    return row.reshape(FLOW_ROWS, LANE)


def from_flat_rows(values, size):
    return values.reshape(1, FLOW_ROWS * LANE)[:, :size].reshape(size)


def triangles(block):
    channels = block.shape[0]
    row = iota((channels, channels), 0)
    column = iota((channels, channels), 1)
    signs = (1 - 2 * (row & 1)).astype(F32)
    diagonal = signs * jnp.exp(jnp.where(row == column, block, 0.0))
    lower = jnp.where(row > column, block, jnp.where(row == column, 1.0, 0.0))
    upper = jnp.where(row < column, block, jnp.where(row == column, diagonal, 0.0))
    reverse = (row + column == channels - 1).astype(F32)
    return lower, upper, reverse, diagonal


def tap_masks(level, images):
    grid = side(level)
    count = positions(level, images)
    lane = iota((8, count), 1)
    shift = grid.bit_length() - 1
    row = lax.shift_right_logical(lane, shift) & (grid - 1)
    column = lane & (grid - 1)
    inside = lane < real_positions(level, images)
    masks = {}
    for row_step in (-1, 0, 1):
        for column_step in (-1, 0, 1):
            good = (
                (row + row_step >= 0)
                & (row + row_step < grid)
                & (column + column_step >= 0)
                & (column + column_step < grid)
                & inside
            )
            masks[(row_step, column_step)] = jnp.where(good, 1.0, 0.0)[0:1]
    return masks


def tap_read(values, masks, level, row_step, column_step):
    count = values.shape[1]
    offset = (row_step * side(level) + column_step) % count
    if offset:
        values = pltpu.roll(values, count - offset, 1)
    if (row_step, column_step) != (0, 0):
        values = values * masks[(row_step, column_step)]
    return values


def tap_stack(values, masks, level, direction):
    return [
        tap_read(values, masks, level, direction * row_step, direction * column_step)
        for row_step, column_step in TAPS
    ]


def tap_sum(values, masks, level, direction, channels):
    total = None
    for tap, (row_step, column_step) in enumerate(TAPS):
        term = tap_read(
            values[tap * channels : (tap + 1) * channels],
            masks,
            level,
            direction * row_step,
            direction * column_step,
        )
        total = term if total is None else total + term
    return total


def pack_kernel(valid_ref, conv_in_ref, mixer_ref, conv_out_ref, bias_ref, whole_ref, *part_refs):
    in_start = 0
    out_start = 0
    for level in range(LEVELS):
        out_ref = whole_ref.at[pack_start(level) : pack_start(level) + pack_rows(level)]
        rows, columns = in_rows(level), 9 * chan(level)
        top = first_rows(level)
        ones = split_three(bias_ref[level, 0:1, :])
        twos = split_three(bias_ref[level, 1:2, :]) + [jnp.zeros((1, LANE), F32)]
        head = [conv_in_ref[in_start : in_start + rows, :]] + ones
        tail = [conv_out_ref[out_start : out_start + columns, :]]
        for part, size, chosen in (
            (head, top, not bias_in_tail(level)),
            (tail, last_rows(level), bias_in_tail(level)),
        ):
            used = sum(piece.shape[0] for piece in part) + (4 if chosen else 0)
            if size > used:
                part.append(jnp.zeros((size - used, LANE), F32))
            if chosen:
                part.extend(twos)
        out_ref[0:top, :] = jnp.concatenate(head, 0).astype(BF16)
        out_ref[top : top + HID, :] = mixer_ref[level].astype(BF16)
        out_ref[top + HID :, :] = jnp.concatenate(tail, 0).astype(BF16)
        in_start = in_start + rows
        out_start = out_start + columns
    pixels = jnp.int32(0)
    for image in range(valid_ref.shape[0]):
        pixels = pixels + valid_ref[image, 0] * valid_ref[image, 1]
    lane = iota((16, LANE), 1)
    digits = jnp.where(lane == 0, pixels & 127, 0)
    for place in (1, 2):
        digits = jnp.where(lane == place, lax.shift_right_logical(pixels, 7 * place) & 127, digits)
    whole_ref[pack_start(-1) :, :] = digits.astype(F32).astype(BF16)
    cut = part_refs[0].shape[0]
    part_refs[0][...] = whole_ref[0:cut, :]
    part_refs[1][...] = whole_ref[cut:, :]


def flow_pre_kernel(seed_ref, valid_ref, image_ref, flow_ref, packed_ref, *out_refs):
    out_refs[LEVELS][...] = packed_ref[...]
    images = image_ref.shape[1]
    flat = to_flat_rows(flow_ref[...])
    turned = jnp.concatenate([flat, jnp.zeros((LANE - FLOW_ROWS, LANE), F32)], 0).T
    blocks = IMG_SIDE * IMG_SIDE // 256
    pieces = []
    for image in range(images):
        position = iota((8, IMG_SIDE * IMG_SIDE), 0) * (IMG_SIDE * IMG_SIDE) + iota(
            (8, IMG_SIDE * IMG_SIDE), 1
        )
        hashed = seed_ref[image] + position * jnp.int32(-1640531527)
        hashed = hashed ^ lax.shift_right_logical(hashed, jnp.full_like(hashed, 15))
        hashed = hashed * jnp.int32(739267321)
        hashed = hashed ^ lax.shift_right_logical(hashed, jnp.full_like(hashed, 13))
        field = ((hashed & jnp.int32(16777215)).astype(F32) + 0.5) * 2.0 ** (-24)
        pixel = jnp.concatenate(
            [image_ref[:, image, :], jnp.zeros((5, IMG_SIDE * IMG_SIDE), F32)], 0
        )
        pixel = pixel + field / 256.0
        for block in range(blocks):
            pieces.append(pixel[:, block * 256 : (block + 1) * 256])
    stacked = jnp.concatenate(pieces, 0)
    source = iota((256, 256), 0)
    target = iota((256, 256), 1)
    row = lax.shift_right_logical(source, 5)
    column = source & 31
    place = (
        ((row & 1) * 2 + (column & 1)) * 64
        + lax.shift_right_logical(row, 1) * 16
        + lax.shift_right_logical(column, 1)
    )
    moved = move_lanes(stacked, (place == target).astype(F32).astype(BF16))
    quarters = []
    for k in range(4):
        quarters.append(
            jnp.concatenate(
                [
                    moved[piece * 8 : (piece + 1) * 8, k * 64 : (k + 1) * 64]
                    for piece in range(images * blocks)
                ],
                1,
            )
        )
    state = exact_dot(order_chooser(3, 8), jnp.concatenate(quarters, 0))
    for level in range(LEVELS):
        channels = chan(level)
        grid = side(level)
        count = positions(level, images)
        offsets = flow_offsets(level)
        block = flow_block(flat, offsets["block"], channels, channels)
        names = column_names(level)
        columns = [flow_column(turned, offset, channels) for _, offset in names]
        lane = iota((channels, LANE), 1)
        held = jnp.zeros((channels, LANE), F32)
        for index, column in enumerate(columns):
            held = jnp.where(lane == index, column, held)
        growth = jnp.exp(columns[1])
        normed = (state + columns[0]) * growth
        lower, upper, reverse, _ = triangles(block)
        mixing = exact_dot(exact_dot(reverse, lower), upper)
        mixed = exact_dot(mixing, normed)
        lane = iota((8, count), 1)
        shift = grid.bit_length() - 1
        image = lax.shift_right_logical(lane, 2 * shift)
        row = lax.shift_right_logical(lane, shift) & (grid - 1)
        column = lane & (grid - 1)
        high = jnp.zeros((8, count), jnp.int32)
        wide = jnp.zeros((8, count), jnp.int32)
        for index in range(images):
            high = jnp.where(image == index, valid_ref[index, 0], high)
            wide = jnp.where(image == index, valid_ref[index, 1], wide)
        unit = 2 ** (level + 1)
        row_share = jnp.clip(high - row * unit, 0, unit).astype(F32) / unit
        column_share = jnp.clip(wide - column * unit, 0, unit).astype(F32) / unit
        share = jnp.where(image < images, row_share * column_share, 0.0)
        out_ref = out_refs[level]
        starts = stage_rows(level)
        out_ref[starts["normed"] : starts["normed"] + channels, :] = normed
        out_ref[starts["mixed"] : starts["mixed"] + channels, :] = mixed
        out_ref[starts["share"] : starts["share"] + 8, :] = share
        out_ref[starts["held"] : starts["held"] + channels, 0:LANE] = held
        out_ref[starts["block"] : starts["block"] + channels, 0:channels] = block
        out_ref[starts["mixing"] : starts["mixing"] + channels, 0:channels] = mixing
        if level > 0:
            order = order_chooser(channels // 4, channels // 4)
            out_ref[starts["turn"] : starts["turn"] + channels, 0:channels] = exact_dot(
                mixing, growth * order
            )
        if level < LEVELS - 1:
            out_ref[starts["prior"] : starts["prior"] + channels // 2, 0:channels] = flow_block(
                flat, offsets["priormatrix"], channels // 2, channels
            )
            state = squeeze(
                mixed[: channels // 2], squeeze_chooser(grid, images), positions(level + 1, images)
            )


def silu_parts(values):
    sigmoid = 1.0 / (1.0 + jnp.exp(-values))
    active = values * sigmoid
    slope = sigmoid + active * (1.0 - sigmoid)
    return active, slope


def net_kernel(level, images, narrow, *refs):
    is_last = level == LEVELS - 1
    index_ref = refs[0]
    weight_refs, tails = refs[1 : 1 + narrow], [None] * narrow
    if isinstance(weight_refs[-1], tuple):
        weight_refs, tails[-1] = (*weight_refs[:-1], weight_refs[-1][0]), weight_refs[-1][1]
    bases = [
        pack_start(level) if ref.shape[0] > pack_start(-1) else gather_start(level)
        for ref in weight_refs
    ]
    out_base = chunk_of(level)[1]
    stage_ref, keep_ref, send_ref, result_ref = refs[1 + narrow : 5 + narrow]
    order_ref, slope_one_ref, slope_two_ref, one_ref, two_ref = refs[5 + narrow :]
    starts = stage_rows(level)
    me = index_ref[0, 0]
    channels = chan(level)
    half = channels // 2
    count = positions(level, images)
    top, rows = first_rows(level), in_rows(level)
    tail, used = last_rows(level), 9 * channels
    bias_block = second_bias_row(level) - 12
    masks = tap_masks(level, images)
    width = HID // narrow

    def weights(start, length):
        parts = []
        for ref, base, tail in zip(weight_refs, bases, tails):
            first = base + start
            if tail is not None and first >= ref.shape[0]:
                ref, first = tail, first - ref.shape[0]
            parts.append(ref[first : first + length, :])
        return jnp.concatenate(parts, 1)

    for r_in in range(narrow):
        for r_out in range(narrow):
            start = pl.multiple_of(bases[r_out] + top + (me ^ r_in) * width, 16)
            order_ref[r_in * width : (r_in + 1) * width, r_out * LANE : (r_out + 1) * LANE] = (
                weight_refs[r_out][pl.ds(start, width), :]
            )
    weight_in = weights(0, top)
    weight_mix = order_ref[...]
    weight_out = weights(top + HID, tail)
    mixed = starts["mixed"]
    first = stage_ref[mixed : mixed + half, :]
    second = stage_ref[mixed + half : mixed + channels, :]
    share = stage_ref[starts["share"] : starts["share"] + 1, :]
    pieces = tap_stack(rounded(first), masks, level, 1)
    pieces.append(jnp.ones((3, count), F32))
    pieces.append(jnp.zeros((top - rows - 3, count), F32))
    stacked = jnp.concatenate(pieces, 0).astype(BF16)
    pick = jnp.where(
        (iota((16, count), 0) >= 12) & (iota((16, count), 0) < 15), 1.0, 0.0
    ).astype(BF16)
    hidden_one = contract_rows(weight_in, stacked)
    active, slope = silu_parts(hidden_one)
    slope_one_ref[...] = slope
    one_ref[...] = active.astype(BF16)
    hidden_two = contract_rows(weight_mix, one_ref[...]) + contract_rows(
        weights(bias_block, 16), pick
    )
    active, slope = silu_parts(hidden_two)
    slope_two_ref[...] = slope
    two_ref[...] = active.astype(BF16)
    spread = plain_dot(weight_out, two_ref[...])
    net_raw = tap_sum(spread, masks, level, 1, channels)
    held = stage_ref[starts["held"] : starts["held"] + channels, 0:LANE]
    out_bias, out_scale = held[:, 2:3], held[:, 3:4]
    growth = jnp.exp(3.0 * out_scale)
    output = (net_raw + out_bias) * growth
    logit = output[half:] + 2.0
    sigmoid = 1.0 / (1.0 + jnp.exp(-logit))
    latent = (second + output[:half]) * sigmoid
    log_sigmoid = jnp.minimum(logit, 0.0) - jnp.log1p(jnp.exp(-jnp.abs(logit)))
    if is_last:
        joined = jnp.concatenate([first, latent], 0)
        mean, scale = held[:, 4:5], held[:, 5:6]
        mean = jnp.broadcast_to(mean, joined.shape)
        scale = jnp.broadcast_to(scale, joined.shape)
    else:
        joined = latent
        prior = stage_ref[starts["prior"] : starts["prior"] + half, 0:channels]
        stats = exact_rows(prior, first) + held[:, 4:5]
        mean, scale = stats[:half], stats[half:]
    gap = joined - mean
    shrink = jnp.exp(-2.0 * scale)
    square = gap * gap * shrink
    log_prior = -0.5 * (LOG_TWO_PI + 2.0 * scale + square)
    total = jnp.sum(jnp.sum(share * log_sigmoid, 0, keepdims=True), 1, keepdims=True) + jnp.sum(
        jnp.sum(share * log_prior, 0, keepdims=True), 1, keepdims=True
    )
    share_total = jnp.sum(share, 1, keepdims=True)
    grad_joined = share * (gap * shrink)
    grad_scale = share * (1.0 - square)
    grad_latent = grad_joined[half:] if is_last else grad_joined
    grad_logit = (grad_latent * latent - share) * (1.0 - sigmoid)
    grad_second = grad_latent * sigmoid
    grad_output = jnp.concatenate([grad_second, grad_logit], 0)
    grad_net = grad_output * growth
    lane = iota((channels, LANE), 1)
    small = jnp.zeros((channels, LANE), F32)

    def put(small, index, values):
        return jnp.where(lane == index, jnp.sum(values, 1, keepdims=True), small)

    small = put(small, 2, grad_net)
    small = put(small, 3, 3.0 * grad_output * output)
    if is_last:
        small = put(small, 4, -grad_joined)
        small = put(small, 5, grad_scale)
        grad_first = grad_joined[:half]
    else:
        grad_stats = jnp.concatenate([-grad_joined, grad_scale], 0)
        small = put(small, 4, grad_stats)
        grad_first = exact_dot(prior, grad_stats)
        prior_grad = exact_columns(first, grad_stats)
        start = starts["prior_grad"]
        result_ref[start : start + half, 0:channels] = prior_grad
    small = jnp.where(lane == 6, -total, small)
    small = jnp.where(lane == 7, share_total, small)
    result_ref[starts["small"] : starts["small"] + channels, 0:LANE] = small
    pieces = tap_stack(rounded(grad_net), masks, level, -1)
    if tail > used:
        pieces.append(jnp.zeros((tail - used, count), F32))
    grad_spread = jnp.concatenate(pieces, 0).astype(BF16)

    def store(start, values):
        for r in range(narrow):
            ref = send_ref if r & 1 else keep_ref
            rows = slice(out_base + start, out_base + start + values.shape[0])
            ref[r // 2, rows, :] = values[:, r * LANE : (r + 1) * LANE]

    grad_out = contract_columns(grad_spread, two_ref[...])
    grad_two = (contract_rows(weight_out, grad_spread) * slope_two_ref[...]).astype(BF16)
    grad_mix = contract_columns(one_ref[...], grad_two)
    for r_in in range(narrow):
        start = pl.multiple_of(out_base + top + (me ^ r_in) * width, 16)
        for r_out in range(narrow):
            ref = send_ref if r_out & 1 else keep_ref
            ref[r_out // 2, pl.ds(start, width), :] = grad_mix[
                r_in * width : (r_in + 1) * width, r_out * LANE : (r_out + 1) * LANE
            ]
    grad_one = (plain_dot(weight_mix, grad_two) * slope_one_ref[...]).astype(BF16)
    grad_in = contract_columns(stacked, grad_one)
    grad_bias = contract_columns(pick, grad_two)
    if bias_in_tail(level):
        grad_out = jnp.concatenate([grad_out[: tail - 16], grad_out[tail - 16 :] + grad_bias], 0)
    else:
        grad_in = jnp.concatenate([grad_in[: top - 16], grad_in[top - 16 :] + grad_bias], 0)
    store(0, grad_in)
    store(top + HID, grad_out)
    grad_stack = plain_dot(weight_in, grad_one)
    grad_first = grad_first + tap_sum(grad_stack, masks, level, -1, half)
    result_ref[0:half, :] = grad_first
    result_ref[half:channels, :] = grad_second


def stage_part(level, ref, name, rows, lanes):
    start = stage_rows(level)[name]
    return ref[start : start + rows, 0:lanes]


def flow_chain(images, stages, results):
    grads = [None] * LEVELS
    carried = None
    for level in (2, 1, 0):
        channels = chan(level)
        count = positions(level, images)
        grad = stage_part(level, results[level], "grad", channels, count)
        if carried is not None:
            grad = grad + jnp.concatenate([carried, jnp.zeros_like(carried)], 0)
        grads[level] = grad
        if level > 0:
            turn = stage_part(level, stages[level], "turn", channels, channels)
            grid = side(level - 1)
            carried = unsqueeze(
                exact_rows(turn, grad), squeeze_chooser(grid, images), images * grid * grid
            )
    return grads


def flow_level(level, images, stage_ref, result_ref, grad):
    channels = chan(level)
    half = channels // 2
    count = positions(level, images)
    offsets = flow_offsets(level)
    normed = stage_part(level, stage_ref, "normed", channels, count)
    held = stage_part(level, stage_ref, "held", channels, LANE)
    block = stage_part(level, stage_ref, "block", channels, channels)
    mixing = stage_part(level, stage_ref, "mixing", channels, channels)
    small = stage_part(level, result_ref, "small", channels, LANE)
    lower, upper, reverse, diagonal = triangles(block)
    grad_normed = exact_rows(mixing, grad)
    grad_mixing = exact_dot(reverse, exact_columns(grad, normed))
    grad_lower = exact_columns(grad_mixing, upper)
    grad_upper = exact_rows(lower, grad_mixing)
    share_total = small[0:1, 7:8]
    row = iota((channels, channels), 0)
    column = iota((channels, channels), 1)
    grad_block = jnp.where(
        row > column,
        grad_lower,
        jnp.where(row < column, grad_upper, grad_upper * diagonal - share_total),
    )
    growth = jnp.exp(held[:, 1:2])
    grad_bias = jnp.sum(grad_normed, 1, keepdims=True) * growth
    grad_logs = jnp.sum(grad_normed * normed, 1, keepdims=True) - share_total
    flat = flow_block_back(grad_block, offsets["block"], channels, channels)
    turned = jnp.zeros((LANE, LANE), F32)
    for index, (name, offset) in enumerate(column_names(level)):
        if name == "bias":
            values = grad_bias
        elif name == "logs":
            values = grad_logs
        else:
            values = small[:, index : index + 1]
        turned = turned + flow_column_back(values, offset)
    if level < LEVELS - 1:
        flat = flat + flow_block_back(
            stage_part(level, result_ref, "prior_grad", half, channels),
            offsets["priormatrix"],
            half,
            channels,
        )
    logs_total = jnp.sum(held[:, 1:2], 0, keepdims=True)
    trace = jnp.sum(
        jnp.sum(jnp.where(row == column, block, 0.0), 0, keepdims=True), 1, keepdims=True
    )
    return flat, turned, small[0:1, 6:7] - share_total * (logs_total + trace)


def flow_back(images, stages, results, weights, out_ref):
    grads = flow_chain(images, stages, results)
    parts = [
        flow_level(level, images, stages[level], results[level], grads[level])
        for level in range(LEVELS)
    ]
    flat = sum(part[0] for part in parts) + sum(part[1] for part in parts).T[:FLOW_ROWS]
    loss = sum(part[2] for part in parts)
    pixels = jnp.zeros((1, 1), F32)
    for ref in weights:
        start = ref.shape[0] - 16
        digits = ref[start : start + 16, :].astype(F32)
        for place in range(3):
            pixels = pixels + 128.0**place * digits[0:1, place : place + 1]
    lane = iota((STATS_ROWS, LANE), 1)
    out_ref[0:FLOW_ROWS, :] = flat
    out_ref[FLOW_ROWS:, :] = jnp.where(lane == 0, loss, jnp.where(lane == 1, pixels, 0.0))


def zero_rows(refs, start):
    for ref in refs:
        rest = ref.shape[1] - start
        if rest:
            ref[:, start:, :] = jnp.zeros((ref.shape[0], rest, LANE), F32)


def nets_kernel(chunk, images, narrow, split, *refs):
    levels = CHUNKS[chunk]
    number = len(levels)
    index_ref = refs[0]
    mine = refs[1 : 1 + narrow]
    at = 1 + narrow
    if split:
        mine = (*mine[:-1], (mine[-1], refs[at]))
        at = at + 1
    stages = refs[at : at + number]
    at = at + number
    keep_ref, send_ref = refs[at : at + 2]
    results = refs[at + 2 : at + 2 + number]
    at = at + 2 + number
    for place, level in enumerate(levels):
        net_kernel(
            level,
            images,
            narrow,
            index_ref,
            *mine,
            stages[place],
            keep_ref,
            send_ref,
            results[place],
            *refs[at + 5 * place : at + 5 * place + 5],
        )
    zero_rows((keep_ref, send_ref), sum(pack_rows(level) for level in levels))


def flow_kernel(images, narrow, *refs):
    stages, results = refs[:LEVELS], refs[LEVELS : 2 * LEVELS]
    weights, out_ref = refs[2 * LEVELS : -1], refs[-1]
    flow_back(images, stages, results, weights, out_ref)


def copy_kernel(*refs):
    half = len(refs) // 2
    for from_ref, to_ref in zip(refs[:half], refs[half:]):
        to_ref[...] = from_ref[...]


def split_copy_kernel(from_ref, *refs):
    half = len(refs) // 2 - 1
    cut = refs[half].shape[0]
    refs[half][...] = from_ref[0:cut, :]
    refs[half + 1][...] = from_ref[cut:, :]
    for source, target in zip(refs[:half], refs[half + 2 :]):
        target[...] = source[...]


def piece_rows(rows):
    return rows + round_up(rows // CODE_BLOCK, 16)


def write_piece(ref, start, values, extra=None):
    rows = values.shape[0]
    blocks = values.reshape(rows // CODE_BLOCK, CODE_BLOCK, LANE)
    scale = rounded(jnp.max(jnp.abs(blocks), axis=1) * 1.01)
    factor = jnp.where(scale > 0.0, CODE_RANGE / scale, 0.0)
    code = jnp.exp(blocks * factor[:, None, :])
    ref[start : start + rows, :] = code.reshape(rows, LANE).astype(BF16)
    tail = [scale] + ([] if extra is None else split_three(extra))
    used = sum(part.shape[0] for part in tail)
    size = round_up(rows // CODE_BLOCK, 16)
    if size > used:
        tail.append(jnp.zeros((size - used, LANE), F32))
    ref[start + rows : start + rows + size, :] = jnp.concatenate(tail, 0).astype(BF16)


def read_piece(ref, start, rows):
    blocks = jnp.log(ref[start : start + rows, :].astype(F32))
    blocks = blocks.reshape(rows // CODE_BLOCK, CODE_BLOCK, LANE)
    scale = ref[start + rows : start + piece_rows(rows), :].astype(F32)
    factor = scale[: rows // CODE_BLOCK] * (1.0 / CODE_RANGE)
    return (blocks * factor[:, None, :]).reshape(rows, LANE)


def read_stats(ref, start, rows):
    first = start + rows + rows // CODE_BLOCK
    tail = ref[first : first + 3, :].astype(F32)
    return tail[0:1] + tail[1:2] + tail[2:3]


def wide_bit(index_ref, bit):
    return jnp.where((index_ref[1, 0] & bit) != 0, 1, 0)


def send_kernel(chunk, index_ref, send_ref, *piece_refs):
    half = 2 * quarter_rows(chunk)
    for shard in range(2):
        for place in range(2):
            values = send_ref[shard, place * half : (place + 1) * half, :]
            write_piece(piece_refs[2 * shard + place], 0, values)


def square_kernel(chunk, index_ref, keep_ref, *refs):
    other_refs, total_ref, refs = refs[:4], refs[-1], refs[4:-1]
    flow = None
    if flow_part(chunk):
        flow_ref, mine_ref, own_flow_ref, *sent_refs = refs
        flow = flow_ref[0:FLOW_ROWS, :]
        stats = flow_ref[FLOW_ROWS : FLOW_ROWS + 1, :]
        write_piece(own_flow_ref, 0, flow, stats)
    else:
        mine_ref, *sent_refs = refs
    half = 2 * quarter_rows(chunk)
    upper = wide_bit(index_ref, 1)
    for shard in range(2):
        for place in range(2):
            picked = slice(place * half, (place + 1) * half)
            total_ref[shard, picked, :] = keep_ref[shard, picked, :] + read_piece(
                other_refs[2 * shard + place], 0, half
            )

    def total(shard, flipped):
        place = 1 - upper if flipped else upper
        return total_ref[shard, pl.ds(pl.multiple_of(place * half, CODE_BLOCK), half), :]

    mine_ref[...] = total(0, 0)
    for ref, (shard, flipped) in zip(sent_refs, ((1, 0), (0, 1), (1, 1))):
        values = total(shard, flipped)
        if flow is None:
            write_piece(ref, 0, values)
        else:
            write_piece(ref, 0, jnp.concatenate([values, flow], 0), stats)


def column_kernel(chunk, index_ref, mine_ref, *refs):
    rows = 2 * quarter_rows(chunk)
    more = flow_part(chunk)
    if more:
        own_flow_ref, *others, keep_ref, own_next_ref, sent_ref, total_ref = refs
    else:
        *others, keep_ref, sent_ref, total_ref = refs
    total = mine_ref[...]
    for flip, other in enumerate(others, 1):
        values = read_piece(other, 0, rows + more)
        total = total + values[:rows]
        if more and flip == 2:
            flow = read_piece(own_flow_ref, 0, FLOW_ROWS) + values[rows:]
            stats = read_stats(own_flow_ref, 0, FLOW_ROWS) + read_stats(other, 0, rows + more)
    total_ref[...] = total
    half = rows // 2
    place = wide_bit(index_ref, 2)
    keep_ref[...] = total_ref[pl.ds(pl.multiple_of(place * half, CODE_BLOCK), half), :]
    values = total_ref[pl.ds(pl.multiple_of((1 - place) * half, CODE_BLOCK), half), :]
    if more:
        write_piece(own_next_ref, 0, flow, stats)
        write_piece(sent_ref, 0, jnp.concatenate([values, flow], 0), stats)
    else:
        write_piece(sent_ref, 0, values)


def code_kernel(chunk, index_ref, mine_ref, *refs):
    rows = quarter_rows(chunk)
    more = flow_part(chunk)
    if more:
        own_flow_ref, other_ref, out_ref = refs
    else:
        other_ref, out_ref = refs
    values = read_piece(other_ref, 0, rows + more)
    total = mine_ref[...] + values[:rows]
    if more:
        flow = read_piece(own_flow_ref, 0, FLOW_ROWS) + values[rows:]
        stats = read_stats(own_flow_ref, 0, FLOW_ROWS) + read_stats(other_ref, 0, rows + more)
        write_piece(out_ref, 0, jnp.concatenate([total, flow], 0), stats)
    else:
        write_piece(out_ref, 0, total)


def recode_kernel(chunk, index_ref, mine_ref, other_ref, out_ref):
    rows = quarter_rows(chunk) + flow_part(chunk)
    stats = None
    if flow_part(chunk):
        stats = read_stats(mine_ref, 0, rows) + read_stats(other_ref, 0, rows)
    write_piece(out_ref, 0, read_piece(mine_ref, 0, rows) + read_piece(other_ref, 0, rows), stats)


def pair_kernel(chunk, index_ref, mine_ref, other_ref, out_ref):
    place = wide_bit(index_ref, 2)
    out_ref[place] = mine_ref[...]
    out_ref[1 - place] = other_ref[...]


def decode_pairs_kernel(chunk, index_ref, mine_ref, other_ref, out_ref):
    rows = quarter_rows(chunk)
    upper = wide_bit(index_ref, 1)
    for place, ref in ((upper, mine_ref), (1 - upper, other_ref)):
        for near in range(2):
            start = pl.multiple_of((2 * place + near) * rows, CODE_BLOCK)
            out_ref[pl.ds(start, rows), :] = read_piece(ref.at[near], 0, rows)


def decode_kernel(chunk, index_ref, *refs):
    parts, outs = refs[:4], refs[4:]
    place = 2 * wide_bit(index_ref, 1) + wide_bit(index_ref, 2)
    rows, more = quarter_rows(chunk), flow_part(chunk)
    for flip, ref in enumerate(parts):
        values = read_piece(ref, 0, rows + more)
        start = pl.multiple_of((place ^ flip) * rows, CODE_BLOCK)
        outs[0][pl.ds(start, rows), :] = values[:rows]
        if more and flip == 0:
            outs[1][0:FLOW_ROWS, :] = values[rows:]
            outs[1][FLOW_ROWS:, :] = jnp.broadcast_to(
                read_stats(ref, 0, rows + more), (STATS_ROWS, LANE)
            )


def moments(weight, gradient, first_old, second_old):
    first_new = FIRST_BETA * first_old + (1.0 - FIRST_BETA) * gradient
    second_new = SECOND_BETA * second_old + (1.0 - SECOND_BETA) * gradient * gradient
    update = (
        first_new
        * (1.0 / (1.0 - FIRST_BETA**STEP))
        / (jnp.sqrt(second_new * (1.0 / (1.0 - SECOND_BETA**STEP))) + EPSILON)
        + WEIGHT_DECAY * weight
    )
    return first_new, second_new, update


def total_of(values):
    return jnp.sum(jnp.sum(values, 0, keepdims=True), 1, keepdims=True)


def squares_rows(sums):
    row = iota((16, LANE), 0)
    held = jnp.zeros((16, LANE), F32)
    for index, value in enumerate(sums):
        held = jnp.where(row == index, value, held)
    return held


def group_totals(values_in, values_mix, values_out, values_bias):
    row = iota(values_in.shape, 0)
    line = iota(values_out.shape, 0)
    sums = []
    start = 0
    for level in range(LEVELS):
        inside = (row >= start) & (row < start + in_rows(level))
        sums.append(total_of(jnp.where(inside, values_in, 0.0)))
        start = start + in_rows(level)
    for level in range(LEVELS):
        sums.append(total_of(values_mix[level]))
    start = 0
    for level in range(LEVELS):
        inside = (line >= start) & (line < start + 9 * chan(level))
        sums.append(total_of(jnp.where(inside, values_out, 0.0)))
        start = start + 9 * chan(level)
    for level in range(LEVELS):
        sums.append(total_of(values_bias[2 * level : 2 * level + 2]))
    return sums


def flow_masks():
    place = iota((FLOW_ROWS, LANE), 0) * LANE + iota((FLOW_ROWS, LANE), 1)
    masks = []
    start = 0
    for length in flow_lengths():
        masks.append((place >= start) & (place < start + length))
        start = start + length
    return masks


def split_grads(refs, scale):
    ins, mixes, outs, biases = [], [], [], []
    for level in range(LEVELS):
        chunk, start = chunk_of(level)
        ref = refs[chunk]

        def rows(first, count):
            return ref[start + first : start + first + count, :] * scale

        top = first_rows(level)
        ins.append(rows(0, in_rows(level)))
        mixes.append(rows(top, HID))
        outs.append(rows(top + HID, 9 * chan(level)))
        biases.append(rows(in_rows(level), 1))
        biases.append(rows(second_bias_row(level), 1))
    return jnp.concatenate(ins, 0), mixes, jnp.concatenate(outs, 0), jnp.concatenate(biases, 0)


def norm_kernel(*refs):
    parts, flow_ref = refs[:2], refs[2]
    weight_in, weight_mix, weight_out, weight_bias = refs[3:7]
    first_in, first_mix, first_out, first_bias = refs[7:11]
    second_in, second_mix, second_out, second_bias = refs[11:15]
    grad_in_ref, grad_mix_ref, grad_out_ref, grad_bias_ref = refs[15:19]
    update_in, update_mix, update_out, update_bias, block_ref = refs[19:]
    stats = flow_ref[FLOW_ROWS : FLOW_ROWS + 1, :]
    scale = 1.0 / (3.0 * stats[:, 1:2] * LOG_TWO)
    grad_in, grad_mix, grad_out, grad_bias = split_grads(parts, scale)
    grad_in_ref[...] = grad_in
    grad_out_ref[...] = grad_out
    grad_bias_ref[...] = grad_bias
    bias = weight_bias[...].reshape(2 * LEVELS, LANE)
    new_in = moments(weight_in[...], grad_in, first_in[...], second_in[...])[2]
    new_out = moments(weight_out[...], grad_out, first_out[...], second_out[...])[2]
    new_bias = moments(
        bias,
        grad_bias,
        first_bias[...].reshape(2 * LEVELS, LANE),
        second_bias[...].reshape(2 * LEVELS, LANE),
    )[2]
    update_in[...] = new_in
    update_out[...] = new_out
    update_bias[...] = new_bias.reshape(LEVELS, 2, LANE)
    mix_squares = []
    mix_updates = []
    for level in range(LEVELS):
        grad_mix_ref[level] = grad_mix[level]
        new_mix = moments(weight_mix[level], grad_mix[level], first_mix[level], second_mix[level])[2]
        update_mix[level] = new_mix
        mix_squares.append(weight_mix[level] * weight_mix[level])
        mix_updates.append(new_mix * new_mix)
    weight_sums = group_totals(
        weight_in[...] * weight_in[...], mix_squares, weight_out[...] * weight_out[...], bias * bias
    )
    update_sums = group_totals(new_in * new_in, mix_updates, new_out * new_out, new_bias * new_bias)
    lane = iota((16, LANE), 1)
    block_ref[0:16, :] = jnp.where(lane == 0, squares_rows(weight_sums), squares_rows(update_sums))
    block_ref[16:, :] = flow_ref[...]


def moment_kernel(*refs):
    grads, firsts, seconds = refs[0:4], refs[4:8], refs[8:12]
    new_firsts, new_seconds = refs[12:16], refs[16:20]
    refs[20][...] = jnp.zeros((8, LANE), F32)
    for grad, first, second, new_first, new_second in zip(
        grads, firsts, seconds, new_firsts, new_seconds
    ):
        gradient = grad[...].reshape(first.shape)
        new_first[...] = FIRST_BETA * first[...] + (1.0 - FIRST_BETA) * gradient
        new_second[...] = SECOND_BETA * second[...] + (1.0 - SECOND_BETA) * gradient * gradient


def apply_kernel(narrow, *refs):
    index_ref = refs[0]
    block_refs = refs[1 : 1 + narrow]
    at = 1 + narrow
    weight_in, weight_mix, weight_out, weight_bias = refs[at : at + 4]
    update_in, update_mix, update_out, update_bias = refs[at + 4 : at + 8]
    flow_ref, flow_first_ref, flow_second_ref = refs[at + 8 : at + 11]
    at = at + 11
    (
        new_in,
        new_mix,
        new_out,
        new_bias,
        new_flow,
        half_in,
        half_mix,
        half_out,
        flow_moment,
        flow_square,
        weight_norm_ref,
        update_norm_ref,
        loss_ref,
        valid_ref,
        order_ref,
    ) = refs[at:]
    for part in range(narrow):
        order_ref[index_ref[0, 0] ^ part] = block_refs[part][...]
    whole = order_ref[0]
    for part in range(1, narrow):
        whole = whole + order_ref[part]
    sums = whole[0:16]
    flow_grad = whole[16 : 16 + FLOW_ROWS]
    loss = whole[16 + FLOW_ROWS : 17 + FLOW_ROWS, 0:1]
    valid_dims = 3.0 * block_refs[0][16 + FLOW_ROWS : 17 + FLOW_ROWS, 1:2]
    scale = 1.0 / (valid_dims * LOG_TWO)
    flow = to_flat_rows(flow_ref[...])
    size = flow_ref.shape[0]
    place = iota((FLOW_ROWS, LANE), 0) * LANE + iota((FLOW_ROWS, LANE), 1)
    flow_grad = jnp.where(place < size, flow_grad * scale, 0.0)
    first_new, second_new, update = moments(
        flow, flow_grad, to_flat_rows(flow_first_ref[...]), to_flat_rows(flow_second_ref[...])
    )
    weight_norms = [jnp.sqrt(sums[index : index + 1, 0:1]) for index in range(12)]
    update_norms = [jnp.sqrt(sums[index : index + 1, 1:2]) for index in range(12)]
    masks = flow_masks()
    for mask in masks:
        weight_norms.append(jnp.sqrt(total_of(jnp.where(mask, flow * flow, 0.0))))
        update_norms.append(jnp.sqrt(total_of(jnp.where(mask, update * update, 0.0))))
    rates = [
        LEARN_RATE * (weight_norm / update_norm)
        for weight_norm, update_norm in zip(weight_norms, update_norms)
    ]
    rate = jnp.zeros((FLOW_ROWS, LANE), F32)
    for mask, value in zip(masks, rates[12:]):
        rate = jnp.where(mask, value, rate)
    new_flow[...] = from_flat_rows(flow - rate * update, size)
    flow_moment[...] = from_flat_rows(first_new, size)
    flow_square[...] = from_flat_rows(second_new, size)
    row = iota(weight_in.shape, 0)
    edge_one, edge_two = in_rows(0), in_rows(0) + in_rows(1)
    rate = jnp.where(row < edge_one, rates[0], jnp.where(row < edge_two, rates[1], rates[2]))
    fresh = weight_in[...] - rate * update_in[...]
    new_in[...] = fresh
    half_in[...] = fresh.astype(BF16)
    for level in range(LEVELS):
        fresh = weight_mix[level] - rates[3 + level] * update_mix[level]
        new_mix[level] = fresh
        half_mix[level] = fresh.astype(BF16)
    row = iota(weight_out.shape, 0)
    edge_one, edge_two = 9 * chan(0), 9 * chan(0) + 9 * chan(1)
    rate = jnp.where(row < edge_one, rates[6], jnp.where(row < edge_two, rates[7], rates[8]))
    fresh = weight_out[...] - rate * update_out[...]
    new_out[...] = fresh
    half_out[...] = fresh.astype(BF16)
    for level in range(LEVELS):
        new_bias[level] = weight_bias[level] - rates[9 + level] * update_bias[level]
    lane = iota((1, LANE), 1)
    for ref, norms in ((weight_norm_ref, weight_norms), (update_norm_ref, update_norms)):
        held = jnp.zeros((1, LANE), F32)
        for index in range(15):
            held = jnp.where(lane == index, norms[index], held)
        ref[...] = held[:, :15].reshape(15)
    loss_ref[...] = loss / LOG_TWO + 8.0 * valid_dims
    valid_ref[...] = valid_dims


def spec_vmem():
    return pl.BlockSpec(memory_space=pltpu.VMEM)


def spec_smem():
    return pl.BlockSpec(memory_space=pltpu.SMEM)


def call(kernel, outs, scalars, arrays, scratch=(), name=None, after=(), vmem=20):
    number = len(scalars) + len(arrays)

    def run(*refs):
        kernel(*refs[:number], *refs[number + len(after) :])

    return pl.pallas_call(
        run,
        out_shape=tuple(jax.ShapeDtypeStruct(shape, dtype) for shape, dtype in outs),
        in_specs=[spec_smem()] * len(scalars)
        + [spec_vmem()] * len(arrays)
        + [pl.BlockSpec(memory_space=pl.ANY)] * len(after),
        out_specs=tuple(spec_vmem() for _ in outs),
        scratch_shapes=list(scratch),
        compiler_params=pltpu.CompilerParams(vmem_limit_bytes=vmem * 1024 * 1024),
        cost_estimate=pl.CostEstimate(
            flops=1000, bytes_accessed=1000, transcendentals=0
        ),
        name=name,
    )(*scalars, *arrays, *after)


def run_pack(valid_shape, conv_in, mixer, conv_out, hidden_bias):
    cut = sum(pack_rows(level) for level in CHUNKS[0])
    rows = pack_start(-1) + 16
    outs = [((size, LANE), BF16) for size in (rows, cut, rows - cut)]
    return call(pack_kernel, outs, (valid_shape,), (conv_in, mixer, conv_out, hidden_bias), name="pack", vmem=56)


def run_flow_pre(noise_seeds, valid_shape, images, flow_params, packed):
    count = images.shape[1]
    outs = [((stage_rows(level)["rows"], positions(level, count)), F32) for level in range(LEVELS)]
    outs.append((packed.shape, BF16))
    return call(
        flow_pre_kernel,
        outs,
        (noise_seeds, valid_shape),
        (images, flow_params, packed),
        name="flow_pre",
    )


def run_nets(chunk, images, index, weights, stages, after):
    narrow = lax.axis_size("narrow")
    outs = [((narrow // 2, 4 * quarter_rows(chunk), LANE), F32)] * 2
    scratch = []
    for level in CHUNKS[chunk]:
        count = positions(level, images)
        outs = outs + [((stage_rows(level)["result_rows"], count), F32)]
        scratch = scratch + net_scratch(count)
    return call(
        functools.partial(nets_kernel, chunk, images, narrow, len(weights) > narrow),
        outs,
        (),
        [index] + list(weights) + [stages[level] for level in CHUNKS[chunk]],
        scratch,
        name="nets_" + "ab"[chunk],
        after=after,
    )


def net_scratch(count):
    return [
        pltpu.VMEM((HID, HID), BF16),
        pltpu.VMEM((HID, count), F32),
        pltpu.VMEM((HID, count), F32),
        pltpu.VMEM((HID, count), BF16),
        pltpu.VMEM((HID, count), BF16),
    ]


def run_flow(images, weights, stages, results, after):
    (out,) = call(
        functools.partial(flow_kernel, images, len(weights)),
        [((FLOW_ROWS + STATS_ROWS, LANE), F32)],
        (),
        list(stages) + list(results) + list(weights),
        name="flow_back",
        after=after,
    )
    return out


def swap(values, wide, narrow):
    width = lax.axis_size("narrow")
    mask = wide * width + narrow
    count = lax.axis_size("wide") * width
    return lax.ppermute(values, ("wide", "narrow"), [(place, place ^ mask) for place in range(count)])


class Summation:
    def __init__(self, chunk, index, send, after):
        self.chunk, self.index = chunk, index
        rows, more = quarter_rows(chunk), flow_part(chunk)
        self.kept, self.others = send, ()
        sent = self.run(send_kernel, [((piece_rows(2 * rows), LANE), BF16)] * 4, "send", after)
        self.token = sent[0]
        self.others = [swap(piece, 0, 1) for piece in sent]
        self.own_piece = [((piece_rows(FLOW_ROWS), LANE), BF16)] if more else []
        self.own = ()
        self.square_piece = ((piece_rows(2 * rows + more), LANE), BF16)
        self.piece = ((piece_rows(rows + more), LANE), BF16)

    def run(self, kernel, outs, name, after, scratch=(), extra=()):
        return call(
            functools.partial(kernel, self.chunk),
            outs,
            (),
            (self.index, self.kept, *extra, *self.others),
            scratch,
            name=name + "_" + "ab"[self.chunk],
            after=after,
        )

    def square(self, keep, flow, after):
        rows = 2 * quarter_rows(self.chunk)
        self.kept, *rest = call(
            functools.partial(square_kernel, self.chunk),
            [((rows, LANE), F32)] + self.own_piece + [self.square_piece] * 3,
            (),
            (self.index, keep, *self.others, *flow),
            [pltpu.VMEM((2, 2 * rows, LANE), F32)],
            name="square_" + "ab"[self.chunk],
            after=after,
        )
        self.own, sent = tuple(rest[:-3]), rest[-3:]
        self.others = [swap(sent[0], 0, 2), swap(sent[1], 1, 0), swap(sent[2], 1, 2)]
        return self.kept

    def column(self, after):
        rows = quarter_rows(self.chunk)
        self.kept, *rest = self.run(
            column_kernel,
            [((rows, LANE), F32)] + self.own_piece + [self.piece],
            "column",
            after,
            [pltpu.VMEM((2 * rows, LANE), F32)],
            self.own,
        )
        self.own = tuple(rest[:-1])
        self.others = [swap(rest[-1], 2, 0)]
        return self.kept

    def code(self, after):
        (self.kept,) = self.run(code_kernel, [self.piece], "code", after, (), self.own)
        self.others = [swap(self.kept, 4, 0)]
        return self.kept

    def spread(self, after):
        step = 4
        while step < lax.axis_size("wide"):
            (self.kept,) = self.run(recode_kernel, [self.piece], "recode_%d" % step, after)
            step = 2 * step
            if step < lax.axis_size("wide"):
                self.others = [swap(self.kept, step, 0)]
        token = self.kept
        if flow_part(self.chunk):
            self.others = [swap(self.kept, place, 0) for place in (2, 1, 3)]
        else:
            self.others = [swap(self.kept, 2, 0)]
            (self.kept,) = self.run(pair_kernel, [((2,) + self.piece[0], BF16)], "pair", ())
            self.others = [swap(self.kept, 1, 0)]
        return token

    def decode(self, after):
        shape = [((4 * quarter_rows(self.chunk), LANE), F32)]
        if flow_part(self.chunk):
            shape.append(((FLOW_ROWS + STATS_ROWS, LANE), F32))
            return self.run(decode_kernel, shape, "decode", after)
        return self.run(decode_pairs_kernel, shape, "decode", after)


def body(
    images,
    noise_seeds,
    valid_shape,
    conv_in,
    mixer,
    conv_out,
    hidden_bias,
    flow_params,
    conv_in_first,
    mixer_first,
    conv_out_first,
    bias_first,
    flow_first,
    conv_in_second,
    mixer_second,
    conv_out_second,
    bias_second,
    flow_second,
):
    count = images.shape[1]
    conv_out, conv_out_first, conv_out_second = conv_out.T, conv_out_first.T, conv_out_second.T
    row = lax.broadcasted_iota(jnp.int32, (8, LANE), 0)
    index = jnp.where(row == 0, lax.axis_index("narrow"), lax.axis_index("wide")).astype(jnp.int32)
    narrow = lax.axis_size("narrow")
    packed, *parts = run_pack(valid_shape, conv_in, mixer, conv_out, hidden_bias)
    paired = swap(packed, 0, 1)
    crossed = [swap(part, 0, 2) for part in parts]
    *stages, own = run_flow_pre(noise_seeds, valid_shape, images, flow_params, packed)
    cut = first_rows(CHUNKS[0][0]) + HID
    shapes = [((rows, LANE), BF16) for rows in (cut, crossed[0].shape[0] - cut)]
    head, tail, *stages = call(
        split_copy_kernel,
        shapes + [(stage.shape, F32) for stage in stages],
        (),
        (crossed[0], *stages),
        name="copy_a",
    )
    gathered = (own, paired, crossed[0], swap(head, 0, 1), swap(tail, 0, 1))
    keep_one, send, *last = run_nets(0, count, index, gathered, stages, ())
    one = Summation(0, index, send, ())
    token = one.square(keep_one, (), ())
    (copied,) = call(
        copy_kernel,
        [(crossed[1].shape, BF16)],
        (),
        (crossed[1],),
        name="copy_b",
        after=(token,),
    )
    gathered = (own, paired, crossed[1], swap(copied, 0, 1))
    keep_two, send, *results = run_nets(1, count, index, gathered, stages, (copied,))
    flow = run_flow(count, gathered, stages, results + last, (keep_two,))
    token = one.column((flow,))
    two = Summation(1, index, send, (token,))
    token = two.square(keep_two, (flow,), ())
    token = one.code((token,))
    token = one.spread((token,))
    token = two.column((token,))
    token = two.code((token,))
    token = two.spread((token,))
    parts = one.decode((token,))
    parts = list(parts) + list(two.decode((parts[0],)))
    weights = (conv_in, mixer, conv_out, hidden_bias)
    firsts = (conv_in_first, mixer_first, conv_out_first, bias_first)
    seconds = (conv_in_second, mixer_second, conv_out_second, bias_second)
    shapes = [(weight.shape, F32) for weight in weights]
    grad_shapes = shapes[:3] + [((2 * LEVELS, LANE), F32)]
    *grads, update_in, update_mix, update_out, update_bias, block = call(
        norm_kernel,
        grad_shapes + shapes + [((16 + FLOW_ROWS + STATS_ROWS, LANE), F32)],
        (),
        tuple(parts) + weights + firsts + seconds,
        name="norms",
    )
    blocks = [block] + [swap(block, 0, part) for part in range(1, narrow)]
    moved = call(
        moment_kernel,
        shapes * 2 + [((8, LANE), F32)],
        (),
        tuple(grads) + firsts + seconds,
        name="moments",
    )
    flow_shape = (flow_params.shape, F32)
    fresh = call(
        functools.partial(apply_kernel, narrow),
        shapes
        + [flow_shape]
        + [(weight.shape, BF16) for weight in weights[:3]]
        + [flow_shape, flow_shape, ((15,), F32), ((15,), F32), ((1, 1), F32), ((1, 1), F32)],

        (),
        (index,)
        + tuple(blocks)
        + weights
        + (update_in, update_mix, update_out, update_bias)
        + (flow_params, flow_first, flow_second),
        scratch=[pltpu.VMEM((narrow,) + block.shape, F32)],
        after=(moved[8],),
        name="apply",
    )
    return (
        fresh[0],
        fresh[1],
        fresh[2].T,
        fresh[3],
        fresh[4],
        moved[0],
        moved[1],
        moved[2].T,
        moved[3],
        fresh[8],
        moved[4],
        moved[5],
        moved[6].T,
        moved[7],
        fresh[9],
        fresh[5],
        fresh[6],
        fresh[7].T,
        fresh[10],
        fresh[11],
        fresh[12].reshape(()),
        fresh[13].reshape(()),
    )


def solution(mesh):
    placed = (
        P(None, ("wide", "narrow"), None),
        P(("wide", "narrow")),
        P(("wide", "narrow"), None),
        P(None, "narrow"),
        P(None, None, "narrow"),
        P("narrow", None),
        P(None, None, "narrow"),
        P(),
    )
    state = (P(None, "narrow"), P(None, None, "narrow"), P("narrow", None), P(None, None, "narrow"), P())
    return jax.shard_map(
        body,
        mesh=mesh,
        in_specs=placed + state + state,
        out_specs=state * 3 + state[:3] + (P(),) * 4,
        check_vma=False,
    )
```

```python
import functools
import jax
import jax.numpy as jnp
from jax import lax
from jax.experimental import pallas as pl
from jax.experimental.pallas import tpu as pltpu
from jax.sharding import PartitionSpec as P

C1 = 12
IMG_SIDE = 32
STEP = 5
HIGHEST_PRECISION = lax.Precision.HIGHEST
LOG_TWO_PI = 1.8378770664093453
LOG_TWO = 0.6931471805599453
FIRST_BETA = 0.5
SECOND_BETA = 0.5
EPSILON = 1e-06
WEIGHT_DECAY = 0.01
LEARN_RATE = 0.25
TAPS = [(-1, -1), (-1, 0), (-1, 1), (0, -1), (0, 0), (0, 1), (1, -1), (1, 0), (1, 1)]
F32 = jnp.float32
BF16 = jnp.bfloat16
HID = 512
LANE = 128
LEVELS = 3
FLOW_ROWS = 32
STATS_ROWS = 8
CODE_BLOCK = 16
CODE_RANGE = 84.0
SQUARE_ORDER = ((1, 3, 2), (2, 1, 3))
RETURN_ORDER = (2, 1, 3)
VMEM_BYTES = 20 * 1024 * 1024


def round_up(value, unit):
    return (value + unit - 1) // unit * unit


def chan(level):
    return C1 * 2**level


def side(level):
    return IMG_SIDE // 2 ** (level + 1)


def real_positions(level, images):
    return images * side(level) ** 2


def positions(level, images):
    return round_up(real_positions(level, images), LANE)


def in_rows(level):
    return 9 * chan(level) // 2


def bias_in_tail(level):
    return round_up(9 * chan(level), 16) - 9 * chan(level) >= 4 and in_rows(level) % 16 > 10


def first_rows(level):
    return round_up(in_rows(level) + (3 if bias_in_tail(level) else 6), 16)


def second_bias_row(level):
    return (pack_rows(level) if bias_in_tail(level) else first_rows(level)) - 4


def last_rows(level):
    return round_up(9 * chan(level), 16)


def pack_rows(level):
    return first_rows(level) + HID + last_rows(level)


def pack_start(level):
    return sum(pack_rows(other) for other in range(LEVELS - 1, level, -1))


CHUNKS = ((2,), (0, 1))


def gather_start(level):
    return pack_start(level) - (0 if level in CHUNKS[0] else pack_start(CHUNKS[0][0] - 1))


def chunk_of(level):
    for chunk, levels in enumerate(CHUNKS):
        if level in levels:
            return chunk, sum(pack_rows(other) for other in levels[: levels.index(level)])
    return None


def quarter_rows(chunk):
    return round_up(sum(pack_rows(level) for level in CHUNKS[chunk]), 4 * CODE_BLOCK) // 4


def flow_part(chunk):
    return FLOW_ROWS if chunk == len(CHUNKS) - 1 else 0


def stage_rows(level):
    padded = round_up(chan(level), 8)
    half = round_up(chan(level) // 2, 8)
    sizes = [
        ("normed", padded),
        ("mixed", padded),
        ("share", 8),
        ("held", padded),
        ("block", padded),
        ("prior", half),
        ("mixing", padded),
        ("turn", padded),
        ("grad", padded),
        ("small", padded),
        ("prior_grad", half),
    ]
    starts = {}
    at = 0
    for name, size in sizes[:8]:
        starts[name] = at
        at = at + size
    starts["rows"] = at
    at = 0
    for name, size in sizes[8:]:
        starts[name] = at
        at = at + size
    starts["result_rows"] = at
    return starts


def flow_lengths():
    return [5 * C1 + 3 * C1 * C1 // 2, 10 * C1 + 6 * C1 * C1, 24 * C1 + 16 * C1 * C1]


def flow_size():
    return sum(flow_lengths())


def flow_offsets(level):
    start = sum(flow_lengths()[:level])
    channels = chan(level)
    offsets = {"bias": start, "logs": start + channels, "block": start + 2 * channels}
    start = start + 2 * channels + channels * channels
    offsets["outbias"] = start
    offsets["outscale"] = start + channels
    start = start + 2 * channels
    if level < LEVELS - 1:
        offsets["priormatrix"] = start
        start = start + channels // 2 * channels
    offsets["priorbias"] = start
    return offsets


def column_names(level):
    channels = chan(level)
    offsets = flow_offsets(level)
    names = [
        ("bias", offsets["bias"]),
        ("logs", offsets["logs"]),
        ("outbias", offsets["outbias"]),
        ("outscale", offsets["outscale"]),
        ("priorbias", offsets["priorbias"]),
    ]
    if level == LEVELS - 1:
        names = names + [("priorscale", offsets["priorbias"] + channels)]
    return names


def exact_dot(first, second):
    return jnp.dot(first, second, precision=HIGHEST_PRECISION, preferred_element_type=F32)


def exact_rows(first, second):
    return lax.dot_general(
        first,
        second,
        (((0,), (0,)), ((), ())),
        precision=HIGHEST_PRECISION,
        preferred_element_type=F32,
    )


def exact_columns(first, second):
    return lax.dot_general(
        first,
        second,
        (((1,), (1,)), ((), ())),
        precision=HIGHEST_PRECISION,
        preferred_element_type=F32,
    )


def plain_dot(first, second):
    return jnp.dot(first, second, preferred_element_type=F32)


def contract_rows(first, second):
    return lax.dot_general(first, second, (((0,), (0,)), ((), ())), preferred_element_type=F32)


def contract_columns(first, second):
    return lax.dot_general(first, second, (((1,), (1,)), ((), ())), preferred_element_type=F32)


def iota(shape, axis):
    return lax.broadcasted_iota(jnp.int32, shape, axis)


def rounded(values):
    return values.astype(BF16).astype(F32)


def split_three(values):
    high = rounded(values)
    rest = values - high
    middle = rounded(rest)
    return [high, middle, rest - middle]


def move_lanes(values, chooser, transposed=False):
    rows = values.shape[0]
    padded = round_up(rows, 8)
    if padded > rows:
        values = jnp.concatenate([values, jnp.zeros((padded - rows, values.shape[1]), F32)], 0)
    pieces = jnp.concatenate(split_three(values), 0).astype(BF16)
    moved = contract_columns(pieces, chooser) if transposed else plain_dot(pieces, chooser)
    moved = moved[:padded] + moved[padded : 2 * padded] + moved[2 * padded :]
    return moved[:rows]


def squeeze_chooser(grid, images):
    count = images * grid * grid
    source = iota((count, count), 0)
    target = iota((count, count), 1)
    shift = grid.bit_length() - 1
    image = lax.shift_right_logical(source, 2 * shift)
    row = lax.shift_right_logical(source, shift) & (grid - 1)
    column = source & (grid - 1)
    half = grid // 2
    place = (
        ((row & 1) * 2 + (column & 1)) * (images * half * half)
        + image * (half * half)
        + lax.shift_right_logical(row, 1) * half
        + lax.shift_right_logical(column, 1)
    )
    return (place == target).astype(F32).astype(BF16)


def order_chooser(channels, stride):
    row = iota((4 * channels, 4 * stride), 0)
    column = iota((4 * channels, 4 * stride), 1)
    return ((row & 3) * stride + lax.shift_right_logical(row, 2) == column).astype(F32)


def squeeze(values, chooser, lanes_out):
    channels, count = values.shape
    moved = move_lanes(values, chooser)
    quarter = count // 4
    stacked = jnp.concatenate([moved[:, k * quarter : (k + 1) * quarter] for k in range(4)], 0)
    ordered = exact_dot(order_chooser(channels, channels), stacked)
    if lanes_out > quarter:
        ordered = jnp.concatenate([ordered, jnp.zeros((4 * channels, lanes_out - quarter), F32)], 1)
    return ordered


def unsqueeze(stacked, chooser, count):
    channels = stacked.shape[0] // 4
    quarter = count // 4
    laid = jnp.concatenate(
        [stacked[k * channels : (k + 1) * channels, :quarter] for k in range(4)], 1
    )
    return move_lanes(laid, chooser, transposed=True)


def slope_roll(values, step):
    step = step % LANE
    while step:
        part = 16 if step >= 16 else 1 << (step.bit_length() - 1)
        values = pltpu.roll(values, 0, 1, stride=part, stride_axis=0)
        step = step - part
    return values


def flow_block(flat, offset, rows, width):
    padded = round_up(rows, 8)
    start = offset + width * iota((padded, FLOW_ROWS), 0)
    line = lax.shift_right_logical(start, 7)
    column = iota((padded, FLOW_ROWS), 1)
    base = -offset % LANE
    if base:
        flat = pltpu.roll(flat, base, 1)
    here = exact_dot((line == column).astype(F32), flat)
    after = exact_dot((line + 1 == column).astype(F32), flat)
    here = slope_roll(here, -width)
    after = slope_roll(after, -width)
    lane = iota((padded, LANE), 1)
    begin = (offset + width * iota((padded, LANE), 0)) & (LANE - 1)
    chosen = jnp.where(lane + begin < LANE, here, after)
    return chosen[:rows, :width]


def flow_block_back(values, offset, rows, width):
    padded = round_up(rows, 8)
    base = offset % LANE
    over = max(base + width - LANE, 0)
    parts = [values[:, width - over :]] if over else []
    if base > over:
        parts.append(jnp.zeros((rows, base - over), F32))
    parts.append(values[:, : width - over])
    if base + width < LANE:
        parts.append(jnp.zeros((rows, LANE - base - width), F32))
    block = jnp.concatenate(parts, 1)
    if padded > rows:
        block = jnp.concatenate([block, jnp.zeros((padded - rows, LANE), F32)], 0)
    block = slope_roll(block, width)
    lane = iota((padded, LANE), 1)
    begin = (offset + width * iota((padded, LANE), 0)) & (LANE - 1)
    here = jnp.where(lane >= begin, block, 0.0)
    after = jnp.where(lane >= begin, 0.0, block)
    line = lax.shift_right_logical(offset + width * iota((FLOW_ROWS, padded), 1), 7)
    row = iota((FLOW_ROWS, padded), 0)
    return exact_dot((line == row).astype(F32), here) + exact_dot(
        (line + 1 == row).astype(F32), after
    )


def flow_column(turned, offset, length):
    line, begin = offset // LANE, offset % LANE
    if begin + length <= LANE:
        return turned[begin : begin + length, line : line + 1]
    return jnp.concatenate(
        [turned[begin:, line : line + 1], turned[: begin + length - LANE, line + 1 : line + 2]], 0
    )


def flow_column_back(values, offset):
    length = values.shape[0]
    line, begin = offset // LANE, offset % LANE
    lane = iota((LANE, LANE), 1)
    head = min(length, LANE - begin)
    parts = []
    if begin:
        parts.append(jnp.zeros((begin, 1), F32))
    parts.append(values[:head])
    if begin + head < LANE:
        parts.append(jnp.zeros((LANE - begin - head, 1), F32))
    column = jnp.concatenate(parts, 0) if len(parts) > 1 else parts[0]
    term = jnp.where(lane == line, column, 0.0)
    if head < length:
        column = jnp.concatenate([values[head:], jnp.zeros((LANE - length + head, 1), F32)], 0)
        term = term + jnp.where(lane == line + 1, column, 0.0)
    return term


def to_flat_rows(values):
    size = values.shape[0]
    row = values.reshape(1, size)
    row = jnp.concatenate([row, jnp.zeros((1, FLOW_ROWS * LANE - size), F32)], 1)
    return row.reshape(FLOW_ROWS, LANE)


def from_flat_rows(values, size):
    return values.reshape(1, FLOW_ROWS * LANE)[:, :size].reshape(size)


def triangles(block):
    channels = block.shape[0]
    row = iota((channels, channels), 0)
    column = iota((channels, channels), 1)
    signs = (1 - 2 * (row & 1)).astype(F32)
    diagonal = signs * jnp.exp(jnp.where(row == column, block, 0.0))
    lower = jnp.where(row > column, block, jnp.where(row == column, 1.0, 0.0))
    upper = jnp.where(row < column, block, jnp.where(row == column, diagonal, 0.0))
    reverse = (row + column == channels - 1).astype(F32)
    return lower, upper, reverse, diagonal


def tap_masks(level, images):
    grid = side(level)
    count = positions(level, images)
    lane = iota((8, count), 1)
    shift = grid.bit_length() - 1
    row = lax.shift_right_logical(lane, shift) & (grid - 1)
    column = lane & (grid - 1)
    inside = lane < real_positions(level, images)
    masks = {}
    for row_step in (-1, 0, 1):
        for column_step in (-1, 0, 1):
            good = (
                (row + row_step >= 0)
                & (row + row_step < grid)
                & (column + column_step >= 0)
                & (column + column_step < grid)
                & inside
            )
            masks[(row_step, column_step)] = jnp.where(good, 1.0, 0.0)[0:1]
    return masks


def tap_read(values, masks, level, row_step, column_step):
    count = values.shape[1]
    offset = (row_step * side(level) + column_step) % count
    if offset:
        values = pltpu.roll(values, count - offset, 1)
    if (row_step, column_step) != (0, 0):
        values = values * masks[(row_step, column_step)]
    return values


def tap_stack(values, masks, level, direction):
    return [
        tap_read(values, masks, level, direction * row_step, direction * column_step)
        for row_step, column_step in TAPS
    ]


def tap_sum(values, masks, level, direction, channels):
    total = None
    for tap, (row_step, column_step) in enumerate(TAPS):
        term = tap_read(
            values[tap * channels : (tap + 1) * channels],
            masks,
            level,
            direction * row_step,
            direction * column_step,
        )
        total = term if total is None else total + term
    return total


def pack_kernel(valid_ref, conv_in_ref, mixer_ref, conv_out_ref, bias_ref, whole_ref, *part_refs):
    in_start = 0
    out_start = 0
    for level in range(LEVELS):
        out_ref = whole_ref.at[pack_start(level) : pack_start(level) + pack_rows(level)]
        rows, columns = in_rows(level), 9 * chan(level)
        top = first_rows(level)
        ones = split_three(bias_ref[level, 0:1, :])
        twos = split_three(bias_ref[level, 1:2, :]) + [jnp.zeros((1, LANE), F32)]
        head = [conv_in_ref[in_start : in_start + rows, :]] + ones
        tail = [conv_out_ref[out_start : out_start + columns, :]]
        for part, size, chosen in (
            (head, top, not bias_in_tail(level)),
            (tail, last_rows(level), bias_in_tail(level)),
        ):
            used = sum(piece.shape[0] for piece in part) + (4 if chosen else 0)
            if size > used:
                part.append(jnp.zeros((size - used, LANE), F32))
            if chosen:
                part.extend(twos)
        out_ref[0:top, :] = jnp.concatenate(head, 0).astype(BF16)
        out_ref[top : top + HID, :] = mixer_ref[level].astype(BF16)
        out_ref[top + HID :, :] = jnp.concatenate(tail, 0).astype(BF16)
        in_start = in_start + rows
        out_start = out_start + columns
    pixels = jnp.int32(0)
    for image in range(valid_ref.shape[0]):
        pixels = pixels + valid_ref[image, 0] * valid_ref[image, 1]
    lane = iota((16, LANE), 1)
    digits = jnp.where(lane == 0, pixels & 127, 0)
    for place in (1, 2):
        digits = jnp.where(lane == place, lax.shift_right_logical(pixels, 7 * place) & 127, digits)
    whole_ref[pack_start(-1) :, :] = digits.astype(F32).astype(BF16)
    cut = part_refs[0].shape[0]
    part_refs[0][...] = whole_ref[0:cut, :]
    part_refs[1][...] = whole_ref[cut:, :]


def flow_pre_kernel(seed_ref, valid_ref, image_ref, flow_ref, packed_ref, *out_refs):
    out_refs[LEVELS][...] = packed_ref[...]
    images = image_ref.shape[1]
    flat = to_flat_rows(flow_ref[...])
    turned = jnp.concatenate([flat, jnp.zeros((LANE - FLOW_ROWS, LANE), F32)], 0).T
    blocks = IMG_SIDE * IMG_SIDE // 256
    pieces = []
    for image in range(images):
        position = iota((8, IMG_SIDE * IMG_SIDE), 0) * (IMG_SIDE * IMG_SIDE) + iota(
            (8, IMG_SIDE * IMG_SIDE), 1
        )
        hashed = seed_ref[image] + position * jnp.int32(-1640531527)
        hashed = hashed ^ lax.shift_right_logical(hashed, jnp.full_like(hashed, 15))
        hashed = hashed * jnp.int32(739267321)
        hashed = hashed ^ lax.shift_right_logical(hashed, jnp.full_like(hashed, 13))
        field = ((hashed & jnp.int32(16777215)).astype(F32) + 0.5) * 2.0 ** (-24)
        pixel = jnp.concatenate(
            [image_ref[:, image, :], jnp.zeros((5, IMG_SIDE * IMG_SIDE), F32)], 0
        )
        pixel = pixel + field / 256.0
        for block in range(blocks):
            pieces.append(pixel[:, block * 256 : (block + 1) * 256])
    stacked = jnp.concatenate(pieces, 0)
    source = iota((256, 256), 0)
    target = iota((256, 256), 1)
    row = lax.shift_right_logical(source, 5)
    column = source & 31
    place = (
        ((row & 1) * 2 + (column & 1)) * 64
        + lax.shift_right_logical(row, 1) * 16
        + lax.shift_right_logical(column, 1)
    )
    moved = move_lanes(stacked, (place == target).astype(F32).astype(BF16))
    quarters = []
    for k in range(4):
        quarters.append(
            jnp.concatenate(
                [
                    moved[piece * 8 : (piece + 1) * 8, k * 64 : (k + 1) * 64]
                    for piece in range(images * blocks)
                ],
                1,
            )
        )
    state = exact_dot(order_chooser(3, 8), jnp.concatenate(quarters, 0))
    for level in range(LEVELS):
        channels = chan(level)
        grid = side(level)
        count = positions(level, images)
        offsets = flow_offsets(level)
        block = flow_block(flat, offsets["block"], channels, channels)
        names = column_names(level)
        columns = [flow_column(turned, offset, channels) for _, offset in names]
        lane = iota((channels, LANE), 1)
        held = jnp.zeros((channels, LANE), F32)
        for index, column in enumerate(columns):
            held = jnp.where(lane == index, column, held)
        growth = jnp.exp(columns[1])
        normed = (state + columns[0]) * growth
        lower, upper, reverse, _ = triangles(block)
        mixing = exact_dot(exact_dot(reverse, lower), upper)
        mixed = exact_dot(mixing, normed)
        lane = iota((8, count), 1)
        shift = grid.bit_length() - 1
        image = lax.shift_right_logical(lane, 2 * shift)
        row = lax.shift_right_logical(lane, shift) & (grid - 1)
        column = lane & (grid - 1)
        high = jnp.zeros((8, count), jnp.int32)
        wide = jnp.zeros((8, count), jnp.int32)
        for index in range(images):
            high = jnp.where(image == index, valid_ref[index, 0], high)
            wide = jnp.where(image == index, valid_ref[index, 1], wide)
        unit = 2 ** (level + 1)
        row_share = jnp.clip(high - row * unit, 0, unit).astype(F32) / unit
        column_share = jnp.clip(wide - column * unit, 0, unit).astype(F32) / unit
        share = jnp.where(image < images, row_share * column_share, 0.0)
        out_ref = out_refs[level]
        starts = stage_rows(level)
        out_ref[starts["normed"] : starts["normed"] + channels, :] = normed
        out_ref[starts["mixed"] : starts["mixed"] + channels, :] = mixed
        out_ref[starts["share"] : starts["share"] + 8, :] = share
        out_ref[starts["held"] : starts["held"] + channels, 0:LANE] = held
        out_ref[starts["block"] : starts["block"] + channels, 0:channels] = block
        out_ref[starts["mixing"] : starts["mixing"] + channels, 0:channels] = mixing
        if level > 0:
            order = order_chooser(channels // 4, channels // 4)
            out_ref[starts["turn"] : starts["turn"] + channels, 0:channels] = exact_dot(
                mixing, growth * order
            )
        if level < LEVELS - 1:
            out_ref[starts["prior"] : starts["prior"] + channels // 2, 0:channels] = flow_block(
                flat, offsets["priormatrix"], channels // 2, channels
            )
            state = squeeze(
                mixed[: channels // 2], squeeze_chooser(grid, images), positions(level + 1, images)
            )


def silu_parts(values):
    sigmoid = 1.0 / (1.0 + jnp.exp(-values))
    active = values * sigmoid
    slope = sigmoid + active * (1.0 - sigmoid)
    return active, slope


def net_kernel(level, images, narrow, *refs):
    is_last = level == LEVELS - 1
    index_ref = refs[0]
    weight_refs, tails = refs[1 : 1 + narrow], [None] * narrow
    if isinstance(weight_refs[-1], tuple):
        weight_refs, tails[-1] = (*weight_refs[:-1], weight_refs[-1][0]), weight_refs[-1][1]
    bases = [
        pack_start(level) if ref.shape[0] > pack_start(-1) else gather_start(level)
        for ref in weight_refs
    ]
    out_base = chunk_of(level)[1]
    stage_ref, keep_ref, send_ref, result_ref = refs[1 + narrow : 5 + narrow]
    order_ref, slope_one_ref, slope_two_ref, one_ref, two_ref = refs[5 + narrow :]
    starts = stage_rows(level)
    me = index_ref[0, 0]
    channels = chan(level)
    half = channels // 2
    count = positions(level, images)
    top, rows = first_rows(level), in_rows(level)
    tail, used = last_rows(level), 9 * channels
    bias_block = second_bias_row(level) - 12
    masks = tap_masks(level, images)
    width = HID // narrow

    def weights(start, length):
        parts = []
        for ref, base, tail in zip(weight_refs, bases, tails):
            first = base + start
            if tail is not None and first >= ref.shape[0]:
                ref, first = tail, first - ref.shape[0]
            parts.append(ref[first : first + length, :])
        return jnp.concatenate(parts, 1)

    for r_in in range(narrow):
        for r_out in range(narrow):
            start = pl.multiple_of(bases[r_out] + top + (me ^ r_in) * width, 16)
            order_ref[r_in * width : (r_in + 1) * width, r_out * LANE : (r_out + 1) * LANE] = (
                weight_refs[r_out][pl.ds(start, width), :]
            )
    weight_in = weights(0, top)
    weight_mix = order_ref[...]
    weight_out = weights(top + HID, tail)
    mixed = starts["mixed"]
    first = stage_ref[mixed : mixed + half, :]
    second = stage_ref[mixed + half : mixed + channels, :]
    share = stage_ref[starts["share"] : starts["share"] + 1, :]
    pieces = tap_stack(rounded(first), masks, level, 1)
    pieces.append(jnp.ones((3, count), F32))
    pieces.append(jnp.zeros((top - rows - 3, count), F32))
    stacked = jnp.concatenate(pieces, 0).astype(BF16)
    pick = jnp.where(
        (iota((16, count), 0) >= 12) & (iota((16, count), 0) < 15), 1.0, 0.0
    ).astype(BF16)
    hidden_one = contract_rows(weight_in, stacked)
    active, slope = silu_parts(hidden_one)
    slope_one_ref[...] = slope
    one_ref[...] = active.astype(BF16)
    hidden_two = contract_rows(weight_mix, one_ref[...]) + contract_rows(
        weights(bias_block, 16), pick
    )
    active, slope = silu_parts(hidden_two)
    slope_two_ref[...] = slope
    two_ref[...] = active.astype(BF16)
    spread = plain_dot(weight_out, two_ref[...])
    net_raw = tap_sum(spread, masks, level, 1, channels)
    held = stage_ref[starts["held"] : starts["held"] + channels, 0:LANE]
    out_bias, out_scale = held[:, 2:3], held[:, 3:4]
    growth = jnp.exp(3.0 * out_scale)
    output = (net_raw + out_bias) * growth
    logit = output[half:] + 2.0
    sigmoid = 1.0 / (1.0 + jnp.exp(-logit))
    latent = (second + output[:half]) * sigmoid
    log_sigmoid = jnp.minimum(logit, 0.0) - jnp.log1p(jnp.exp(-jnp.abs(logit)))
    if is_last:
        joined = jnp.concatenate([first, latent], 0)
        mean, scale = held[:, 4:5], held[:, 5:6]
        mean = jnp.broadcast_to(mean, joined.shape)
        scale = jnp.broadcast_to(scale, joined.shape)
    else:
        joined = latent
        prior = stage_ref[starts["prior"] : starts["prior"] + half, 0:channels]
        stats = exact_rows(prior, first) + held[:, 4:5]
        mean, scale = stats[:half], stats[half:]
    gap = joined - mean
    shrink = jnp.exp(-2.0 * scale)
    square = gap * gap * shrink
    log_prior = -0.5 * (LOG_TWO_PI + 2.0 * scale + square)
    total = jnp.sum(jnp.sum(share * log_sigmoid, 0, keepdims=True), 1, keepdims=True) + jnp.sum(
        jnp.sum(share * log_prior, 0, keepdims=True), 1, keepdims=True
    )
    share_total = jnp.sum(share, 1, keepdims=True)
    grad_joined = share * (gap * shrink)
    grad_scale = share * (1.0 - square)
    grad_latent = grad_joined[half:] if is_last else grad_joined
    grad_logit = (grad_latent * latent - share) * (1.0 - sigmoid)
    grad_second = grad_latent * sigmoid
    grad_output = jnp.concatenate([grad_second, grad_logit], 0)
    grad_net = grad_output * growth
    lane = iota((channels, LANE), 1)
    small = jnp.zeros((channels, LANE), F32)

    def put(small, index, values):
        return jnp.where(lane == index, jnp.sum(values, 1, keepdims=True), small)

    small = put(small, 2, grad_net)
    small = put(small, 3, 3.0 * grad_output * output)
    if is_last:
        small = put(small, 4, -grad_joined)
        small = put(small, 5, grad_scale)
        grad_first = grad_joined[:half]
    else:
        grad_stats = jnp.concatenate([-grad_joined, grad_scale], 0)
        small = put(small, 4, grad_stats)
        grad_first = exact_dot(prior, grad_stats)
        prior_grad = exact_columns(first, grad_stats)
        start = starts["prior_grad"]
        result_ref[start : start + half, 0:channels] = prior_grad
    small = jnp.where(lane == 6, -total, small)
    small = jnp.where(lane == 7, share_total, small)
    result_ref[starts["small"] : starts["small"] + channels, 0:LANE] = small
    pieces = tap_stack(rounded(grad_net), masks, level, -1)
    if tail > used:
        pieces.append(jnp.zeros((tail - used, count), F32))
    grad_spread = jnp.concatenate(pieces, 0).astype(BF16)

    def store(start, values):
        for r in range(narrow):
            ref = send_ref if r & 1 else keep_ref
            rows = slice(out_base + start, out_base + start + values.shape[0])
            ref[r // 2, rows, :] = values[:, r * LANE : (r + 1) * LANE]

    grad_out = contract_columns(grad_spread, two_ref[...])
    grad_two = (contract_rows(weight_out, grad_spread) * slope_two_ref[...]).astype(BF16)
    grad_mix = contract_columns(one_ref[...], grad_two)
    for r_in in range(narrow):
        start = pl.multiple_of(out_base + top + (me ^ r_in) * width, 16)
        for r_out in range(narrow):
            ref = send_ref if r_out & 1 else keep_ref
            ref[r_out // 2, pl.ds(start, width), :] = grad_mix[
                r_in * width : (r_in + 1) * width, r_out * LANE : (r_out + 1) * LANE
            ]
    grad_one = (plain_dot(weight_mix, grad_two) * slope_one_ref[...]).astype(BF16)
    grad_in = contract_columns(stacked, grad_one)
    grad_bias = contract_columns(pick, grad_two)
    if bias_in_tail(level):
        grad_out = jnp.concatenate([grad_out[: tail - 16], grad_out[tail - 16 :] + grad_bias], 0)
    else:
        grad_in = jnp.concatenate([grad_in[: top - 16], grad_in[top - 16 :] + grad_bias], 0)
    store(0, grad_in)
    store(top + HID, grad_out)
    grad_stack = plain_dot(weight_in, grad_one)
    grad_first = grad_first + tap_sum(grad_stack, masks, level, -1, half)
    result_ref[0:half, :] = grad_first
    result_ref[half:channels, :] = grad_second


def stage_part(level, ref, name, rows, lanes):
    start = stage_rows(level)[name]
    return ref[start : start + rows, 0:lanes]


def flow_chain(images, stages, results):
    grads = [None] * LEVELS
    carried = None
    for level in (2, 1, 0):
        channels = chan(level)
        count = positions(level, images)
        grad = stage_part(level, results[level], "grad", channels, count)
        if carried is not None:
            grad = grad + jnp.concatenate([carried, jnp.zeros_like(carried)], 0)
        grads[level] = grad
        if level > 0:
            turn = stage_part(level, stages[level], "turn", channels, channels)
            grid = side(level - 1)
            carried = unsqueeze(
                exact_rows(turn, grad), squeeze_chooser(grid, images), images * grid * grid
            )
    return grads


def flow_level(level, images, stage_ref, result_ref, grad):
    channels = chan(level)
    half = channels // 2
    count = positions(level, images)
    offsets = flow_offsets(level)
    normed = stage_part(level, stage_ref, "normed", channels, count)
    held = stage_part(level, stage_ref, "held", channels, LANE)
    block = stage_part(level, stage_ref, "block", channels, channels)
    mixing = stage_part(level, stage_ref, "mixing", channels, channels)
    small = stage_part(level, result_ref, "small", channels, LANE)
    lower, upper, reverse, diagonal = triangles(block)
    grad_normed = exact_rows(mixing, grad)
    grad_mixing = exact_dot(reverse, exact_columns(grad, normed))
    grad_lower = exact_columns(grad_mixing, upper)
    grad_upper = exact_rows(lower, grad_mixing)
    share_total = small[0:1, 7:8]
    row = iota((channels, channels), 0)
    column = iota((channels, channels), 1)
    grad_block = jnp.where(
        row > column,
        grad_lower,
        jnp.where(row < column, grad_upper, grad_upper * diagonal - share_total),
    )
    growth = jnp.exp(held[:, 1:2])
    grad_bias = jnp.sum(grad_normed, 1, keepdims=True) * growth
    grad_logs = jnp.sum(grad_normed * normed, 1, keepdims=True) - share_total
    flat = flow_block_back(grad_block, offsets["block"], channels, channels)
    turned = jnp.zeros((LANE, LANE), F32)
    for index, (name, offset) in enumerate(column_names(level)):
        if name == "bias":
            values = grad_bias
        elif name == "logs":
            values = grad_logs
        else:
            values = small[:, index : index + 1]
        turned = turned + flow_column_back(values, offset)
    if level < LEVELS - 1:
        flat = flat + flow_block_back(
            stage_part(level, result_ref, "prior_grad", half, channels),
            offsets["priormatrix"],
            half,
            channels,
        )
    logs_total = jnp.sum(held[:, 1:2], 0, keepdims=True)
    trace = jnp.sum(
        jnp.sum(jnp.where(row == column, block, 0.0), 0, keepdims=True), 1, keepdims=True
    )
    return flat, turned, small[0:1, 6:7] - share_total * (logs_total + trace)


def flow_back(images, stages, results, weights, out_ref):
    grads = flow_chain(images, stages, results)
    parts = [
        flow_level(level, images, stages[level], results[level], grads[level])
        for level in range(LEVELS)
    ]
    flat = sum(part[0] for part in parts) + sum(part[1] for part in parts).T[:FLOW_ROWS]
    loss = sum(part[2] for part in parts)
    pixels = jnp.zeros((1, 1), F32)
    for ref in weights:
        start = ref.shape[0] - 16
        digits = ref[start : start + 16, :].astype(F32)
        for place in range(3):
            pixels = pixels + 128.0**place * digits[0:1, place : place + 1]
    lane = iota((STATS_ROWS, LANE), 1)
    out_ref[0:FLOW_ROWS, :] = flat
    out_ref[FLOW_ROWS:, :] = jnp.where(lane == 0, loss, jnp.where(lane == 1, pixels, 0.0))


def zero_rows(refs, start):
    for ref in refs:
        rest = ref.shape[1] - start
        if rest:
            ref[:, start:, :] = jnp.zeros((ref.shape[0], rest, LANE), F32)


def nets_kernel(chunk, images, narrow, split, *refs):
    levels = CHUNKS[chunk]
    number = len(levels)
    index_ref = refs[0]
    mine = refs[1 : 1 + narrow]
    at = 1 + narrow
    if split:
        mine = (*mine[:-1], (mine[-1], refs[at]))
        at = at + 1
    stages = refs[at : at + number]
    at = at + number
    keep_ref, send_ref = refs[at : at + 2]
    results = refs[at + 2 : at + 2 + number]
    at = at + 2 + number
    for place, level in enumerate(levels):
        net_kernel(
            level,
            images,
            narrow,
            index_ref,
            *mine,
            stages[place],
            keep_ref,
            send_ref,
            results[place],
            *refs[at + 5 * place : at + 5 * place + 5],
        )
    zero_rows((keep_ref, send_ref), sum(pack_rows(level) for level in levels))


def flow_kernel(images, narrow, *refs):
    stages, results = refs[:LEVELS], refs[LEVELS : 2 * LEVELS]
    weights, out_ref = refs[2 * LEVELS : -1], refs[-1]
    flow_back(images, stages, results, weights, out_ref)


def copy_kernel(*refs):
    half = len(refs) // 2
    for from_ref, to_ref in zip(refs[:half], refs[half:]):
        to_ref[...] = from_ref[...]


def split_copy_kernel(from_ref, *refs):
    half = len(refs) // 2 - 1
    cut = refs[half].shape[0]
    refs[half][...] = from_ref[0:cut, :]
    refs[half + 1][...] = from_ref[cut:, :]
    for source, target in zip(refs[:half], refs[half + 2 :]):
        target[...] = source[...]


def piece_rows(rows):
    return rows + round_up(rows // CODE_BLOCK, 16)


def write_piece(ref, start, values, extra=None):
    rows = values.shape[0]
    blocks = values.reshape(rows // CODE_BLOCK, CODE_BLOCK, LANE)
    scale = rounded(jnp.max(jnp.abs(blocks), axis=1) * 1.01)
    factor = jnp.where(scale > 0.0, CODE_RANGE / scale, 0.0)
    code = jnp.exp(blocks * factor[:, None, :])
    ref[start : start + rows, :] = code.reshape(rows, LANE).astype(BF16)
    tail = [scale] + ([] if extra is None else split_three(extra))
    used = sum(part.shape[0] for part in tail)
    size = round_up(rows // CODE_BLOCK, 16)
    if size > used:
        tail.append(jnp.zeros((size - used, LANE), F32))
    ref[start + rows : start + rows + size, :] = jnp.concatenate(tail, 0).astype(BF16)


def read_piece(ref, start, rows):
    blocks = jnp.log(ref[start : start + rows, :].astype(F32))
    blocks = blocks.reshape(rows // CODE_BLOCK, CODE_BLOCK, LANE)
    scale = ref[start + rows : start + piece_rows(rows), :].astype(F32)
    factor = scale[: rows // CODE_BLOCK] * (1.0 / CODE_RANGE)
    return (blocks * factor[:, None, :]).reshape(rows, LANE)


def read_stats(ref, start, rows):
    first = start + rows + rows // CODE_BLOCK
    tail = ref[first : first + 3, :].astype(F32)
    return tail[0:1] + tail[1:2] + tail[2:3]


def wide_bit(index_ref, bit):
    return jnp.where((index_ref[1, 0] & bit) != 0, 1, 0)


def send_kernel(chunk, index_ref, send_ref, *piece_refs):
    half = 2 * quarter_rows(chunk)
    for shard in range(2):
        for place in range(2):
            values = send_ref[shard, place * half : (place + 1) * half, :]
            write_piece(piece_refs[2 * shard + place], 0, values)


def square_kernel(chunk, index_ref, keep_ref, *refs):
    other_refs, total_ref, refs = refs[:4], refs[-1], refs[4:-1]
    flow = None
    if flow_part(chunk):
        flow_ref, mine_ref, own_flow_ref, *sent_refs = refs
        flow = flow_ref[0:FLOW_ROWS, :]
        stats = flow_ref[FLOW_ROWS : FLOW_ROWS + 1, :]
        write_piece(own_flow_ref, 0, flow, stats)
    else:
        mine_ref, *sent_refs = refs
    half = 2 * quarter_rows(chunk)
    upper = wide_bit(index_ref, 1)
    for shard in range(2):
        for place in range(2):
            picked = slice(place * half, (place + 1) * half)
            total_ref[shard, picked, :] = keep_ref[shard, picked, :] + read_piece(
                other_refs[2 * shard + place], 0, half
            )

    def total(shard, flipped):
        place = 1 - upper if flipped else upper
        return total_ref[shard, pl.ds(pl.multiple_of(place * half, CODE_BLOCK), half), :]

    mine_ref[...] = total(0, 0)
    for ref, (shard, flipped) in zip(sent_refs, ((1, 0), (0, 1), (1, 1))):
        values = total(shard, flipped)
        if flow is None:
            write_piece(ref, 0, values)
        else:
            write_piece(ref, 0, jnp.concatenate([values, flow], 0), stats)


def column_kernel(chunk, index_ref, mine_ref, *refs):
    rows = 2 * quarter_rows(chunk)
    more = flow_part(chunk)
    if more:
        own_flow_ref, *others, keep_ref, own_next_ref, sent_ref, total_ref = refs
    else:
        *others, keep_ref, sent_ref, total_ref = refs
    total = mine_ref[...]
    for flip, other in zip(SQUARE_ORDER[chunk], others):
        values = read_piece(other, 0, rows + more)
        total = total + values[:rows]
        if more and flip == 2:
            flow = read_piece(own_flow_ref, 0, FLOW_ROWS) + values[rows:]
            stats = read_stats(own_flow_ref, 0, FLOW_ROWS) + read_stats(other, 0, rows + more)
    total_ref[...] = total
    half = rows // 2
    place = wide_bit(index_ref, 2)
    keep_ref[...] = total_ref[pl.ds(pl.multiple_of(place * half, CODE_BLOCK), half), :]
    values = total_ref[pl.ds(pl.multiple_of((1 - place) * half, CODE_BLOCK), half), :]
    if more:
        write_piece(own_next_ref, 0, flow, stats)
        write_piece(sent_ref, 0, jnp.concatenate([values, flow], 0), stats)
    else:
        write_piece(sent_ref, 0, values)


def code_kernel(chunk, index_ref, mine_ref, *refs):
    rows = quarter_rows(chunk)
    more = flow_part(chunk)
    if more:
        own_flow_ref, other_ref, out_ref = refs
    else:
        other_ref, out_ref = refs
    values = read_piece(other_ref, 0, rows + more)
    total = mine_ref[...] + values[:rows]
    if more:
        flow = read_piece(own_flow_ref, 0, FLOW_ROWS) + values[rows:]
        stats = read_stats(own_flow_ref, 0, FLOW_ROWS) + read_stats(other_ref, 0, rows + more)
        write_piece(out_ref, 0, jnp.concatenate([total, flow], 0), stats)
    else:
        write_piece(out_ref, 0, total)


def recode_kernel(chunk, index_ref, mine_ref, other_ref, out_ref):
    rows = quarter_rows(chunk) + flow_part(chunk)
    stats = None
    if flow_part(chunk):
        stats = read_stats(mine_ref, 0, rows) + read_stats(other_ref, 0, rows)
    write_piece(out_ref, 0, read_piece(mine_ref, 0, rows) + read_piece(other_ref, 0, rows), stats)


def pair_kernel(chunk, index_ref, mine_ref, other_ref, out_ref):
    place = wide_bit(index_ref, 2)
    out_ref[place] = mine_ref[...]
    out_ref[1 - place] = other_ref[...]


def decode_pairs_kernel(chunk, index_ref, mine_ref, other_ref, out_ref):
    rows = quarter_rows(chunk)
    upper = wide_bit(index_ref, 1)
    for place, ref in ((upper, mine_ref), (1 - upper, other_ref)):
        for near in range(2):
            start = pl.multiple_of((2 * place + near) * rows, CODE_BLOCK)
            out_ref[pl.ds(start, rows), :] = read_piece(ref.at[near], 0, rows)


def decode_kernel(chunk, index_ref, *refs):
    parts, outs = refs[:4], refs[4:]
    place = 2 * wide_bit(index_ref, 1) + wide_bit(index_ref, 2)
    rows, more = quarter_rows(chunk), flow_part(chunk)
    for flip, ref in zip((0, *RETURN_ORDER), parts):
        values = read_piece(ref, 0, rows + more)
        start = pl.multiple_of((place ^ flip) * rows, CODE_BLOCK)
        outs[0][pl.ds(start, rows), :] = values[:rows]
        if more and flip == 0:
            outs[1][0:FLOW_ROWS, :] = values[rows:]
            outs[1][FLOW_ROWS:, :] = jnp.broadcast_to(
                read_stats(ref, 0, rows + more), (STATS_ROWS, LANE)
            )


def moments(weight, gradient, first_old, second_old):
    first_new = FIRST_BETA * first_old + (1.0 - FIRST_BETA) * gradient
    second_new = SECOND_BETA * second_old + (1.0 - SECOND_BETA) * gradient * gradient
    update = (
        first_new
        * (1.0 / (1.0 - FIRST_BETA**STEP))
        / (jnp.sqrt(second_new * (1.0 / (1.0 - SECOND_BETA**STEP))) + EPSILON)
        + WEIGHT_DECAY * weight
    )
    return first_new, second_new, update


def total_of(values):
    return jnp.sum(jnp.sum(values, 0, keepdims=True), 1, keepdims=True)


def squares_rows(sums):
    row = iota((16, LANE), 0)
    held = jnp.zeros((16, LANE), F32)
    for index, value in sums:
        held = jnp.where(row == index, value, held)
    return held


def chunk_spans(chunk):
    levels = CHUNKS[chunk]
    base = min(levels)
    spans = []
    for size in (in_rows, lambda level: 9 * chan(level), lambda level: 1, lambda level: 2):
        start = sum(size(level) for level in range(base))
        spans.append((start, start + sum(size(level) for level in levels)))
    return spans


def level_totals(chunk, values, size):
    row = iota(values.shape, 0)
    totals = []
    start = 0
    for level in sorted(CHUNKS[chunk]):
        stop = start + size(level)
        inside = values
        if stop - start < values.shape[0]:
            inside = jnp.where((row >= start) & (row < stop), values, 0.0)
        totals.append(total_of(inside))
        start = stop
    return totals


def group_totals(chunk, values_in, values_mix, values_out, values_bias):
    levels = sorted(CHUNKS[chunk])
    sums = (
        (0, level_totals(chunk, values_in, in_rows)),
        (3, [total_of(values) for values in values_mix]),
        (6, level_totals(chunk, values_out, lambda level: 9 * chan(level))),
        (9, level_totals(chunk, values_bias, lambda level: 2)),
    )
    return [(base + level, total) for base, totals in sums for level, total in zip(levels, totals)]


def flow_masks():
    place = iota((FLOW_ROWS, LANE), 0) * LANE + iota((FLOW_ROWS, LANE), 1)
    masks = []
    start = 0
    for length in flow_lengths():
        masks.append((place >= start) & (place < start + length))
        start = start + length
    return masks


def split_grads(chunk, ref, scale):
    ins, mixes, outs, biases = [], [], [], []
    for level in sorted(CHUNKS[chunk]):
        start = chunk_of(level)[1]

        def rows(first, count):
            return ref[start + first : start + first + count, :] * scale

        top = first_rows(level)
        ins.append(rows(0, in_rows(level)))
        mixes.append(rows(top, HID))
        outs.append(rows(top + HID, 9 * chan(level)))
        biases.append(rows(in_rows(level), 1))
        biases.append(rows(second_bias_row(level), 1))
    join = lambda parts: parts[0] if len(parts) == 1 else jnp.concatenate(parts, 0)
    return join(ins), mixes, join(outs), join(biases)


def norm_kernel(chunk, *refs):
    last = chunk == len(CHUNKS) - 1
    part_ref, flow_ref, refs = refs[0], refs[1], refs[2:]
    if last:
        sums_ref, refs = refs[0], refs[1:]
        stats = flow_ref[FLOW_ROWS : FLOW_ROWS + 1, :]
    else:
        stats = read_stats(flow_ref, 0, quarter_rows(1) + flow_part(1))
    weights, firsts, seconds = refs[0:4], refs[4:8], refs[8:12]
    grads, updates, block_ref = refs[12:16], refs[16:20], refs[20]
    scale = 1.0 / (3.0 * stats[:, 1:2] * LOG_TWO)
    grad_in, grad_mix, grad_out, grad_bias = split_grads(chunk, part_ref, scale)
    in_span, out_span, mix_span, bias_span = chunk_spans(chunk)
    weight_squares = [None] * 4
    update_squares = [None] * 4
    for place, span, gradient in ((0, in_span, grad_in), (2, out_span, grad_out)):
        picked = slice(*span)
        weight = weights[place][picked, :]
        update = moments(weight, gradient, firsts[place][picked, :], seconds[place][picked, :])[2]
        grads[place][...] = gradient
        updates[place][...] = update
        weight_squares[place] = weight * weight
        update_squares[place] = update * update
    old = [ref[...].reshape(2 * LEVELS, LANE)[slice(*bias_span)] for ref in (weights[3], firsts[3], seconds[3])]
    update = moments(old[0], grad_bias, old[1], old[2])[2]
    grads[3][...] = grad_bias
    updates[3][...] = update
    weight_squares[3], update_squares[3] = old[0] * old[0], update * update
    weight_squares[1], update_squares[1] = [], []
    for place, level in enumerate(range(*mix_span)):
        weight = weights[1][level]
        grads[1][place] = grad_mix[place]
        update = moments(weight, grad_mix[place], firsts[1][level], seconds[1][level])[2]
        updates[1][place] = update
        weight_squares[1].append(weight * weight)
        update_squares[1].append(update * update)
    lane = iota((16, LANE), 1)
    sums = jnp.where(
        lane == 0,
        squares_rows(group_totals(chunk, *weight_squares)),
        squares_rows(group_totals(chunk, *update_squares)),
    )
    if last:
        block_ref[0:16, :] = sums + sums_ref[...]
        block_ref[16:, :] = flow_ref[...]
    else:
        block_ref[...] = sums


def join_chunks(first, last):
    return jnp.concatenate([last[...], first[...]], 0)


def moment_kernel(*refs):
    one, two, firsts, seconds = refs[0:4], refs[4:8], refs[8:12], refs[12:16]
    new_firsts, new_seconds = refs[16:20], refs[20:24]
    refs[24][...] = jnp.zeros((8, LANE), F32)
    for place in range(4):
        gradient = join_chunks(one[place], two[place]).reshape(firsts[place].shape)
        new_firsts[place][...] = FIRST_BETA * firsts[place][...] + (1.0 - FIRST_BETA) * gradient
        new_seconds[place][...] = (
            SECOND_BETA * seconds[place][...] + (1.0 - SECOND_BETA) * gradient * gradient
        )


def apply_kernel(narrow, *refs):
    index_ref = refs[0]
    block_refs = refs[1 : 1 + narrow]
    at = 1 + narrow
    weight_in, weight_mix, weight_out, weight_bias = refs[at : at + 4]
    one, two = refs[at + 4 : at + 8], refs[at + 8 : at + 12]
    flow_ref, flow_first_ref, flow_second_ref = refs[at + 12 : at + 15]
    at = at + 15
    update_in, update_out = join_chunks(one[0], two[0]), join_chunks(one[2], two[2])
    update_bias = join_chunks(one[3], two[3]).reshape(LEVELS, 2, LANE)
    update_mix = [two[1].at[0], two[1].at[1], one[1].at[0]]
    (
        new_in,
        new_mix,
        new_out,
        new_bias,
        new_flow,
        half_in,
        half_mix,
        half_out,
        flow_moment,
        flow_square,
        weight_norm_ref,
        update_norm_ref,
        loss_ref,
        valid_ref,
        order_ref,
    ) = refs[at:]
    for part in range(narrow):
        order_ref[index_ref[0, 0] ^ part] = block_refs[part][...]
    whole = order_ref[0]
    for part in range(1, narrow):
        whole = whole + order_ref[part]
    sums = whole[0:16]
    flow_grad = whole[16 : 16 + FLOW_ROWS]
    loss = whole[16 + FLOW_ROWS : 17 + FLOW_ROWS, 0:1]
    valid_dims = 3.0 * block_refs[0][16 + FLOW_ROWS : 17 + FLOW_ROWS, 1:2]
    scale = 1.0 / (valid_dims * LOG_TWO)
    flow = to_flat_rows(flow_ref[...])
    size = flow_ref.shape[0]
    place = iota((FLOW_ROWS, LANE), 0) * LANE + iota((FLOW_ROWS, LANE), 1)
    flow_grad = jnp.where(place < size, flow_grad * scale, 0.0)
    first_new, second_new, update = moments(
        flow, flow_grad, to_flat_rows(flow_first_ref[...]), to_flat_rows(flow_second_ref[...])
    )
    weight_norms = [jnp.sqrt(sums[index : index + 1, 0:1]) for index in range(12)]
    update_norms = [jnp.sqrt(sums[index : index + 1, 1:2]) for index in range(12)]
    masks = flow_masks()
    for mask in masks:
        weight_norms.append(jnp.sqrt(total_of(jnp.where(mask, flow * flow, 0.0))))
        update_norms.append(jnp.sqrt(total_of(jnp.where(mask, update * update, 0.0))))
    rates = [
        LEARN_RATE * (weight_norm / update_norm)
        for weight_norm, update_norm in zip(weight_norms, update_norms)
    ]
    rate = jnp.zeros((FLOW_ROWS, LANE), F32)
    for mask, value in zip(masks, rates[12:]):
        rate = jnp.where(mask, value, rate)
    new_flow[...] = from_flat_rows(flow - rate * update, size)
    flow_moment[...] = from_flat_rows(first_new, size)
    flow_square[...] = from_flat_rows(second_new, size)
    row = iota(weight_in.shape, 0)
    edge_one, edge_two = in_rows(0), in_rows(0) + in_rows(1)
    rate = jnp.where(row < edge_one, rates[0], jnp.where(row < edge_two, rates[1], rates[2]))
    fresh = weight_in[...] - rate * update_in
    new_in[...] = fresh
    half_in[...] = fresh.astype(BF16)
    for level in range(LEVELS):
        fresh = weight_mix[level] - rates[3 + level] * update_mix[level][...]
        new_mix[level] = fresh
        half_mix[level] = fresh.astype(BF16)
    row = iota(weight_out.shape, 0)
    edge_one, edge_two = 9 * chan(0), 9 * chan(0) + 9 * chan(1)
    rate = jnp.where(row < edge_one, rates[6], jnp.where(row < edge_two, rates[7], rates[8]))
    fresh = weight_out[...] - rate * update_out
    new_out[...] = fresh
    half_out[...] = fresh.astype(BF16)
    for level in range(LEVELS):
        new_bias[level] = weight_bias[level] - rates[9 + level] * update_bias[level]
    lane = iota((1, LANE), 1)
    for ref, norms in ((weight_norm_ref, weight_norms), (update_norm_ref, update_norms)):
        held = jnp.zeros((1, LANE), F32)
        for index in range(15):
            held = jnp.where(lane == index, norms[index], held)
        ref[...] = held[:, :15].reshape(15)
    loss_ref[...] = loss / LOG_TWO + 8.0 * valid_dims
    valid_ref[...] = valid_dims


def spec_vmem():
    return pl.BlockSpec(memory_space=pltpu.VMEM)


def spec_smem():
    return pl.BlockSpec(memory_space=pltpu.SMEM)


def call(kernel, outs, scalars, arrays, scratch=(), name=None, after=(), vmem=20):
    number = len(scalars) + len(arrays)

    def run(*refs):
        kernel(*refs[:number], *refs[number + len(after) :])

    return pl.pallas_call(
        run,
        out_shape=tuple(jax.ShapeDtypeStruct(shape, dtype) for shape, dtype in outs),
        in_specs=[spec_smem()] * len(scalars)
        + [spec_vmem()] * len(arrays)
        + [pl.BlockSpec(memory_space=pl.ANY)] * len(after),
        out_specs=tuple(spec_vmem() for _ in outs),
        scratch_shapes=list(scratch),
        compiler_params=pltpu.CompilerParams(vmem_limit_bytes=vmem * 1024 * 1024),
        cost_estimate=pl.CostEstimate(
            flops=1000, bytes_accessed=1000, transcendentals=0
        ),
        name=name,
    )(*scalars, *arrays, *after)


def run_pack(valid_shape, conv_in, mixer, conv_out, hidden_bias):
    cut = sum(pack_rows(level) for level in CHUNKS[0])
    rows = pack_start(-1) + 16
    outs = [((size, LANE), BF16) for size in (rows, cut, rows - cut)]
    return call(pack_kernel, outs, (valid_shape,), (conv_in, mixer, conv_out, hidden_bias), name="pack", vmem=56)


def run_flow_pre(noise_seeds, valid_shape, images, flow_params, packed):
    count = images.shape[1]
    outs = [((stage_rows(level)["rows"], positions(level, count)), F32) for level in range(LEVELS)]
    outs.append((packed.shape, BF16))
    return call(
        flow_pre_kernel,
        outs,
        (noise_seeds, valid_shape),
        (images, flow_params, packed),
        name="flow_pre",
    )


def run_nets(chunk, images, index, weights, stages, after):
    narrow = lax.axis_size("narrow")
    outs = [((narrow // 2, 4 * quarter_rows(chunk), LANE), F32)] * 2
    scratch = []
    for level in CHUNKS[chunk]:
        count = positions(level, images)
        outs = outs + [((stage_rows(level)["result_rows"], count), F32)]
        scratch = scratch + net_scratch(count)
    return call(
        functools.partial(nets_kernel, chunk, images, narrow, len(weights) > narrow),
        outs,
        (),
        [index] + list(weights) + [stages[level] for level in CHUNKS[chunk]],
        scratch,
        name="nets_" + "ab"[chunk],
        after=after,
    )


def net_scratch(count):
    return [
        pltpu.VMEM((HID, HID), BF16),
        pltpu.VMEM((HID, count), F32),
        pltpu.VMEM((HID, count), F32),
        pltpu.VMEM((HID, count), BF16),
        pltpu.VMEM((HID, count), BF16),
    ]


def run_flow(images, weights, stages, results, after):
    (out,) = call(
        functools.partial(flow_kernel, images, len(weights)),
        [((FLOW_ROWS + STATS_ROWS, LANE), F32)],
        (),
        list(stages) + list(results) + list(weights),
        name="flow_back",
        after=after,
    )
    return out


def swap(values, wide, narrow):
    width = lax.axis_size("narrow")
    mask = wide * width + narrow
    count = lax.axis_size("wide") * width
    return lax.ppermute(values, ("wide", "narrow"), [(place, place ^ mask) for place in range(count)])


class Summation:
    def __init__(self, chunk, index, send, after):
        self.chunk, self.index = chunk, index
        rows, more = quarter_rows(chunk), flow_part(chunk)
        self.kept, self.others = send, ()
        sent = self.run(send_kernel, [((piece_rows(2 * rows), LANE), BF16)] * 4, "send", after)
        self.token = sent[0]
        self.others = [swap(piece, 0, 1) for piece in sent]
        self.own_piece = [((piece_rows(FLOW_ROWS), LANE), BF16)] if more else []
        self.own = ()
        self.square_piece = ((piece_rows(2 * rows + more), LANE), BF16)
        self.piece = ((piece_rows(rows + more), LANE), BF16)

    def run(self, kernel, outs, name, after, scratch=(), extra=()):
        return call(
            functools.partial(kernel, self.chunk),
            outs,
            (),
            (self.index, self.kept, *extra, *self.others),
            scratch,
            name=name + "_" + "ab"[self.chunk],
            after=after,
        )

    def square(self, keep, flow, after):
        rows = 2 * quarter_rows(self.chunk)
        self.kept, *rest = call(
            functools.partial(square_kernel, self.chunk),
            [((rows, LANE), F32)] + self.own_piece + [self.square_piece] * 3,
            (),
            (self.index, keep, *self.others, *flow),
            [pltpu.VMEM((2, 2 * rows, LANE), F32)],
            name="square_" + "ab"[self.chunk],
            after=after,
        )
        self.own, sent = tuple(rest[:-3]), rest[-3:]
        partners = {1: (0, 2), 2: (1, 0), 3: (1, 2)}
        order = SQUARE_ORDER[self.chunk]
        self.others = [swap(sent[flip - 1], *partners[flip]) for flip in order]
        return self.kept

    def column(self, after):
        rows = quarter_rows(self.chunk)
        self.kept, *rest = self.run(
            column_kernel,
            [((rows, LANE), F32)] + self.own_piece + [self.piece],
            "column",
            after,
            [pltpu.VMEM((2 * rows, LANE), F32)],
            self.own,
        )
        self.own = tuple(rest[:-1])
        self.others = [swap(rest[-1], 2, 0)]
        return self.kept

    def code(self, after):
        (self.kept,) = self.run(code_kernel, [self.piece], "code", after, (), self.own)
        self.others = [swap(self.kept, 4, 0)]
        return self.kept

    def spread(self, after):
        step = 4
        while step < lax.axis_size("wide"):
            (self.kept,) = self.run(recode_kernel, [self.piece], "recode_%d" % step, after)
            step = 2 * step
            if step < lax.axis_size("wide"):
                self.others = [swap(self.kept, step, 0)]
        token = self.kept
        if flow_part(self.chunk):
            partners = {1: 2, 2: 1, 3: 3}
            self.others = [swap(self.kept, partners[flip], 0) for flip in RETURN_ORDER]
        else:
            self.others = [swap(self.kept, 2, 0)]
            (self.kept,) = self.run(pair_kernel, [((2,) + self.piece[0], BF16)], "pair", ())
            self.others = [swap(self.kept, 1, 0)]
        return token

    def decode(self, after):
        shape = [((4 * quarter_rows(self.chunk), LANE), F32)]
        if flow_part(self.chunk):
            shape.append(((FLOW_ROWS + STATS_ROWS, LANE), F32))
            return self.run(decode_kernel, shape, "decode", after)
        return self.run(decode_pairs_kernel, shape, "decode", after)


def body(
    images,
    noise_seeds,
    valid_shape,
    conv_in,
    mixer,
    conv_out,
    hidden_bias,
    flow_params,
    conv_in_first,
    mixer_first,
    conv_out_first,
    bias_first,
    flow_first,
    conv_in_second,
    mixer_second,
    conv_out_second,
    bias_second,
    flow_second,
):
    count = images.shape[1]
    conv_out, conv_out_first, conv_out_second = conv_out.T, conv_out_first.T, conv_out_second.T
    row = lax.broadcasted_iota(jnp.int32, (8, LANE), 0)
    index = jnp.where(row == 0, lax.axis_index("narrow"), lax.axis_index("wide")).astype(jnp.int32)
    narrow = lax.axis_size("narrow")
    packed, *parts = run_pack(valid_shape, conv_in, mixer, conv_out, hidden_bias)
    paired = swap(packed, 0, 1)
    crossed = [swap(part, 0, 2) for part in parts]
    *stages, own = run_flow_pre(noise_seeds, valid_shape, images, flow_params, packed)
    cut = first_rows(CHUNKS[0][0]) + HID
    shapes = [((rows, LANE), BF16) for rows in (cut, crossed[0].shape[0] - cut)]
    head, tail, *stages = call(
        split_copy_kernel,
        shapes + [(stage.shape, F32) for stage in stages],
        (),
        (crossed[0], *stages),
        name="copy_a",
    )
    gathered = (own, paired, crossed[0], swap(head, 0, 1), swap(tail, 0, 1))
    keep_one, send, *last = run_nets(0, count, index, gathered, stages, ())
    one = Summation(0, index, send, ())
    token = one.square(keep_one, (), ())
    (copied,) = call(
        copy_kernel,
        [(crossed[1].shape, BF16)],
        (),
        (crossed[1],),
        name="copy_b",
        after=(token,),
    )
    gathered = (own, paired, crossed[1], swap(copied, 0, 1))
    keep_two, send, *results = run_nets(1, count, index, gathered, stages, (copied,))
    flow = run_flow(count, gathered, stages, results + last, (keep_two,))
    token = one.column((flow,))
    two = Summation(1, index, send, (token,))
    token = two.square(keep_two, (flow,), ())
    token = one.code((token,))
    token = one.spread((token,))
    token = two.column((token,))
    token = two.code((token,))
    token = two.spread((token,))
    weights = (conv_in, mixer, conv_out, hidden_bias)
    firsts = (conv_in_first, mixer_first, conv_out_first, bias_first)
    seconds = (conv_in_second, mixer_second, conv_out_second, bias_second)
    shapes = [(weight.shape, F32) for weight in weights]

    def norms(chunk, arrays):
        spans = [stop - start for start, stop in chunk_spans(chunk)]
        rows = (spans[0], spans[1], spans[3])
        in_shape, out_shape, bias_shape = [((count, LANE), F32) for count in rows]
        part = [in_shape, ((spans[2], HID, LANE), F32), out_shape, bias_shape]
        size = 16 if chunk == 0 else 16 + FLOW_ROWS + STATS_ROWS
        *outs, block = call(
            functools.partial(norm_kernel, chunk),
            part * 2 + [((size, LANE), F32)],
            (),
            tuple(arrays) + weights + firsts + seconds,
            name="norms_" + "ab"[chunk],
        )
        return tuple(outs[:4]), tuple(outs[4:]), block

    (part,) = one.decode((token,))
    grads_one, updates_one, sums = norms(0, (part, token))
    part, flow = two.decode((sums,))
    grads_two, updates_two, block = norms(1, (part, flow, sums))
    blocks = [block] + [swap(block, 0, part) for part in range(1, narrow)]
    moved = call(
        moment_kernel,
        shapes * 2 + [((8, LANE), F32)],
        (),
        grads_one + grads_two + firsts + seconds,
        name="moments",
    )
    flow_shape = (flow_params.shape, F32)
    fresh = call(
        functools.partial(apply_kernel, narrow),
        shapes
        + [flow_shape]
        + [(weight.shape, BF16) for weight in weights[:3]]
        + [flow_shape, flow_shape, ((15,), F32), ((15,), F32), ((1, 1), F32), ((1, 1), F32)],

        (),
        (index,)
        + tuple(blocks)
        + weights
        + updates_one
        + updates_two
        + (flow_params, flow_first, flow_second),
        scratch=[pltpu.VMEM((narrow,) + block.shape, F32)],
        after=(moved[8],),
        name="apply",
    )
    return (
        fresh[0],
        fresh[1],
        fresh[2].T,
        fresh[3],
        fresh[4],
        moved[0],
        moved[1],
        moved[2].T,
        moved[3],
        fresh[8],
        moved[4],
        moved[5],
        moved[6].T,
        moved[7],
        fresh[9],
        fresh[5],
        fresh[6],
        fresh[7].T,
        fresh[10],
        fresh[11],
        fresh[12].reshape(()),
        fresh[13].reshape(()),
    )


def solution(mesh):
    placed = (
        P(None, ("wide", "narrow"), None),
        P(("wide", "narrow")),
        P(("wide", "narrow"), None),
        P(None, "narrow"),
        P(None, None, "narrow"),
        P("narrow", None),
        P(None, None, "narrow"),
        P(),
    )
    state = (P(None, "narrow"), P(None, None, "narrow"), P("narrow", None), P(None, None, "narrow"), P())
    return jax.shard_map(
        body,
        mesh=mesh,
        in_specs=placed + state + state,
        out_specs=state * 3 + state[:3] + (P(),) * 4,
        check_vma=False,
    )
```

```python
import functools
import jax
import jax.numpy as jnp
from jax import lax
from jax.experimental import pallas as pl
from jax.experimental.pallas import tpu as pltpu
from jax.sharding import PartitionSpec as P

C1 = 12
IMG_SIDE = 32
STEP = 5
HIGHEST_PRECISION = lax.Precision.HIGHEST
LOG_TWO_PI = 1.8378770664093453
LOG_TWO = 0.6931471805599453
FIRST_BETA = 0.5
SECOND_BETA = 0.5
EPSILON = 1e-06
WEIGHT_DECAY = 0.01
LEARN_RATE = 0.25
TAPS = [(-1, -1), (-1, 0), (-1, 1), (0, -1), (0, 0), (0, 1), (1, -1), (1, 0), (1, 1)]
F32 = jnp.float32
BF16 = jnp.bfloat16
HID = 512
LANE = 128
LEVELS = 3
FLOW_ROWS = 32
STATS_ROWS = 8
CODE_BLOCK = 16
CODE_RANGE = 84.0
SQUARE_ORDER = ((2, 1, 3), (2, 1, 3))
RETURN_ORDER = (2, 1, 3)
VMEM_BYTES = 20 * 1024 * 1024


def round_up(value, unit):
    return (value + unit - 1) // unit * unit


def chan(level):
    return C1 * 2**level


def side(level):
    return IMG_SIDE // 2 ** (level + 1)


def real_positions(level, images):
    return images * side(level) ** 2


def positions(level, images):
    return round_up(real_positions(level, images), LANE)


def in_rows(level):
    return 9 * chan(level) // 2


def bias_in_tail(level):
    return round_up(9 * chan(level), 16) - 9 * chan(level) >= 4 and in_rows(level) % 16 > 10


def first_rows(level):
    return round_up(in_rows(level) + (3 if bias_in_tail(level) else 6), 16)


def second_bias_row(level):
    return (pack_rows(level) if bias_in_tail(level) else first_rows(level)) - 4


def last_rows(level):
    return round_up(9 * chan(level), 16)


def pack_rows(level):
    return first_rows(level) + HID + last_rows(level)


def pack_start(level):
    return sum(pack_rows(other) for other in range(LEVELS - 1, level, -1))


CHUNKS = ((2,), (0, 1))


def gather_start(level):
    return pack_start(level) - (0 if level in CHUNKS[0] else pack_start(CHUNKS[0][0] - 1))


def chunk_of(level):
    for chunk, levels in enumerate(CHUNKS):
        if level in levels:
            return chunk, sum(pack_rows(other) for other in levels[: levels.index(level)])
    return None


def quarter_rows(chunk):
    return round_up(sum(pack_rows(level) for level in CHUNKS[chunk]), 4 * CODE_BLOCK) // 4


def flow_part(chunk):
    return FLOW_ROWS if chunk == len(CHUNKS) - 1 else 0


def stage_rows(level):
    padded = round_up(chan(level), 8)
    half = round_up(chan(level) // 2, 8)
    sizes = [
        ("normed", padded),
        ("mixed", padded),
        ("share", 8),
        ("held", padded),
        ("block", padded),
        ("prior", half),
        ("mixing", padded),
        ("turn", padded),
        ("grad", padded),
        ("small", padded),
        ("prior_grad", half),
    ]
    starts = {}
    at = 0
    for name, size in sizes[:8]:
        starts[name] = at
        at = at + size
    starts["rows"] = at
    at = 0
    for name, size in sizes[8:]:
        starts[name] = at
        at = at + size
    starts["result_rows"] = at
    return starts


def flow_lengths():
    return [5 * C1 + 3 * C1 * C1 // 2, 10 * C1 + 6 * C1 * C1, 24 * C1 + 16 * C1 * C1]


def flow_size():
    return sum(flow_lengths())


def flow_offsets(level):
    start = sum(flow_lengths()[:level])
    channels = chan(level)
    offsets = {"bias": start, "logs": start + channels, "block": start + 2 * channels}
    start = start + 2 * channels + channels * channels
    offsets["outbias"] = start
    offsets["outscale"] = start + channels
    start = start + 2 * channels
    if level < LEVELS - 1:
        offsets["priormatrix"] = start
        start = start + channels // 2 * channels
    offsets["priorbias"] = start
    return offsets


def column_names(level):
    channels = chan(level)
    offsets = flow_offsets(level)
    names = [
        ("bias", offsets["bias"]),
        ("logs", offsets["logs"]),
        ("outbias", offsets["outbias"]),
        ("outscale", offsets["outscale"]),
        ("priorbias", offsets["priorbias"]),
    ]
    if level == LEVELS - 1:
        names = names + [("priorscale", offsets["priorbias"] + channels)]
    return names


def exact_dot(first, second):
    return jnp.dot(first, second, precision=HIGHEST_PRECISION, preferred_element_type=F32)


def exact_rows(first, second):
    return lax.dot_general(
        first,
        second,
        (((0,), (0,)), ((), ())),
        precision=HIGHEST_PRECISION,
        preferred_element_type=F32,
    )


def exact_columns(first, second):
    return lax.dot_general(
        first,
        second,
        (((1,), (1,)), ((), ())),
        precision=HIGHEST_PRECISION,
        preferred_element_type=F32,
    )


def plain_dot(first, second):
    return jnp.dot(first, second, preferred_element_type=F32)


def contract_rows(first, second):
    return lax.dot_general(first, second, (((0,), (0,)), ((), ())), preferred_element_type=F32)


def contract_columns(first, second):
    return lax.dot_general(first, second, (((1,), (1,)), ((), ())), preferred_element_type=F32)


def iota(shape, axis):
    return lax.broadcasted_iota(jnp.int32, shape, axis)


def rounded(values):
    return values.astype(BF16).astype(F32)


def split_three(values):
    high = rounded(values)
    rest = values - high
    middle = rounded(rest)
    return [high, middle, rest - middle]


def move_lanes(values, chooser, transposed=False):
    rows = values.shape[0]
    padded = round_up(rows, 8)
    if padded > rows:
        values = jnp.concatenate([values, jnp.zeros((padded - rows, values.shape[1]), F32)], 0)
    pieces = jnp.concatenate(split_three(values), 0).astype(BF16)
    moved = contract_columns(pieces, chooser) if transposed else plain_dot(pieces, chooser)
    moved = moved[:padded] + moved[padded : 2 * padded] + moved[2 * padded :]
    return moved[:rows]


def squeeze_chooser(grid, images):
    count = images * grid * grid
    source = iota((count, count), 0)
    target = iota((count, count), 1)
    shift = grid.bit_length() - 1
    image = lax.shift_right_logical(source, 2 * shift)
    row = lax.shift_right_logical(source, shift) & (grid - 1)
    column = source & (grid - 1)
    half = grid // 2
    place = (
        ((row & 1) * 2 + (column & 1)) * (images * half * half)
        + image * (half * half)
        + lax.shift_right_logical(row, 1) * half
        + lax.shift_right_logical(column, 1)
    )
    return (place == target).astype(F32).astype(BF16)


def order_chooser(channels, stride):
    row = iota((4 * channels, 4 * stride), 0)
    column = iota((4 * channels, 4 * stride), 1)
    return ((row & 3) * stride + lax.shift_right_logical(row, 2) == column).astype(F32)


def squeeze(values, chooser, lanes_out):
    channels, count = values.shape
    moved = move_lanes(values, chooser)
    quarter = count // 4
    stacked = jnp.concatenate([moved[:, k * quarter : (k + 1) * quarter] for k in range(4)], 0)
    ordered = exact_dot(order_chooser(channels, channels), stacked)
    if lanes_out > quarter:
        ordered = jnp.concatenate([ordered, jnp.zeros((4 * channels, lanes_out - quarter), F32)], 1)
    return ordered


def unsqueeze(stacked, chooser, count):
    channels = stacked.shape[0] // 4
    quarter = count // 4
    laid = jnp.concatenate(
        [stacked[k * channels : (k + 1) * channels, :quarter] for k in range(4)], 1
    )
    return move_lanes(laid, chooser, transposed=True)


def slope_roll(values, step):
    step = step % LANE
    while step:
        part = 16 if step >= 16 else 1 << (step.bit_length() - 1)
        values = pltpu.roll(values, 0, 1, stride=part, stride_axis=0)
        step = step - part
    return values


def flow_block(flat, offset, rows, width):
    padded = round_up(rows, 8)
    start = offset + width * iota((padded, FLOW_ROWS), 0)
    line = lax.shift_right_logical(start, 7)
    column = iota((padded, FLOW_ROWS), 1)
    base = -offset % LANE
    if base:
        flat = pltpu.roll(flat, base, 1)
    here = exact_dot((line == column).astype(F32), flat)
    after = exact_dot((line + 1 == column).astype(F32), flat)
    here = slope_roll(here, -width)
    after = slope_roll(after, -width)
    lane = iota((padded, LANE), 1)
    begin = (offset + width * iota((padded, LANE), 0)) & (LANE - 1)
    chosen = jnp.where(lane + begin < LANE, here, after)
    return chosen[:rows, :width]


def flow_block_back(values, offset, rows, width):
    padded = round_up(rows, 8)
    base = offset % LANE
    over = max(base + width - LANE, 0)
    parts = [values[:, width - over :]] if over else []
    if base > over:
        parts.append(jnp.zeros((rows, base - over), F32))
    parts.append(values[:, : width - over])
    if base + width < LANE:
        parts.append(jnp.zeros((rows, LANE - base - width), F32))
    block = jnp.concatenate(parts, 1)
    if padded > rows:
        block = jnp.concatenate([block, jnp.zeros((padded - rows, LANE), F32)], 0)
    block = slope_roll(block, width)
    lane = iota((padded, LANE), 1)
    begin = (offset + width * iota((padded, LANE), 0)) & (LANE - 1)
    here = jnp.where(lane >= begin, block, 0.0)
    after = jnp.where(lane >= begin, 0.0, block)
    line = lax.shift_right_logical(offset + width * iota((FLOW_ROWS, padded), 1), 7)
    row = iota((FLOW_ROWS, padded), 0)
    return exact_dot((line == row).astype(F32), here) + exact_dot(
        (line + 1 == row).astype(F32), after
    )


def flow_column(turned, offset, length):
    line, begin = offset // LANE, offset % LANE
    if begin + length <= LANE:
        return turned[begin : begin + length, line : line + 1]
    return jnp.concatenate(
        [turned[begin:, line : line + 1], turned[: begin + length - LANE, line + 1 : line + 2]], 0
    )


def flow_column_back(values, offset):
    length = values.shape[0]
    line, begin = offset // LANE, offset % LANE
    lane = iota((LANE, LANE), 1)
    head = min(length, LANE - begin)
    parts = []
    if begin:
        parts.append(jnp.zeros((begin, 1), F32))
    parts.append(values[:head])
    if begin + head < LANE:
        parts.append(jnp.zeros((LANE - begin - head, 1), F32))
    column = jnp.concatenate(parts, 0) if len(parts) > 1 else parts[0]
    term = jnp.where(lane == line, column, 0.0)
    if head < length:
        column = jnp.concatenate([values[head:], jnp.zeros((LANE - length + head, 1), F32)], 0)
        term = term + jnp.where(lane == line + 1, column, 0.0)
    return term


def to_flat_rows(values):
    size = values.shape[0]
    row = values.reshape(1, size)
    row = jnp.concatenate([row, jnp.zeros((1, FLOW_ROWS * LANE - size), F32)], 1)
    return row.reshape(FLOW_ROWS, LANE)


def from_flat_rows(values, size):
    return values.reshape(1, FLOW_ROWS * LANE)[:, :size].reshape(size)


def triangles(block):
    channels = block.shape[0]
    row = iota((channels, channels), 0)
    column = iota((channels, channels), 1)
    signs = (1 - 2 * (row & 1)).astype(F32)
    diagonal = signs * jnp.exp(jnp.where(row == column, block, 0.0))
    lower = jnp.where(row > column, block, jnp.where(row == column, 1.0, 0.0))
    upper = jnp.where(row < column, block, jnp.where(row == column, diagonal, 0.0))
    reverse = (row + column == channels - 1).astype(F32)
    return lower, upper, reverse, diagonal


def tap_masks(level, images):
    grid = side(level)
    count = positions(level, images)
    lane = iota((8, count), 1)
    shift = grid.bit_length() - 1
    row = lax.shift_right_logical(lane, shift) & (grid - 1)
    column = lane & (grid - 1)
    inside = lane < real_positions(level, images)
    masks = {}
    for row_step in (-1, 0, 1):
        for column_step in (-1, 0, 1):
            good = (
                (row + row_step >= 0)
                & (row + row_step < grid)
                & (column + column_step >= 0)
                & (column + column_step < grid)
                & inside
            )
            masks[(row_step, column_step)] = jnp.where(good, 1.0, 0.0)[0:1]
    return masks


def tap_read(values, masks, level, row_step, column_step):
    count = values.shape[1]
    offset = (row_step * side(level) + column_step) % count
    if offset:
        values = pltpu.roll(values, count - offset, 1)
    if (row_step, column_step) != (0, 0):
        values = values * masks[(row_step, column_step)]
    return values


def tap_stack(values, masks, level, direction):
    return [
        tap_read(values, masks, level, direction * row_step, direction * column_step)
        for row_step, column_step in TAPS
    ]


def tap_sum(values, masks, level, direction, channels):
    total = None
    for tap, (row_step, column_step) in enumerate(TAPS):
        term = tap_read(
            values[tap * channels : (tap + 1) * channels],
            masks,
            level,
            direction * row_step,
            direction * column_step,
        )
        total = term if total is None else total + term
    return total


def pack_kernel(valid_ref, conv_in_ref, mixer_ref, conv_out_ref, bias_ref, whole_ref, *part_refs):
    in_start = 0
    out_start = 0
    for level in range(LEVELS):
        out_ref = whole_ref.at[pack_start(level) : pack_start(level) + pack_rows(level)]
        rows, columns = in_rows(level), 9 * chan(level)
        top = first_rows(level)
        ones = split_three(bias_ref[level, 0:1, :])
        twos = split_three(bias_ref[level, 1:2, :]) + [jnp.zeros((1, LANE), F32)]
        head = [conv_in_ref[in_start : in_start + rows, :]] + ones
        tail = [conv_out_ref[out_start : out_start + columns, :]]
        for part, size, chosen in (
            (head, top, not bias_in_tail(level)),
            (tail, last_rows(level), bias_in_tail(level)),
        ):
            used = sum(piece.shape[0] for piece in part) + (4 if chosen else 0)
            if size > used:
                part.append(jnp.zeros((size - used, LANE), F32))
            if chosen:
                part.extend(twos)
        out_ref[0:top, :] = jnp.concatenate(head, 0).astype(BF16)
        out_ref[top : top + HID, :] = mixer_ref[level].astype(BF16)
        out_ref[top + HID :, :] = jnp.concatenate(tail, 0).astype(BF16)
        in_start = in_start + rows
        out_start = out_start + columns
    pixels = jnp.int32(0)
    for image in range(valid_ref.shape[0]):
        pixels = pixels + valid_ref[image, 0] * valid_ref[image, 1]
    lane = iota((16, LANE), 1)
    digits = jnp.where(lane == 0, pixels & 127, 0)
    for place in (1, 2):
        digits = jnp.where(lane == place, lax.shift_right_logical(pixels, 7 * place) & 127, digits)
    whole_ref[pack_start(-1) :, :] = digits.astype(F32).astype(BF16)
    cut = part_refs[0].shape[0]
    part_refs[0][...] = whole_ref[0:cut, :]
    part_refs[1][...] = whole_ref[cut:, :]


def flow_pre_kernel(seed_ref, valid_ref, image_ref, flow_ref, packed_ref, *out_refs):
    out_refs[LEVELS][...] = packed_ref[...]
    images = image_ref.shape[1]
    flat = to_flat_rows(flow_ref[...])
    turned = jnp.concatenate([flat, jnp.zeros((LANE - FLOW_ROWS, LANE), F32)], 0).T
    blocks = IMG_SIDE * IMG_SIDE // 256
    pieces = []
    for image in range(images):
        position = iota((8, IMG_SIDE * IMG_SIDE), 0) * (IMG_SIDE * IMG_SIDE) + iota(
            (8, IMG_SIDE * IMG_SIDE), 1
        )
        hashed = seed_ref[image] + position * jnp.int32(-1640531527)
        hashed = hashed ^ lax.shift_right_logical(hashed, jnp.full_like(hashed, 15))
        hashed = hashed * jnp.int32(739267321)
        hashed = hashed ^ lax.shift_right_logical(hashed, jnp.full_like(hashed, 13))
        field = ((hashed & jnp.int32(16777215)).astype(F32) + 0.5) * 2.0 ** (-24)
        pixel = jnp.concatenate(
            [image_ref[:, image, :], jnp.zeros((5, IMG_SIDE * IMG_SIDE), F32)], 0
        )
        pixel = pixel + field / 256.0
        for block in range(blocks):
            pieces.append(pixel[:, block * 256 : (block + 1) * 256])
    stacked = jnp.concatenate(pieces, 0)
    source = iota((256, 256), 0)
    target = iota((256, 256), 1)
    row = lax.shift_right_logical(source, 5)
    column = source & 31
    place = (
        ((row & 1) * 2 + (column & 1)) * 64
        + lax.shift_right_logical(row, 1) * 16
        + lax.shift_right_logical(column, 1)
    )
    moved = move_lanes(stacked, (place == target).astype(F32).astype(BF16))
    quarters = []
    for k in range(4):
        quarters.append(
            jnp.concatenate(
                [
                    moved[piece * 8 : (piece + 1) * 8, k * 64 : (k + 1) * 64]
                    for piece in range(images * blocks)
                ],
                1,
            )
        )
    state = exact_dot(order_chooser(3, 8), jnp.concatenate(quarters, 0))
    for level in range(LEVELS):
        channels = chan(level)
        grid = side(level)
        count = positions(level, images)
        offsets = flow_offsets(level)
        block = flow_block(flat, offsets["block"], channels, channels)
        names = column_names(level)
        columns = [flow_column(turned, offset, channels) for _, offset in names]
        lane = iota((channels, LANE), 1)
        held = jnp.zeros((channels, LANE), F32)
        for index, column in enumerate(columns):
            held = jnp.where(lane == index, column, held)
        growth = jnp.exp(columns[1])
        normed = (state + columns[0]) * growth
        lower, upper, reverse, _ = triangles(block)
        mixing = exact_dot(exact_dot(reverse, lower), upper)
        mixed = exact_dot(mixing, normed)
        lane = iota((8, count), 1)
        shift = grid.bit_length() - 1
        image = lax.shift_right_logical(lane, 2 * shift)
        row = lax.shift_right_logical(lane, shift) & (grid - 1)
        column = lane & (grid - 1)
        high = jnp.zeros((8, count), jnp.int32)
        wide = jnp.zeros((8, count), jnp.int32)
        for index in range(images):
            high = jnp.where(image == index, valid_ref[index, 0], high)
            wide = jnp.where(image == index, valid_ref[index, 1], wide)
        unit = 2 ** (level + 1)
        row_share = jnp.clip(high - row * unit, 0, unit).astype(F32) / unit
        column_share = jnp.clip(wide - column * unit, 0, unit).astype(F32) / unit
        share = jnp.where(image < images, row_share * column_share, 0.0)
        out_ref = out_refs[level]
        starts = stage_rows(level)
        out_ref[starts["normed"] : starts["normed"] + channels, :] = normed
        out_ref[starts["mixed"] : starts["mixed"] + channels, :] = mixed
        out_ref[starts["share"] : starts["share"] + 8, :] = share
        out_ref[starts["held"] : starts["held"] + channels, 0:LANE] = held
        out_ref[starts["block"] : starts["block"] + channels, 0:channels] = block
        out_ref[starts["mixing"] : starts["mixing"] + channels, 0:channels] = mixing
        if level > 0:
            order = order_chooser(channels // 4, channels // 4)
            out_ref[starts["turn"] : starts["turn"] + channels, 0:channels] = exact_dot(
                mixing, growth * order
            )
        if level < LEVELS - 1:
            out_ref[starts["prior"] : starts["prior"] + channels // 2, 0:channels] = flow_block(
                flat, offsets["priormatrix"], channels // 2, channels
            )
            state = squeeze(
                mixed[: channels // 2], squeeze_chooser(grid, images), positions(level + 1, images)
            )


def silu_parts(values):
    sigmoid = 1.0 / (1.0 + jnp.exp(-values))
    active = values * sigmoid
    slope = sigmoid + active * (1.0 - sigmoid)
    return active, slope


def net_kernel(level, images, narrow, *refs):
    is_last = level == LEVELS - 1
    index_ref = refs[0]
    weight_refs, tails = refs[1 : 1 + narrow], [None] * narrow
    if isinstance(weight_refs[-1], tuple):
        weight_refs, tails[-1] = (*weight_refs[:-1], weight_refs[-1][0]), weight_refs[-1][1]
    bases = [
        pack_start(level) if ref.shape[0] > pack_start(-1) else gather_start(level)
        for ref in weight_refs
    ]
    out_base = chunk_of(level)[1]
    stage_ref, keep_ref, send_ref, result_ref = refs[1 + narrow : 5 + narrow]
    order_ref, slope_one_ref, slope_two_ref, one_ref, two_ref = refs[5 + narrow :]
    starts = stage_rows(level)
    me = index_ref[0, 0]
    channels = chan(level)
    half = channels // 2
    count = positions(level, images)
    top, rows = first_rows(level), in_rows(level)
    tail, used = last_rows(level), 9 * channels
    bias_block = second_bias_row(level) - 12
    masks = tap_masks(level, images)
    width = HID // narrow

    def weights(start, length):
        parts = []
        for ref, base, tail in zip(weight_refs, bases, tails):
            first = base + start
            if tail is not None and first >= ref.shape[0]:
                ref, first = tail, first - ref.shape[0]
            parts.append(ref[first : first + length, :])
        return jnp.concatenate(parts, 1)

    for r_in in range(narrow):
        for r_out in range(narrow):
            start = pl.multiple_of(bases[r_out] + top + (me ^ r_in) * width, 16)
            order_ref[r_in * width : (r_in + 1) * width, r_out * LANE : (r_out + 1) * LANE] = (
                weight_refs[r_out][pl.ds(start, width), :]
            )
    weight_in = weights(0, top)
    weight_mix = order_ref[...]
    weight_out = weights(top + HID, tail)
    mixed = starts["mixed"]
    first = stage_ref[mixed : mixed + half, :]
    second = stage_ref[mixed + half : mixed + channels, :]
    share = stage_ref[starts["share"] : starts["share"] + 1, :]
    pieces = tap_stack(rounded(first), masks, level, 1)
    pieces.append(jnp.ones((3, count), F32))
    pieces.append(jnp.zeros((top - rows - 3, count), F32))
    stacked = jnp.concatenate(pieces, 0).astype(BF16)
    pick = jnp.where(
        (iota((16, count), 0) >= 12) & (iota((16, count), 0) < 15), 1.0, 0.0
    ).astype(BF16)
    hidden_one = contract_rows(weight_in, stacked)
    active, slope = silu_parts(hidden_one)
    slope_one_ref[...] = slope
    one_ref[...] = active.astype(BF16)
    hidden_two = contract_rows(weight_mix, one_ref[...]) + contract_rows(
        weights(bias_block, 16), pick
    )
    active, slope = silu_parts(hidden_two)
    slope_two_ref[...] = slope
    two_ref[...] = active.astype(BF16)
    spread = plain_dot(weight_out, two_ref[...])
    net_raw = tap_sum(spread, masks, level, 1, channels)
    held = stage_ref[starts["held"] : starts["held"] + channels, 0:LANE]
    out_bias, out_scale = held[:, 2:3], held[:, 3:4]
    growth = jnp.exp(3.0 * out_scale)
    output = (net_raw + out_bias) * growth
    logit = output[half:] + 2.0
    sigmoid = 1.0 / (1.0 + jnp.exp(-logit))
    latent = (second + output[:half]) * sigmoid
    log_sigmoid = jnp.minimum(logit, 0.0) - jnp.log1p(jnp.exp(-jnp.abs(logit)))
    if is_last:
        joined = jnp.concatenate([first, latent], 0)
        mean, scale = held[:, 4:5], held[:, 5:6]
        mean = jnp.broadcast_to(mean, joined.shape)
        scale = jnp.broadcast_to(scale, joined.shape)
    else:
        joined = latent
        prior = stage_ref[starts["prior"] : starts["prior"] + half, 0:channels]
        stats = exact_rows(prior, first) + held[:, 4:5]
        mean, scale = stats[:half], stats[half:]
    gap = joined - mean
    shrink = jnp.exp(-2.0 * scale)
    square = gap * gap * shrink
    log_prior = -0.5 * (LOG_TWO_PI + 2.0 * scale + square)
    total = jnp.sum(jnp.sum(share * log_sigmoid, 0, keepdims=True), 1, keepdims=True) + jnp.sum(
        jnp.sum(share * log_prior, 0, keepdims=True), 1, keepdims=True
    )
    share_total = jnp.sum(share, 1, keepdims=True)
    grad_joined = share * (gap * shrink)
    grad_scale = share * (1.0 - square)
    grad_latent = grad_joined[half:] if is_last else grad_joined
    grad_logit = (grad_latent * latent - share) * (1.0 - sigmoid)
    grad_second = grad_latent * sigmoid
    grad_output = jnp.concatenate([grad_second, grad_logit], 0)
    grad_net = grad_output * growth
    lane = iota((channels, LANE), 1)
    small = jnp.zeros((channels, LANE), F32)

    def put(small, index, values):
        return jnp.where(lane == index, jnp.sum(values, 1, keepdims=True), small)

    small = put(small, 2, grad_net)
    small = put(small, 3, 3.0 * grad_output * output)
    if is_last:
        small = put(small, 4, -grad_joined)
        small = put(small, 5, grad_scale)
        grad_first = grad_joined[:half]
    else:
        grad_stats = jnp.concatenate([-grad_joined, grad_scale], 0)
        small = put(small, 4, grad_stats)
        grad_first = exact_dot(prior, grad_stats)
        prior_grad = exact_columns(first, grad_stats)
        start = starts["prior_grad"]
        result_ref[start : start + half, 0:channels] = prior_grad
    small = jnp.where(lane == 6, -total, small)
    small = jnp.where(lane == 7, share_total, small)
    result_ref[starts["small"] : starts["small"] + channels, 0:LANE] = small
    pieces = tap_stack(rounded(grad_net), masks, level, -1)
    if tail > used:
        pieces.append(jnp.zeros((tail - used, count), F32))
    grad_spread = jnp.concatenate(pieces, 0).astype(BF16)

    def store(start, values):
        for r in range(narrow):
            ref = send_ref if r & 1 else keep_ref
            rows = slice(out_base + start, out_base + start + values.shape[0])
            ref[r // 2, rows, :] = values[:, r * LANE : (r + 1) * LANE]

    grad_out = contract_columns(grad_spread, two_ref[...])
    grad_two = (contract_rows(weight_out, grad_spread) * slope_two_ref[...]).astype(BF16)
    grad_mix = contract_columns(one_ref[...], grad_two)
    for r_in in range(narrow):
        start = pl.multiple_of(out_base + top + (me ^ r_in) * width, 16)
        for r_out in range(narrow):
            ref = send_ref if r_out & 1 else keep_ref
            ref[r_out // 2, pl.ds(start, width), :] = grad_mix[
                r_in * width : (r_in + 1) * width, r_out * LANE : (r_out + 1) * LANE
            ]
    grad_one = (plain_dot(weight_mix, grad_two) * slope_one_ref[...]).astype(BF16)
    grad_in = contract_columns(stacked, grad_one)
    grad_bias = contract_columns(pick, grad_two)
    if bias_in_tail(level):
        grad_out = jnp.concatenate([grad_out[: tail - 16], grad_out[tail - 16 :] + grad_bias], 0)
    else:
        grad_in = jnp.concatenate([grad_in[: top - 16], grad_in[top - 16 :] + grad_bias], 0)
    store(0, grad_in)
    store(top + HID, grad_out)
    grad_stack = plain_dot(weight_in, grad_one)
    grad_first = grad_first + tap_sum(grad_stack, masks, level, -1, half)
    result_ref[0:half, :] = grad_first
    result_ref[half:channels, :] = grad_second


def stage_part(level, ref, name, rows, lanes):
    start = stage_rows(level)[name]
    return ref[start : start + rows, 0:lanes]


def flow_chain(images, stages, results):
    grads = [None] * LEVELS
    carried = None
    for level in (2, 1, 0):
        channels = chan(level)
        count = positions(level, images)
        grad = stage_part(level, results[level], "grad", channels, count)
        if carried is not None:
            grad = grad + jnp.concatenate([carried, jnp.zeros_like(carried)], 0)
        grads[level] = grad
        if level > 0:
            turn = stage_part(level, stages[level], "turn", channels, channels)
            grid = side(level - 1)
            carried = unsqueeze(
                exact_rows(turn, grad), squeeze_chooser(grid, images), images * grid * grid
            )
    return grads


def flow_level(level, images, stage_ref, result_ref, grad):
    channels = chan(level)
    half = channels // 2
    count = positions(level, images)
    offsets = flow_offsets(level)
    normed = stage_part(level, stage_ref, "normed", channels, count)
    held = stage_part(level, stage_ref, "held", channels, LANE)
    block = stage_part(level, stage_ref, "block", channels, channels)
    mixing = stage_part(level, stage_ref, "mixing", channels, channels)
    small = stage_part(level, result_ref, "small", channels, LANE)
    lower, upper, reverse, diagonal = triangles(block)
    grad_normed = exact_rows(mixing, grad)
    grad_mixing = exact_dot(reverse, exact_columns(grad, normed))
    grad_lower = exact_columns(grad_mixing, upper)
    grad_upper = exact_rows(lower, grad_mixing)
    share_total = small[0:1, 7:8]
    row = iota((channels, channels), 0)
    column = iota((channels, channels), 1)
    grad_block = jnp.where(
        row > column,
        grad_lower,
        jnp.where(row < column, grad_upper, grad_upper * diagonal - share_total),
    )
    growth = jnp.exp(held[:, 1:2])
    grad_bias = jnp.sum(grad_normed, 1, keepdims=True) * growth
    grad_logs = jnp.sum(grad_normed * normed, 1, keepdims=True) - share_total
    flat = flow_block_back(grad_block, offsets["block"], channels, channels)
    turned = jnp.zeros((LANE, LANE), F32)
    for index, (name, offset) in enumerate(column_names(level)):
        if name == "bias":
            values = grad_bias
        elif name == "logs":
            values = grad_logs
        else:
            values = small[:, index : index + 1]
        turned = turned + flow_column_back(values, offset)
    if level < LEVELS - 1:
        flat = flat + flow_block_back(
            stage_part(level, result_ref, "prior_grad", half, channels),
            offsets["priormatrix"],
            half,
            channels,
        )
    logs_total = jnp.sum(held[:, 1:2], 0, keepdims=True)
    trace = jnp.sum(
        jnp.sum(jnp.where(row == column, block, 0.0), 0, keepdims=True), 1, keepdims=True
    )
    return flat, turned, small[0:1, 6:7] - share_total * (logs_total + trace)


def flow_back(images, stages, results, weights, out_ref):
    grads = flow_chain(images, stages, results)
    parts = [
        flow_level(level, images, stages[level], results[level], grads[level])
        for level in range(LEVELS)
    ]
    flat = sum(part[0] for part in parts) + sum(part[1] for part in parts).T[:FLOW_ROWS]
    loss = sum(part[2] for part in parts)
    pixels = jnp.zeros((1, 1), F32)
    for ref in weights:
        start = ref.shape[0] - 16
        digits = ref[start : start + 16, :].astype(F32)
        for place in range(3):
            pixels = pixels + 128.0**place * digits[0:1, place : place + 1]
    lane = iota((STATS_ROWS, LANE), 1)
    out_ref[0:FLOW_ROWS, :] = flat
    out_ref[FLOW_ROWS:, :] = jnp.where(lane == 0, loss, jnp.where(lane == 1, pixels, 0.0))


def zero_rows(refs, start):
    for ref in refs:
        rest = ref.shape[1] - start
        if rest:
            ref[:, start:, :] = jnp.zeros((ref.shape[0], rest, LANE), F32)


def nets_kernel(chunk, images, narrow, split, *refs):
    levels = CHUNKS[chunk]
    number = len(levels)
    index_ref = refs[0]
    mine = refs[1 : 1 + narrow]
    at = 1 + narrow
    if split:
        mine = (*mine[:-1], (mine[-1], refs[at]))
        at = at + 1
    stages = refs[at : at + number]
    at = at + number
    keep_ref, send_ref = refs[at : at + 2]
    results = refs[at + 2 : at + 2 + number]
    at = at + 2 + number
    for place, level in enumerate(levels):
        net_kernel(
            level,
            images,
            narrow,
            index_ref,
            *mine,
            stages[place],
            keep_ref,
            send_ref,
            results[place],
            *refs[at + 5 * place : at + 5 * place + 5],
        )
    zero_rows((keep_ref, send_ref), sum(pack_rows(level) for level in levels))


def flow_kernel(images, narrow, *refs):
    stages, results = refs[:LEVELS], refs[LEVELS : 2 * LEVELS]
    weights, out_ref = refs[2 * LEVELS : -1], refs[-1]
    flow_back(images, stages, results, weights, out_ref)


def copy_kernel(*refs):
    half = len(refs) // 2
    for from_ref, to_ref in zip(refs[:half], refs[half:]):
        to_ref[...] = from_ref[...]


def split_copy_kernel(from_ref, *refs):
    half = len(refs) // 2 - 1
    cut = refs[half].shape[0]
    refs[half][...] = from_ref[0:cut, :]
    refs[half + 1][...] = from_ref[cut:, :]
    for source, target in zip(refs[:half], refs[half + 2 :]):
        target[...] = source[...]


def piece_rows(rows):
    return rows + round_up(rows // CODE_BLOCK, 16)


def write_piece(ref, start, values, extra=None):
    rows = values.shape[0]
    blocks = values.reshape(rows // CODE_BLOCK, CODE_BLOCK, LANE)
    scale = rounded(jnp.max(jnp.abs(blocks), axis=1) * 1.01)
    factor = jnp.where(scale > 0.0, CODE_RANGE / scale, 0.0)
    code = jnp.exp(blocks * factor[:, None, :])
    ref[start : start + rows, :] = code.reshape(rows, LANE).astype(BF16)
    tail = [scale] + ([] if extra is None else split_three(extra))
    used = sum(part.shape[0] for part in tail)
    size = round_up(rows // CODE_BLOCK, 16)
    if size > used:
        tail.append(jnp.zeros((size - used, LANE), F32))
    ref[start + rows : start + rows + size, :] = jnp.concatenate(tail, 0).astype(BF16)


def read_piece(ref, start, rows):
    blocks = jnp.log(ref[start : start + rows, :].astype(F32))
    blocks = blocks.reshape(rows // CODE_BLOCK, CODE_BLOCK, LANE)
    scale = ref[start + rows : start + piece_rows(rows), :].astype(F32)
    factor = scale[: rows // CODE_BLOCK] * (1.0 / CODE_RANGE)
    return (blocks * factor[:, None, :]).reshape(rows, LANE)


def read_stats(ref, start, rows):
    first = start + rows + rows // CODE_BLOCK
    tail = ref[first : first + 3, :].astype(F32)
    return tail[0:1] + tail[1:2] + tail[2:3]


def wide_bit(index_ref, bit):
    return jnp.where((index_ref[1, 0] & bit) != 0, 1, 0)


def send_kernel(chunk, index_ref, send_ref, *piece_refs):
    half = 2 * quarter_rows(chunk)
    for shard in range(2):
        for place in range(2):
            values = send_ref[shard, place * half : (place + 1) * half, :]
            write_piece(piece_refs[2 * shard + place], 0, values)


def square_kernel(chunk, index_ref, keep_ref, *refs):
    other_refs, total_ref, refs = refs[:4], refs[-1], refs[4:-1]
    flow = None
    if flow_part(chunk):
        flow_ref, mine_ref, own_flow_ref, *sent_refs = refs
        flow = flow_ref[0:FLOW_ROWS, :]
        stats = flow_ref[FLOW_ROWS : FLOW_ROWS + 1, :]
        write_piece(own_flow_ref, 0, flow, stats)
    else:
        mine_ref, *sent_refs = refs
    half = 2 * quarter_rows(chunk)
    upper = wide_bit(index_ref, 1)
    for shard in range(2):
        for place in range(2):
            picked = slice(place * half, (place + 1) * half)
            total_ref[shard, picked, :] = keep_ref[shard, picked, :] + read_piece(
                other_refs[2 * shard + place], 0, half
            )

    def total(shard, flipped):
        place = 1 - upper if flipped else upper
        return total_ref[shard, pl.ds(pl.multiple_of(place * half, CODE_BLOCK), half), :]

    mine_ref[...] = total(0, 0)
    for ref, (shard, flipped) in zip(sent_refs, ((1, 0), (0, 1), (1, 1))):
        values = total(shard, flipped)
        if flow is None:
            write_piece(ref, 0, values)
        else:
            write_piece(ref, 0, jnp.concatenate([values, flow], 0), stats)


def column_kernel(chunk, index_ref, mine_ref, *refs):
    rows = 2 * quarter_rows(chunk)
    more = flow_part(chunk)
    if more:
        own_flow_ref, *others, keep_ref, own_next_ref, sent_ref, total_ref = refs
    else:
        *others, keep_ref, sent_ref, total_ref = refs
    total = mine_ref[...]
    for flip, other in zip(SQUARE_ORDER[chunk], others):
        values = read_piece(other, 0, rows + more)
        total = total + values[:rows]
        if more and flip == 2:
            flow = read_piece(own_flow_ref, 0, FLOW_ROWS) + values[rows:]
            stats = read_stats(own_flow_ref, 0, FLOW_ROWS) + read_stats(other, 0, rows + more)
    total_ref[...] = total
    half = rows // 2
    place = wide_bit(index_ref, 2)
    keep_ref[...] = total_ref[pl.ds(pl.multiple_of(place * half, CODE_BLOCK), half), :]
    values = total_ref[pl.ds(pl.multiple_of((1 - place) * half, CODE_BLOCK), half), :]
    if more:
        write_piece(own_next_ref, 0, flow, stats)
        write_piece(sent_ref, 0, jnp.concatenate([values, flow], 0), stats)
    else:
        write_piece(sent_ref, 0, values)


def code_kernel(chunk, index_ref, mine_ref, *refs):
    rows = quarter_rows(chunk)
    more = flow_part(chunk)
    if more:
        own_flow_ref, other_ref, out_ref = refs
    else:
        other_ref, out_ref = refs
    values = read_piece(other_ref, 0, rows + more)
    total = mine_ref[...] + values[:rows]
    if more:
        flow = read_piece(own_flow_ref, 0, FLOW_ROWS) + values[rows:]
        stats = read_stats(own_flow_ref, 0, FLOW_ROWS) + read_stats(other_ref, 0, rows + more)
        write_piece(out_ref, 0, jnp.concatenate([total, flow], 0), stats)
    else:
        write_piece(out_ref, 0, total)


def recode_kernel(chunk, final, index_ref, mine_ref, other_ref, out_ref, *flow_refs):
    count, more = quarter_rows(chunk), flow_part(chunk)
    rows = count + more
    total = read_piece(mine_ref, 0, rows) + read_piece(other_ref, 0, rows)
    stats = None
    if more:
        stats = read_stats(mine_ref, 0, rows) + read_stats(other_ref, 0, rows)
    if more and final:
        write_piece(out_ref, 0, total[:count])
        flow_refs[0][0:FLOW_ROWS, :] = total[count:]
        flow_refs[0][FLOW_ROWS:, :] = jnp.broadcast_to(stats, (STATS_ROWS, LANE))
    else:
        write_piece(out_ref, 0, total, stats)


def pair_kernel(chunk, index_ref, mine_ref, other_ref, out_ref):
    place = wide_bit(index_ref, 2)
    out_ref[place] = mine_ref[...]
    out_ref[1 - place] = other_ref[...]


def decode_pairs_kernel(chunk, index_ref, mine_ref, other_ref, out_ref):
    rows = quarter_rows(chunk)
    upper = wide_bit(index_ref, 1)
    for place, ref in ((upper, mine_ref), (1 - upper, other_ref)):
        for near in range(2):
            start = pl.multiple_of((2 * place + near) * rows, CODE_BLOCK)
            out_ref[pl.ds(start, rows), :] = read_piece(ref.at[near], 0, rows)


def decode_kernel(chunk, index_ref, *refs):
    parts, out_ref = refs[:4], refs[4]
    place = 2 * wide_bit(index_ref, 1) + wide_bit(index_ref, 2)
    rows = quarter_rows(chunk)
    for flip, ref in zip((0, *RETURN_ORDER), parts):
        start = pl.multiple_of((place ^ flip) * rows, CODE_BLOCK)
        out_ref[pl.ds(start, rows), :] = read_piece(ref, 0, rows)


def moments(weight, gradient, first_old, second_old):
    first_new = FIRST_BETA * first_old + (1.0 - FIRST_BETA) * gradient
    second_new = SECOND_BETA * second_old + (1.0 - SECOND_BETA) * gradient * gradient
    update = (
        first_new
        * (1.0 / (1.0 - FIRST_BETA**STEP))
        / (jnp.sqrt(second_new * (1.0 / (1.0 - SECOND_BETA**STEP))) + EPSILON)
        + WEIGHT_DECAY * weight
    )
    return first_new, second_new, update


def total_of(values):
    return jnp.sum(jnp.sum(values, 0, keepdims=True), 1, keepdims=True)


def squares_rows(sums):
    row = iota((16, LANE), 0)
    held = jnp.zeros((16, LANE), F32)
    for index, value in sums:
        held = jnp.where(row == index, value, held)
    return held


def chunk_spans(chunk):
    levels = CHUNKS[chunk]
    base = min(levels)
    spans = []
    for size in (in_rows, lambda level: 9 * chan(level), lambda level: 1, lambda level: 2):
        start = sum(size(level) for level in range(base))
        spans.append((start, start + sum(size(level) for level in levels)))
    return spans


def level_totals(chunk, values, size):
    row = iota(values.shape, 0)
    totals = []
    start = 0
    for level in sorted(CHUNKS[chunk]):
        stop = start + size(level)
        inside = values
        if stop - start < values.shape[0]:
            inside = jnp.where((row >= start) & (row < stop), values, 0.0)
        totals.append(total_of(inside))
        start = stop
    return totals


def group_totals(chunk, values_in, values_mix, values_out, values_bias):
    levels = sorted(CHUNKS[chunk])
    sums = (
        (0, level_totals(chunk, values_in, in_rows)),
        (3, [total_of(values) for values in values_mix]),
        (6, level_totals(chunk, values_out, lambda level: 9 * chan(level))),
        (9, level_totals(chunk, values_bias, lambda level: 2)),
    )
    return [(base + level, total) for base, totals in sums for level, total in zip(levels, totals)]


def flow_masks():
    place = iota((FLOW_ROWS, LANE), 0) * LANE + iota((FLOW_ROWS, LANE), 1)
    masks = []
    start = 0
    for length in flow_lengths():
        masks.append((place >= start) & (place < start + length))
        start = start + length
    return masks


def split_grads(chunk, ref, scale):
    ins, mixes, outs, biases = [], [], [], []
    for level in sorted(CHUNKS[chunk]):
        start = chunk_of(level)[1]

        def rows(first, count):
            return ref[start + first : start + first + count, :] * scale

        top = first_rows(level)
        ins.append(rows(0, in_rows(level)))
        mixes.append(rows(top, HID))
        outs.append(rows(top + HID, 9 * chan(level)))
        biases.append(rows(in_rows(level), 1))
        biases.append(rows(second_bias_row(level), 1))
    join = lambda parts: parts[0] if len(parts) == 1 else jnp.concatenate(parts, 0)
    return join(ins), mixes, join(outs), join(biases)


def norm_kernel(chunk, *refs):
    last = chunk == len(CHUNKS) - 1
    part_ref, flow_ref, refs = refs[0], refs[1], refs[2:]
    if last:
        sums_ref, refs = refs[0], refs[1:]
    stats = flow_ref[FLOW_ROWS : FLOW_ROWS + 1, :]
    weights, firsts, seconds = refs[0:4], refs[4:8], refs[8:12]
    grads, updates, block_ref = refs[12:16], refs[16:20], refs[20]
    scale = 1.0 / (3.0 * stats[:, 1:2] * LOG_TWO)
    grad_in, grad_mix, grad_out, grad_bias = split_grads(chunk, part_ref, scale)
    in_span, out_span, mix_span, bias_span = chunk_spans(chunk)
    weight_squares = [None] * 4
    update_squares = [None] * 4
    for place, span, gradient in ((0, in_span, grad_in), (2, out_span, grad_out)):
        picked = slice(*span)
        weight = weights[place][picked, :]
        update = moments(weight, gradient, firsts[place][picked, :], seconds[place][picked, :])[2]
        grads[place][...] = gradient
        updates[place][...] = update
        weight_squares[place] = weight * weight
        update_squares[place] = update * update
    old = [ref[...].reshape(2 * LEVELS, LANE)[slice(*bias_span)] for ref in (weights[3], firsts[3], seconds[3])]
    update = moments(old[0], grad_bias, old[1], old[2])[2]
    grads[3][...] = grad_bias
    updates[3][...] = update
    weight_squares[3], update_squares[3] = old[0] * old[0], update * update
    weight_squares[1], update_squares[1] = [], []
    for place, level in enumerate(range(*mix_span)):
        weight = weights[1][level]
        grads[1][place] = grad_mix[place]
        update = moments(weight, grad_mix[place], firsts[1][level], seconds[1][level])[2]
        updates[1][place] = update
        weight_squares[1].append(weight * weight)
        update_squares[1].append(update * update)
    lane = iota((16, LANE), 1)
    sums = jnp.where(
        lane == 0,
        squares_rows(group_totals(chunk, *weight_squares)),
        squares_rows(group_totals(chunk, *update_squares)),
    )
    if last:
        block_ref[0:16, :] = sums + sums_ref[...]
        block_ref[16:, :] = flow_ref[...]
    else:
        block_ref[...] = sums


def join_chunks(first, last):
    return jnp.concatenate([last[...], first[...]], 0)


def moment_kernel(*refs):
    one, two, firsts, seconds = refs[0:4], refs[4:8], refs[8:12], refs[12:16]
    new_firsts, new_seconds = refs[16:20], refs[20:24]
    refs[24][...] = jnp.zeros((8, LANE), F32)
    for place in range(4):
        gradient = join_chunks(one[place], two[place]).reshape(firsts[place].shape)
        new_firsts[place][...] = FIRST_BETA * firsts[place][...] + (1.0 - FIRST_BETA) * gradient
        new_seconds[place][...] = (
            SECOND_BETA * seconds[place][...] + (1.0 - SECOND_BETA) * gradient * gradient
        )


def apply_kernel(narrow, *refs):
    index_ref = refs[0]
    block_refs = refs[1 : 1 + narrow]
    at = 1 + narrow
    weight_in, weight_mix, weight_out, weight_bias = refs[at : at + 4]
    one, two = refs[at + 4 : at + 8], refs[at + 8 : at + 12]
    flow_ref, flow_first_ref, flow_second_ref = refs[at + 12 : at + 15]
    at = at + 15
    update_in, update_out = join_chunks(one[0], two[0]), join_chunks(one[2], two[2])
    update_bias = join_chunks(one[3], two[3]).reshape(LEVELS, 2, LANE)
    update_mix = [two[1].at[0], two[1].at[1], one[1].at[0]]
    (
        new_in,
        new_mix,
        new_out,
        new_bias,
        new_flow,
        half_in,
        half_mix,
        half_out,
        flow_moment,
        flow_square,
        weight_norm_ref,
        update_norm_ref,
        loss_ref,
        valid_ref,
        order_ref,
    ) = refs[at:]
    for part in range(narrow):
        order_ref[index_ref[0, 0] ^ part] = block_refs[part][...]
    whole = order_ref[0]
    for part in range(1, narrow):
        whole = whole + order_ref[part]
    sums = whole[0:16]
    flow_grad = whole[16 : 16 + FLOW_ROWS]
    loss = whole[16 + FLOW_ROWS : 17 + FLOW_ROWS, 0:1]
    valid_dims = 3.0 * block_refs[0][16 + FLOW_ROWS : 17 + FLOW_ROWS, 1:2]
    scale = 1.0 / (valid_dims * LOG_TWO)
    flow = to_flat_rows(flow_ref[...])
    size = flow_ref.shape[0]
    place = iota((FLOW_ROWS, LANE), 0) * LANE + iota((FLOW_ROWS, LANE), 1)
    flow_grad = jnp.where(place < size, flow_grad * scale, 0.0)
    first_new, second_new, update = moments(
        flow, flow_grad, to_flat_rows(flow_first_ref[...]), to_flat_rows(flow_second_ref[...])
    )
    weight_norms = [jnp.sqrt(sums[index : index + 1, 0:1]) for index in range(12)]
    update_norms = [jnp.sqrt(sums[index : index + 1, 1:2]) for index in range(12)]
    masks = flow_masks()
    for mask in masks:
        weight_norms.append(jnp.sqrt(total_of(jnp.where(mask, flow * flow, 0.0))))
        update_norms.append(jnp.sqrt(total_of(jnp.where(mask, update * update, 0.0))))
    rates = [
        LEARN_RATE * (weight_norm / update_norm)
        for weight_norm, update_norm in zip(weight_norms, update_norms)
    ]
    rate = jnp.zeros((FLOW_ROWS, LANE), F32)
    for mask, value in zip(masks, rates[12:]):
        rate = jnp.where(mask, value, rate)
    new_flow[...] = from_flat_rows(flow - rate * update, size)
    flow_moment[...] = from_flat_rows(first_new, size)
    flow_square[...] = from_flat_rows(second_new, size)
    row = iota(weight_in.shape, 0)
    edge_one, edge_two = in_rows(0), in_rows(0) + in_rows(1)
    rate = jnp.where(row < edge_one, rates[0], jnp.where(row < edge_two, rates[1], rates[2]))
    fresh = weight_in[...] - rate * update_in
    new_in[...] = fresh
    half_in[...] = fresh.astype(BF16)
    for level in range(LEVELS):
        fresh = weight_mix[level] - rates[3 + level] * update_mix[level][...]
        new_mix[level] = fresh
        half_mix[level] = fresh.astype(BF16)
    row = iota(weight_out.shape, 0)
    edge_one, edge_two = 9 * chan(0), 9 * chan(0) + 9 * chan(1)
    rate = jnp.where(row < edge_one, rates[6], jnp.where(row < edge_two, rates[7], rates[8]))
    fresh = weight_out[...] - rate * update_out
    new_out[...] = fresh
    half_out[...] = fresh.astype(BF16)
    for level in range(LEVELS):
        new_bias[level] = weight_bias[level] - rates[9 + level] * update_bias[level]
    lane = iota((1, LANE), 1)
    for ref, norms in ((weight_norm_ref, weight_norms), (update_norm_ref, update_norms)):
        held = jnp.zeros((1, LANE), F32)
        for index in range(15):
            held = jnp.where(lane == index, norms[index], held)
        ref[...] = held[:, :15].reshape(15)
    loss_ref[...] = loss / LOG_TWO + 8.0 * valid_dims
    valid_ref[...] = valid_dims


def spec_vmem():
    return pl.BlockSpec(memory_space=pltpu.VMEM)


def spec_smem():
    return pl.BlockSpec(memory_space=pltpu.SMEM)


def call(kernel, outs, scalars, arrays, scratch=(), name=None, after=(), vmem=20):
    number = len(scalars) + len(arrays)

    def run(*refs):
        kernel(*refs[:number], *refs[number + len(after) :])

    return pl.pallas_call(
        run,
        out_shape=tuple(jax.ShapeDtypeStruct(shape, dtype) for shape, dtype in outs),
        in_specs=[spec_smem()] * len(scalars)
        + [spec_vmem()] * len(arrays)
        + [pl.BlockSpec(memory_space=pl.ANY)] * len(after),
        out_specs=tuple(spec_vmem() for _ in outs),
        scratch_shapes=list(scratch),
        compiler_params=pltpu.CompilerParams(vmem_limit_bytes=vmem * 1024 * 1024),
        cost_estimate=pl.CostEstimate(
            flops=1000, bytes_accessed=1000, transcendentals=0
        ),
        name=name,
    )(*scalars, *arrays, *after)


def run_pack(valid_shape, conv_in, mixer, conv_out, hidden_bias):
    cut = sum(pack_rows(level) for level in CHUNKS[0])
    rows = pack_start(-1) + 16
    outs = [((size, LANE), BF16) for size in (rows, cut, rows - cut)]
    return call(pack_kernel, outs, (valid_shape,), (conv_in, mixer, conv_out, hidden_bias), name="pack", vmem=56)


def run_flow_pre(noise_seeds, valid_shape, images, flow_params, packed):
    count = images.shape[1]
    outs = [((stage_rows(level)["rows"], positions(level, count)), F32) for level in range(LEVELS)]
    outs.append((packed.shape, BF16))
    return call(
        flow_pre_kernel,
        outs,
        (noise_seeds, valid_shape),
        (images, flow_params, packed),
        name="flow_pre",
    )


def run_nets(chunk, images, index, weights, stages, after):
    narrow = lax.axis_size("narrow")
    outs = [((narrow // 2, 4 * quarter_rows(chunk), LANE), F32)] * 2
    scratch = []
    for level in CHUNKS[chunk]:
        count = positions(level, images)
        outs = outs + [((stage_rows(level)["result_rows"], count), F32)]
        scratch = scratch + net_scratch(count)
    return call(
        functools.partial(nets_kernel, chunk, images, narrow, len(weights) > narrow),
        outs,
        (),
        [index] + list(weights) + [stages[level] for level in CHUNKS[chunk]],
        scratch,
        name="nets_" + "ab"[chunk],
        after=after,
    )


def net_scratch(count):
    return [
        pltpu.VMEM((HID, HID), BF16),
        pltpu.VMEM((HID, count), F32),
        pltpu.VMEM((HID, count), F32),
        pltpu.VMEM((HID, count), BF16),
        pltpu.VMEM((HID, count), BF16),
    ]


def run_flow(images, weights, stages, results, after):
    (out,) = call(
        functools.partial(flow_kernel, images, len(weights)),
        [((FLOW_ROWS + STATS_ROWS, LANE), F32)],
        (),
        list(stages) + list(results) + list(weights),
        name="flow_back",
        after=after,
    )
    return out


def swap(values, wide, narrow):
    width = lax.axis_size("narrow")
    mask = wide * width + narrow
    count = lax.axis_size("wide") * width
    return lax.ppermute(values, ("wide", "narrow"), [(place, place ^ mask) for place in range(count)])


class Summation:
    def __init__(self, chunk, index, send, after):
        self.chunk, self.index = chunk, index
        rows, more = quarter_rows(chunk), flow_part(chunk)
        self.kept, self.others = send, ()
        sent = self.run(send_kernel, [((piece_rows(2 * rows), LANE), BF16)] * 4, "send", after)
        self.token = sent[0]
        self.others = [swap(piece, 0, 1) for piece in sent]
        self.own_piece = [((piece_rows(FLOW_ROWS), LANE), BF16)] if more else []
        self.own = ()
        self.square_piece = ((piece_rows(2 * rows + more), LANE), BF16)
        self.piece = ((piece_rows(rows + more), LANE), BF16)

    def run(self, kernel, outs, name, after, scratch=(), extra=(), more=()):
        return call(
            functools.partial(kernel, self.chunk, *more),
            outs,
            (),
            (self.index, self.kept, *extra, *self.others),
            scratch,
            name=name + "_" + "ab"[self.chunk],
            after=after,
        )

    def square(self, keep, flow, after):
        rows = 2 * quarter_rows(self.chunk)
        self.kept, *rest = call(
            functools.partial(square_kernel, self.chunk),
            [((rows, LANE), F32)] + self.own_piece + [self.square_piece] * 3,
            (),
            (self.index, keep, *self.others, *flow),
            [pltpu.VMEM((2, 2 * rows, LANE), F32)],
            name="square_" + "ab"[self.chunk],
            after=after,
        )
        self.own, sent = tuple(rest[:-3]), rest[-3:]
        partners = {1: (0, 2), 2: (1, 0), 3: (1, 2)}
        order = SQUARE_ORDER[self.chunk]
        self.others = [swap(sent[flip - 1], *partners[flip]) for flip in order]
        return self.kept

    def column(self, after):
        rows = quarter_rows(self.chunk)
        self.kept, *rest = self.run(
            column_kernel,
            [((rows, LANE), F32)] + self.own_piece + [self.piece],
            "column",
            after,
            [pltpu.VMEM((2 * rows, LANE), F32)],
            self.own,
        )
        self.own = tuple(rest[:-1])
        self.others = [swap(rest[-1], 2, 0)]
        return self.kept

    def code(self, after):
        (self.kept,) = self.run(code_kernel, [self.piece], "code", after, (), self.own)
        self.others = [swap(self.kept, 4, 0)]
        return self.kept

    def spread(self, after):
        step = 4
        while step < lax.axis_size("wide"):
            final = 2 * step >= lax.axis_size("wide")
            shapes = [self.piece]
            if final and flow_part(self.chunk):
                rows = quarter_rows(self.chunk)
                shapes = [((piece_rows(rows), LANE), BF16), ((FLOW_ROWS + STATS_ROWS, LANE), F32)]
            self.kept, *self.flow = self.run(
                recode_kernel, shapes, "recode_%d" % step, after, (), (), (final,)
            )
            step = 2 * step
            if step < lax.axis_size("wide"):
                self.others = [swap(self.kept, step, 0)]
        token = self.kept
        if flow_part(self.chunk):
            partners = {1: 2, 2: 1, 3: 3}
            self.others = [swap(self.kept, partners[flip], 0) for flip in RETURN_ORDER]
        else:
            self.others = [swap(self.kept, 2, 0)]
            (self.kept,) = self.run(pair_kernel, [((2,) + self.piece[0], BF16)], "pair", ())
            self.others = [swap(self.kept, 1, 0)]
        return token

    def decode(self, after):
        shape = [((4 * quarter_rows(self.chunk), LANE), F32)]
        if flow_part(self.chunk):
            return self.run(decode_kernel, shape, "decode", after)
        return self.run(decode_pairs_kernel, shape, "decode", after)


def body(
    images,
    noise_seeds,
    valid_shape,
    conv_in,
    mixer,
    conv_out,
    hidden_bias,
    flow_params,
    conv_in_first,
    mixer_first,
    conv_out_first,
    bias_first,
    flow_first,
    conv_in_second,
    mixer_second,
    conv_out_second,
    bias_second,
    flow_second,
):
    count = images.shape[1]
    conv_out, conv_out_first, conv_out_second = conv_out.T, conv_out_first.T, conv_out_second.T
    row = lax.broadcasted_iota(jnp.int32, (8, LANE), 0)
    index = jnp.where(row == 0, lax.axis_index("narrow"), lax.axis_index("wide")).astype(jnp.int32)
    narrow = lax.axis_size("narrow")
    packed, *parts = run_pack(valid_shape, conv_in, mixer, conv_out, hidden_bias)
    paired = swap(packed, 0, 1)
    crossed = [swap(part, 0, 2) for part in parts]
    *stages, own = run_flow_pre(noise_seeds, valid_shape, images, flow_params, packed)
    cut = first_rows(CHUNKS[0][0]) + HID
    shapes = [((rows, LANE), BF16) for rows in (cut, crossed[0].shape[0] - cut)]
    head, tail, *stages = call(
        split_copy_kernel,
        shapes + [(stage.shape, F32) for stage in stages],
        (),
        (crossed[0], *stages),
        name="copy_a",
    )
    gathered = (own, paired, crossed[0], swap(head, 0, 1), swap(tail, 0, 1))
    keep_one, send, *last = run_nets(0, count, index, gathered, stages, ())
    one = Summation(0, index, send, ())
    token = one.square(keep_one, (), ())
    (copied,) = call(
        copy_kernel,
        [(crossed[1].shape, BF16)],
        (),
        (crossed[1],),
        name="copy_b",
        after=(token,),
    )
    gathered = (own, paired, crossed[1], swap(copied, 0, 1))
    keep_two, send, *results = run_nets(1, count, index, gathered, stages, (copied,))
    flow = run_flow(count, gathered, stages, results + last, (keep_two,))
    token = one.column((flow,))
    two = Summation(1, index, send, (token,))
    token = two.square(keep_two, (flow,), ())
    token = one.code((token,))
    token = one.spread((token,))
    token = two.column((token,))
    token = two.code((token,))
    token = two.spread((token,))
    weights = (conv_in, mixer, conv_out, hidden_bias)
    firsts = (conv_in_first, mixer_first, conv_out_first, bias_first)
    seconds = (conv_in_second, mixer_second, conv_out_second, bias_second)
    shapes = [(weight.shape, F32) for weight in weights]

    def norms(chunk, arrays):
        spans = [stop - start for start, stop in chunk_spans(chunk)]
        rows = (spans[0], spans[1], spans[3])
        in_shape, out_shape, bias_shape = [((count, LANE), F32) for count in rows]
        part = [in_shape, ((spans[2], HID, LANE), F32), out_shape, bias_shape]
        size = 16 if chunk == 0 else 16 + FLOW_ROWS + STATS_ROWS
        *outs, block = call(
            functools.partial(norm_kernel, chunk),
            part * 2 + [((size, LANE), F32)],
            (),
            tuple(arrays) + weights + firsts + seconds,
            name="norms_" + "ab"[chunk],
        )
        return tuple(outs[:4]), tuple(outs[4:]), block

    (part,) = one.decode((token,))
    (flow,) = two.flow
    grads_one, updates_one, sums = norms(0, (part, flow))
    (part,) = two.decode((sums,))
    grads_two, updates_two, block = norms(1, (part, flow, sums))
    blocks = [block] + [swap(block, 0, part) for part in range(1, narrow)]
    moved = call(
        moment_kernel,
        shapes * 2 + [((8, LANE), F32)],
        (),
        grads_one + grads_two + firsts + seconds,
        name="moments",
    )
    flow_shape = (flow_params.shape, F32)
    fresh = call(
        functools.partial(apply_kernel, narrow),
        shapes
        + [flow_shape]
        + [(weight.shape, BF16) for weight in weights[:3]]
        + [flow_shape, flow_shape, ((15,), F32), ((15,), F32), ((1, 1), F32), ((1, 1), F32)],

        (),
        (index,)
        + tuple(blocks)
        + weights
        + updates_one
        + updates_two
        + (flow_params, flow_first, flow_second),
        scratch=[pltpu.VMEM((narrow,) + block.shape, F32)],
        after=(moved[8],),
        name="apply",
    )
    return (
        fresh[0],
        fresh[1],
        fresh[2].T,
        fresh[3],
        fresh[4],
        moved[0],
        moved[1],
        moved[2].T,
        moved[3],
        fresh[8],
        moved[4],
        moved[5],
        moved[6].T,
        moved[7],
        fresh[9],
        fresh[5],
        fresh[6],
        fresh[7].T,
        fresh[10],
        fresh[11],
        fresh[12].reshape(()),
        fresh[13].reshape(()),
    )


def solution(mesh):
    placed = (
        P(None, ("wide", "narrow"), None),
        P(("wide", "narrow")),
        P(("wide", "narrow"), None),
        P(None, "narrow"),
        P(None, None, "narrow"),
        P("narrow", None),
        P(None, None, "narrow"),
        P(),
    )
    state = (P(None, "narrow"), P(None, None, "narrow"), P("narrow", None), P(None, None, "narrow"), P())
    return jax.shard_map(
        body,
        mesh=mesh,
        in_specs=placed + state + state,
        out_specs=state * 3 + state[:3] + (P(),) * 4,
        check_vma=False,
    )
```
